32 devices in a mesh: dp: 4 (over x, core), seq: 8 (over z, y).
Axes of the slice: x: 2, y: 2, z: 4, core: 2. Of those that a mesh axis runs over, the one named last changes fastest.
Arguments:
- hidden_in: bfloat16 [32, 2048, 576], P('dp', 'seq'), may hold values from -6 to 6
- span_order: int32 [16], replicated, may hold values from 0 to 15, each once
- attn_gain: bfloat16 [576], replicated, may hold values from 0.099609375 to 1.8984375
- q_weight: bfloat16 [576, 576], P('dp', 'seq'), may hold values from -0.25 to 0.25
- k_weight: bfloat16 [576, 192], P('dp', 'seq'), may hold values from -0.25 to 0.25
- v_weight: bfloat16 [576, 192], P('dp', 'seq'), may hold values from -0.25 to 0.25
- o_weight: bfloat16 [576, 576], P('dp', 'seq'), may hold values from -1.5 to 1.5
- mlp_gain: bfloat16 [576], replicated, may hold values from 0.099609375 to 1.8984375
- gate_weight: bfloat16 [576, 1536], P('dp', 'seq'), may hold values from -0.25 to 0.25
- up_weight: bfloat16 [576, 1536], P('dp', 'seq'), may hold values from -0.25 to 0.25
- down_weight: bfloat16 [1536, 576], P('dp', 'seq'), may hold values from -0.15625 to 0.15625
- out_grad: bfloat16 [32, 2048, 576], P('dp', 'seq'), may hold values from -6 to 6
Outputs:
- hidden_out: bfloat16 [32, 2048, 576], P('dp', 'seq')
- grad_in: float32 [32, 2048, 576], P('dp', 'seq')
- attn_gain_grad: float32 [576], replicated
- q_weight_grad: float32 [576, 576], P('dp', 'seq')
- k_weight_grad: float32 [576, 192], P('dp', 'seq')
- v_weight_grad: float32 [576, 192], P('dp', 'seq')
- o_weight_grad: float32 [576, 576], P('dp', 'seq')
- mlp_gain_grad: float32 [576], replicated
- gate_weight_grad: float32 [576, 1536], P('dp', 'seq')
- up_weight_grad: float32 [576, 1536], P('dp', 'seq')
- down_weight_grad: float32 [1536, 576], P('dp', 'seq')
The draws below stay inside these ranges and needn't reach their ends.
Inputs may be any that keep to these rules, and one draw needn't show every extreme that they name: `span_order`: every span number appears exactly once; the same order holds for every sequence.
All inputs are finite; a program needn't handle non-finite values.
Results may differ from the reference program's by a relative error of at most 0.02.
Values may be sent and summed in bfloat16 or wider, within the bound.
A program may use at most 256 MiB of HBM per device.

```python
import jax
import jax.numpy as jnp
from jax import lax

D = 576
HEADS = 9
KV_HEADS = 3
HD = 64
FF = 1536
LENGTH = 2048
SEQS = 32
SPANS = 16
SPAN = 128
KVD = 192


def steps_of(key, extent, split, low, top_value):
    def one(axis_at, blocks):
        heights = jax.random.uniform(jax.random.fold_in(jax.random.fold_in(key, 6), axis_at), (blocks,), jnp.float32, low / len(split), top_value / len(split))
        return jnp.repeat(jnp.exp(heights), extent[axis_at] // blocks).reshape((-1,) + (1,) * (len(extent) - axis_at - 1))

    loudness = one(*split[0])
    for cut in split[1:]:
        loudness = loudness * one(*cut)
    return loudness


def scatter_about(stream_key, dims, scale, most, shards=(), held_as=jnp.bfloat16):
    entries = jax.random.normal(stream_key, dims, jnp.float32) * scale
    if len(shards) > 0:
        entries = steps_of(stream_key, dims, shards, -0.22, 0.18) * entries
    return jnp.clip(entries, min=-most, max=most).astype(held_as)


def setup_inputs(seed: int = 0) -> dict:
    streams_of = jax.random.split(jax.random.key(seed), 13)
    hidden_in = scatter_about(streams_of[0], (SEQS, LENGTH, D), 1.0, 6.0, ((0, 4), (1, 8)))
    span_order = jax.random.permutation(streams_of[1], SPANS).astype(jnp.int32)
    attn_gain = jnp.clip(1.0 + 0.18 * jax.random.normal(streams_of[2], (D,), jnp.float32), 0.099609375, 1.8984375).astype(jnp.bfloat16)
    q_weight = scatter_about(streams_of[3], (D, D), D ** -0.5, 0.25, ((0, 4), (1, 8)))
    k_weight = scatter_about(streams_of[4], (D, KVD), D ** -0.5, 0.25, ((0, 4), (1, 8)))
    v_weight = scatter_about(streams_of[5], (D, KVD), D ** -0.5, 0.25, ((0, 4), (1, 8)))
    o_weight = scatter_about(streams_of[6], (D, D), (HD // 4) ** -0.5, 1.5, ((0, 4), (1, 8)))
    mlp_gain = jnp.clip(1.0 + 0.18 * jax.random.normal(streams_of[7], (D,), jnp.float32), 0.099609375, 1.8984375).astype(jnp.bfloat16)
    gate_weight = scatter_about(streams_of[8], (D, FF), D ** -0.5, 0.25, ((0, 4), (1, 8)))
    up_weight = scatter_about(streams_of[9], (D, FF), D ** -0.5, 0.25, ((0, 4), (1, 8)))
    down_weight = scatter_about(streams_of[10], (FF, D), FF ** -0.5, 0.15625, ((0, 4), (1, 8)))
    out_grad = scatter_about(streams_of[11], (SEQS, LENGTH, D), 1.0, 6.0, ((0, 4), (1, 8)))
    return {"hidden_in": hidden_in, "span_order": span_order, "attn_gain": attn_gain, "q_weight": q_weight, "k_weight": k_weight, "v_weight": v_weight, "o_weight": o_weight, "mlp_gain": mlp_gain, "gate_weight": gate_weight, "up_weight": up_weight, "down_weight": down_weight, "out_grad": out_grad}


@jax.custom_vjp
def low(v):
    return lax.optimization_barrier(v.astype(jnp.bfloat16)).astype(jnp.float32)

@jax.custom_vjp
def low_back(v):
    return v

def low_keep(v):
    return (low(v), None)

def low_pass(kept, grad):
    return (grad,)

def back_keep(v):
    return (v, None)

def back_low(kept, grad):
    return (low(grad),)
low.defvjp(low_keep, low_pass)
low_back.defvjp(back_keep, back_low)
eps_norm = 1e-05
rope_base = 100000.0
neg_big = -1e+30
highest = lax.Precision.HIGHEST

def matmul(left, right):
    return jnp.dot(left, right, precision=highest, preferred_element_type=jnp.float32)

def positions(span_order):
    slot_ids = jnp.arange(LENGTH, dtype=jnp.int32)
    return (span_order[slot_ids // SPAN] * SPAN + slot_ids % SPAN).astype(jnp.int32)

def rope_tables(slot_pos):
    half_width = HD // 2
    inv_freq = rope_base ** (-(jnp.arange(half_width, dtype=jnp.float32) * 2.0) / HD)
    angles = slot_pos.astype(jnp.float32)[:, None] * inv_freq[None, :]
    cosine = jnp.concatenate([jnp.cos(angles), jnp.cos(angles)], axis=1)
    sine_tab = jnp.concatenate([jnp.sin(angles), jnp.sin(angles)], axis=1)
    return (cosine[:, None, :], sine_tab[:, None, :])

def rotate(vector, cosine, sine_tab):
    half_width = vector.shape[-1] // 2
    turned = jnp.concatenate([-vector[..., half_width:], vector[..., :half_width]], axis=-1)
    return vector * cosine + turned * sine_tab

def rms_norm(vector, gain_vec):
    return vector * lax.rsqrt(lax.optimization_barrier(jnp.mean(vector * vector, axis=-1, keepdims=True)) + eps_norm) * gain_vec

def attention(query_rot, key_rot, value_low, slot_pos):
    group_size = HEADS // KV_HEADS
    block_rows = min(512, LENGTH)
    score_scale = HD ** (-0.5)
    query_grp = query_rot.reshape(LENGTH // block_rows, block_rows, KV_HEADS, group_size, HD)
    pos_blocks = slot_pos.reshape(LENGTH // block_rows, block_rows)

    @jax.checkpoint
    def attend(q_block):
        queries, query_pos = q_block
        scores = jnp.einsum('rkgd,lkd->kgrl', queries, key_rot, precision=highest) * score_scale
        scores = low_back(scores)
        allowed = query_pos[:, None] >= slot_pos[None, :]
        scores = jnp.where(allowed, scores, neg_big)
        row_peak = lax.optimization_barrier(jnp.max(scores, axis=-1, keepdims=True))
        exp_scores = jnp.exp(scores - row_peak)
        attn_probs = exp_scores / lax.optimization_barrier(jnp.sum(exp_scores, axis=-1, keepdims=True))
        mixed = jnp.einsum('kgrl,lkd->rkgd', low(attn_probs), value_low, precision=highest)
        return low(low_back(mixed))
    mixed = lax.map(attend, (query_grp, pos_blocks))
    return mixed.reshape(LENGTH, HEADS * HD)

def decoder_layer(tokens_f, weights, tables):
    attn_gain, q_weight, k_weight, v_weight, o_weight, mlp_gain, gate_weight, up_weight, down_weight = weights
    cosine, sine_tab, slot_pos = tables
    normed_one = low(rms_norm(tokens_f, attn_gain))
    query = low_back(matmul(normed_one, q_weight))
    key_lin = low_back(matmul(normed_one, k_weight))
    value_lin = low_back(matmul(normed_one, v_weight))
    query_rot = low(rotate(query.reshape(LENGTH, HEADS, HD), cosine, sine_tab))
    key_rot = low(rotate(key_lin.reshape(LENGTH, KV_HEADS, HD), cosine, sine_tab))
    value_low = low(value_lin.reshape(LENGTH, KV_HEADS, HD))
    mixed = attention(query_rot, key_rot, value_low, slot_pos)
    attn_out = low_back(matmul(mixed, o_weight))
    hidden_mid = tokens_f + attn_out
    normed_two = low(rms_norm(hidden_mid, mlp_gain))
    gate = low_back(matmul(normed_two, gate_weight))
    up_lin = low_back(matmul(normed_two, up_weight))
    inner = low(gate * jax.nn.sigmoid(gate) * up_lin)
    return hidden_mid + low_back(matmul(inner, down_weight))

def reference(hidden_in, span_order, attn_gain, q_weight, k_weight, v_weight, o_weight, mlp_gain, gate_weight, up_weight, down_weight, out_grad):
    slot_pos = positions(span_order)
    cosine, sine_tab = rope_tables(slot_pos)
    params = (attn_gain.astype(jnp.float32), q_weight.astype(jnp.float32), k_weight.astype(jnp.float32), v_weight.astype(jnp.float32), o_weight.astype(jnp.float32), mlp_gain.astype(jnp.float32), gate_weight.astype(jnp.float32), up_weight.astype(jnp.float32), down_weight.astype(jnp.float32))

    def forward(inputs, weights):
        one_sequence = jax.checkpoint(lambda tokens_f: decoder_layer(tokens_f, weights, (cosine, sine_tab, slot_pos)))
        return lax.map(one_sequence, inputs)
    result, pullback = jax.vjp(forward, hidden_in.astype(jnp.float32), params)
    grad_in, grad_tuple = pullback(out_grad.astype(jnp.float32))
    return (result.astype(jnp.bfloat16), grad_in, grad_tuple[0], grad_tuple[1], grad_tuple[2], grad_tuple[3], grad_tuple[4], grad_tuple[5], grad_tuple[6], grad_tuple[7], grad_tuple[8])
```

```python
import functools

import jax
import jax.numpy as jnp
from jax import lax
from jax.experimental import pallas as pl
from jax.experimental.pallas import tpu as pltpu
from jax.sharding import PartitionSpec as P

HD = 64
MICRO = 2


eps_norm = 1e-05
rope_base = 100000.0
neg_big = -1e30


def slot_positions(slot_ids, span_order, span_len):
    span_ids = slot_ids // span_len
    span_hits = span_ids[:, None] == jnp.arange(span_order.shape[0], dtype=jnp.int32)[None, :]
    starts = jnp.sum(jnp.where(span_hits, span_order[None, :], 0), axis=1)
    return starts * span_len + slot_ids % span_len


def rope_tables(slot_pos):
    half_width = HD // 2
    inv_freq = rope_base ** (-(jnp.arange(half_width, dtype=jnp.float32) * 2.0) / HD)
    angles = slot_pos.astype(jnp.float32)[:, None] * inv_freq[None, :]
    cosine = jnp.concatenate([jnp.cos(angles), jnp.cos(angles)], axis=1)
    sine_tab = jnp.concatenate([jnp.sin(angles), jnp.sin(angles)], axis=1)
    return (cosine[:, None, :], sine_tab[:, None, :])


def rotate(vector, cosine, sine_tab):
    half_width = vector.shape[-1] // 2
    turned = jnp.concatenate([-vector[..., half_width:], vector[..., :half_width]], axis=-1)
    return vector * cosine + turned * sine_tab


def rotate_back(grad_out, cosine, sine_tab):
    half_width = grad_out.shape[-1] // 2
    scaled = grad_out * sine_tab
    turned = jnp.concatenate([scaled[..., half_width:], -scaled[..., :half_width]], axis=-1)
    return grad_out * cosine + turned


def norm_back(vector, rstd_vec, gain_vec, grad_n):
    scaled = grad_n * gain_vec
    gain_term = jnp.sum(grad_n * vector * rstd_vec, axis=0)
    grad_vec = rstd_vec * scaled - vector * rstd_vec**3 * jnp.mean(
        scaled * vector, axis=-1, keepdims=True
    )
    return (grad_vec, gain_term)


def add_tuples(old_sums, new_terms):
    if old_sums is None:
        return tuple(new_terms)
    return tuple((old_sum + new_term for old_sum, new_term in zip(old_sums, new_terms)))


def shards_general(
    hidden_in,
    span_order,
    attn_gain,
    q_weight,
    k_weight,
    v_weight,
    o_weight,
    mlp_gain,
    gate_weight,
    up_weight,
    down_weight,
    out_grad,
):
    local_seqs, row_count, model_width = hidden_in.shape
    seq_parts = lax.axis_size("seq")
    full_length = row_count * seq_parts
    span_len = full_length // (2 * seq_parts)
    per_micro = local_seqs // MICRO
    kv_width = k_weight.shape[1] * seq_parts
    kv_heads = kv_width // HD
    head_count = model_width // HD
    group_size = head_count // kv_heads
    tok_count = per_micro * row_count
    score_scale = HD ** (-0.5)
    own_slots = lax.axis_index("seq") * row_count + jnp.arange(row_count, dtype=jnp.int32)
    own_pos = slot_positions(own_slots, span_order, span_len)
    all_pos = slot_positions(jnp.arange(full_length, dtype=jnp.int32), span_order, span_len)
    allowed = own_pos[:, None] >= all_pos[None, :]
    cos_own, sin_own = rope_tables(own_pos)
    gain_attn = attn_gain.astype(jnp.float32)
    gain_mlp = mlp_gain.astype(jnp.float32)

    def attend(inputs):
        queries, key_rows, value_rows = inputs
        query_grp = queries.reshape(row_count, kv_heads, group_size, HD)
        key_grp = key_rows.reshape(full_length, kv_heads, HD)
        value_grp = value_rows.reshape(full_length, kv_heads, HD)
        scores = (
            jnp.einsum("rkgd,lkd->kgrl", query_grp, key_grp, preferred_element_type=jnp.float32)
            * score_scale
        )
        scores = jnp.where(allowed, scores, neg_big)
        row_peak = jnp.max(scores, axis=-1, keepdims=True)
        exp_scores = jnp.exp(scores - row_peak)
        row_total = jnp.sum(exp_scores, axis=-1, keepdims=True)
        attn_probs = exp_scores / row_total
        log_total = row_peak + jnp.log(row_total)
        mixed = jnp.einsum(
            "kgrl,lkd->rkgd",
            attn_probs.astype(jnp.bfloat16),
            value_grp,
            preferred_element_type=jnp.float32,
        )
        return (mixed.astype(jnp.bfloat16).reshape(row_count, model_width), log_total)

    def attend_back(inputs):
        queries, key_rows, value_rows, grad_mix, log_total = inputs
        query_grp = queries.reshape(row_count, kv_heads, group_size, HD)
        key_grp = key_rows.reshape(full_length, kv_heads, HD)
        value_grp = value_rows.reshape(full_length, kv_heads, HD)
        grad_grp = grad_mix.reshape(row_count, kv_heads, group_size, HD)
        scores = (
            jnp.einsum("rkgd,lkd->kgrl", query_grp, key_grp, preferred_element_type=jnp.float32)
            * score_scale
        )
        scores = jnp.where(allowed, scores, neg_big)
        attn_probs = jnp.exp(scores - log_total)
        probs_low = attn_probs.astype(jnp.bfloat16)
        grad_probs = jnp.einsum(
            "rkgd,lkd->kgrl", grad_grp, value_grp, preferred_element_type=jnp.float32
        )
        row_delta = jnp.sum(attn_probs * grad_probs, axis=-1, keepdims=True)
        grad_scores = (attn_probs * (grad_probs - row_delta)).astype(jnp.bfloat16)
        grad_query_rot = (
            jnp.einsum("kgrl,lkd->rkgd", grad_scores, key_grp, preferred_element_type=jnp.float32)
            * score_scale
        )
        key_term = (
            jnp.einsum("kgrl,rkgd->lkd", grad_scores, query_grp, preferred_element_type=jnp.float32)
            * score_scale
        )
        value_term = jnp.einsum(
            "kgrl,rkgd->lkd", probs_low, grad_grp, preferred_element_type=jnp.float32
        )
        return (
            grad_query_rot.reshape(row_count, head_count, HD),
            key_term.reshape(full_length, kv_width),
            value_term.reshape(full_length, kv_width),
        )

    outputs = []
    in_grads = []
    totals = None
    for micro_idx in range(MICRO):
        first_seq = micro_idx * per_micro
        block_in = hidden_in[first_seq : first_seq + per_micro]
        block_grad = out_grad[first_seq : first_seq + per_micro]
        col_parts = (
            lax.all_gather(q_weight, "seq", axis=1, tiled=True),
            lax.all_gather(k_weight, "seq", axis=1, tiled=True),
            lax.all_gather(v_weight, "seq", axis=1, tiled=True),
            lax.all_gather(o_weight, "seq", axis=1, tiled=True),
            lax.all_gather(gate_weight, "seq", axis=1, tiled=True),
            lax.all_gather(up_weight, "seq", axis=1, tiled=True),
            lax.all_gather(down_weight, "seq", axis=1, tiled=True),
        )
        query_mat, key_mat, value_mat, out_mat, gate_mat, up_mat, down_mat = (
            lax.all_gather(col_parts[0], "dp", axis=0, tiled=True),
            lax.all_gather(col_parts[1], "dp", axis=0, tiled=True),
            lax.all_gather(col_parts[2], "dp", axis=0, tiled=True),
            lax.all_gather(col_parts[3], "dp", axis=0, tiled=True),
            lax.all_gather(col_parts[4], "dp", axis=0, tiled=True),
            lax.all_gather(col_parts[5], "dp", axis=0, tiled=True),
            lax.all_gather(col_parts[6], "dp", axis=0, tiled=True),
        )
        resid_in = block_in.astype(jnp.float32).reshape(tok_count, model_width)
        rstd_one = lax.rsqrt(jnp.mean(resid_in * resid_in, axis=-1, keepdims=True) + eps_norm)
        normed_one = (resid_in * rstd_one * gain_attn).astype(jnp.bfloat16)
        query_lin = jnp.dot(normed_one, query_mat, preferred_element_type=jnp.float32)
        key_lin = jnp.dot(normed_one, key_mat, preferred_element_type=jnp.float32)
        value_lin = jnp.dot(normed_one, value_mat, preferred_element_type=jnp.float32)
        query_rot = rotate(
            query_lin.reshape(per_micro, row_count, head_count, HD), cos_own, sin_own
        ).astype(jnp.bfloat16)
        key_rot = (
            rotate(key_lin.reshape(per_micro, row_count, kv_heads, HD), cos_own, sin_own)
            .astype(jnp.bfloat16)
            .reshape(per_micro, row_count, kv_width)
        )
        value_low = value_lin.astype(jnp.bfloat16).reshape(per_micro, row_count, kv_width)
        key_all, value_all = (
            lax.all_gather(key_rot, "seq", axis=1, tiled=True),
            lax.all_gather(value_low, "seq", axis=1, tiled=True),
        )
        mixed_seq, log_total = lax.map(attend, (query_rot, key_all, value_all))
        mixed_low = mixed_seq.reshape(tok_count, model_width)
        hidden_mid = resid_in + jnp.dot(mixed_low, out_mat, preferred_element_type=jnp.float32)
        rstd_two = lax.rsqrt(jnp.mean(hidden_mid * hidden_mid, axis=-1, keepdims=True) + eps_norm)
        normed_two = (hidden_mid * rstd_two * gain_mlp).astype(jnp.bfloat16)
        gate_lin = jnp.dot(normed_two, gate_mat, preferred_element_type=jnp.float32)
        up_lin = jnp.dot(normed_two, up_mat, preferred_element_type=jnp.float32)
        gate_sig = jax.nn.sigmoid(gate_lin)
        inner_low = (gate_lin * gate_sig * up_lin).astype(jnp.bfloat16)
        mlp_out = jnp.dot(inner_low, down_mat, preferred_element_type=jnp.float32)
        outputs.append(
            (hidden_mid + mlp_out).astype(jnp.bfloat16).reshape(per_micro, row_count, model_width)
        )
        col_again = (
            lax.all_gather(q_weight, "seq", axis=1, tiled=True),
            lax.all_gather(k_weight, "seq", axis=1, tiled=True),
            lax.all_gather(v_weight, "seq", axis=1, tiled=True),
            lax.all_gather(o_weight, "seq", axis=1, tiled=True),
            lax.all_gather(gate_weight, "seq", axis=1, tiled=True),
            lax.all_gather(up_weight, "seq", axis=1, tiled=True),
            lax.all_gather(down_weight, "seq", axis=1, tiled=True),
        )
        query_mat, key_mat, value_mat, out_mat, gate_mat, up_mat, down_mat = (
            lax.all_gather(col_again[0], "dp", axis=0, tiled=True),
            lax.all_gather(col_again[1], "dp", axis=0, tiled=True),
            lax.all_gather(col_again[2], "dp", axis=0, tiled=True),
            lax.all_gather(col_again[3], "dp", axis=0, tiled=True),
            lax.all_gather(col_again[4], "dp", axis=0, tiled=True),
            lax.all_gather(col_again[5], "dp", axis=0, tiled=True),
            lax.all_gather(col_again[6], "dp", axis=0, tiled=True),
        )
        key_all, value_all = (
            lax.all_gather(key_rot, "seq", axis=1, tiled=True),
            lax.all_gather(value_low, "seq", axis=1, tiled=True),
        )
        grad_top = block_grad.astype(jnp.float32).reshape(tok_count, model_width)
        grad_top_low = grad_top.astype(jnp.bfloat16)
        down_term = jnp.einsum(
            "tf,td->fd", inner_low, grad_top_low, preferred_element_type=jnp.float32
        )
        grad_inner = jnp.einsum(
            "td,fd->tf", grad_top_low, down_mat, preferred_element_type=jnp.float32
        )
        grad_gate = (grad_inner * up_lin * gate_sig * (1.0 + gate_lin * (1.0 - gate_sig))).astype(
            jnp.bfloat16
        )
        grad_up = (grad_inner * gate_lin * gate_sig).astype(jnp.bfloat16)
        gate_term = jnp.einsum(
            "td,tf->df", normed_two, grad_gate, preferred_element_type=jnp.float32
        )
        up_term = jnp.einsum("td,tf->df", normed_two, grad_up, preferred_element_type=jnp.float32)
        grad_normed_two = jnp.einsum(
            "tf,df->td", grad_gate, gate_mat, preferred_element_type=jnp.float32
        ) + jnp.einsum("tf,df->td", grad_up, up_mat, preferred_element_type=jnp.float32)
        grad_mid_norm, gain_mlp_term = norm_back(hidden_mid, rstd_two, gain_mlp, grad_normed_two)
        grad_mid = grad_top + grad_mid_norm
        grad_mid_low = grad_mid.astype(jnp.bfloat16)
        out_term = jnp.einsum(
            "td,te->de", mixed_low, grad_mid_low, preferred_element_type=jnp.float32
        )
        grad_mixed = jnp.einsum(
            "te,de->td", grad_mid_low, out_mat, preferred_element_type=jnp.float32
        ).astype(jnp.bfloat16)
        grad_query_rot, key_terms, value_terms = lax.map(
            attend_back,
            (
                query_rot,
                key_all,
                value_all,
                grad_mixed.reshape(per_micro, row_count, model_width),
                log_total,
            ),
        )
        key_share, value_share = (
            lax.psum_scatter(key_terms, "seq", scatter_dimension=1, tiled=True),
            lax.psum_scatter(value_terms, "seq", scatter_dimension=1, tiled=True),
        )
        grad_query = (
            rotate_back(grad_query_rot, cos_own, sin_own)
            .astype(jnp.bfloat16)
            .reshape(tok_count, model_width)
        )
        grad_key = (
            rotate_back(key_share.reshape(per_micro, row_count, kv_heads, HD), cos_own, sin_own)
            .astype(jnp.bfloat16)
            .reshape(tok_count, kv_width)
        )
        grad_value = value_share.astype(jnp.bfloat16).reshape(tok_count, kv_width)
        query_term = jnp.einsum(
            "td,te->de", normed_one, grad_query, preferred_element_type=jnp.float32
        )
        key_term = jnp.einsum("td,te->de", normed_one, grad_key, preferred_element_type=jnp.float32)
        value_term = jnp.einsum(
            "td,te->de", normed_one, grad_value, preferred_element_type=jnp.float32
        )
        grad_normed_one = (
            jnp.einsum("te,de->td", grad_query, query_mat, preferred_element_type=jnp.float32)
            + jnp.einsum("te,de->td", grad_key, key_mat, preferred_element_type=jnp.float32)
            + jnp.einsum("te,de->td", grad_value, value_mat, preferred_element_type=jnp.float32)
        )
        grad_in_norm, gain_attn_term = norm_back(resid_in, rstd_one, gain_attn, grad_normed_one)
        in_grads.append((grad_mid + grad_in_norm).reshape(per_micro, row_count, model_width))
        totals = add_tuples(
            totals,
            (
                query_term,
                key_term,
                value_term,
                out_term,
                gate_term,
                up_term,
                down_term,
                gain_attn_term,
                gain_mlp_term,
            ),
        )
    col_sums = (
        lax.psum_scatter(
            totals[0].astype(jnp.bfloat16), "seq", scatter_dimension=1, tiled=True
        ).astype(jnp.float32),
        lax.psum_scatter(
            totals[1].astype(jnp.bfloat16), "seq", scatter_dimension=1, tiled=True
        ).astype(jnp.float32),
        lax.psum_scatter(
            totals[2].astype(jnp.bfloat16), "seq", scatter_dimension=1, tiled=True
        ).astype(jnp.float32),
        lax.psum_scatter(
            totals[3].astype(jnp.bfloat16), "seq", scatter_dimension=1, tiled=True
        ).astype(jnp.float32),
        lax.psum_scatter(
            totals[4].astype(jnp.bfloat16), "seq", scatter_dimension=1, tiled=True
        ).astype(jnp.float32),
        lax.psum_scatter(
            totals[5].astype(jnp.bfloat16), "seq", scatter_dimension=1, tiled=True
        ).astype(jnp.float32),
        lax.psum_scatter(
            totals[6].astype(jnp.bfloat16), "seq", scatter_dimension=1, tiled=True
        ).astype(jnp.float32),
    )
    owned = (
        lax.psum_scatter(
            col_sums[0].astype(jnp.bfloat16), "dp", scatter_dimension=0, tiled=True
        ).astype(jnp.float32),
        lax.psum_scatter(
            col_sums[1].astype(jnp.bfloat16), "dp", scatter_dimension=0, tiled=True
        ).astype(jnp.float32),
        lax.psum_scatter(
            col_sums[2].astype(jnp.bfloat16), "dp", scatter_dimension=0, tiled=True
        ).astype(jnp.float32),
        lax.psum_scatter(
            col_sums[3].astype(jnp.bfloat16), "dp", scatter_dimension=0, tiled=True
        ).astype(jnp.float32),
        lax.psum_scatter(
            col_sums[4].astype(jnp.bfloat16), "dp", scatter_dimension=0, tiled=True
        ).astype(jnp.float32),
        lax.psum_scatter(
            col_sums[5].astype(jnp.bfloat16), "dp", scatter_dimension=0, tiled=True
        ).astype(jnp.float32),
        lax.psum_scatter(
            col_sums[6].astype(jnp.bfloat16), "dp", scatter_dimension=0, tiled=True
        ).astype(jnp.float32),
    )
    gain_sums = lax.psum((totals[7], totals[8]), ("dp", "seq"))
    return (
        jnp.concatenate(outputs, axis=0),
        jnp.concatenate(in_grads, axis=0),
        gain_sums[0],
        owned[0],
        owned[1],
        owned[2],
        owned[3],
        gain_sums[1],
        owned[4],
        owned[5],
        owned[6],
    )


F32 = jnp.float32
BF16 = jnp.bfloat16
VMEM_BYTES = 56 * 2**20


def dot(left, right, left_dim, right_dim):
    dims = (((left_dim,), (right_dim,)), ((), ()))
    return lax.dot_general(left, right, dims, preferred_element_type=F32)


def span_slice(inv_ref, place, span):
    return pl.ds(pl.multiple_of(inv_ref[place] * span, span), span)


def lane_pair(ref, rows, inv_ref, block, span):
    first = ref[rows, span_slice(inv_ref, 2 * block, span)]
    second = ref[rows, span_slice(inv_ref, 2 * block + 1, span)]
    return jnp.concatenate([first, second], axis=1)


def row_pair(ref, head, inv_ref, block, span):
    first = ref[head, span_slice(inv_ref, 2 * block, span), :]
    second = ref[head, span_slice(inv_ref, 2 * block + 1, span), :]
    return jnp.concatenate([first, second], axis=0)


def qkv_kernel(x_ref, gain_ref, w_ref, cos_ref, sin_ref, q_ref, kt_ref, vt_ref, k_ref, v_ref, *, heads, kv_heads):
    half = HD // 2
    x = x_ref[...].astype(F32)
    rstd = lax.rsqrt(jnp.mean(x * x, axis=-1, keepdims=True) + eps_norm)
    normed = (x * rstd * gain_ref[...]).astype(BF16)
    lin = dot(w_ref[...], normed, 1, 1)
    cos, sin = cos_ref[...], sin_ref[...]
    for head in range(heads + kv_heads):
        top = lin[HD * head : HD * head + half]
        low = lin[HD * head + half : HD * head + HD]
        rot = jnp.concatenate([top * cos - low * sin, low * cos + top * sin], axis=0).astype(BF16)
        if head < heads:
            q_ref[HD * head : HD * head + HD, :] = rot * jnp.asarray(HD**-0.5, BF16)
        else:
            kv = head - heads
            kt_ref[HD * kv : HD * kv + HD, :] = rot
            k_ref[kv] = rot.T
    for kv in range(kv_heads):
        first = HD * (heads + kv_heads + kv)
        val = lin[first : first + HD].astype(BF16)
        vt_ref[HD * kv : HD * kv + HD, :] = val
        v_ref[kv] = val.T


def project_qkv(x, gain, w_t, cos_t, sin_t, heads, kv_heads, block=512):
    tokens, width = x.shape
    col = lambda rows: pl.BlockSpec((rows, block), lambda i: (0, i))
    nat = pl.BlockSpec((kv_heads, block, HD), lambda i: (0, i, 0))
    return pl.pallas_call(
        functools.partial(qkv_kernel, heads=heads, kv_heads=kv_heads),
        grid=(tokens // block,),
        in_specs=[
            pl.BlockSpec((block, width), lambda i: (i, 0)),
            pl.BlockSpec((1, width), lambda i: (0, 0)),
            pl.BlockSpec(w_t.shape, lambda i: (0, 0)),
            col(HD // 2),
            col(HD // 2),
        ],
        out_specs=[col(heads * HD), col(kv_heads * HD), col(kv_heads * HD), nat, nat],
        out_shape=[
            jax.ShapeDtypeStruct((heads * HD, tokens), BF16),
            jax.ShapeDtypeStruct((kv_heads * HD, tokens), BF16),
            jax.ShapeDtypeStruct((kv_heads * HD, tokens), BF16),
            jax.ShapeDtypeStruct((kv_heads, tokens, HD), BF16),
            jax.ShapeDtypeStruct((kv_heads, tokens, HD), BF16),
        ],
        compiler_params=pltpu.CompilerParams(vmem_limit_bytes=VMEM_BYTES),
        cost_estimate=pl.CostEstimate(
            flops=4 * tokens * width * w_t.shape[0], bytes_accessed=tokens * 5000, transcendentals=0
        ),
        name="project_qkv",
    )(x, gain, w_t, cos_t, sin_t)


def attend_kernel(inv_ref, q_ref, k_ref, v_ref, o_ref, on_ref, l_ref, *, blocks, span, group):
    wide = 2 * span
    row = lax.broadcasted_iota(jnp.int32, (wide, wide), 0)
    col = lax.broadcasted_iota(jnp.int32, (wide, wide), 1)
    keep = row <= col

    def q_block(block, _):
        queries = [
            lane_pair(q_ref, slice(HD * h, HD * h + HD), inv_ref, block, span) for h in range(group)
        ]

        def scores_of(j):
            keys = row_pair(k_ref, 0, inv_ref, j, span)
            return tuple(dot(keys, query, 1, 0) for query in queries)

        def take(j, scores, carry, masked):
            values = lane_pair(v_ref, slice(0, HD), inv_ref, j, span)
            out = []
            for score, (peak, total, mixed) in zip(scores, carry):
                if masked:
                    score = jnp.where(keep, score, neg_big)
                new_peak = jnp.maximum(peak, jnp.max(score, axis=0, keepdims=True))
                prob = jnp.exp(score - new_peak)
                shrink = jnp.exp(peak - new_peak)
                total = total * shrink + jnp.sum(prob, axis=0, keepdims=True)
                mixed = mixed * shrink + dot(values, prob.astype(BF16), 1, 0)
                out.append((new_peak, total, mixed))
            return tuple(out)

        def body(j, carry):
            scores, state = carry
            following = scores_of(j + 1)
            return following, take(j, scores, state, False)

        empty = tuple(
            (jnp.full((1, wide), neg_big, F32), jnp.zeros((1, wide), F32), jnp.zeros((HD, wide), F32))
            for _ in range(group)
        )
        scores, state = lax.fori_loop(0, block, body, (scores_of(0), empty))
        state = take(block, scores, state, True)
        mixed = jnp.concatenate([m * (1.0 / t) for (_, t, m) in state], axis=0)
        logs = jnp.concatenate(
            [p + jnp.log(t) for (p, t, _) in state] + [jnp.zeros((8 - group, wide), F32)], axis=0
        )
        mixed_low = mixed.astype(BF16)
        natural = mixed.T.astype(BF16)
        for part in range(2):
            where = span_slice(inv_ref, 2 * block + part, span)
            cols = slice(part * span, part * span + span)
            o_ref[:, where] = mixed_low[:, cols]
            on_ref[0, where, :] = natural[cols, :]
            l_ref[0, :, where] = logs[:, cols]
        return 0

    lax.fori_loop(0, blocks, q_block, 0)


def attention_forward(inv, q_t, k_nat, v_t, span):
    tokens = q_t.shape[1]
    kv_heads = k_nat.shape[0]
    group = q_t.shape[0] // (kv_heads * HD)
    pairs = kv_heads * group * tokens * tokens
    wide_spec = pl.BlockSpec((group * HD, tokens), lambda g, i: (g, 0))
    nat_spec = pl.BlockSpec((1, tokens, HD), lambda g, i: (g, 0, 0))
    return pl.pallas_call(
        functools.partial(attend_kernel, blocks=tokens // (2 * span), span=span, group=group),
        grid_spec=pltpu.PrefetchScalarGridSpec(
            num_scalar_prefetch=1,
            grid=(kv_heads,),
            in_specs=[wide_spec, nat_spec, pl.BlockSpec((HD, tokens), lambda g, i: (g, 0))],
            out_specs=[
                wide_spec,
                pl.BlockSpec((1, tokens, group * HD), lambda g, i: (g, 0, 0)),
                pl.BlockSpec((1, 8, tokens), lambda g, i: (g, 0, 0)),
            ],
        ),
        out_shape=[
            jax.ShapeDtypeStruct(q_t.shape, BF16),
            jax.ShapeDtypeStruct((kv_heads, tokens, group * HD), BF16),
            jax.ShapeDtypeStruct((kv_heads, 8, tokens), F32),
        ],
        compiler_params=pltpu.CompilerParams(vmem_limit_bytes=VMEM_BYTES),
        cost_estimate=pl.CostEstimate(
            flops=16 * pairs * HD, bytes_accessed=tokens * 6000, transcendentals=pairs // 2
        ),
        name="attention_forward",
    )(inv, q_t, k_nat, v_t)


def attend_back_kernel(
    inv_ref, q_ref, kt_ref, k_ref, v_ref, o_ref, do_ref, l_ref, cos_ref, sin_ref,
    dq_ref, dk_ref, dv_ref, dk_sum, dv_sum, *, blocks, span, group,
):
    wide = 2 * span
    row = lax.broadcasted_iota(jnp.int32, (wide, wide), 0)
    col = lax.broadcasted_iota(jnp.int32, (wide, wide), 1)
    keep = row <= col
    half = HD // 2
    dk_sum[...] = jnp.zeros_like(dk_sum)
    dv_sum[...] = jnp.zeros_like(dv_sum)

    def rope_back(grad, cos, sin):
        top, low = grad[:half], grad[half:]
        return jnp.concatenate([top * cos + low * sin, low * cos - top * sin], axis=0)

    def q_block(step, _):
        block = blocks - 1 - step
        rows = [slice(HD * h, HD * h + HD) for h in range(group)]
        queries = [lane_pair(q_ref, r, inv_ref, block, span) for r in rows]
        grads = [lane_pair(do_ref, r, inv_ref, block, span) for r in rows]
        logs = lane_pair(l_ref.at[0], slice(None), inv_ref, block, span)
        deltas = [
            jnp.sum(
                lane_pair(o_ref, r, inv_ref, block, span).astype(F32) * grad.astype(F32),
                axis=0,
                keepdims=True,
            )
            for r, grad in zip(rows, grads)
        ]

        def take(j, dqs, masked):
            keys = row_pair(k_ref, 0, inv_ref, j, span)
            values = row_pair(v_ref, 0, inv_ref, j, span)
            keys_t = lane_pair(kt_ref, slice(0, HD), inv_ref, j, span)
            out = []
            dk = dv = None
            for h in range(group):
                prob = jnp.exp(dot(keys, queries[h], 1, 0) - logs[h : h + 1])
                if masked:
                    prob = jnp.where(keep, prob, 0.0)
                dprob = dot(values, grads[h], 1, 0)
                dscore = (prob * (dprob - deltas[h])).astype(BF16)
                dk_term = dot(queries[h], dscore, 1, 1)
                dv_term = dot(grads[h], prob.astype(BF16), 1, 1)
                dk = dk_term if dk is None else dk + dk_term
                dv = dv_term if dv is None else dv + dv_term
                out.append(dqs[h] + dot(keys_t, dscore, 1, 0))
            place = pl.ds(pl.multiple_of(j * wide, wide), wide)
            dk_sum[:, place] += dk
            dv_sum[:, place] += dv
            return tuple(out)

        dqs = tuple(jnp.zeros((HD, wide), F32) for _ in range(group))
        dqs = lax.fori_loop(0, block, lambda j, c: take(j, c, False), dqs)
        dqs = take(block, dqs, True)
        cos = lane_pair(cos_ref, slice(None), inv_ref, block, span)
        sin = lane_pair(sin_ref, slice(None), inv_ref, block, span)
        dq = jnp.concatenate([rope_back(g * HD**-0.5, cos, sin) for g in dqs], axis=0).astype(BF16)
        place = pl.ds(pl.multiple_of(block * wide, wide), wide)
        dk = rope_back(dk_sum[:, place], cos, sin).astype(BF16)
        dv = dv_sum[:, place].astype(BF16)
        for part in range(2):
            where = span_slice(inv_ref, 2 * block + part, span)
            cols = slice(part * span, part * span + span)
            dq_ref[:, where] = dq[:, cols]
            dk_ref[:, where] = dk[:, cols]
            dv_ref[:, where] = dv[:, cols]
        return 0

    lax.fori_loop(0, blocks, q_block, 0)


def attention_backward(inv, q_t, k_t, k_nat, v_nat, o_t, do_t, logs, cos_t, sin_t, span):
    tokens = q_t.shape[1]
    kv_heads = k_nat.shape[0]
    group = q_t.shape[0] // (kv_heads * HD)
    pairs = kv_heads * group * tokens * tokens
    wide_spec = pl.BlockSpec((group * HD, tokens), lambda g, i: (g, 0))
    kv_spec = pl.BlockSpec((HD, tokens), lambda g, i: (g, 0))
    nat_spec = pl.BlockSpec((1, tokens, HD), lambda g, i: (g, 0, 0))
    tab_spec = pl.BlockSpec((HD // 2, tokens), lambda g, i: (0, 0))
    return pl.pallas_call(
        functools.partial(attend_back_kernel, blocks=tokens // (2 * span), span=span, group=group),
        grid_spec=pltpu.PrefetchScalarGridSpec(
            num_scalar_prefetch=1,
            grid=(kv_heads,),
            in_specs=[
                wide_spec, kv_spec, nat_spec, nat_spec, wide_spec, wide_spec,
                pl.BlockSpec((1, 8, tokens), lambda g, i: (g, 0, 0)), tab_spec, tab_spec,
            ],
            out_specs=[wide_spec, kv_spec, kv_spec],
            scratch_shapes=[pltpu.VMEM((HD, tokens), F32), pltpu.VMEM((HD, tokens), F32)],
        ),
        out_shape=[
            jax.ShapeDtypeStruct(q_t.shape, BF16),
            jax.ShapeDtypeStruct(k_t.shape, BF16),
            jax.ShapeDtypeStruct(k_t.shape, BF16),
        ],
        compiler_params=pltpu.CompilerParams(vmem_limit_bytes=VMEM_BYTES),
        cost_estimate=pl.CostEstimate(
            flops=32 * pairs * HD, bytes_accessed=tokens * 9000, transcendentals=pairs // 2
        ),
        name="attention_backward",
    )(inv, q_t, k_t, k_nat, v_nat, o_t, do_t, logs, cos_t, sin_t)


def mlp_kernel(
    x_ref, mixed_ref, mixed_t_ref, dy_ref, gain_ref, o_ref, gate_ref, up_ref, down_ref,
    out_ref, dmid_ref, dmixed_ref, o_grad_ref, gate_grad_ref, up_grad_ref, down_grad_ref, gain_grad_ref,
    o_sum, gate_sum, up_sum, down_sum, gain_sum, *, chunk,
):
    step, steps = pl.program_id(0), pl.num_programs(0)
    groups, _, group_width = mixed_ref.shape
    ff = gate_ref.shape[1]

    @pl.when(step == 0)
    def _():
        o_sum[...] = jnp.zeros_like(o_sum)
        gate_sum[...] = jnp.zeros_like(gate_sum)
        up_sum[...] = jnp.zeros_like(up_sum)
        down_sum[...] = jnp.zeros_like(down_sum)
        gain_sum[...] = jnp.zeros_like(gain_sum)

    gain = gain_ref[...]
    mid = x_ref[...].astype(F32)
    for g in range(groups):
        mid += dot(mixed_ref[g], o_ref[g * group_width : (g + 1) * group_width, :], 1, 0)
    rstd = lax.rsqrt(jnp.mean(mid * mid, axis=-1, keepdims=True) + eps_norm)
    normed = (mid * rstd * gain).astype(BF16)
    normed_t = normed.T
    dy = dy_ref[...]
    dy_t = dy.T
    mlp_out = jnp.zeros_like(mid)
    dnormed = jnp.zeros_like(mid)
    for first in range(0, ff, chunk):
        cols = slice(first, first + chunk)
        gate = dot(normed, gate_ref[:, cols], 1, 0)
        up = dot(normed, up_ref[:, cols], 1, 0)
        dinner = dot(dy, down_ref[:, cols], 1, 0)
        sig = 1.0 / (1.0 + jnp.exp(-gate))
        silu = gate * sig
        inner = (silu * up).astype(BF16)
        dup = (dinner * silu).astype(BF16)
        dgate = (dinner * up * sig * (1.0 + gate * (1.0 - sig))).astype(BF16)
        mlp_out += dot(inner, down_ref[:, cols], 1, 1)
        dnormed += dot(dgate, gate_ref[:, cols], 1, 1)
        dnormed += dot(dup, up_ref[:, cols], 1, 1)
        down_sum[:, cols] += dot(dy_t, inner, 1, 0)
        gate_sum[:, cols] += dot(normed_t, dgate, 1, 0)
        up_sum[:, cols] += dot(normed_t, dup, 1, 0)
    out_ref[...] = (mid + mlp_out).astype(BF16)
    scaled_mid = mid * rstd
    gain_sum[...] += jnp.sum((dnormed * scaled_mid).reshape(-1, 8, mid.shape[1]), axis=0)
    scaled = dnormed * gain
    pull = jnp.mean(scaled * mid, axis=-1, keepdims=True)
    dmid = dy.astype(F32) + rstd * scaled - scaled_mid * (rstd * rstd * pull)
    dmid_ref[...] = dmid
    dmid_low = dmid.astype(BF16)
    o_sum[...] += dot(mixed_t_ref[...], dmid_low, 1, 0)
    dmixed_ref[...] = dot(o_ref[...], dmid_low, 1, 1).astype(BF16)

    @pl.when(step == steps - 1)
    def _():
        o_grad_ref[...] = o_sum[...].astype(BF16)
        gate_grad_ref[...] = gate_sum[...].astype(BF16)
        up_grad_ref[...] = up_sum[...].astype(BF16)
        down_grad_ref[...] = down_sum[...].astype(BF16)
        gain_grad_ref[...] = jnp.sum(gain_sum[...], axis=0, keepdims=True)


def mlp_both(x, mixed, mixed_t, dy, gain, o_w, gate_w, up_w, down_t, block=256, chunk=512):
    tokens, width = x.shape
    groups, _, group_width = mixed.shape
    ff = gate_w.shape[1]
    tok = pl.BlockSpec((block, width), lambda i: (i, 0))
    col = pl.BlockSpec((width, block), lambda i: (0, i))
    once = lambda shape: pl.BlockSpec(shape, lambda i: (0, 0), pipeline_mode=pl.Buffered(1))
    return pl.pallas_call(
        functools.partial(mlp_kernel, chunk=chunk),
        grid=(tokens // block,),
        in_specs=[
            tok,
            pl.BlockSpec((groups, block, group_width), lambda i: (0, i, 0)),
            col,
            tok,
            once((1, width)),
            once((width, width)),
            once((width, ff)),
            once((width, ff)),
            once((width, ff)),
        ],
        out_specs=[
            tok, tok, col,
            once((width, width)), once((width, ff)), once((width, ff)), once((width, ff)), once((1, width)),
        ],
        out_shape=[
            jax.ShapeDtypeStruct((tokens, width), BF16),
            jax.ShapeDtypeStruct((tokens, width), F32),
            jax.ShapeDtypeStruct((width, tokens), BF16),
            jax.ShapeDtypeStruct((width, width), BF16),
            jax.ShapeDtypeStruct((width, ff), BF16),
            jax.ShapeDtypeStruct((width, ff), BF16),
            jax.ShapeDtypeStruct((width, ff), BF16),
            jax.ShapeDtypeStruct((1, width), F32),
        ],
        scratch_shapes=[
            pltpu.VMEM((width, width), F32),
            pltpu.VMEM((width, ff), F32),
            pltpu.VMEM((width, ff), F32),
            pltpu.VMEM((width, ff), F32),
            pltpu.VMEM((8, width), F32),
        ],
        compiler_params=pltpu.CompilerParams(vmem_limit_bytes=VMEM_BYTES),
        cost_estimate=pl.CostEstimate(
            flops=2 * tokens * width * (9 * ff + 3 * width),
            bytes_accessed=tokens * width * 14,
            transcendentals=tokens * ff,
        ),
        name="mlp_both",
    )(x, mixed, mixed_t, dy, gain, o_w, gate_w, up_w, down_t)


def qkv_back_kernel(
    x_ref, dmid_ref, dq_ref, dk_ref, dv_ref, gain_ref, w_ref,
    din_ref, w_grad_ref, gain_grad_ref, w_sum, gain_sum,
):
    step, steps = pl.program_id(0), pl.num_programs(0)

    @pl.when(step == 0)
    def _():
        w_sum[...] = jnp.zeros_like(w_sum)
        gain_sum[...] = jnp.zeros_like(gain_sum)

    gain = gain_ref[...]
    x = x_ref[...].astype(F32)
    rstd = lax.rsqrt(jnp.mean(x * x, axis=-1, keepdims=True) + eps_norm)
    scaled_x = x * rstd
    normed = (scaled_x * gain).astype(BF16)
    dlin = jnp.concatenate([dq_ref[...], dk_ref[...], dv_ref[...]], axis=0)
    w_sum[...] += dot(dlin, normed, 1, 0)
    dnormed = dot(dlin, w_ref[...], 0, 0)
    gain_sum[...] += jnp.sum((dnormed * scaled_x).reshape(-1, 8, x.shape[1]), axis=0)
    scaled = dnormed * gain
    pull = jnp.mean(scaled * x, axis=-1, keepdims=True)
    din_ref[...] = (dmid_ref[...] + rstd * scaled - scaled_x * (rstd * rstd * pull)).astype(BF16)

    @pl.when(step == steps - 1)
    def _():
        w_grad_ref[...] = w_sum[...].astype(BF16)
        gain_grad_ref[...] = jnp.sum(gain_sum[...], axis=0, keepdims=True)


def project_back(x, dmid, dq_t, dk_t, dv_t, gain, w_t, block=512):
    tokens, width = x.shape
    feats = w_t.shape[0]
    tok = pl.BlockSpec((block, width), lambda i: (i, 0))
    col = lambda rows: pl.BlockSpec((rows, block), lambda i: (0, i))
    once = lambda shape: pl.BlockSpec(shape, lambda i: (0, 0), pipeline_mode=pl.Buffered(1))
    return pl.pallas_call(
        qkv_back_kernel,
        grid=(tokens // block,),
        in_specs=[
            tok, tok, col(dq_t.shape[0]), col(dk_t.shape[0]), col(dv_t.shape[0]),
            once((1, width)), once((feats, width)),
        ],
        out_specs=[tok, once((feats, width)), once((1, width))],
        out_shape=[
            jax.ShapeDtypeStruct((tokens, width), BF16),
            jax.ShapeDtypeStruct((feats, width), BF16),
            jax.ShapeDtypeStruct((1, width), F32),
        ],
        scratch_shapes=[pltpu.VMEM((feats, width), F32), pltpu.VMEM((8, width), F32)],
        compiler_params=pltpu.CompilerParams(vmem_limit_bytes=VMEM_BYTES),
        cost_estimate=pl.CostEstimate(
            flops=4 * tokens * width * feats, bytes_accessed=tokens * width * 12, transcendentals=0
        ),
        name="project_back",
    )(x, dmid, dq_t, dk_t, dv_t, gain, w_t)


def swap(array, axis, bit):
    size = lax.axis_size(axis)
    return lax.ppermute(array, axis, [(i, i ^ bit) for i in range(size)])


def bits_of(axis):
    size = lax.axis_size(axis)
    return [1 << i for i in range(size.bit_length() - 1)]


def gather_doubling(array):
    whole = array[None]
    for axis in ("seq", "dp"):
        for bit in bits_of(axis):
            upper = (lax.axis_index(axis) // bit) % 2 == 1
            other = swap(whole, axis, bit)
            whole = jnp.concatenate([jnp.where(upper, other, whole), jnp.where(upper, whole, other)], axis=0)
    return whole.reshape(lax.axis_size("dp"), lax.axis_size("seq"), *array.shape)


def scatter_halving(array):
    rows, lanes = array.shape[2:]
    part = array.reshape(-1, rows, lanes)
    order = [("dp", b) for b in bits_of("dp")]
    seq_bits = [("seq", b) for b in bits_of("seq")]
    seq_size = lax.axis_size("seq")
    dims = [2] * (len(order) + len(seq_bits))
    part = part.reshape(*dims, rows, lanes)
    names = [("dp", b) for b in reversed(bits_of("dp"))] + [("seq", b) for b in reversed(bits_of("seq"))]
    for axis, bit in order + seq_bits:
        place = names.index((axis, bit))
        names.pop(place)
        upper = (lax.axis_index(axis) // bit) % 2
        mine = lax.dynamic_index_in_dim(part, upper, place, keepdims=False)
        other = lax.dynamic_index_in_dim(part, 1 - upper, place, keepdims=False)
        part = (mine.astype(F32) + swap(other, axis, bit).astype(F32)).astype(BF16)
    return part.reshape(rows, lanes)


def sum_doubling(array):
    for axis in ("dp", "seq"):
        for bit in bits_of(axis):
            array = array + swap(array, axis, bit)
    return array


def to_sequences(block):
    moved = lax.all_to_all(block, "seq", 0, 0, tiled=True)
    return moved.reshape(-1, block.shape[2])


def to_slots(tokens, seqs):
    moved = lax.all_to_all(tokens.reshape(seqs, -1, tokens.shape[1]), "seq", 0, 0, tiled=True)
    return moved


def fold(matrix, lanes=128):
    rows, cols = matrix.shape[-2:]
    full = cols // lanes * lanes
    parts = [matrix[..., :, c : c + lanes] for c in range(0, full, lanes)]
    if full < cols:
        rest = matrix[..., :, full:]
        parts.append(jnp.concatenate([rest[..., : rows // 2, :], rest[..., rows // 2 :, :]], axis=-1))
    return jnp.concatenate(parts, axis=-2)


def unfold(packed, rows, cols, lanes=128):
    full = cols // lanes
    parts = [packed[..., i * rows : (i + 1) * rows, :] for i in range(full)]
    if full * lanes < cols:
        rest = packed[..., full * rows :, :]
        parts.append(jnp.concatenate([rest[..., :, : lanes // 2], rest[..., :, lanes // 2 :]], axis=-2))
    return jnp.concatenate(parts, axis=-1)


def pad_lanes(matrix, lanes=128):
    return jnp.pad(matrix, [(0, 0)] * (matrix.ndim - 1) + [(0, lanes - matrix.shape[-1])])


def join(blocks):
    dp, seq, rows, cols = blocks.shape
    return blocks.transpose(0, 2, 1, 3).reshape(dp * rows, seq * cols)


def cut(matrix, dp, seq):
    rows, cols = matrix.shape
    return matrix.reshape(dp, rows // dp, seq, cols // seq).transpose(0, 2, 1, 3)


def shards_sequences(
    hidden_in, span_order, attn_gain, q_weight, k_weight, v_weight, o_weight, mlp_gain,
    gate_weight, up_weight, down_weight, out_grad,
):
    seqs, slots, width = hidden_in.shape
    dp, seq = lax.axis_size("dp"), lax.axis_size("seq")
    tokens = slots * seq
    spans = span_order.shape[0]
    span = tokens // spans
    heads = width // HD
    kv_heads = k_weight.shape[1] * seq // HD
    rows, q_cols = q_weight.shape
    kv_cols = k_weight.shape[1]

    x = to_sequences(hidden_in)
    qkv_shard = pad_lanes(jnp.concatenate([q_weight, k_weight, v_weight], axis=1))
    qkv_all = gather_doubling(qkv_shard)
    dy = to_sequences(out_grad)

    rest_shard = jnp.concatenate(
        [fold(gate_weight), fold(up_weight), fold(down_weight.T), pad_lanes(o_weight)], axis=0
    )
    rest_all = lax.all_gather(rest_shard, ("dp", "seq"), axis=0, tiled=False)
    rest_all = rest_all.reshape(dp, seq, *rest_shard.shape)

    inv = jnp.argsort(span_order).astype(jnp.int32)
    slot_pos = slot_positions(jnp.arange(tokens, dtype=jnp.int32), span_order, span)
    inv_freq = rope_base ** (-(jnp.arange(HD // 2, dtype=F32) * 2.0) / HD)
    angles = slot_pos.astype(F32)[None, :] * inv_freq[:, None]
    cos_t, sin_t = jnp.cos(angles), jnp.sin(angles)
    gain_one = attn_gain.astype(F32)[None]
    gain_two = mlp_gain.astype(F32)[None]

    by_feature = qkv_all.transpose(1, 3, 0, 2).reshape(seq, qkv_shard.shape[1], width)
    w_t = jnp.concatenate(
        [
            by_feature[:, :q_cols].reshape(-1, width),
            by_feature[:, q_cols : q_cols + kv_cols].reshape(-1, width),
            by_feature[:, q_cols + kv_cols : q_cols + 2 * kv_cols].reshape(-1, width),
        ],
        axis=0,
    )
    q_t, k_t, v_t, k_nat, v_nat = project_qkv(x, gain_one, w_t, cos_t, sin_t, heads, kv_heads)
    o_t, o_nat, logs = attention_forward(inv, q_t, k_nat, v_t, span)

    g_rows, g_cols = gate_weight.shape
    d_rows, d_cols = down_weight.shape
    part = g_rows * g_cols // 128
    down_part = d_rows * d_cols // 128
    gate_w = join(unfold(rest_all[:, :, :part], g_rows, g_cols))
    up_w = join(unfold(rest_all[:, :, part : 2 * part], g_rows, g_cols))
    down_blocks = unfold(rest_all[:, :, 2 * part : 2 * part + down_part], d_cols, d_rows)
    down_t = down_blocks.transpose(1, 2, 0, 3).reshape(seq * d_cols, dp * d_rows)
    o_cols = o_weight.shape[1]
    o_w = join(rest_all[:, :, 2 * part + down_part :, :o_cols])

    out, dmid, do_t, o_grad, gate_grad, up_grad, down_grad_t, gain_two_grad = mlp_both(
        x, o_nat, o_t, dy, gain_two, o_w, gate_w, up_w, down_t
    )
    hidden_out = to_slots(out, seqs)
    down_cut = down_grad_t.reshape(seq, d_cols, dp, d_rows).transpose(2, 0, 1, 3)
    rest_grads = jnp.concatenate(
        [
            fold(cut(gate_grad, dp, seq)),
            fold(cut(up_grad, dp, seq)),
            fold(down_cut),
            pad_lanes(cut(o_grad, dp, seq)),
        ],
        axis=2,
    )
    rest_sum = lax.psum_scatter(
        rest_grads.reshape(dp * seq, *rest_grads.shape[2:]), ("dp", "seq"), scatter_dimension=0, tiled=True
    )[0].astype(F32)

    dq_t, dk_t, dv_t = attention_backward(
        inv, q_t, k_t, k_nat, v_nat, o_t, do_t, logs, cos_t, sin_t, span
    )
    din, w_grad_t, gain_one_grad = project_back(x, dmid, dq_t, dk_t, dv_t, gain_one, w_t)
    grad_in = to_slots(din, seqs).astype(F32)

    q_part = w_grad_t[:width].reshape(seq, q_cols, dp, rows)
    k_part = w_grad_t[width : width + kv_cols * seq].reshape(seq, kv_cols, dp, rows)
    v_part = w_grad_t[width + kv_cols * seq :].reshape(seq, kv_cols, dp, rows)
    qkv_grads = jnp.concatenate([q_part, k_part, v_part], axis=1).transpose(2, 0, 3, 1)
    qkv_sum = scatter_halving(pad_lanes(qkv_grads)).astype(F32)
    gains = sum_doubling(jnp.concatenate([gain_one_grad, gain_two_grad], axis=0))
    return (
        hidden_out,
        grad_in,
        gains[0],
        qkv_sum[:, :q_cols],
        qkv_sum[:, q_cols : q_cols + kv_cols],
        qkv_sum[:, q_cols + kv_cols : q_cols + 2 * kv_cols],
        rest_sum[2 * part + down_part :, :o_cols],
        gains[1],
        unfold(rest_sum[:part], g_rows, g_cols),
        unfold(rest_sum[part : 2 * part], g_rows, g_cols),
        unfold(rest_sum[2 * part : 2 * part + down_part], d_cols, d_rows).T,
    )


def shards(*args):
    hidden_in = args[0]
    if hidden_in.shape[0] == lax.axis_size("seq"):
        return shards_sequences(*args)
    return shards_general(*args)


def solution(mesh):
    placed = (
        P("dp", "seq", None),
        P(),
        P(),
        P("dp", "seq"),
        P("dp", "seq"),
        P("dp", "seq"),
        P("dp", "seq"),
        P(),
        P("dp", "seq"),
        P("dp", "seq"),
        P("dp", "seq"),
        P("dp", "seq", None),
    )
    return jax.shard_map(
        shards,
        mesh=mesh,
        in_specs=placed,
        out_specs=(
            P("dp", "seq", None),
            P("dp", "seq", None),
            P(),
            P("dp", "seq"),
            P("dp", "seq"),
            P("dp", "seq"),
            P("dp", "seq"),
            P(),
            P("dp", "seq"),
            P("dp", "seq"),
            P("dp", "seq"),
        ),
        check_vma=False,
    )
```

```python
import functools

import jax
import jax.numpy as jnp
from jax import lax
from jax.experimental import pallas as pl
from jax.experimental.pallas import tpu as pltpu
from jax.sharding import PartitionSpec as P

HD = 64
MICRO = 2


eps_norm = 1e-05
rope_base = 100000.0
neg_big = -1e30


def slot_positions(slot_ids, span_order, span_len):
    span_ids = slot_ids // span_len
    span_hits = span_ids[:, None] == jnp.arange(span_order.shape[0], dtype=jnp.int32)[None, :]
    starts = jnp.sum(jnp.where(span_hits, span_order[None, :], 0), axis=1)
    return starts * span_len + slot_ids % span_len


def rope_tables(slot_pos):
    half_width = HD // 2
    inv_freq = rope_base ** (-(jnp.arange(half_width, dtype=jnp.float32) * 2.0) / HD)
    angles = slot_pos.astype(jnp.float32)[:, None] * inv_freq[None, :]
    cosine = jnp.concatenate([jnp.cos(angles), jnp.cos(angles)], axis=1)
    sine_tab = jnp.concatenate([jnp.sin(angles), jnp.sin(angles)], axis=1)
    return (cosine[:, None, :], sine_tab[:, None, :])


def rotate(vector, cosine, sine_tab):
    half_width = vector.shape[-1] // 2
    turned = jnp.concatenate([-vector[..., half_width:], vector[..., :half_width]], axis=-1)
    return vector * cosine + turned * sine_tab


def rotate_back(grad_out, cosine, sine_tab):
    half_width = grad_out.shape[-1] // 2
    scaled = grad_out * sine_tab
    turned = jnp.concatenate([scaled[..., half_width:], -scaled[..., :half_width]], axis=-1)
    return grad_out * cosine + turned


def norm_back(vector, rstd_vec, gain_vec, grad_n):
    scaled = grad_n * gain_vec
    gain_term = jnp.sum(grad_n * vector * rstd_vec, axis=0)
    grad_vec = rstd_vec * scaled - vector * rstd_vec**3 * jnp.mean(
        scaled * vector, axis=-1, keepdims=True
    )
    return (grad_vec, gain_term)


def add_tuples(old_sums, new_terms):
    if old_sums is None:
        return tuple(new_terms)
    return tuple((old_sum + new_term for old_sum, new_term in zip(old_sums, new_terms)))


def shards_general(
    hidden_in,
    span_order,
    attn_gain,
    q_weight,
    k_weight,
    v_weight,
    o_weight,
    mlp_gain,
    gate_weight,
    up_weight,
    down_weight,
    out_grad,
):
    local_seqs, row_count, model_width = hidden_in.shape
    seq_parts = lax.axis_size("seq")
    full_length = row_count * seq_parts
    span_len = full_length // (2 * seq_parts)
    per_micro = local_seqs // MICRO
    kv_width = k_weight.shape[1] * seq_parts
    kv_heads = kv_width // HD
    head_count = model_width // HD
    group_size = head_count // kv_heads
    tok_count = per_micro * row_count
    score_scale = HD ** (-0.5)
    own_slots = lax.axis_index("seq") * row_count + jnp.arange(row_count, dtype=jnp.int32)
    own_pos = slot_positions(own_slots, span_order, span_len)
    all_pos = slot_positions(jnp.arange(full_length, dtype=jnp.int32), span_order, span_len)
    allowed = own_pos[:, None] >= all_pos[None, :]
    cos_own, sin_own = rope_tables(own_pos)
    gain_attn = attn_gain.astype(jnp.float32)
    gain_mlp = mlp_gain.astype(jnp.float32)

    def attend(inputs):
        queries, key_rows, value_rows = inputs
        query_grp = queries.reshape(row_count, kv_heads, group_size, HD)
        key_grp = key_rows.reshape(full_length, kv_heads, HD)
        value_grp = value_rows.reshape(full_length, kv_heads, HD)
        scores = (
            jnp.einsum("rkgd,lkd->kgrl", query_grp, key_grp, preferred_element_type=jnp.float32)
            * score_scale
        )
        scores = jnp.where(allowed, scores, neg_big)
        row_peak = jnp.max(scores, axis=-1, keepdims=True)
        exp_scores = jnp.exp(scores - row_peak)
        row_total = jnp.sum(exp_scores, axis=-1, keepdims=True)
        attn_probs = exp_scores / row_total
        log_total = row_peak + jnp.log(row_total)
        mixed = jnp.einsum(
            "kgrl,lkd->rkgd",
            attn_probs.astype(jnp.bfloat16),
            value_grp,
            preferred_element_type=jnp.float32,
        )
        return (mixed.astype(jnp.bfloat16).reshape(row_count, model_width), log_total)

    def attend_back(inputs):
        queries, key_rows, value_rows, grad_mix, log_total = inputs
        query_grp = queries.reshape(row_count, kv_heads, group_size, HD)
        key_grp = key_rows.reshape(full_length, kv_heads, HD)
        value_grp = value_rows.reshape(full_length, kv_heads, HD)
        grad_grp = grad_mix.reshape(row_count, kv_heads, group_size, HD)
        scores = (
            jnp.einsum("rkgd,lkd->kgrl", query_grp, key_grp, preferred_element_type=jnp.float32)
            * score_scale
        )
        scores = jnp.where(allowed, scores, neg_big)
        attn_probs = jnp.exp(scores - log_total)
        probs_low = attn_probs.astype(jnp.bfloat16)
        grad_probs = jnp.einsum(
            "rkgd,lkd->kgrl", grad_grp, value_grp, preferred_element_type=jnp.float32
        )
        row_delta = jnp.sum(attn_probs * grad_probs, axis=-1, keepdims=True)
        grad_scores = (attn_probs * (grad_probs - row_delta)).astype(jnp.bfloat16)
        grad_query_rot = (
            jnp.einsum("kgrl,lkd->rkgd", grad_scores, key_grp, preferred_element_type=jnp.float32)
            * score_scale
        )
        key_term = (
            jnp.einsum("kgrl,rkgd->lkd", grad_scores, query_grp, preferred_element_type=jnp.float32)
            * score_scale
        )
        value_term = jnp.einsum(
            "kgrl,rkgd->lkd", probs_low, grad_grp, preferred_element_type=jnp.float32
        )
        return (
            grad_query_rot.reshape(row_count, head_count, HD),
            key_term.reshape(full_length, kv_width),
            value_term.reshape(full_length, kv_width),
        )

    outputs = []
    in_grads = []
    totals = None
    for micro_idx in range(MICRO):
        first_seq = micro_idx * per_micro
        block_in = hidden_in[first_seq : first_seq + per_micro]
        block_grad = out_grad[first_seq : first_seq + per_micro]
        col_parts = (
            lax.all_gather(q_weight, "seq", axis=1, tiled=True),
            lax.all_gather(k_weight, "seq", axis=1, tiled=True),
            lax.all_gather(v_weight, "seq", axis=1, tiled=True),
            lax.all_gather(o_weight, "seq", axis=1, tiled=True),
            lax.all_gather(gate_weight, "seq", axis=1, tiled=True),
            lax.all_gather(up_weight, "seq", axis=1, tiled=True),
            lax.all_gather(down_weight, "seq", axis=1, tiled=True),
        )
        query_mat, key_mat, value_mat, out_mat, gate_mat, up_mat, down_mat = (
            lax.all_gather(col_parts[0], "dp", axis=0, tiled=True),
            lax.all_gather(col_parts[1], "dp", axis=0, tiled=True),
            lax.all_gather(col_parts[2], "dp", axis=0, tiled=True),
            lax.all_gather(col_parts[3], "dp", axis=0, tiled=True),
            lax.all_gather(col_parts[4], "dp", axis=0, tiled=True),
            lax.all_gather(col_parts[5], "dp", axis=0, tiled=True),
            lax.all_gather(col_parts[6], "dp", axis=0, tiled=True),
        )
        resid_in = block_in.astype(jnp.float32).reshape(tok_count, model_width)
        rstd_one = lax.rsqrt(jnp.mean(resid_in * resid_in, axis=-1, keepdims=True) + eps_norm)
        normed_one = (resid_in * rstd_one * gain_attn).astype(jnp.bfloat16)
        query_lin = jnp.dot(normed_one, query_mat, preferred_element_type=jnp.float32)
        key_lin = jnp.dot(normed_one, key_mat, preferred_element_type=jnp.float32)
        value_lin = jnp.dot(normed_one, value_mat, preferred_element_type=jnp.float32)
        query_rot = rotate(
            query_lin.reshape(per_micro, row_count, head_count, HD), cos_own, sin_own
        ).astype(jnp.bfloat16)
        key_rot = (
            rotate(key_lin.reshape(per_micro, row_count, kv_heads, HD), cos_own, sin_own)
            .astype(jnp.bfloat16)
            .reshape(per_micro, row_count, kv_width)
        )
        value_low = value_lin.astype(jnp.bfloat16).reshape(per_micro, row_count, kv_width)
        key_all, value_all = (
            lax.all_gather(key_rot, "seq", axis=1, tiled=True),
            lax.all_gather(value_low, "seq", axis=1, tiled=True),
        )
        mixed_seq, log_total = lax.map(attend, (query_rot, key_all, value_all))
        mixed_low = mixed_seq.reshape(tok_count, model_width)
        hidden_mid = resid_in + jnp.dot(mixed_low, out_mat, preferred_element_type=jnp.float32)
        rstd_two = lax.rsqrt(jnp.mean(hidden_mid * hidden_mid, axis=-1, keepdims=True) + eps_norm)
        normed_two = (hidden_mid * rstd_two * gain_mlp).astype(jnp.bfloat16)
        gate_lin = jnp.dot(normed_two, gate_mat, preferred_element_type=jnp.float32)
        up_lin = jnp.dot(normed_two, up_mat, preferred_element_type=jnp.float32)
        gate_sig = jax.nn.sigmoid(gate_lin)
        inner_low = (gate_lin * gate_sig * up_lin).astype(jnp.bfloat16)
        mlp_out = jnp.dot(inner_low, down_mat, preferred_element_type=jnp.float32)
        outputs.append(
            (hidden_mid + mlp_out).astype(jnp.bfloat16).reshape(per_micro, row_count, model_width)
        )
        col_again = (
            lax.all_gather(q_weight, "seq", axis=1, tiled=True),
            lax.all_gather(k_weight, "seq", axis=1, tiled=True),
            lax.all_gather(v_weight, "seq", axis=1, tiled=True),
            lax.all_gather(o_weight, "seq", axis=1, tiled=True),
            lax.all_gather(gate_weight, "seq", axis=1, tiled=True),
            lax.all_gather(up_weight, "seq", axis=1, tiled=True),
            lax.all_gather(down_weight, "seq", axis=1, tiled=True),
        )
        query_mat, key_mat, value_mat, out_mat, gate_mat, up_mat, down_mat = (
            lax.all_gather(col_again[0], "dp", axis=0, tiled=True),
            lax.all_gather(col_again[1], "dp", axis=0, tiled=True),
            lax.all_gather(col_again[2], "dp", axis=0, tiled=True),
            lax.all_gather(col_again[3], "dp", axis=0, tiled=True),
            lax.all_gather(col_again[4], "dp", axis=0, tiled=True),
            lax.all_gather(col_again[5], "dp", axis=0, tiled=True),
            lax.all_gather(col_again[6], "dp", axis=0, tiled=True),
        )
        key_all, value_all = (
            lax.all_gather(key_rot, "seq", axis=1, tiled=True),
            lax.all_gather(value_low, "seq", axis=1, tiled=True),
        )
        grad_top = block_grad.astype(jnp.float32).reshape(tok_count, model_width)
        grad_top_low = grad_top.astype(jnp.bfloat16)
        down_term = jnp.einsum(
            "tf,td->fd", inner_low, grad_top_low, preferred_element_type=jnp.float32
        )
        grad_inner = jnp.einsum(
            "td,fd->tf", grad_top_low, down_mat, preferred_element_type=jnp.float32
        )
        grad_gate = (grad_inner * up_lin * gate_sig * (1.0 + gate_lin * (1.0 - gate_sig))).astype(
            jnp.bfloat16
        )
        grad_up = (grad_inner * gate_lin * gate_sig).astype(jnp.bfloat16)
        gate_term = jnp.einsum(
            "td,tf->df", normed_two, grad_gate, preferred_element_type=jnp.float32
        )
        up_term = jnp.einsum("td,tf->df", normed_two, grad_up, preferred_element_type=jnp.float32)
        grad_normed_two = jnp.einsum(
            "tf,df->td", grad_gate, gate_mat, preferred_element_type=jnp.float32
        ) + jnp.einsum("tf,df->td", grad_up, up_mat, preferred_element_type=jnp.float32)
        grad_mid_norm, gain_mlp_term = norm_back(hidden_mid, rstd_two, gain_mlp, grad_normed_two)
        grad_mid = grad_top + grad_mid_norm
        grad_mid_low = grad_mid.astype(jnp.bfloat16)
        out_term = jnp.einsum(
            "td,te->de", mixed_low, grad_mid_low, preferred_element_type=jnp.float32
        )
        grad_mixed = jnp.einsum(
            "te,de->td", grad_mid_low, out_mat, preferred_element_type=jnp.float32
        ).astype(jnp.bfloat16)
        grad_query_rot, key_terms, value_terms = lax.map(
            attend_back,
            (
                query_rot,
                key_all,
                value_all,
                grad_mixed.reshape(per_micro, row_count, model_width),
                log_total,
            ),
        )
        key_share, value_share = (
            lax.psum_scatter(key_terms, "seq", scatter_dimension=1, tiled=True),
            lax.psum_scatter(value_terms, "seq", scatter_dimension=1, tiled=True),
        )
        grad_query = (
            rotate_back(grad_query_rot, cos_own, sin_own)
            .astype(jnp.bfloat16)
            .reshape(tok_count, model_width)
        )
        grad_key = (
            rotate_back(key_share.reshape(per_micro, row_count, kv_heads, HD), cos_own, sin_own)
            .astype(jnp.bfloat16)
            .reshape(tok_count, kv_width)
        )
        grad_value = value_share.astype(jnp.bfloat16).reshape(tok_count, kv_width)
        query_term = jnp.einsum(
            "td,te->de", normed_one, grad_query, preferred_element_type=jnp.float32
        )
        key_term = jnp.einsum("td,te->de", normed_one, grad_key, preferred_element_type=jnp.float32)
        value_term = jnp.einsum(
            "td,te->de", normed_one, grad_value, preferred_element_type=jnp.float32
        )
        grad_normed_one = (
            jnp.einsum("te,de->td", grad_query, query_mat, preferred_element_type=jnp.float32)
            + jnp.einsum("te,de->td", grad_key, key_mat, preferred_element_type=jnp.float32)
            + jnp.einsum("te,de->td", grad_value, value_mat, preferred_element_type=jnp.float32)
        )
        grad_in_norm, gain_attn_term = norm_back(resid_in, rstd_one, gain_attn, grad_normed_one)
        in_grads.append((grad_mid + grad_in_norm).reshape(per_micro, row_count, model_width))
        totals = add_tuples(
            totals,
            (
                query_term,
                key_term,
                value_term,
                out_term,
                gate_term,
                up_term,
                down_term,
                gain_attn_term,
                gain_mlp_term,
            ),
        )
    col_sums = (
        lax.psum_scatter(
            totals[0].astype(jnp.bfloat16), "seq", scatter_dimension=1, tiled=True
        ).astype(jnp.float32),
        lax.psum_scatter(
            totals[1].astype(jnp.bfloat16), "seq", scatter_dimension=1, tiled=True
        ).astype(jnp.float32),
        lax.psum_scatter(
            totals[2].astype(jnp.bfloat16), "seq", scatter_dimension=1, tiled=True
        ).astype(jnp.float32),
        lax.psum_scatter(
            totals[3].astype(jnp.bfloat16), "seq", scatter_dimension=1, tiled=True
        ).astype(jnp.float32),
        lax.psum_scatter(
            totals[4].astype(jnp.bfloat16), "seq", scatter_dimension=1, tiled=True
        ).astype(jnp.float32),
        lax.psum_scatter(
            totals[5].astype(jnp.bfloat16), "seq", scatter_dimension=1, tiled=True
        ).astype(jnp.float32),
        lax.psum_scatter(
            totals[6].astype(jnp.bfloat16), "seq", scatter_dimension=1, tiled=True
        ).astype(jnp.float32),
    )
    owned = (
        lax.psum_scatter(
            col_sums[0].astype(jnp.bfloat16), "dp", scatter_dimension=0, tiled=True
        ).astype(jnp.float32),
        lax.psum_scatter(
            col_sums[1].astype(jnp.bfloat16), "dp", scatter_dimension=0, tiled=True
        ).astype(jnp.float32),
        lax.psum_scatter(
            col_sums[2].astype(jnp.bfloat16), "dp", scatter_dimension=0, tiled=True
        ).astype(jnp.float32),
        lax.psum_scatter(
            col_sums[3].astype(jnp.bfloat16), "dp", scatter_dimension=0, tiled=True
        ).astype(jnp.float32),
        lax.psum_scatter(
            col_sums[4].astype(jnp.bfloat16), "dp", scatter_dimension=0, tiled=True
        ).astype(jnp.float32),
        lax.psum_scatter(
            col_sums[5].astype(jnp.bfloat16), "dp", scatter_dimension=0, tiled=True
        ).astype(jnp.float32),
        lax.psum_scatter(
            col_sums[6].astype(jnp.bfloat16), "dp", scatter_dimension=0, tiled=True
        ).astype(jnp.float32),
    )
    gain_sums = lax.psum((totals[7], totals[8]), ("dp", "seq"))
    return (
        jnp.concatenate(outputs, axis=0),
        jnp.concatenate(in_grads, axis=0),
        gain_sums[0],
        owned[0],
        owned[1],
        owned[2],
        owned[3],
        gain_sums[1],
        owned[4],
        owned[5],
        owned[6],
    )


F32 = jnp.float32
BF16 = jnp.bfloat16
VMEM_BYTES = 56 * 2**20


def dot(left, right, left_dim, right_dim):
    dims = (((left_dim,), (right_dim,)), ((), ()))
    return lax.dot_general(left, right, dims, preferred_element_type=F32)


def span_slice(inv_ref, place, span):
    return pl.ds(pl.multiple_of(inv_ref[place] * span, span), span)


def lane_pair(ref, rows, inv_ref, block, span):
    first = ref[rows, span_slice(inv_ref, 2 * block, span)]
    second = ref[rows, span_slice(inv_ref, 2 * block + 1, span)]
    return jnp.concatenate([first, second], axis=1)


def row_pair(ref, head, inv_ref, block, span):
    first = ref[head, span_slice(inv_ref, 2 * block, span), :]
    second = ref[head, span_slice(inv_ref, 2 * block + 1, span), :]
    return jnp.concatenate([first, second], axis=0)


def attend_kernel(inv_ref, q_ref, k_ref, v_ref, o_ref, l_ref, *, blocks, span, group):
    wide = 2 * span
    row = lax.broadcasted_iota(jnp.int32, (wide, wide), 0)
    col = lax.broadcasted_iota(jnp.int32, (wide, wide), 1)
    keep = row <= col

    def q_block(block, _):
        queries = [
            lane_pair(q_ref, slice(HD * h, HD * h + HD), inv_ref, block, span) for h in range(group)
        ]

        def scores_of(j):
            keys = row_pair(k_ref, 0, inv_ref, j, span)
            return tuple(dot(keys, query, 1, 0) for query in queries)

        def take(j, scores, carry, masked):
            values = lane_pair(v_ref, slice(0, HD), inv_ref, j, span)
            out = []
            for score, (peak, total, mixed) in zip(scores, carry):
                if masked:
                    score = jnp.where(keep, score, neg_big)
                new_peak = jnp.maximum(peak, jnp.max(score, axis=0, keepdims=True))
                prob = jnp.exp(score - new_peak)
                shrink = jnp.exp(peak - new_peak)
                total = total * shrink + jnp.sum(prob, axis=0, keepdims=True)
                mixed = mixed * shrink + dot(values, prob.astype(BF16), 1, 0)
                out.append((new_peak, total, mixed))
            return tuple(out)

        def body(j, carry):
            scores, state = carry
            following = scores_of(j + 1)
            return following, take(j, scores, state, False)

        empty = tuple(
            (jnp.full((1, wide), neg_big, F32), jnp.zeros((1, wide), F32), jnp.zeros((HD, wide), F32))
            for _ in range(group)
        )
        scores, state = lax.fori_loop(0, block, body, (scores_of(0), empty))
        state = take(block, scores, state, True)
        mixed = jnp.concatenate([m * (1.0 / t) for (_, t, m) in state], axis=0)
        logs = jnp.concatenate(
            [p + jnp.log(t) for (p, t, _) in state] + [jnp.zeros((8 - group, wide), F32)], axis=0
        )
        mixed_low = mixed.astype(BF16)
        for part in range(2):
            where = span_slice(inv_ref, 2 * block + part, span)
            cols = slice(part * span, part * span + span)
            o_ref[:, where] = mixed_low[:, cols]
            l_ref[0, :, where] = logs[:, cols]
        return 0

    lax.fori_loop(0, blocks, q_block, 0)


def attention_forward(inv, q_t, k_nat, v_t, span):
    tokens = q_t.shape[1]
    kv_heads = k_nat.shape[0]
    group = q_t.shape[0] // (kv_heads * HD)
    pairs = kv_heads * group * tokens * tokens
    wide_spec = pl.BlockSpec((group * HD, tokens), lambda g, i: (g, 0))
    nat_spec = pl.BlockSpec((1, tokens, HD), lambda g, i: (g, 0, 0))
    return pl.pallas_call(
        functools.partial(attend_kernel, blocks=tokens // (2 * span), span=span, group=group),
        grid_spec=pltpu.PrefetchScalarGridSpec(
            num_scalar_prefetch=1,
            grid=(kv_heads,),
            in_specs=[wide_spec, nat_spec, pl.BlockSpec((HD, tokens), lambda g, i: (g, 0))],
            out_specs=[
                wide_spec,
                pl.BlockSpec((1, 8, tokens), lambda g, i: (g, 0, 0)),
            ],
        ),
        out_shape=[
            jax.ShapeDtypeStruct(q_t.shape, BF16),
            jax.ShapeDtypeStruct((kv_heads, 8, tokens), F32),
        ],
        compiler_params=pltpu.CompilerParams(vmem_limit_bytes=VMEM_BYTES),
        cost_estimate=pl.CostEstimate(
            flops=16 * pairs * HD, bytes_accessed=tokens * 6000, transcendentals=pairs // 2
        ),
        name="attention_forward",
    )(inv, q_t, k_nat, v_t)


def attend_back_kernel(
    inv_ref, q_ref, kt_ref, k_ref, v_ref, o_ref, do_ref, l_ref, cos_ref, sin_ref,
    dq_ref, dk_ref, dv_ref, dk_sum, dv_sum, *, blocks, span, group,
):
    wide = 2 * span
    row = lax.broadcasted_iota(jnp.int32, (wide, wide), 0)
    col = lax.broadcasted_iota(jnp.int32, (wide, wide), 1)
    keep = row <= col
    half = HD // 2
    dk_sum[...] = jnp.zeros_like(dk_sum)
    dv_sum[...] = jnp.zeros_like(dv_sum)

    def rope_back(grad, cos, sin):
        top, low = grad[:half], grad[half:]
        return jnp.concatenate([top * cos + low * sin, low * cos - top * sin], axis=0)

    def q_block(step, _):
        block = blocks - 1 - step
        rows = [slice(HD * h, HD * h + HD) for h in range(group)]
        queries = [lane_pair(q_ref, r, inv_ref, block, span) for r in rows]
        grads = [lane_pair(do_ref, r, inv_ref, block, span) for r in rows]
        logs = lane_pair(l_ref.at[0], slice(None), inv_ref, block, span)
        deltas = [
            jnp.sum(
                lane_pair(o_ref, r, inv_ref, block, span).astype(F32) * grad.astype(F32),
                axis=0,
                keepdims=True,
            )
            for r, grad in zip(rows, grads)
        ]

        def take(j, dqs, masked):
            keys = row_pair(k_ref, 0, inv_ref, j, span)
            values = row_pair(v_ref, 0, inv_ref, j, span)
            keys_t = lane_pair(kt_ref, slice(0, HD), inv_ref, j, span)
            out = []
            dk = dv = None
            for h in range(group):
                prob = jnp.exp(dot(keys, queries[h], 1, 0) - logs[h : h + 1])
                if masked:
                    prob = jnp.where(keep, prob, 0.0)
                dprob = dot(values, grads[h], 1, 0)
                dscore = (prob * (dprob - deltas[h])).astype(BF16)
                dk_term = dot(queries[h], dscore, 1, 1)
                dv_term = dot(grads[h], prob.astype(BF16), 1, 1)
                dk = dk_term if dk is None else dk + dk_term
                dv = dv_term if dv is None else dv + dv_term
                out.append(dqs[h] + dot(keys_t, dscore, 1, 0))
            place = pl.ds(pl.multiple_of(j * wide, wide), wide)
            dk_sum[:, place] += dk
            dv_sum[:, place] += dv
            return tuple(out)

        dqs = tuple(jnp.zeros((HD, wide), F32) for _ in range(group))
        dqs = lax.fori_loop(0, block, lambda j, c: take(j, c, False), dqs)
        dqs = take(block, dqs, True)
        cos = lane_pair(cos_ref, slice(None), inv_ref, block, span)
        sin = lane_pair(sin_ref, slice(None), inv_ref, block, span)
        dq = jnp.concatenate([rope_back(g * HD**-0.5, cos, sin) for g in dqs], axis=0).astype(BF16)
        place = pl.ds(pl.multiple_of(block * wide, wide), wide)
        dk = rope_back(dk_sum[:, place], cos, sin).astype(BF16)
        dv = dv_sum[:, place].astype(BF16)
        for part in range(2):
            where = span_slice(inv_ref, 2 * block + part, span)
            cols = slice(part * span, part * span + span)
            dq_ref[:, where] = dq[:, cols]
            dk_ref[:, where] = dk[:, cols]
            dv_ref[:, where] = dv[:, cols]
        return 0

    lax.fori_loop(0, blocks, q_block, 0)


def attention_backward(inv, q_t, k_t, k_nat, v_nat, o_t, do_t, logs, cos_t, sin_t, span):
    tokens = q_t.shape[1]
    kv_heads = k_nat.shape[0]
    group = q_t.shape[0] // (kv_heads * HD)
    pairs = kv_heads * group * tokens * tokens
    wide_spec = pl.BlockSpec((group * HD, tokens), lambda g, i: (g, 0))
    kv_spec = pl.BlockSpec((HD, tokens), lambda g, i: (g, 0))
    nat_spec = pl.BlockSpec((1, tokens, HD), lambda g, i: (g, 0, 0))
    tab_spec = pl.BlockSpec((HD // 2, tokens), lambda g, i: (0, 0))
    return pl.pallas_call(
        functools.partial(attend_back_kernel, blocks=tokens // (2 * span), span=span, group=group),
        grid_spec=pltpu.PrefetchScalarGridSpec(
            num_scalar_prefetch=1,
            grid=(kv_heads,),
            in_specs=[
                wide_spec, kv_spec, nat_spec, nat_spec, wide_spec, wide_spec,
                pl.BlockSpec((1, 8, tokens), lambda g, i: (g, 0, 0)), tab_spec, tab_spec,
            ],
            out_specs=[wide_spec, kv_spec, kv_spec],
            scratch_shapes=[pltpu.VMEM((HD, tokens), F32), pltpu.VMEM((HD, tokens), F32)],
        ),
        out_shape=[
            jax.ShapeDtypeStruct(q_t.shape, BF16),
            jax.ShapeDtypeStruct(k_t.shape, BF16),
            jax.ShapeDtypeStruct(k_t.shape, BF16),
        ],
        compiler_params=pltpu.CompilerParams(vmem_limit_bytes=VMEM_BYTES),
        cost_estimate=pl.CostEstimate(
            flops=32 * pairs * HD, bytes_accessed=tokens * 9000, transcendentals=pairs // 2
        ),
        name="attention_backward",
    )(inv, q_t, k_t, k_nat, v_nat, o_t, do_t, logs, cos_t, sin_t)


def flip(index, bits):
    for bit in bits:
        index = index + bit * (1 - 2 * ((index // bit) % 2))
    return index


def bits_of(size):
    return [1 << i for i in range(size.bit_length() - 1)]


def chains(dp, seq):
    far, near = [("seq", b) for b in reversed(bits_of(seq)[1:])], [("seq", b) for b in bits_of(seq)[:1]]
    chip, core = [("dp", b) for b in reversed(bits_of(dp)[1:])], [("dp", b) for b in bits_of(dp)[:1]]
    return far + near + chip + core, far + chip + near + core


def arrival_order(stages, dp, seq, my_dp, my_seq):
    ids = jnp.arange(dp * seq, dtype=jnp.int32)
    away = {"dp": (ids // seq) ^ my_dp, "seq": (ids % seq) ^ my_seq}
    place = jnp.zeros_like(ids)
    for at, (axis, bit) in enumerate(stages):
        place = place + (1 << at) * ((away[axis] // bit) % 2)
    return place


def bring_kernel(x_ref, first_ref, second_ref, out_ref, all_one_ref, all_two_ref,
                 local_sem, x_send, x_recv, w_send, w_recv, *, dp, seq):
    my_dp, my_seq = lax.axis_index("dp"), lax.axis_index("seq")
    orders = chains(dp, seq)
    barrier = pltpu.get_barrier_semaphore()
    peers = [(my_dp, flip(my_seq, [b for b in bits_of(seq) if away & b])) for away in range(1, seq)]
    peers += [(flip(my_dp, [b]), my_seq) for b in bits_of(dp)]
    for peer in peers:
        pl.semaphore_signal(barrier, inc=1, device_id=peer, device_id_type=pl.DeviceIdType.MESH)
    pl.semaphore_wait(barrier, len(peers))

    shards_in = (first_ref, second_ref)
    gathered = (all_one_ref, all_two_ref)

    def weight_copy(chain, stage):
        axis, bit = orders[chain][stage]
        held = 1 << stage
        peer = (flip(my_dp, [bit]), my_seq) if axis == "dp" else (my_dp, flip(my_seq, [bit]))
        source = shards_in[chain] if stage == 0 else gathered[chain].at[pl.ds(0, held)]
        return pltpu.make_async_remote_copy(
            src_ref=source,
            dst_ref=gathered[chain].at[pl.ds(held, held)],
            send_sem=w_send.at[chain, stage],
            recv_sem=w_recv.at[chain, stage],
            device_id=peer,
            device_id_type=pl.DeviceIdType.MESH,
        )

    own = [
        pltpu.make_async_copy(shards_in[c], gathered[c].at[pl.ds(0, 1)], local_sem.at[c]) for c in range(2)
    ]
    own.append(pltpu.make_async_copy(x_ref.at[my_seq], out_ref.at[my_seq], local_sem.at[2]))
    for copy in own:
        copy.start()
    copies = [[weight_copy(c, s) for s in range(len(orders[c]))] for c in range(2)]
    for c in range(2):
        copies[c][0].start()
    moves = []
    for away in range(1, seq):
        peer = flip(my_seq, [b for b in bits_of(seq) if away & b])
        moves.append(
            pltpu.make_async_remote_copy(
                src_ref=x_ref.at[peer],
                dst_ref=out_ref.at[my_seq],
                send_sem=x_send.at[away - 1],
                recv_sem=x_recv.at[away - 1],
                device_id=(my_dp, peer),
                device_id_type=pl.DeviceIdType.MESH,
            )
        )
    for move in moves:
        move.start()
    for c in range(2):
        own[c].wait()
    for stage in range(1, len(orders[0])):
        for c in range(2):
            copies[c][stage - 1].wait_recv()
            copies[c][stage].start()
    for c in range(2):
        copies[c][-1].wait_recv()
        for copy in copies[c]:
            copy.wait_send()
    for move in moves:
        move.wait()
    own[2].wait()


def bring(x, first, second):
    dp, seq = lax.axis_size("dp"), lax.axis_size("seq")
    stages = len(chains(dp, seq)[0])
    hbm = pl.BlockSpec(memory_space=pl.ANY)
    return pl.pallas_call(
        functools.partial(bring_kernel, dp=dp, seq=seq),
        in_specs=[hbm] * 3,
        out_specs=[hbm] * 3,
        out_shape=[
            jax.ShapeDtypeStruct(x.shape, x.dtype),
            jax.ShapeDtypeStruct((dp * seq, *first.shape[1:]), first.dtype),
            jax.ShapeDtypeStruct((dp * seq, *second.shape[1:]), second.dtype),
        ],
        scratch_shapes=[
            pltpu.SemaphoreType.DMA((3,)),
            pltpu.SemaphoreType.DMA((seq - 1,)),
            pltpu.SemaphoreType.DMA((seq - 1,)),
            pltpu.SemaphoreType.DMA((2, stages)),
            pltpu.SemaphoreType.DMA((2, stages)),
        ],
        compiler_params=pltpu.CompilerParams(
            collective_id=1, has_side_effects=True, vmem_limit_bytes=VMEM_BYTES
        ),
        name="bring",
    )(x, first, second)


def qkv_kernel(where_ref, x_ref, gain_ref, packed_ref, cos_ref, sin_ref,
               q_ref, kt_ref, vt_ref, k_ref, v_ref, w_ref, w_wide, *, heads, kv_heads, dp, seq):
    half = HD // 2
    width = w_ref.shape[1]
    q_cols, kv_cols = width // seq, kv_heads * HD // seq
    kv_width = kv_heads * HD

    @pl.when(pl.program_id(0) == 0)
    def _():
        for s in range(seq):
            block = jnp.concatenate([packed_ref[where_ref[d * seq + s]] for d in range(dp)], axis=0)
            turned = block.astype(F32).T
            w_wide[q_cols * s : q_cols * s + q_cols, :] = turned[:q_cols]
            first = width + kv_cols * s
            w_wide[first : first + kv_cols, :] = turned[q_cols : q_cols + kv_cols]
            first += kv_width
            w_wide[first : first + kv_cols, :] = turned[q_cols + kv_cols : q_cols + 2 * kv_cols]
        w_ref[...] = w_wide[...].astype(BF16)

    x = x_ref[0].astype(F32)
    rstd = lax.rsqrt(jnp.mean(x * x, axis=0, keepdims=True) + eps_norm)
    normed = (x * rstd * gain_ref[...]).astype(BF16)
    lin = dot(w_ref[...], normed, 1, 0)
    cos, sin = cos_ref[...], sin_ref[...]
    for head in range(heads + kv_heads):
        top = lin[HD * head : HD * head + half]
        low = lin[HD * head + half : HD * head + HD]
        rot = jnp.concatenate([top * cos - low * sin, low * cos + top * sin], axis=0)
        if head < heads:
            q_ref[HD * head : HD * head + HD, :] = rot.astype(BF16) * jnp.asarray(HD**-0.5, BF16)
        else:
            kv = head - heads
            kt_ref[HD * kv : HD * kv + HD, :] = rot.astype(BF16)
            k_ref[kv] = rot.T.astype(BF16)
    for kv in range(kv_heads):
        first = HD * (heads + kv_heads + kv)
        val = lin[first : first + HD]
        vt_ref[HD * kv : HD * kv + HD, :] = val.astype(BF16)
        v_ref[kv] = val.T.astype(BF16)


def project_qkv(where, x, gain, packed, cos_t, sin_t, heads, kv_heads, rows):
    blocks, width, block = x.shape
    tokens = blocks * block
    feats = (heads + 2 * kv_heads) * HD
    dp, seq = lax.axis_size("dp"), lax.axis_size("seq")
    col = lambda rows: pl.BlockSpec((rows, block), lambda i, w: (0, i))
    nat = pl.BlockSpec((kv_heads, block, HD), lambda i, w: (0, i, 0))
    return pl.pallas_call(
        functools.partial(qkv_kernel, heads=heads, kv_heads=kv_heads, dp=dp, seq=seq),
        grid_spec=pltpu.PrefetchScalarGridSpec(
            num_scalar_prefetch=1,
            grid=(blocks,),
            in_specs=[
                pl.BlockSpec((1, width, block), lambda i, w: (i, 0, 0)),
                pl.BlockSpec((width, 1), lambda i, w: (0, 0)),
                pl.BlockSpec((dp * seq, rows, packed.shape[2]), lambda i, w: (0, 0, 0)),
                col(HD // 2),
                col(HD // 2),
            ],
            out_specs=[
                col(heads * HD), col(kv_heads * HD), col(kv_heads * HD), nat, nat,
                pl.BlockSpec((feats, width), lambda i, w: (0, 0)),
            ],
            scratch_shapes=[pltpu.VMEM((feats, width), F32)],
        ),
        out_shape=[
            jax.ShapeDtypeStruct((heads * HD, tokens), BF16),
            jax.ShapeDtypeStruct((kv_heads * HD, tokens), BF16),
            jax.ShapeDtypeStruct((kv_heads * HD, tokens), BF16),
            jax.ShapeDtypeStruct((kv_heads, tokens, HD), BF16),
            jax.ShapeDtypeStruct((kv_heads, tokens, HD), BF16),
            jax.ShapeDtypeStruct((feats, width), BF16),
        ],
        compiler_params=pltpu.CompilerParams(vmem_limit_bytes=VMEM_BYTES),
        cost_estimate=pl.CostEstimate(
            flops=4 * tokens * width * feats, bytes_accessed=tokens * 5000, transcendentals=0
        ),
        name="project_qkv",
    )(where, x, gain, packed, cos_t, sin_t)


def side_by_side(ref):
    return jnp.concatenate([ref[i] for i in range(ref.shape[0])], axis=1)


def mlp_kernel(
    one_ref, two_ref, x_ref, mixed_ref, dy_ref, gain_ref, o_pack, gate_pack, rest_pack,
    out_ref, dmid_ref, dmixed_ref, grads_ref, gain_grad_ref,
    o_w, o_t, gate_w, gate_t, up_w, up_t, down_w, down_t, o_sum, gate_sum, up_sum, down_sum, gain_sum,
    *, chunk, dp, seq,
):
    step, steps = pl.program_id(0), pl.num_programs(0)
    width, ff = gate_w.shape
    lanes = o_pack.shape[2]
    rows = width // dp
    o_cols, ff_cols, ff_rows = width // seq, ff // seq, ff // dp
    spare = ff_cols - lanes
    padded = -(-o_cols // 16) * 16

    @pl.when(step == 0)
    def _():
        for total in (o_sum, gate_sum, up_sum, down_sum, gain_sum):
            total[...] = jnp.zeros_like(total)
        for s in range(seq):
            ones = [one_ref[d * seq + s] for d in range(dp)]
            twos = [two_ref[d * seq + s] for d in range(dp)]
            stack = lambda ref, where, first: jnp.concatenate(
                [ref[w, first : first + rows, :] for w in where], axis=0
            ).astype(F32).T
            o_sum[o_cols * s : o_cols * s + o_cols, :] = stack(o_pack, ones, 0)[:o_cols]
            gate_t[ff_cols * s : ff_cols * s + lanes, :] = stack(gate_pack, ones, 0).astype(BF16)
            up_t[ff_cols * s : ff_cols * s + lanes, :] = stack(rest_pack, twos, 0).astype(BF16)
            both = stack(rest_pack, twos, rows).astype(BF16)
            gate_t[ff_cols * s + lanes : ff_cols * (s + 1), :] = both[:spare]
            up_t[ff_cols * s + lanes : ff_cols * (s + 1), :] = both[spare : 2 * spare]
            for d in range(dp):
                for t in range(ff_rows // lanes):
                    first = 2 * rows + padded * t
                    piece = rest_pack[twos[d], first : first + padded, :].astype(F32)[:o_cols]
                    cols = slice(ff_rows * d + lanes * t, ff_rows * d + lanes * (t + 1))
                    down_sum[o_cols * s : o_cols * s + o_cols, cols] = piece
        o_t[...] = o_sum[...].astype(BF16)
        o_w[...] = o_sum[...].T.astype(BF16)
        down_t[...] = down_sum[...].astype(BF16)
        for first in range(0, ff, lanes):
            part = slice(first, first + lanes)
            down_w[part, :] = down_sum[:, part].T.astype(BF16)
            gate_w[:, part] = gate_t[part, :].T
            up_w[:, part] = up_t[part, :].T
        o_sum[...] = jnp.zeros_like(o_sum)
        down_sum[...] = jnp.zeros_like(down_sum)

    gain = gain_ref[...]
    mixed = mixed_ref[...]
    mid = dot(o_t[...], mixed, 1, 0) + side_by_side(x_ref).astype(F32)
    rstd = lax.rsqrt(jnp.mean(mid * mid, axis=0, keepdims=True) + eps_norm)
    normed = (mid * rstd * gain).astype(BF16)
    dy = side_by_side(dy_ref)
    added = jnp.zeros_like(mid)
    dnormed = jnp.zeros_like(mid)
    for first in range(0, ff, chunk):
        part = slice(first, first + chunk)
        gate = dot(gate_t[part, :], normed, 1, 0)
        up = dot(up_t[part, :], normed, 1, 0)
        dinner = dot(down_w[part, :], dy, 1, 0)
        sig = 1.0 / (1.0 + jnp.exp(-gate))
        silu = gate * sig
        inner = (silu * up).astype(BF16)
        dup = (dinner * silu).astype(BF16)
        dgate = (dinner * up * sig * (1.0 + gate * (1.0 - sig))).astype(BF16)
        added += dot(down_t[:, part], inner, 1, 0)
        dnormed += dot(gate_w[:, part], dgate, 1, 0)
        dnormed += dot(up_w[:, part], dup, 1, 0)
        down_sum[:, part] += dot(dy, inner, 1, 1)
        gate_sum[part, :] += dot(dgate, normed, 1, 1)
        up_sum[part, :] += dot(dup, normed, 1, 1)
    out = (mid + added).astype(BF16)
    scaled_mid = mid * rstd
    product = dnormed * scaled_mid
    gain_sum[...] += sum(product[:, c : c + lanes] for c in range(0, product.shape[1], lanes))
    scaled = dnormed * gain
    pull = jnp.mean(scaled * mid, axis=0, keepdims=True)
    dmid = dy.astype(F32) + rstd * scaled - scaled_mid * (rstd * rstd * pull)
    dmid_low = dmid.astype(BF16)
    block = out_ref.shape[2]
    for i in range(out_ref.shape[0]):
        out_ref[i] = out[:, block * i : block * (i + 1)]
        dmid_ref[i] = dmid[:, block * i : block * (i + 1)]
    o_sum[...] += dot(dmid_low, mixed, 1, 1)
    dmixed_ref[...] = dot(o_w[...], dmid_low, 1, 0).astype(BF16)

    @pl.when(step == steps - 1)
    def _():
        gain_grad_ref[...] = gain_sum[...]
        for s in range(seq):
            tall = lambda total, first, count: total[first : first + count, :]
            blank = jnp.zeros((lanes - o_cols, width), F32)
            o_piece = jnp.concatenate([tall(o_sum, o_cols * s, o_cols), blank], axis=0).T.astype(BF16)
            gate_piece = tall(gate_sum, ff_cols * s, lanes).T.astype(BF16)
            up_piece = tall(up_sum, ff_cols * s, lanes).T.astype(BF16)
            both = jnp.concatenate(
                [tall(gate_sum, ff_cols * s + lanes, spare), tall(up_sum, ff_cols * s + lanes, spare)], axis=0
            ).T.astype(BF16)
            for d in range(dp):
                at = d * seq + s
                band = slice(rows * d, rows * (d + 1))
                for i, piece in enumerate((o_piece, gate_piece, up_piece, both)):
                    grads_ref[at, rows * i : rows * (i + 1), :] = piece[band]
                for t in range(ff_rows // lanes):
                    first = 4 * rows + padded * t
                    cols = slice(ff_rows * d + lanes * t, ff_rows * d + lanes * (t + 1))
                    piece = down_sum[o_cols * s : o_cols * (s + 1), cols]
                    piece = jnp.concatenate([piece, jnp.zeros((padded - o_cols, lanes), F32)], axis=0)
                    grads_ref[at, first : first + padded, :] = piece.astype(BF16)


def mlp_both(one, two, x, mixed, dy, gain, first_pack, second_pack, ff, rows, batch=2, chunk=512):
    blocks, width, block = x.shape
    tokens = blocks * block
    dp, seq = lax.axis_size("dp"), lax.axis_size("seq")
    lanes = first_pack.shape[2]
    tok = pl.BlockSpec((batch, width, block), lambda i, a, b: (i, 0, 0))
    col = pl.BlockSpec((width, batch * block), lambda i, a, b: (0, i))
    single = pl.Buffered(1)
    once = lambda shape: pl.BlockSpec(shape, lambda i, a, b: (0,) * len(shape), pipeline_mode=single)
    pick = lambda which: pl.BlockSpec(
        (dp * seq, rows, lanes), lambda i, a, b: (0, which, 0), pipeline_mode=single
    )
    grad_rows = first_pack.shape[1] - rows + second_pack.shape[1]
    return pl.pallas_call(
        functools.partial(mlp_kernel, chunk=chunk, dp=dp, seq=seq),
        grid_spec=pltpu.PrefetchScalarGridSpec(
            num_scalar_prefetch=2,
            grid=(blocks // batch,),
            in_specs=[tok, col, tok, once((width, 1)), pick(1), pick(2), once(second_pack.shape)],
            out_specs=[tok, tok, col, once((dp * seq, grad_rows, lanes)), once((width, lanes))],
            scratch_shapes=[
                pltpu.VMEM((width, width), BF16),
                pltpu.VMEM((width, width), BF16),
                pltpu.VMEM((width, ff), BF16),
                pltpu.VMEM((ff, width), BF16),
                pltpu.VMEM((width, ff), BF16),
                pltpu.VMEM((ff, width), BF16),
                pltpu.VMEM((ff, width), BF16),
                pltpu.VMEM((width, ff), BF16),
                pltpu.VMEM((width, width), F32),
                pltpu.VMEM((ff, width), F32),
                pltpu.VMEM((ff, width), F32),
                pltpu.VMEM((width, ff), F32),
                pltpu.VMEM((width, lanes), F32),
            ],
        ),
        out_shape=[
            jax.ShapeDtypeStruct(x.shape, BF16),
            jax.ShapeDtypeStruct(x.shape, F32),
            jax.ShapeDtypeStruct((width, tokens), BF16),
            jax.ShapeDtypeStruct((dp * seq, grad_rows, lanes), BF16),
            jax.ShapeDtypeStruct((width, lanes), F32),
        ],
        compiler_params=pltpu.CompilerParams(vmem_limit_bytes=60 * 2**20),
        cost_estimate=pl.CostEstimate(
            flops=2 * tokens * width * (9 * ff + 3 * width),
            bytes_accessed=tokens * width * 14,
            transcendentals=tokens * ff,
        ),
        name="mlp_both",
    )(one, two, x, mixed, dy, gain, first_pack, first_pack, second_pack)


def qkv_back_kernel(
    x_ref, dmid_ref, dq_ref, dk_ref, dv_ref, gain_ref, w_t_ref,
    din_ref, grads_ref, gain_grad_ref, w_nat, w_sum, gain_sum, *, dp, seq, kv_width,
):
    step, steps = pl.program_id(0), pl.num_programs(0)
    width = w_nat.shape[0]
    lanes = grads_ref.shape[2]
    rows = width // dp
    q_cols, kv_cols = width // seq, kv_width // seq

    @pl.when(step == 0)
    def _():
        w_sum[...] = jnp.zeros_like(w_sum)
        gain_sum[...] = jnp.zeros_like(gain_sum)
        w_nat[...] = w_t_ref[...].T

    gain = gain_ref[...]
    x = side_by_side(x_ref).astype(F32)
    rstd = lax.rsqrt(jnp.mean(x * x, axis=0, keepdims=True) + eps_norm)
    scaled_x = x * rstd
    normed = (scaled_x * gain).astype(BF16)
    dlin = jnp.concatenate([dq_ref[...], dk_ref[...], dv_ref[...]], axis=0)
    w_sum[...] += dot(dlin, normed, 1, 1)
    dnormed = dot(w_nat[...], dlin, 1, 0)
    product = dnormed * scaled_x
    gain_sum[...] += sum(product[:, c : c + lanes] for c in range(0, product.shape[1], lanes))
    scaled = dnormed * gain
    pull = jnp.mean(scaled * x, axis=0, keepdims=True)
    din = side_by_side(dmid_ref) + rstd * scaled - scaled_x * (rstd * rstd * pull)
    block = din_ref.shape[2]
    for i in range(din_ref.shape[0]):
        din_ref[i] = din[:, block * i : block * (i + 1)].astype(BF16)

    @pl.when(step == steps - 1)
    def _():
        gain_grad_ref[...] = gain_sum[...]
        blank = jnp.zeros((lanes - q_cols - 2 * kv_cols, width), F32)
        for s in range(seq):
            first = width + kv_cols * s
            piece = jnp.concatenate(
                [
                    w_sum[q_cols * s : q_cols * (s + 1), :],
                    w_sum[first : first + kv_cols, :],
                    w_sum[first + kv_width : first + kv_width + kv_cols, :],
                    blank,
                ],
                axis=0,
            ).T.astype(BF16)
            for d in range(dp):
                grads_ref[d * seq + s] = piece[rows * d : rows * (d + 1)]


def project_back(x, dmid, dq_t, dk_t, dv_t, gain, w_t, lanes, batch=2):
    blocks, width, block = x.shape
    tokens = blocks * block
    feats = w_t.shape[0]
    dp, seq = lax.axis_size("dp"), lax.axis_size("seq")
    tok = pl.BlockSpec((batch, width, block), lambda i: (i, 0, 0))
    col = lambda rows: pl.BlockSpec((rows, batch * block), lambda i: (0, i))
    once = lambda shape: pl.BlockSpec(shape, lambda i: (0,) * len(shape), pipeline_mode=pl.Buffered(1))
    packed = (dp * seq, width // dp, lanes)
    return pl.pallas_call(
        functools.partial(qkv_back_kernel, dp=dp, seq=seq, kv_width=dk_t.shape[0]),
        grid=(blocks // batch,),
        in_specs=[
            tok, tok, col(dq_t.shape[0]), col(dk_t.shape[0]), col(dv_t.shape[0]),
            once((width, 1)), once((feats, width)),
        ],
        out_specs=[tok, once(packed), once((width, lanes))],
        out_shape=[
            jax.ShapeDtypeStruct(x.shape, BF16),
            jax.ShapeDtypeStruct(packed, BF16),
            jax.ShapeDtypeStruct((width, lanes), F32),
        ],
        scratch_shapes=[
            pltpu.VMEM((width, feats), BF16), pltpu.VMEM((feats, width), F32), pltpu.VMEM((width, lanes), F32),
        ],
        compiler_params=pltpu.CompilerParams(vmem_limit_bytes=VMEM_BYTES),
        cost_estimate=pl.CostEstimate(
            flops=4 * tokens * width * feats, bytes_accessed=tokens * width * 12, transcendentals=0
        ),
        name="project_back",
    )(x, dmid, dq_t, dk_t, dv_t, gain, w_t)


def swap(array, axis, bit):
    size = lax.axis_size(axis)
    return lax.ppermute(array, axis, [(i, i ^ bit) for i in range(size)])


def scatter_halving(array, dp, seq):
    rows, lanes = array.shape[1:]
    names = [("dp", b) for b in reversed(bits_of(dp))] + [("seq", b) for b in reversed(bits_of(seq))]
    part = array.reshape(*[2] * len(names), rows, lanes)
    for axis, bit in [("dp", b) for b in bits_of(dp)] + [("seq", b) for b in bits_of(seq)]:
        place = names.index((axis, bit))
        names.pop(place)
        upper = (lax.axis_index(axis) // bit) % 2
        mine = lax.dynamic_index_in_dim(part, upper, place, keepdims=False)
        other = lax.dynamic_index_in_dim(part, 1 - upper, place, keepdims=False)
        part = (mine.astype(F32) + swap(other, axis, bit).astype(F32)).astype(BF16)
    return part.reshape(rows, lanes)


def sum_doubling(array, dp, seq):
    for axis, size in (("dp", dp), ("seq", seq)):
        for bit in bits_of(size):
            array = array + swap(array, axis, bit)
    return array


def exchange(blocks):
    return lax.all_to_all(blocks, "seq", 0, 0, tiled=True)


def pad_lanes(matrix, lanes):
    return jnp.pad(matrix, ((0, 0), (0, lanes - matrix.shape[1])))


def shards_sequences(
    hidden_in, span_order, attn_gain, q_weight, k_weight, v_weight, o_weight, mlp_gain,
    gate_weight, up_weight, down_weight, out_grad,
):
    lanes = 128
    seqs, slots, width = hidden_in.shape
    dp, seq = lax.axis_size("dp"), lax.axis_size("seq")
    tokens = slots * seq
    span = tokens // span_order.shape[0]
    heads = width // HD
    kv_heads = k_weight.shape[1] * seq // HD
    rows, q_cols = q_weight.shape
    kv_cols = k_weight.shape[1]
    ff = down_weight.shape[0] * dp
    ff_rows = down_weight.shape[0]
    padded = -(-q_cols // 16) * 16

    first = jnp.concatenate(
        [
            pad_lanes(jnp.concatenate([q_weight, k_weight, v_weight], axis=1), lanes),
            pad_lanes(o_weight, lanes),
            gate_weight[:, :lanes],
        ],
        axis=0,
    )
    down_turned = jnp.pad(down_weight.T, ((0, padded - q_cols), (0, 0)))
    second = jnp.concatenate(
        [up_weight[:, :lanes], jnp.concatenate([gate_weight[:, lanes:], up_weight[:, lanes:]], axis=1)]
        + [down_turned[:, c : c + lanes] for c in range(0, ff_rows, lanes)],
        axis=0,
    )
    x, first_all, second_all = bring(hidden_in.transpose(0, 2, 1), first[None], second[None])
    out_grad, x = lax.optimization_barrier((out_grad, x))
    dy = exchange(out_grad.transpose(0, 2, 1))

    my_dp, my_seq = lax.axis_index("dp"), lax.axis_index("seq")
    where_one, where_two = [arrival_order(c, dp, seq, my_dp, my_seq) for c in chains(dp, seq)]
    inv = jnp.argsort(span_order).astype(jnp.int32)
    slot_pos = slot_positions(jnp.arange(tokens, dtype=jnp.int32), span_order, span)
    inv_freq = rope_base ** (-(jnp.arange(HD // 2, dtype=F32) * 2.0) / HD)
    angles = slot_pos.astype(F32)[None, :] * inv_freq[:, None]
    cos_t, sin_t = jnp.cos(angles), jnp.sin(angles)
    gain_one = attn_gain.astype(F32)[:, None]
    gain_two = mlp_gain.astype(F32)[:, None]

    q_t, k_t, v_t, k_nat, v_nat, w_t = project_qkv(
        where_one, x, gain_one, first_all, cos_t, sin_t, heads, kv_heads, rows
    )
    o_t, logs = attention_forward(inv, q_t, k_nat, v_t, span)
    out, dmid, do_t, rest_grads, gain_two_terms = mlp_both(
        where_one, where_two, x, o_t, dy, gain_two, first_all, second_all, ff, rows
    )
    hidden_out = exchange(out).transpose(0, 2, 1)
    rest_sum = lax.psum_scatter(rest_grads, ("dp", "seq"), scatter_dimension=0, tiled=True)[0].astype(F32)

    dq_t, dk_t, dv_t = attention_backward(
        inv, q_t, k_t, k_nat, v_nat, o_t, do_t, logs, cos_t, sin_t, span
    )
    din, qkv_grads, gain_one_terms = project_back(x, dmid, dq_t, dk_t, dv_t, gain_one, w_t, lanes)
    grad_in = exchange(din).astype(F32).transpose(0, 2, 1)
    qkv_sum = scatter_halving(qkv_grads, dp, seq).astype(F32)
    gains = sum_doubling(
        jnp.stack([jnp.sum(gain_one_terms, axis=1), jnp.sum(gain_two_terms, axis=1)]), dp, seq
    )
    o_sum, gate_sum, up_sum, both_sum = [rest_sum[rows * i : rows * (i + 1)] for i in range(4)]
    spare = gate_weight.shape[1] - lanes
    down_sum = jnp.concatenate(
        [
            rest_sum[4 * rows + padded * t : 4 * rows + padded * t + q_cols]
            for t in range(ff_rows // lanes)
        ],
        axis=1,
    )
    return (
        hidden_out,
        grad_in,
        gains[0],
        qkv_sum[:, :q_cols],
        qkv_sum[:, q_cols : q_cols + kv_cols],
        qkv_sum[:, q_cols + kv_cols : q_cols + 2 * kv_cols],
        o_sum[:, :q_cols],
        gains[1],
        jnp.concatenate([gate_sum, both_sum[:, :spare]], axis=1),
        jnp.concatenate([up_sum, both_sum[:, spare:]], axis=1),
        down_sum.T,
    )


def shards(*args):
    if args[0].shape[0] == lax.axis_size("seq"):
        return shards_sequences(*args)
    return shards_general(*args)


def solution(mesh):
    placed = (
        P("dp", "seq", None),
        P(),
        P(),
        P("dp", "seq"),
        P("dp", "seq"),
        P("dp", "seq"),
        P("dp", "seq"),
        P(),
        P("dp", "seq"),
        P("dp", "seq"),
        P("dp", "seq"),
        P("dp", "seq", None),
    )
    return jax.shard_map(
        shards,
        mesh=mesh,
        in_specs=placed,
        out_specs=(
            P("dp", "seq", None),
            P("dp", "seq", None),
            P(),
            P("dp", "seq"),
            P("dp", "seq"),
            P("dp", "seq"),
            P("dp", "seq"),
            P(),
            P("dp", "seq"),
            P("dp", "seq"),
            P("dp", "seq"),
        ),
        check_vma=False,
    )
```

```python
import functools

import jax
import jax.numpy as jnp
from jax import lax
from jax.experimental import pallas as pl
from jax.experimental.pallas import tpu as pltpu
from jax.sharding import PartitionSpec as P

HD = 64
MICRO = 2


eps_norm = 1e-05
rope_base = 100000.0
neg_big = -1e30


def slot_positions(slot_ids, span_order, span_len):
    span_ids = slot_ids // span_len
    span_hits = span_ids[:, None] == jnp.arange(span_order.shape[0], dtype=jnp.int32)[None, :]
    starts = jnp.sum(jnp.where(span_hits, span_order[None, :], 0), axis=1)
    return starts * span_len + slot_ids % span_len


def rope_tables(slot_pos):
    half_width = HD // 2
    inv_freq = rope_base ** (-(jnp.arange(half_width, dtype=jnp.float32) * 2.0) / HD)
    angles = slot_pos.astype(jnp.float32)[:, None] * inv_freq[None, :]
    cosine = jnp.concatenate([jnp.cos(angles), jnp.cos(angles)], axis=1)
    sine_tab = jnp.concatenate([jnp.sin(angles), jnp.sin(angles)], axis=1)
    return (cosine[:, None, :], sine_tab[:, None, :])


def rotate(vector, cosine, sine_tab):
    half_width = vector.shape[-1] // 2
    turned = jnp.concatenate([-vector[..., half_width:], vector[..., :half_width]], axis=-1)
    return vector * cosine + turned * sine_tab


def rotate_back(grad_out, cosine, sine_tab):
    half_width = grad_out.shape[-1] // 2
    scaled = grad_out * sine_tab
    turned = jnp.concatenate([scaled[..., half_width:], -scaled[..., :half_width]], axis=-1)
    return grad_out * cosine + turned


def norm_back(vector, rstd_vec, gain_vec, grad_n):
    scaled = grad_n * gain_vec
    gain_term = jnp.sum(grad_n * vector * rstd_vec, axis=0)
    grad_vec = rstd_vec * scaled - vector * rstd_vec**3 * jnp.mean(
        scaled * vector, axis=-1, keepdims=True
    )
    return (grad_vec, gain_term)


def add_tuples(old_sums, new_terms):
    if old_sums is None:
        return tuple(new_terms)
    return tuple((old_sum + new_term for old_sum, new_term in zip(old_sums, new_terms)))


def shards_general(
    hidden_in,
    span_order,
    attn_gain,
    q_weight,
    k_weight,
    v_weight,
    o_weight,
    mlp_gain,
    gate_weight,
    up_weight,
    down_weight,
    out_grad,
):
    local_seqs, row_count, model_width = hidden_in.shape
    seq_parts = lax.axis_size("seq")
    full_length = row_count * seq_parts
    span_len = full_length // (2 * seq_parts)
    per_micro = local_seqs // MICRO
    kv_width = k_weight.shape[1] * seq_parts
    kv_heads = kv_width // HD
    head_count = model_width // HD
    group_size = head_count // kv_heads
    tok_count = per_micro * row_count
    score_scale = HD ** (-0.5)
    own_slots = lax.axis_index("seq") * row_count + jnp.arange(row_count, dtype=jnp.int32)
    own_pos = slot_positions(own_slots, span_order, span_len)
    all_pos = slot_positions(jnp.arange(full_length, dtype=jnp.int32), span_order, span_len)
    allowed = own_pos[:, None] >= all_pos[None, :]
    cos_own, sin_own = rope_tables(own_pos)
    gain_attn = attn_gain.astype(jnp.float32)
    gain_mlp = mlp_gain.astype(jnp.float32)

    def attend(inputs):
        queries, key_rows, value_rows = inputs
        query_grp = queries.reshape(row_count, kv_heads, group_size, HD)
        key_grp = key_rows.reshape(full_length, kv_heads, HD)
        value_grp = value_rows.reshape(full_length, kv_heads, HD)
        scores = (
            jnp.einsum("rkgd,lkd->kgrl", query_grp, key_grp, preferred_element_type=jnp.float32)
            * score_scale
        )
        scores = jnp.where(allowed, scores, neg_big)
        row_peak = jnp.max(scores, axis=-1, keepdims=True)
        exp_scores = jnp.exp(scores - row_peak)
        row_total = jnp.sum(exp_scores, axis=-1, keepdims=True)
        attn_probs = exp_scores / row_total
        log_total = row_peak + jnp.log(row_total)
        mixed = jnp.einsum(
            "kgrl,lkd->rkgd",
            attn_probs.astype(jnp.bfloat16),
            value_grp,
            preferred_element_type=jnp.float32,
        )
        return (mixed.astype(jnp.bfloat16).reshape(row_count, model_width), log_total)

    def attend_back(inputs):
        queries, key_rows, value_rows, grad_mix, log_total = inputs
        query_grp = queries.reshape(row_count, kv_heads, group_size, HD)
        key_grp = key_rows.reshape(full_length, kv_heads, HD)
        value_grp = value_rows.reshape(full_length, kv_heads, HD)
        grad_grp = grad_mix.reshape(row_count, kv_heads, group_size, HD)
        scores = (
            jnp.einsum("rkgd,lkd->kgrl", query_grp, key_grp, preferred_element_type=jnp.float32)
            * score_scale
        )
        scores = jnp.where(allowed, scores, neg_big)
        attn_probs = jnp.exp(scores - log_total)
        probs_low = attn_probs.astype(jnp.bfloat16)
        grad_probs = jnp.einsum(
            "rkgd,lkd->kgrl", grad_grp, value_grp, preferred_element_type=jnp.float32
        )
        row_delta = jnp.sum(attn_probs * grad_probs, axis=-1, keepdims=True)
        grad_scores = (attn_probs * (grad_probs - row_delta)).astype(jnp.bfloat16)
        grad_query_rot = (
            jnp.einsum("kgrl,lkd->rkgd", grad_scores, key_grp, preferred_element_type=jnp.float32)
            * score_scale
        )
        key_term = (
            jnp.einsum("kgrl,rkgd->lkd", grad_scores, query_grp, preferred_element_type=jnp.float32)
            * score_scale
        )
        value_term = jnp.einsum(
            "kgrl,rkgd->lkd", probs_low, grad_grp, preferred_element_type=jnp.float32
        )
        return (
            grad_query_rot.reshape(row_count, head_count, HD),
            key_term.reshape(full_length, kv_width),
            value_term.reshape(full_length, kv_width),
        )

    outputs = []
    in_grads = []
    totals = None
    for micro_idx in range(MICRO):
        first_seq = micro_idx * per_micro
        block_in = hidden_in[first_seq : first_seq + per_micro]
        block_grad = out_grad[first_seq : first_seq + per_micro]
        col_parts = (
            lax.all_gather(q_weight, "seq", axis=1, tiled=True),
            lax.all_gather(k_weight, "seq", axis=1, tiled=True),
            lax.all_gather(v_weight, "seq", axis=1, tiled=True),
            lax.all_gather(o_weight, "seq", axis=1, tiled=True),
            lax.all_gather(gate_weight, "seq", axis=1, tiled=True),
            lax.all_gather(up_weight, "seq", axis=1, tiled=True),
            lax.all_gather(down_weight, "seq", axis=1, tiled=True),
        )
        query_mat, key_mat, value_mat, out_mat, gate_mat, up_mat, down_mat = (
            lax.all_gather(col_parts[0], "dp", axis=0, tiled=True),
            lax.all_gather(col_parts[1], "dp", axis=0, tiled=True),
            lax.all_gather(col_parts[2], "dp", axis=0, tiled=True),
            lax.all_gather(col_parts[3], "dp", axis=0, tiled=True),
            lax.all_gather(col_parts[4], "dp", axis=0, tiled=True),
            lax.all_gather(col_parts[5], "dp", axis=0, tiled=True),
            lax.all_gather(col_parts[6], "dp", axis=0, tiled=True),
        )
        resid_in = block_in.astype(jnp.float32).reshape(tok_count, model_width)
        rstd_one = lax.rsqrt(jnp.mean(resid_in * resid_in, axis=-1, keepdims=True) + eps_norm)
        normed_one = (resid_in * rstd_one * gain_attn).astype(jnp.bfloat16)
        query_lin = jnp.dot(normed_one, query_mat, preferred_element_type=jnp.float32)
        key_lin = jnp.dot(normed_one, key_mat, preferred_element_type=jnp.float32)
        value_lin = jnp.dot(normed_one, value_mat, preferred_element_type=jnp.float32)
        query_rot = rotate(
            query_lin.reshape(per_micro, row_count, head_count, HD), cos_own, sin_own
        ).astype(jnp.bfloat16)
        key_rot = (
            rotate(key_lin.reshape(per_micro, row_count, kv_heads, HD), cos_own, sin_own)
            .astype(jnp.bfloat16)
            .reshape(per_micro, row_count, kv_width)
        )
        value_low = value_lin.astype(jnp.bfloat16).reshape(per_micro, row_count, kv_width)
        key_all, value_all = (
            lax.all_gather(key_rot, "seq", axis=1, tiled=True),
            lax.all_gather(value_low, "seq", axis=1, tiled=True),
        )
        mixed_seq, log_total = lax.map(attend, (query_rot, key_all, value_all))
        mixed_low = mixed_seq.reshape(tok_count, model_width)
        hidden_mid = resid_in + jnp.dot(mixed_low, out_mat, preferred_element_type=jnp.float32)
        rstd_two = lax.rsqrt(jnp.mean(hidden_mid * hidden_mid, axis=-1, keepdims=True) + eps_norm)
        normed_two = (hidden_mid * rstd_two * gain_mlp).astype(jnp.bfloat16)
        gate_lin = jnp.dot(normed_two, gate_mat, preferred_element_type=jnp.float32)
        up_lin = jnp.dot(normed_two, up_mat, preferred_element_type=jnp.float32)
        gate_sig = jax.nn.sigmoid(gate_lin)
        inner_low = (gate_lin * gate_sig * up_lin).astype(jnp.bfloat16)
        mlp_out = jnp.dot(inner_low, down_mat, preferred_element_type=jnp.float32)
        outputs.append(
            (hidden_mid + mlp_out).astype(jnp.bfloat16).reshape(per_micro, row_count, model_width)
        )
        col_again = (
            lax.all_gather(q_weight, "seq", axis=1, tiled=True),
            lax.all_gather(k_weight, "seq", axis=1, tiled=True),
            lax.all_gather(v_weight, "seq", axis=1, tiled=True),
            lax.all_gather(o_weight, "seq", axis=1, tiled=True),
            lax.all_gather(gate_weight, "seq", axis=1, tiled=True),
            lax.all_gather(up_weight, "seq", axis=1, tiled=True),
            lax.all_gather(down_weight, "seq", axis=1, tiled=True),
        )
        query_mat, key_mat, value_mat, out_mat, gate_mat, up_mat, down_mat = (
            lax.all_gather(col_again[0], "dp", axis=0, tiled=True),
            lax.all_gather(col_again[1], "dp", axis=0, tiled=True),
            lax.all_gather(col_again[2], "dp", axis=0, tiled=True),
            lax.all_gather(col_again[3], "dp", axis=0, tiled=True),
            lax.all_gather(col_again[4], "dp", axis=0, tiled=True),
            lax.all_gather(col_again[5], "dp", axis=0, tiled=True),
            lax.all_gather(col_again[6], "dp", axis=0, tiled=True),
        )
        key_all, value_all = (
            lax.all_gather(key_rot, "seq", axis=1, tiled=True),
            lax.all_gather(value_low, "seq", axis=1, tiled=True),
        )
        grad_top = block_grad.astype(jnp.float32).reshape(tok_count, model_width)
        grad_top_low = grad_top.astype(jnp.bfloat16)
        down_term = jnp.einsum(
            "tf,td->fd", inner_low, grad_top_low, preferred_element_type=jnp.float32
        )
        grad_inner = jnp.einsum(
            "td,fd->tf", grad_top_low, down_mat, preferred_element_type=jnp.float32
        )
        grad_gate = (grad_inner * up_lin * gate_sig * (1.0 + gate_lin * (1.0 - gate_sig))).astype(
            jnp.bfloat16
        )
        grad_up = (grad_inner * gate_lin * gate_sig).astype(jnp.bfloat16)
        gate_term = jnp.einsum(
            "td,tf->df", normed_two, grad_gate, preferred_element_type=jnp.float32
        )
        up_term = jnp.einsum("td,tf->df", normed_two, grad_up, preferred_element_type=jnp.float32)
        grad_normed_two = jnp.einsum(
            "tf,df->td", grad_gate, gate_mat, preferred_element_type=jnp.float32
        ) + jnp.einsum("tf,df->td", grad_up, up_mat, preferred_element_type=jnp.float32)
        grad_mid_norm, gain_mlp_term = norm_back(hidden_mid, rstd_two, gain_mlp, grad_normed_two)
        grad_mid = grad_top + grad_mid_norm
        grad_mid_low = grad_mid.astype(jnp.bfloat16)
        out_term = jnp.einsum(
            "td,te->de", mixed_low, grad_mid_low, preferred_element_type=jnp.float32
        )
        grad_mixed = jnp.einsum(
            "te,de->td", grad_mid_low, out_mat, preferred_element_type=jnp.float32
        ).astype(jnp.bfloat16)
        grad_query_rot, key_terms, value_terms = lax.map(
            attend_back,
            (
                query_rot,
                key_all,
                value_all,
                grad_mixed.reshape(per_micro, row_count, model_width),
                log_total,
            ),
        )
        key_share, value_share = (
            lax.psum_scatter(key_terms, "seq", scatter_dimension=1, tiled=True),
            lax.psum_scatter(value_terms, "seq", scatter_dimension=1, tiled=True),
        )
        grad_query = (
            rotate_back(grad_query_rot, cos_own, sin_own)
            .astype(jnp.bfloat16)
            .reshape(tok_count, model_width)
        )
        grad_key = (
            rotate_back(key_share.reshape(per_micro, row_count, kv_heads, HD), cos_own, sin_own)
            .astype(jnp.bfloat16)
            .reshape(tok_count, kv_width)
        )
        grad_value = value_share.astype(jnp.bfloat16).reshape(tok_count, kv_width)
        query_term = jnp.einsum(
            "td,te->de", normed_one, grad_query, preferred_element_type=jnp.float32
        )
        key_term = jnp.einsum("td,te->de", normed_one, grad_key, preferred_element_type=jnp.float32)
        value_term = jnp.einsum(
            "td,te->de", normed_one, grad_value, preferred_element_type=jnp.float32
        )
        grad_normed_one = (
            jnp.einsum("te,de->td", grad_query, query_mat, preferred_element_type=jnp.float32)
            + jnp.einsum("te,de->td", grad_key, key_mat, preferred_element_type=jnp.float32)
            + jnp.einsum("te,de->td", grad_value, value_mat, preferred_element_type=jnp.float32)
        )
        grad_in_norm, gain_attn_term = norm_back(resid_in, rstd_one, gain_attn, grad_normed_one)
        in_grads.append((grad_mid + grad_in_norm).reshape(per_micro, row_count, model_width))
        totals = add_tuples(
            totals,
            (
                query_term,
                key_term,
                value_term,
                out_term,
                gate_term,
                up_term,
                down_term,
                gain_attn_term,
                gain_mlp_term,
            ),
        )
    col_sums = (
        lax.psum_scatter(
            totals[0].astype(jnp.bfloat16), "seq", scatter_dimension=1, tiled=True
        ).astype(jnp.float32),
        lax.psum_scatter(
            totals[1].astype(jnp.bfloat16), "seq", scatter_dimension=1, tiled=True
        ).astype(jnp.float32),
        lax.psum_scatter(
            totals[2].astype(jnp.bfloat16), "seq", scatter_dimension=1, tiled=True
        ).astype(jnp.float32),
        lax.psum_scatter(
            totals[3].astype(jnp.bfloat16), "seq", scatter_dimension=1, tiled=True
        ).astype(jnp.float32),
        lax.psum_scatter(
            totals[4].astype(jnp.bfloat16), "seq", scatter_dimension=1, tiled=True
        ).astype(jnp.float32),
        lax.psum_scatter(
            totals[5].astype(jnp.bfloat16), "seq", scatter_dimension=1, tiled=True
        ).astype(jnp.float32),
        lax.psum_scatter(
            totals[6].astype(jnp.bfloat16), "seq", scatter_dimension=1, tiled=True
        ).astype(jnp.float32),
    )
    owned = (
        lax.psum_scatter(
            col_sums[0].astype(jnp.bfloat16), "dp", scatter_dimension=0, tiled=True
        ).astype(jnp.float32),
        lax.psum_scatter(
            col_sums[1].astype(jnp.bfloat16), "dp", scatter_dimension=0, tiled=True
        ).astype(jnp.float32),
        lax.psum_scatter(
            col_sums[2].astype(jnp.bfloat16), "dp", scatter_dimension=0, tiled=True
        ).astype(jnp.float32),
        lax.psum_scatter(
            col_sums[3].astype(jnp.bfloat16), "dp", scatter_dimension=0, tiled=True
        ).astype(jnp.float32),
        lax.psum_scatter(
            col_sums[4].astype(jnp.bfloat16), "dp", scatter_dimension=0, tiled=True
        ).astype(jnp.float32),
        lax.psum_scatter(
            col_sums[5].astype(jnp.bfloat16), "dp", scatter_dimension=0, tiled=True
        ).astype(jnp.float32),
        lax.psum_scatter(
            col_sums[6].astype(jnp.bfloat16), "dp", scatter_dimension=0, tiled=True
        ).astype(jnp.float32),
    )
    gain_sums = lax.psum((totals[7], totals[8]), ("dp", "seq"))
    return (
        jnp.concatenate(outputs, axis=0),
        jnp.concatenate(in_grads, axis=0),
        gain_sums[0],
        owned[0],
        owned[1],
        owned[2],
        owned[3],
        gain_sums[1],
        owned[4],
        owned[5],
        owned[6],
    )


F32 = jnp.float32
BF16 = jnp.bfloat16
VMEM_BYTES = 56 * 2**20


def dot(left, right, left_dim, right_dim):
    dims = (((left_dim,), (right_dim,)), ((), ()))
    return lax.dot_general(left, right, dims, preferred_element_type=F32)


def span_slice(inv_ref, place, span):
    return pl.ds(pl.multiple_of(inv_ref[place] * span, span), span)


def lane_pair(ref, rows, inv_ref, block, span):
    first = ref[rows, span_slice(inv_ref, 2 * block, span)]
    second = ref[rows, span_slice(inv_ref, 2 * block + 1, span)]
    return jnp.concatenate([first, second], axis=1)


def row_pair(ref, head, inv_ref, block, span):
    first = ref[head, span_slice(inv_ref, 2 * block, span), :]
    second = ref[head, span_slice(inv_ref, 2 * block + 1, span), :]
    return jnp.concatenate([first, second], axis=0)


def attend_kernel(inv_ref, q_ref, k_ref, v_ref, o_ref, l_ref, *, blocks, span, group):
    wide = 2 * span
    row = lax.broadcasted_iota(jnp.int32, (wide, wide), 0)
    col = lax.broadcasted_iota(jnp.int32, (wide, wide), 1)
    keep = row <= col

    def q_block(block, _):
        queries = [
            lane_pair(q_ref, slice(HD * h, HD * h + HD), inv_ref, block, span) for h in range(group)
        ]

        def scores_of(j):
            keys = row_pair(k_ref, 0, inv_ref, j, span)
            return tuple(dot(keys, query, 1, 0) for query in queries)

        def take(j, scores, carry, masked):
            values = lane_pair(v_ref, slice(0, HD), inv_ref, j, span)
            out = []
            for score, (peak, total, mixed) in zip(scores, carry):
                if masked:
                    score = jnp.where(keep, score, neg_big)
                new_peak = jnp.maximum(peak, jnp.max(score, axis=0, keepdims=True))
                prob = jnp.exp(score - new_peak)
                shrink = jnp.exp(peak - new_peak)
                total = total * shrink + jnp.sum(prob, axis=0, keepdims=True)
                mixed = mixed * shrink + dot(values, prob.astype(BF16), 1, 0)
                out.append((new_peak, total, mixed))
            return tuple(out)

        def body(j, carry):
            scores, state = carry
            following = scores_of(j + 1)
            return following, take(j, scores, state, False)

        empty = tuple(
            (jnp.full((1, wide), neg_big, F32), jnp.zeros((1, wide), F32), jnp.zeros((HD, wide), F32))
            for _ in range(group)
        )
        scores, state = lax.fori_loop(0, block, body, (scores_of(0), empty))
        state = take(block, scores, state, True)
        mixed = jnp.concatenate([m * (1.0 / t) for (_, t, m) in state], axis=0)
        logs = jnp.concatenate(
            [p + jnp.log(t) for (p, t, _) in state] + [jnp.zeros((8 - group, wide), F32)], axis=0
        )
        mixed_low = mixed.astype(BF16)
        for part in range(2):
            where = span_slice(inv_ref, 2 * block + part, span)
            cols = slice(part * span, part * span + span)
            o_ref[:, where] = mixed_low[:, cols]
            l_ref[0, :, where] = logs[:, cols]
        return 0

    lax.fori_loop(0, blocks, q_block, 0)


def attention_forward(inv, q_t, k_nat, v_t, span):
    tokens = q_t.shape[1]
    kv_heads = k_nat.shape[0]
    group = q_t.shape[0] // (kv_heads * HD)
    pairs = kv_heads * group * tokens * tokens
    wide_spec = pl.BlockSpec((group * HD, tokens), lambda g, i: (g, 0))
    nat_spec = pl.BlockSpec((1, tokens, HD), lambda g, i: (g, 0, 0))
    return pl.pallas_call(
        functools.partial(attend_kernel, blocks=tokens // (2 * span), span=span, group=group),
        grid_spec=pltpu.PrefetchScalarGridSpec(
            num_scalar_prefetch=1,
            grid=(kv_heads,),
            in_specs=[wide_spec, nat_spec, pl.BlockSpec((HD, tokens), lambda g, i: (g, 0))],
            out_specs=[
                wide_spec,
                pl.BlockSpec((1, 8, tokens), lambda g, i: (g, 0, 0)),
            ],
        ),
        out_shape=[
            jax.ShapeDtypeStruct(q_t.shape, BF16),
            jax.ShapeDtypeStruct((kv_heads, 8, tokens), F32),
        ],
        compiler_params=pltpu.CompilerParams(vmem_limit_bytes=VMEM_BYTES),
        cost_estimate=pl.CostEstimate(
            flops=16 * pairs * HD, bytes_accessed=tokens * 6000, transcendentals=pairs // 2
        ),
        name="attention_forward",
    )(inv, q_t, k_nat, v_t)


def attend_back_kernel(
    inv_ref, q_ref, kt_ref, k_ref, v_ref, o_ref, do_ref, l_ref, cos_ref, sin_ref,
    dq_ref, dk_ref, dv_ref, dk_sum, dv_sum, *, blocks, span, group,
):
    wide = 2 * span
    row = lax.broadcasted_iota(jnp.int32, (wide, wide), 0)
    col = lax.broadcasted_iota(jnp.int32, (wide, wide), 1)
    keep = row <= col
    half = HD // 2
    dk_sum[...] = jnp.zeros_like(dk_sum)
    dv_sum[...] = jnp.zeros_like(dv_sum)

    def rope_back(grad, cos, sin):
        top, low = grad[:half], grad[half:]
        return jnp.concatenate([top * cos + low * sin, low * cos - top * sin], axis=0)

    def q_block(step, _):
        block = blocks - 1 - step
        rows = [slice(HD * h, HD * h + HD) for h in range(group)]
        queries = [lane_pair(q_ref, r, inv_ref, block, span) for r in rows]
        grads = [lane_pair(do_ref, r, inv_ref, block, span) for r in rows]
        logs = lane_pair(l_ref.at[0], slice(None), inv_ref, block, span)
        deltas = [
            jnp.sum(
                lane_pair(o_ref, r, inv_ref, block, span).astype(F32) * grad.astype(F32),
                axis=0,
                keepdims=True,
            )
            for r, grad in zip(rows, grads)
        ]

        def take(j, dqs, masked):
            keys = row_pair(k_ref, 0, inv_ref, j, span)
            values = row_pair(v_ref, 0, inv_ref, j, span)
            keys_t = lane_pair(kt_ref, slice(0, HD), inv_ref, j, span)
            out = []
            dk = dv = None
            for h in range(group):
                prob = jnp.exp(dot(keys, queries[h], 1, 0) - logs[h : h + 1])
                if masked:
                    prob = jnp.where(keep, prob, 0.0)
                dprob = dot(values, grads[h], 1, 0)
                dscore = (prob * (dprob - deltas[h])).astype(BF16)
                dk_term = dot(queries[h], dscore, 1, 1)
                dv_term = dot(grads[h], prob.astype(BF16), 1, 1)
                dk = dk_term if dk is None else dk + dk_term
                dv = dv_term if dv is None else dv + dv_term
                out.append(dqs[h] + dot(keys_t, dscore, 1, 0))
            place = pl.ds(pl.multiple_of(j * wide, wide), wide)
            dk_sum[:, place] += dk
            dv_sum[:, place] += dv
            return tuple(out)

        dqs = tuple(jnp.zeros((HD, wide), F32) for _ in range(group))
        dqs = lax.fori_loop(0, block, lambda j, c: take(j, c, False), dqs)
        dqs = take(block, dqs, True)
        cos = lane_pair(cos_ref, slice(None), inv_ref, block, span)
        sin = lane_pair(sin_ref, slice(None), inv_ref, block, span)
        dq = jnp.concatenate([rope_back(g * HD**-0.5, cos, sin) for g in dqs], axis=0).astype(BF16)
        place = pl.ds(pl.multiple_of(block * wide, wide), wide)
        dk = rope_back(dk_sum[:, place], cos, sin).astype(BF16)
        dv = dv_sum[:, place].astype(BF16)
        for part in range(2):
            where = span_slice(inv_ref, 2 * block + part, span)
            cols = slice(part * span, part * span + span)
            dq_ref[:, where] = dq[:, cols]
            dk_ref[:, where] = dk[:, cols]
            dv_ref[:, where] = dv[:, cols]
        return 0

    lax.fori_loop(0, blocks, q_block, 0)


def attention_backward(inv, q_t, k_t, k_nat, v_nat, o_t, do_t, logs, cos_t, sin_t, span):
    tokens = q_t.shape[1]
    kv_heads = k_nat.shape[0]
    group = q_t.shape[0] // (kv_heads * HD)
    pairs = kv_heads * group * tokens * tokens
    wide_spec = pl.BlockSpec((group * HD, tokens), lambda g, i: (g, 0))
    kv_spec = pl.BlockSpec((HD, tokens), lambda g, i: (g, 0))
    nat_spec = pl.BlockSpec((1, tokens, HD), lambda g, i: (g, 0, 0))
    tab_spec = pl.BlockSpec((HD // 2, tokens), lambda g, i: (0, 0))
    return pl.pallas_call(
        functools.partial(attend_back_kernel, blocks=tokens // (2 * span), span=span, group=group),
        grid_spec=pltpu.PrefetchScalarGridSpec(
            num_scalar_prefetch=1,
            grid=(kv_heads,),
            in_specs=[
                wide_spec, kv_spec, nat_spec, nat_spec, wide_spec, wide_spec,
                pl.BlockSpec((1, 8, tokens), lambda g, i: (g, 0, 0)), tab_spec, tab_spec,
            ],
            out_specs=[wide_spec, kv_spec, kv_spec],
            scratch_shapes=[pltpu.VMEM((HD, tokens), F32), pltpu.VMEM((HD, tokens), F32)],
        ),
        out_shape=[
            jax.ShapeDtypeStruct(q_t.shape, BF16),
            jax.ShapeDtypeStruct(k_t.shape, BF16),
            jax.ShapeDtypeStruct(k_t.shape, BF16),
        ],
        compiler_params=pltpu.CompilerParams(vmem_limit_bytes=VMEM_BYTES),
        cost_estimate=pl.CostEstimate(
            flops=32 * pairs * HD, bytes_accessed=tokens * 9000, transcendentals=pairs // 2
        ),
        name="attention_backward",
    )(inv, q_t, k_t, k_nat, v_nat, o_t, do_t, logs, cos_t, sin_t)


def flip(index, bits):
    for bit in bits:
        index = index + bit * (1 - 2 * ((index // bit) % 2))
    return index


def bits_of(size):
    return [1 << i for i in range(size.bit_length() - 1)]


def seq_stages(seq):
    return [("seq", b) for b in reversed(bits_of(seq)[1:])] + [("seq", b) for b in bits_of(seq)[:1]]


def all_stages(dp, seq):
    return seq_stages(seq) + [("dp", b) for b in reversed(bits_of(dp))]


def arrival_order(stages, dp, seq, my_dp, my_seq):
    ids = jnp.arange(dp * seq, dtype=jnp.int32)
    away = {"dp": (ids // seq) ^ my_dp, "seq": (ids % seq) ^ my_seq}
    place = jnp.zeros_like(ids)
    for at, (axis, bit) in enumerate(stages):
        place = place + (1 << at) * ((away[axis] // bit) % 2)
    return place


def greet(peers):
    barrier = pltpu.get_barrier_semaphore()
    for peer in peers:
        pl.semaphore_signal(barrier, inc=1, device_id=peer, device_id_type=pl.DeviceIdType.MESH)
    pl.semaphore_wait(barrier, len(peers))


def seq_peer(my_dp, my_seq, away, seq):
    return my_dp, flip(my_seq, [b for b in bits_of(seq) if away & b])


def stage_peer(my_dp, my_seq, stage):
    axis, bit = stage
    return (flip(my_dp, [bit]), my_seq) if axis == "dp" else (my_dp, flip(my_seq, [bit]))


def all_peers(my_dp, my_seq, dp, seq):
    peers = [seq_peer(my_dp, my_seq, away, seq) for away in range(1, seq)]
    return peers + [(flip(my_dp, [b]), my_seq) for b in bits_of(dp)]


def bring_kernel(x_ref, first_ref, second_ref, out_ref, all_one_ref, all_two_ref,
                 local_sem, x_send, x_recv, w_send, w_recv, *, dp, seq):
    my_dp, my_seq = lax.axis_index("dp"), lax.axis_index("seq")
    orders = all_stages(dp, seq), seq_stages(seq)
    greet(all_peers(my_dp, my_seq, dp, seq))
    shards_in = (first_ref, second_ref)
    gathered = (all_one_ref, all_two_ref)

    def weight_copy(chain, stage):
        held = 1 << stage
        source = shards_in[chain] if stage == 0 else gathered[chain].at[pl.ds(0, held)]
        return pltpu.make_async_remote_copy(
            src_ref=source,
            dst_ref=gathered[chain].at[pl.ds(held, held)],
            send_sem=w_send.at[chain, stage],
            recv_sem=w_recv.at[chain, stage],
            device_id=stage_peer(my_dp, my_seq, orders[chain][stage]),
            device_id_type=pl.DeviceIdType.MESH,
        )

    copies = [[weight_copy(c, s) for s in range(len(orders[c]))] for c in range(2)]
    for c in range(2):
        copies[c][0].start()
    own = [
        pltpu.make_async_copy(shards_in[c], gathered[c].at[pl.ds(0, 1)], local_sem.at[c]) for c in range(2)
    ]
    own.append(pltpu.make_async_copy(x_ref.at[my_seq], out_ref.at[my_seq], local_sem.at[2]))
    for copy in own:
        copy.start()
    moves = []
    for away in range(1, seq):
        peer = seq_peer(my_dp, my_seq, away, seq)
        moves.append(
            pltpu.make_async_remote_copy(
                src_ref=x_ref.at[peer[1]],
                dst_ref=out_ref.at[my_seq],
                send_sem=x_send.at[away - 1],
                recv_sem=x_recv.at[away - 1],
                device_id=peer,
                device_id_type=pl.DeviceIdType.MESH,
            )
        )
    for c in range(2):
        own[c].wait()
    for stage in range(1, len(orders[0])):
        for c in range(2):
            if stage < len(orders[c]):
                copies[c][stage - 1].wait_recv()
                copies[c][stage].start()
        if stage == 1:
            for move in moves:
                move.start()
    for c in range(2):
        copies[c][-1].wait_recv()
        for copy in copies[c]:
            copy.wait_send()
    for move in moves:
        move.wait()
    own[2].wait()


def bring(x, first, second):
    dp, seq = lax.axis_size("dp"), lax.axis_size("seq")
    stages = len(all_stages(dp, seq))
    hbm = pl.BlockSpec(memory_space=pl.ANY)
    return pl.pallas_call(
        functools.partial(bring_kernel, dp=dp, seq=seq),
        in_specs=[hbm] * 3,
        out_specs=[hbm] * 3,
        out_shape=[
            jax.ShapeDtypeStruct(x.shape, x.dtype),
            jax.ShapeDtypeStruct((dp * seq, *first.shape[1:]), first.dtype),
            jax.ShapeDtypeStruct((seq, *second.shape[1:]), second.dtype),
        ],
        scratch_shapes=[
            pltpu.SemaphoreType.DMA((3,)),
            pltpu.SemaphoreType.DMA((seq - 1,)),
            pltpu.SemaphoreType.DMA((seq - 1,)),
            pltpu.SemaphoreType.DMA((2, stages)),
            pltpu.SemaphoreType.DMA((2, stages)),
        ],
        compiler_params=pltpu.CompilerParams(
            collective_id=1, has_side_effects=True, vmem_limit_bytes=VMEM_BYTES
        ),
        name="bring",
    )(x, first, second)


def qkv_kernel(where_ref, x_ref, gain_ref, packed_ref, cos_ref, sin_ref,
               q_ref, kt_ref, vt_ref, k_ref, v_ref, w_ref, w_wide, *, heads, kv_heads, dp, seq):
    half = HD // 2
    width = w_ref.shape[1]
    q_cols, kv_cols = width // seq, kv_heads * HD // seq
    kv_width = kv_heads * HD

    @pl.when(pl.program_id(0) == 0)
    def _():
        for s in range(seq):
            block = jnp.concatenate([packed_ref[where_ref[d * seq + s]] for d in range(dp)], axis=0)
            turned = block.astype(F32).T
            w_wide[q_cols * s : q_cols * s + q_cols, :] = turned[:q_cols]
            first = width + kv_cols * s
            w_wide[first : first + kv_cols, :] = turned[q_cols : q_cols + kv_cols]
            first += kv_width
            w_wide[first : first + kv_cols, :] = turned[q_cols + kv_cols : q_cols + 2 * kv_cols]
        w_ref[...] = w_wide[...].astype(BF16)

    x = x_ref[0].astype(F32)
    rstd = lax.rsqrt(jnp.mean(x * x, axis=0, keepdims=True) + eps_norm)
    normed = (x * rstd * gain_ref[...]).astype(BF16)
    lin = dot(w_ref[...], normed, 1, 0)
    cos, sin = cos_ref[...], sin_ref[...]
    for head in range(heads + kv_heads):
        top = lin[HD * head : HD * head + half]
        low = lin[HD * head + half : HD * head + HD]
        rot = jnp.concatenate([top * cos - low * sin, low * cos + top * sin], axis=0)
        if head < heads:
            q_ref[HD * head : HD * head + HD, :] = rot.astype(BF16) * jnp.asarray(HD**-0.5, BF16)
        else:
            kv = head - heads
            kt_ref[HD * kv : HD * kv + HD, :] = rot.astype(BF16)
            k_ref[kv] = rot.T.astype(BF16)
    for kv in range(kv_heads):
        first = HD * (heads + kv_heads + kv)
        val = lin[first : first + HD]
        vt_ref[HD * kv : HD * kv + HD, :] = val.astype(BF16)
        v_ref[kv] = val.T.astype(BF16)


def project_qkv(where, x, gain, packed, cos_t, sin_t, heads, kv_heads, rows):
    blocks, width, block = x.shape
    tokens = blocks * block
    feats = (heads + 2 * kv_heads) * HD
    dp, seq = lax.axis_size("dp"), lax.axis_size("seq")
    col = lambda rows: pl.BlockSpec((rows, block), lambda i, w: (0, i))
    nat = pl.BlockSpec((kv_heads, block, HD), lambda i, w: (0, i, 0))
    return pl.pallas_call(
        functools.partial(qkv_kernel, heads=heads, kv_heads=kv_heads, dp=dp, seq=seq),
        grid_spec=pltpu.PrefetchScalarGridSpec(
            num_scalar_prefetch=1,
            grid=(blocks,),
            in_specs=[
                pl.BlockSpec((1, width, block), lambda i, w: (i, 0, 0)),
                pl.BlockSpec((width, 1), lambda i, w: (0, 0)),
                pl.BlockSpec((dp * seq, rows, packed.shape[2]), lambda i, w: (0, 0, 0)),
                col(HD // 2),
                col(HD // 2),
            ],
            out_specs=[
                col(heads * HD), col(kv_heads * HD), col(kv_heads * HD), nat, nat,
                pl.BlockSpec((feats, width), lambda i, w: (0, 0)),
            ],
            scratch_shapes=[pltpu.VMEM((feats, width), F32)],
        ),
        out_shape=[
            jax.ShapeDtypeStruct((heads * HD, tokens), BF16),
            jax.ShapeDtypeStruct((kv_heads * HD, tokens), BF16),
            jax.ShapeDtypeStruct((kv_heads * HD, tokens), BF16),
            jax.ShapeDtypeStruct((kv_heads, tokens, HD), BF16),
            jax.ShapeDtypeStruct((kv_heads, tokens, HD), BF16),
            jax.ShapeDtypeStruct((feats, width), BF16),
        ],
        compiler_params=pltpu.CompilerParams(vmem_limit_bytes=VMEM_BYTES),
        cost_estimate=pl.CostEstimate(
            flops=4 * tokens * width * feats, bytes_accessed=tokens * 5000, transcendentals=0
        ),
        name="project_qkv",
    )(where, x, gain, packed, cos_t, sin_t)


def side_by_side(ref):
    return jnp.concatenate([ref[i] for i in range(ref.shape[0])], axis=1)


def mlp_kernel(
    where_ref, x_ref, mixed_ref, dy_ref, gain_ref, *more, chunk, dp, seq,
):
    packs = more[:dp]
    out_ref, dmid_ref, dmixed_ref, grads_ref, gain_grad_ref = more[dp : dp + 5]
    (o_w, o_t, gate_w, gate_t, up_w, up_t, down_w, down_t, o_sum, gate_sum, up_sum, down_sum, gain_sum,
     pack, pack_sem) = more[dp + 5 :]
    step, steps = pl.program_id(0), pl.num_programs(0)
    width, ff = gate_w.shape
    lanes = pack.shape[3]
    rows = width // dp
    o_cols, ff_cols, ff_rows = width // seq, ff // seq, ff // dp
    spare = ff_cols - lanes
    padded = -(-o_cols // 16) * 16

    @pl.when(step == 0)
    def _():
        for total in (o_sum, gate_sum, up_sum, down_sum, gain_sum):
            total[...] = jnp.zeros_like(total)
        fetches = [
            pltpu.make_async_copy(
                packs[i], pack.at[flip(lax.axis_index("dp"), row_bits(i, dp))], pack_sem.at[i]
            )
            for i in range(dp)
        ]
        for fetch in fetches:
            fetch.start()
        for fetch in fetches:
            fetch.wait()
        for s in range(seq):
            at = where_ref[s]
            stack = lambda first: jnp.concatenate(
                [pack[d, at, first : first + rows, :] for d in range(dp)], axis=0
            ).astype(F32).T
            o_sum[o_cols * s : o_cols * s + o_cols, :] = stack(0)[:o_cols]
            gate_t[ff_cols * s : ff_cols * s + lanes, :] = stack(rows).astype(BF16)
            up_t[ff_cols * s : ff_cols * s + lanes, :] = stack(2 * rows).astype(BF16)
            both = stack(3 * rows).astype(BF16)
            gate_t[ff_cols * s + lanes : ff_cols * (s + 1), :] = both[:spare]
            up_t[ff_cols * s + lanes : ff_cols * (s + 1), :] = both[spare : 2 * spare]
            for d in range(dp):
                for t in range(ff_rows // lanes):
                    first = 4 * rows + padded * t
                    piece = pack[d, at, first : first + padded, :].astype(F32)[:o_cols]
                    cols = slice(ff_rows * d + lanes * t, ff_rows * d + lanes * (t + 1))
                    down_sum[o_cols * s : o_cols * s + o_cols, cols] = piece
        o_t[...] = o_sum[...].astype(BF16)
        o_w[...] = o_sum[...].T.astype(BF16)
        down_t[...] = down_sum[...].astype(BF16)
        for first in range(0, ff, lanes):
            part = slice(first, first + lanes)
            down_w[part, :] = down_sum[:, part].T.astype(BF16)
            gate_w[:, part] = gate_t[part, :].T
            up_w[:, part] = up_t[part, :].T
        o_sum[...] = jnp.zeros_like(o_sum)
        down_sum[...] = jnp.zeros_like(down_sum)

    gain = gain_ref[...]
    mixed = mixed_ref[...]
    mid = dot(o_t[...], mixed, 1, 0) + side_by_side(x_ref).astype(F32)
    rstd = lax.rsqrt(jnp.mean(mid * mid, axis=0, keepdims=True) + eps_norm)
    normed = (mid * rstd * gain).astype(BF16)
    dy = side_by_side(dy_ref)
    added = jnp.zeros_like(mid)
    dnormed = jnp.zeros_like(mid)
    for first in range(0, ff, chunk):
        part = slice(first, first + chunk)
        gate = dot(gate_t[part, :], normed, 1, 0)
        up = dot(up_t[part, :], normed, 1, 0)
        dinner = dot(down_w[part, :], dy, 1, 0)
        sig = 1.0 / (1.0 + jnp.exp(-gate))
        silu = gate * sig
        inner = (silu * up).astype(BF16)
        dup = (dinner * silu).astype(BF16)
        dgate = (dinner * up * sig * (1.0 + gate * (1.0 - sig))).astype(BF16)
        added += dot(down_t[:, part], inner, 1, 0)
        dnormed += dot(gate_w[:, part], dgate, 1, 0)
        dnormed += dot(up_w[:, part], dup, 1, 0)
        down_sum[:, part] += dot(dy, inner, 1, 1)
        gate_sum[part, :] += dot(dgate, normed, 1, 1)
        up_sum[part, :] += dot(dup, normed, 1, 1)
    out = (mid + added).astype(BF16)
    scaled_mid = mid * rstd
    product = dnormed * scaled_mid
    gain_sum[...] += sum(product[:, c : c + lanes] for c in range(0, product.shape[1], lanes))
    scaled = dnormed * gain
    pull = jnp.mean(scaled * mid, axis=0, keepdims=True)
    dmid = dy.astype(F32) + rstd * scaled - scaled_mid * (rstd * rstd * pull)
    dmid_low = dmid.astype(BF16)
    block = out_ref.shape[2]
    for i in range(out_ref.shape[0]):
        out_ref[i] = out[:, block * i : block * (i + 1)]
        dmid_ref[i] = dmid[:, block * i : block * (i + 1)]
    o_sum[...] += dot(dmid_low, mixed, 1, 1)
    dmixed_ref[...] = dot(o_w[...], dmid_low, 1, 0).astype(BF16)

    @pl.when(step == steps - 1)
    def _():
        gain_grad_ref[...] = jnp.sum(gain_sum[...].T, axis=0, keepdims=True)
        for s in range(seq):
            tall = lambda total, first, count: total[first : first + count, :]
            blank = jnp.zeros((lanes - o_cols, width), F32)
            o_piece = jnp.concatenate([tall(o_sum, o_cols * s, o_cols), blank], axis=0).T.astype(BF16)
            gate_piece = tall(gate_sum, ff_cols * s, lanes).T.astype(BF16)
            up_piece = tall(up_sum, ff_cols * s, lanes).T.astype(BF16)
            both = jnp.concatenate(
                [tall(gate_sum, ff_cols * s + lanes, spare), tall(up_sum, ff_cols * s + lanes, spare)], axis=0
            ).T.astype(BF16)
            for d in range(dp):
                at = d * seq + s
                band = slice(rows * d, rows * (d + 1))
                for i, piece in enumerate((o_piece, gate_piece, up_piece, both)):
                    grads_ref[at, rows * i : rows * (i + 1), :] = piece[band]
                for t in range(ff_rows // lanes):
                    first = 4 * rows + padded * t
                    cols = slice(ff_rows * d + lanes * t, ff_rows * d + lanes * (t + 1))
                    piece = down_sum[o_cols * s : o_cols * (s + 1), cols]
                    piece = jnp.concatenate([piece, jnp.zeros((padded - o_cols, lanes), F32)], axis=0)
                    grads_ref[at, first : first + padded, :] = piece.astype(BF16)


def row_bits(at, dp):
    return [b for i, b in enumerate(reversed(bits_of(dp))) if (at >> i) & 1]


def gather_rows(array, dp):
    held = [array]
    for at in range(1, dp):
        mask = sum(row_bits(at, dp))
        held.append(lax.ppermute(array, "dp", [(i, i ^ mask) for i in range(dp)]))
    return held


def mlp_both(where, x, mixed, dy, gain, packs, ff, batch=2, chunk=512):
    blocks, width, block = x.shape
    tokens = blocks * block
    dp, seq = lax.axis_size("dp"), lax.axis_size("seq")
    grad_rows, lanes = packs[0].shape[1:]
    tok = pl.BlockSpec((batch, width, block), lambda i, w: (i, 0, 0))
    col = pl.BlockSpec((width, batch * block), lambda i, w: (0, i))
    once = lambda shape: pl.BlockSpec(
        shape, lambda i, w: (0,) * len(shape), pipeline_mode=pl.Buffered(1)
    )
    hbm = pl.BlockSpec(memory_space=pl.ANY)
    return pl.pallas_call(
        functools.partial(mlp_kernel, chunk=chunk, dp=dp, seq=seq),
        grid_spec=pltpu.PrefetchScalarGridSpec(
            num_scalar_prefetch=1,
            grid=(blocks // batch,),
            in_specs=[tok, col, tok, once((width, 1))] + [hbm] * dp,
            out_specs=[tok, tok, col, once((dp * seq, grad_rows, lanes)), once((1, width))],
            scratch_shapes=[
                pltpu.VMEM((width, width), BF16),
                pltpu.VMEM((width, width), BF16),
                pltpu.VMEM((width, ff), BF16),
                pltpu.VMEM((ff, width), BF16),
                pltpu.VMEM((width, ff), BF16),
                pltpu.VMEM((ff, width), BF16),
                pltpu.VMEM((ff, width), BF16),
                pltpu.VMEM((width, ff), BF16),
                pltpu.VMEM((width, width), F32),
                pltpu.VMEM((ff, width), F32),
                pltpu.VMEM((ff, width), F32),
                pltpu.VMEM((width, ff), F32),
                pltpu.VMEM((width, lanes), F32),
                pltpu.VMEM((dp, *packs[0].shape), BF16),
                pltpu.SemaphoreType.DMA((dp,)),
            ],
        ),
        out_shape=[
            jax.ShapeDtypeStruct(x.shape, BF16),
            jax.ShapeDtypeStruct(x.shape, F32),
            jax.ShapeDtypeStruct((width, tokens), BF16),
            jax.ShapeDtypeStruct((dp * seq, grad_rows, lanes), BF16),
            jax.ShapeDtypeStruct((1, width), F32),
        ],
        compiler_params=pltpu.CompilerParams(vmem_limit_bytes=60 * 2**20),
        cost_estimate=pl.CostEstimate(
            flops=2 * tokens * width * (9 * ff + 3 * width),
            bytes_accessed=tokens * width * 14,
            transcendentals=tokens * ff,
        ),
        name="mlp_both",
    )(where, x, mixed, dy, gain, *packs)


def across(index, other, size):
    for bit in bits_of(size):
        index = index + bit * ((other // bit) % 2) * (1 - 2 * ((index // bit) % 2))
    return index


def finish_kernel(
    x_ref, dmid_ref, dq_ref, dk_ref, dv_ref, gain_ref, w_t_ref, other_gain_ref,
    out_ref, grads_ref, gains_ref,
    w_nat, w_sum, gain_sum, din, packed, landed, gain_held, gain_landed,
    own_sem, d_send, d_recv, r_send, r_recv, g_send, g_recv, *, dp, seq, kv_width,
):
    step, steps = pl.program_id(0), seq // 2
    my_dp, my_seq = lax.axis_index("dp"), lax.axis_index("seq")
    width = w_nat.shape[0]
    lanes = grads_ref.shape[1]
    rows = width // dp
    q_cols, kv_cols = width // seq, kv_width // seq
    stages = all_stages(dp, seq)

    @pl.when(step == 0)
    def _():
        greet(all_peers(my_dp, my_seq, dp, seq))
        w_sum[...] = jnp.zeros_like(w_sum)
        gain_sum[...] = jnp.zeros_like(gain_sum)
        w_nat[...] = w_t_ref[...].T

    gain = gain_ref[...]
    x = side_by_side(x_ref).astype(F32)
    rstd = lax.rsqrt(jnp.mean(x * x, axis=0, keepdims=True) + eps_norm)
    scaled_x = x * rstd
    normed = (scaled_x * gain).astype(BF16)
    dlin = jnp.concatenate([dq_ref[...], dk_ref[...], dv_ref[...]], axis=0)
    w_sum[...] += dot(dlin, normed, 1, 1)
    dnormed = dot(w_nat[...], dlin, 1, 0)
    product = dnormed * scaled_x
    gain_sum[...] += sum(product[:, c : c + lanes] for c in range(0, product.shape[1], lanes))
    scaled = dnormed * gain
    pull = jnp.mean(scaled * x, axis=0, keepdims=True)
    total = side_by_side(dmid_ref) + rstd * scaled - scaled_x * (rstd * rstd * pull)
    pair = across(my_seq // 2, steps - 1 - step, seq // 2)
    block = din.shape[2]
    for i in range(2):
        din[2 * pair + i] = total[:, block * i : block * (i + 1)].astype(BF16)

    def move(away):
        peer = seq_peer(my_dp, my_seq, away, seq)
        return pltpu.make_async_remote_copy(
            src_ref=din.at[peer[1]],
            dst_ref=out_ref.at[my_seq],
            send_sem=d_send.at[away - 1],
            recv_sem=d_recv.at[away - 1],
            device_id=peer,
            device_id_type=pl.DeviceIdType.MESH,
        )

    for back in range(1, steps):

        @pl.when(step == steps - 1 - back)
        def _():
            move(2 * back).start()
            move(2 * back + 1).start()

    @pl.when(step == steps - 1)
    def _():
        move(1).start()
        own = pltpu.make_async_copy(din.at[my_seq], out_ref.at[my_seq], own_sem)
        own.start()
        blank = jnp.zeros((lanes - q_cols - 2 * kv_cols, width), F32)
        for s in range(seq):
            first = width + kv_cols * s
            piece = jnp.concatenate(
                [
                    w_sum[q_cols * s : q_cols * (s + 1), :],
                    w_sum[first : first + kv_cols, :],
                    w_sum[first + kv_width : first + kv_width + kv_cols, :],
                    blank,
                ],
                axis=0,
            ).T.astype(BF16)
            for d in range(dp):
                place = 0
                for at, (axis, bit) in enumerate(stages):
                    mine = ((my_dp if axis == "dp" else my_seq) // bit) % 2
                    theirs = ((d if axis == "dp" else s) // bit) % 2
                    place = place + (1 << at) * (1 - mine if theirs else mine)
                packed[place] = piece[rows * d : rows * (d + 1)]
        gain_row = jnp.sum(gain_sum[...].T, axis=0, keepdims=True)
        gain_held[0] = jnp.concatenate(
            [gain_row, other_gain_ref[...], jnp.zeros((6, width), F32)], axis=0
        )
        sent = []
        for turn, at in enumerate(reversed(range(len(stages)))):
            half = 1 << at
            peer = stage_peer(my_dp, my_seq, stages[at])
            send = pltpu.make_async_remote_copy(
                src_ref=packed.at[pl.ds(half, half)],
                dst_ref=landed.at[pl.ds(half, half)],
                send_sem=r_send.at[at],
                recv_sem=r_recv.at[at],
                device_id=peer,
                device_id_type=pl.DeviceIdType.MESH,
            )
            gain_copy = pltpu.make_async_remote_copy(
                src_ref=gain_held.at[turn],
                dst_ref=gain_landed.at[turn],
                send_sem=g_send.at[turn],
                recv_sem=g_recv.at[turn],
                device_id=peer,
                device_id_type=pl.DeviceIdType.MESH,
            )
            send.start()
            gain_copy.start()
            sent += [send, gain_copy]
            gain_copy.wait_recv()
            gain_held[turn + 1] = gain_held[turn] + gain_landed[turn]
            send.wait_recv()
            both = packed[0:half].astype(F32) + landed[half : 2 * half].astype(F32)
            if at == 0:
                grads_ref[...] = both[0]
            else:
                packed[0:half] = both.astype(BF16)
        gains_ref[...] = gain_held[len(stages)]
        for copy in sent:
            copy.wait_send()
        for away in range(1, seq):
            move(away).wait()
        own.wait()


def finish(x, dmid, dq_t, dk_t, dv_t, gain, w_t, other_gain, lanes):
    blocks, width, block = x.shape
    tokens = blocks * block
    feats = w_t.shape[0]
    dp, seq = lax.axis_size("dp"), lax.axis_size("seq")
    rows = width // dp
    stages = len(all_stages(dp, seq))

    def pair(i):
        return across(lax.axis_index("seq") // 2, seq // 2 - 1 - i, seq // 2)

    tok = pl.BlockSpec((2, width, block), lambda i: (pair(i), 0, 0))
    col = lambda rows: pl.BlockSpec((rows, 2 * block), lambda i: (0, pair(i)))
    once = lambda shape: pl.BlockSpec(shape, lambda i: (0,) * len(shape), pipeline_mode=pl.Buffered(1))
    return pl.pallas_call(
        functools.partial(finish_kernel, dp=dp, seq=seq, kv_width=dk_t.shape[0]),
        grid=(blocks // 2,),
        in_specs=[
            tok, tok, col(dq_t.shape[0]), col(dk_t.shape[0]), col(dv_t.shape[0]),
            once((width, 1)), once((feats, width)), once((1, width)),
        ],
        out_specs=[pl.BlockSpec(memory_space=pl.ANY), once((rows, lanes)), once((8, width))],
        out_shape=[
            jax.ShapeDtypeStruct(x.shape, BF16),
            jax.ShapeDtypeStruct((rows, lanes), F32),
            jax.ShapeDtypeStruct((8, width), F32),
        ],
        scratch_shapes=[
            pltpu.VMEM((width, feats), BF16),
            pltpu.VMEM((feats, width), F32),
            pltpu.VMEM((width, lanes), F32),
            pltpu.VMEM(x.shape, BF16),
            pltpu.VMEM((dp * seq, rows, lanes), BF16),
            pltpu.VMEM((dp * seq, rows, lanes), BF16),
            pltpu.VMEM((stages + 1, 8, width), F32),
            pltpu.VMEM((stages, 8, width), F32),
            pltpu.SemaphoreType.DMA,
            pltpu.SemaphoreType.DMA((seq - 1,)),
            pltpu.SemaphoreType.DMA((seq - 1,)),
            pltpu.SemaphoreType.DMA((stages,)),
            pltpu.SemaphoreType.DMA((stages,)),
            pltpu.SemaphoreType.DMA((stages,)),
            pltpu.SemaphoreType.DMA((stages,)),
        ],
        compiler_params=pltpu.CompilerParams(
            collective_id=2, has_side_effects=True, vmem_limit_bytes=VMEM_BYTES
        ),
        cost_estimate=pl.CostEstimate(
            flops=4 * tokens * width * feats, bytes_accessed=tokens * width * 12, transcendentals=0
        ),
        name="finish",
    )(x, dmid, dq_t, dk_t, dv_t, gain, w_t, other_gain)


def exchange(blocks):
    return lax.all_to_all(blocks, "seq", 0, 0, tiled=True)


def pad_lanes(matrix, lanes):
    return jnp.pad(matrix, ((0, 0), (0, lanes - matrix.shape[1])))


def shards_sequences(
    hidden_in, span_order, attn_gain, q_weight, k_weight, v_weight, o_weight, mlp_gain,
    gate_weight, up_weight, down_weight, out_grad,
):
    lanes = 128
    seqs, slots, width = hidden_in.shape
    dp, seq = lax.axis_size("dp"), lax.axis_size("seq")
    tokens = slots * seq
    span = tokens // span_order.shape[0]
    heads = width // HD
    kv_heads = k_weight.shape[1] * seq // HD
    rows, q_cols = q_weight.shape
    kv_cols = k_weight.shape[1]
    ff = down_weight.shape[0] * dp
    ff_rows = down_weight.shape[0]
    padded = -(-q_cols // 16) * 16

    first = pad_lanes(jnp.concatenate([q_weight, k_weight, v_weight], axis=1), lanes)
    down_turned = jnp.pad(down_weight.T, ((0, padded - q_cols), (0, 0)))
    second = jnp.concatenate(
        [
            pad_lanes(o_weight, lanes),
            gate_weight[:, :lanes],
            up_weight[:, :lanes],
            jnp.concatenate([gate_weight[:, lanes:], up_weight[:, lanes:]], axis=1),
        ]
        + [down_turned[:, c : c + lanes] for c in range(0, ff_rows, lanes)],
        axis=0,
    )
    x, first_all, second_row = bring(hidden_in.transpose(0, 2, 1), first[None], second[None])
    out_grad, x = lax.optimization_barrier((out_grad, x))
    dy = exchange(out_grad.transpose(0, 2, 1))
    second_all = gather_rows(second_row, dp)

    my_dp, my_seq = lax.axis_index("dp"), lax.axis_index("seq")
    where_first = arrival_order(all_stages(dp, seq), dp, seq, my_dp, my_seq)
    where_second = arrival_order(seq_stages(seq), dp, seq, my_dp, my_seq)[:seq]
    inv = jnp.argsort(span_order).astype(jnp.int32)
    slot_pos = slot_positions(jnp.arange(tokens, dtype=jnp.int32), span_order, span)
    inv_freq = rope_base ** (-(jnp.arange(HD // 2, dtype=F32) * 2.0) / HD)
    angles = slot_pos.astype(F32)[None, :] * inv_freq[:, None]
    cos_t, sin_t = jnp.cos(angles), jnp.sin(angles)
    gain_one = attn_gain.astype(F32)[:, None]
    gain_two = mlp_gain.astype(F32)[:, None]

    q_t, k_t, v_t, k_nat, v_nat, w_t = project_qkv(
        where_first, x, gain_one, first_all, cos_t, sin_t, heads, kv_heads, rows
    )
    o_t, logs = attention_forward(inv, q_t, k_nat, v_t, span)
    out, dmid, do_t, rest_grads, gain_two_term = mlp_both(
        where_second, x, o_t, dy, gain_two, second_all, ff
    )
    hidden_out = exchange(out).transpose(0, 2, 1)
    rest_sum = lax.psum_scatter(rest_grads, ("dp", "seq"), scatter_dimension=0, tiled=True)[0].astype(F32)

    dq_t, dk_t, dv_t = attention_backward(
        inv, q_t, k_t, k_nat, v_nat, o_t, do_t, logs, cos_t, sin_t, span
    )
    din, qkv_sum, gains = finish(x, dmid, dq_t, dk_t, dv_t, gain_one, w_t, gain_two_term, lanes)
    grad_in = din.astype(F32).transpose(0, 2, 1)
    o_sum, gate_sum, up_sum, both_sum = [rest_sum[rows * i : rows * (i + 1)] for i in range(4)]
    spare = gate_weight.shape[1] - lanes
    down_sum = jnp.concatenate(
        [
            rest_sum[4 * rows + padded * t : 4 * rows + padded * t + q_cols]
            for t in range(ff_rows // lanes)
        ],
        axis=1,
    )
    return (
        hidden_out,
        grad_in,
        gains[0],
        qkv_sum[:, :q_cols],
        qkv_sum[:, q_cols : q_cols + kv_cols],
        qkv_sum[:, q_cols + kv_cols : q_cols + 2 * kv_cols],
        o_sum[:, :q_cols],
        gains[1],
        jnp.concatenate([gate_sum, both_sum[:, :spare]], axis=1),
        jnp.concatenate([up_sum, both_sum[:, spare:]], axis=1),
        down_sum.T,
    )


def shards(*args):
    if args[0].shape[0] == lax.axis_size("seq"):
        return shards_sequences(*args)
    return shards_general(*args)


def solution(mesh):
    placed = (
        P("dp", "seq", None),
        P(),
        P(),
        P("dp", "seq"),
        P("dp", "seq"),
        P("dp", "seq"),
        P("dp", "seq"),
        P(),
        P("dp", "seq"),
        P("dp", "seq"),
        P("dp", "seq"),
        P("dp", "seq", None),
    )
    return jax.shard_map(
        shards,
        mesh=mesh,
        in_specs=placed,
        out_specs=(
            P("dp", "seq", None),
            P("dp", "seq", None),
            P(),
            P("dp", "seq"),
            P("dp", "seq"),
            P("dp", "seq"),
            P("dp", "seq"),
            P(),
            P("dp", "seq"),
            P("dp", "seq"),
            P("dp", "seq"),
        ),
        check_vma=False,
    )
```

```python
import functools

import jax
import jax.numpy as jnp
from jax import lax
from jax.experimental import pallas as pl
from jax.experimental.pallas import tpu as pltpu
from jax.sharding import PartitionSpec as P

HD = 64
MICRO = 2


eps_norm = 1e-05
rope_base = 100000.0
neg_big = -1e30


def slot_positions(slot_ids, span_order, span_len):
    span_ids = slot_ids // span_len
    span_hits = span_ids[:, None] == jnp.arange(span_order.shape[0], dtype=jnp.int32)[None, :]
    starts = jnp.sum(jnp.where(span_hits, span_order[None, :], 0), axis=1)
    return starts * span_len + slot_ids % span_len


def rope_tables(slot_pos):
    half_width = HD // 2
    inv_freq = rope_base ** (-(jnp.arange(half_width, dtype=jnp.float32) * 2.0) / HD)
    angles = slot_pos.astype(jnp.float32)[:, None] * inv_freq[None, :]
    cosine = jnp.concatenate([jnp.cos(angles), jnp.cos(angles)], axis=1)
    sine_tab = jnp.concatenate([jnp.sin(angles), jnp.sin(angles)], axis=1)
    return (cosine[:, None, :], sine_tab[:, None, :])


def rotate(vector, cosine, sine_tab):
    half_width = vector.shape[-1] // 2
    turned = jnp.concatenate([-vector[..., half_width:], vector[..., :half_width]], axis=-1)
    return vector * cosine + turned * sine_tab


def rotate_back(grad_out, cosine, sine_tab):
    half_width = grad_out.shape[-1] // 2
    scaled = grad_out * sine_tab
    turned = jnp.concatenate([scaled[..., half_width:], -scaled[..., :half_width]], axis=-1)
    return grad_out * cosine + turned


def norm_back(vector, rstd_vec, gain_vec, grad_n):
    scaled = grad_n * gain_vec
    gain_term = jnp.sum(grad_n * vector * rstd_vec, axis=0)
    grad_vec = rstd_vec * scaled - vector * rstd_vec**3 * jnp.mean(
        scaled * vector, axis=-1, keepdims=True
    )
    return (grad_vec, gain_term)


def add_tuples(old_sums, new_terms):
    if old_sums is None:
        return tuple(new_terms)
    return tuple((old_sum + new_term for old_sum, new_term in zip(old_sums, new_terms)))


def shards_general(
    hidden_in,
    span_order,
    attn_gain,
    q_weight,
    k_weight,
    v_weight,
    o_weight,
    mlp_gain,
    gate_weight,
    up_weight,
    down_weight,
    out_grad,
):
    local_seqs, row_count, model_width = hidden_in.shape
    seq_parts = lax.axis_size("seq")
    full_length = row_count * seq_parts
    span_len = full_length // (2 * seq_parts)
    per_micro = local_seqs // MICRO
    kv_width = k_weight.shape[1] * seq_parts
    kv_heads = kv_width // HD
    head_count = model_width // HD
    group_size = head_count // kv_heads
    tok_count = per_micro * row_count
    score_scale = HD ** (-0.5)
    own_slots = lax.axis_index("seq") * row_count + jnp.arange(row_count, dtype=jnp.int32)
    own_pos = slot_positions(own_slots, span_order, span_len)
    all_pos = slot_positions(jnp.arange(full_length, dtype=jnp.int32), span_order, span_len)
    allowed = own_pos[:, None] >= all_pos[None, :]
    cos_own, sin_own = rope_tables(own_pos)
    gain_attn = attn_gain.astype(jnp.float32)
    gain_mlp = mlp_gain.astype(jnp.float32)

    def attend(inputs):
        queries, key_rows, value_rows = inputs
        query_grp = queries.reshape(row_count, kv_heads, group_size, HD)
        key_grp = key_rows.reshape(full_length, kv_heads, HD)
        value_grp = value_rows.reshape(full_length, kv_heads, HD)
        scores = (
            jnp.einsum("rkgd,lkd->kgrl", query_grp, key_grp, preferred_element_type=jnp.float32)
            * score_scale
        )
        scores = jnp.where(allowed, scores, neg_big)
        row_peak = jnp.max(scores, axis=-1, keepdims=True)
        exp_scores = jnp.exp(scores - row_peak)
        row_total = jnp.sum(exp_scores, axis=-1, keepdims=True)
        attn_probs = exp_scores / row_total
        log_total = row_peak + jnp.log(row_total)
        mixed = jnp.einsum(
            "kgrl,lkd->rkgd",
            attn_probs.astype(jnp.bfloat16),
            value_grp,
            preferred_element_type=jnp.float32,
        )
        return (mixed.astype(jnp.bfloat16).reshape(row_count, model_width), log_total)

    def attend_back(inputs):
        queries, key_rows, value_rows, grad_mix, log_total = inputs
        query_grp = queries.reshape(row_count, kv_heads, group_size, HD)
        key_grp = key_rows.reshape(full_length, kv_heads, HD)
        value_grp = value_rows.reshape(full_length, kv_heads, HD)
        grad_grp = grad_mix.reshape(row_count, kv_heads, group_size, HD)
        scores = (
            jnp.einsum("rkgd,lkd->kgrl", query_grp, key_grp, preferred_element_type=jnp.float32)
            * score_scale
        )
        scores = jnp.where(allowed, scores, neg_big)
        attn_probs = jnp.exp(scores - log_total)
        probs_low = attn_probs.astype(jnp.bfloat16)
        grad_probs = jnp.einsum(
            "rkgd,lkd->kgrl", grad_grp, value_grp, preferred_element_type=jnp.float32
        )
        row_delta = jnp.sum(attn_probs * grad_probs, axis=-1, keepdims=True)
        grad_scores = (attn_probs * (grad_probs - row_delta)).astype(jnp.bfloat16)
        grad_query_rot = (
            jnp.einsum("kgrl,lkd->rkgd", grad_scores, key_grp, preferred_element_type=jnp.float32)
            * score_scale
        )
        key_term = (
            jnp.einsum("kgrl,rkgd->lkd", grad_scores, query_grp, preferred_element_type=jnp.float32)
            * score_scale
        )
        value_term = jnp.einsum(
            "kgrl,rkgd->lkd", probs_low, grad_grp, preferred_element_type=jnp.float32
        )
        return (
            grad_query_rot.reshape(row_count, head_count, HD),
            key_term.reshape(full_length, kv_width),
            value_term.reshape(full_length, kv_width),
        )

    outputs = []
    in_grads = []
    totals = None
    for micro_idx in range(MICRO):
        first_seq = micro_idx * per_micro
        block_in = hidden_in[first_seq : first_seq + per_micro]
        block_grad = out_grad[first_seq : first_seq + per_micro]
        col_parts = (
            lax.all_gather(q_weight, "seq", axis=1, tiled=True),
            lax.all_gather(k_weight, "seq", axis=1, tiled=True),
            lax.all_gather(v_weight, "seq", axis=1, tiled=True),
            lax.all_gather(o_weight, "seq", axis=1, tiled=True),
            lax.all_gather(gate_weight, "seq", axis=1, tiled=True),
            lax.all_gather(up_weight, "seq", axis=1, tiled=True),
            lax.all_gather(down_weight, "seq", axis=1, tiled=True),
        )
        query_mat, key_mat, value_mat, out_mat, gate_mat, up_mat, down_mat = (
            lax.all_gather(col_parts[0], "dp", axis=0, tiled=True),
            lax.all_gather(col_parts[1], "dp", axis=0, tiled=True),
            lax.all_gather(col_parts[2], "dp", axis=0, tiled=True),
            lax.all_gather(col_parts[3], "dp", axis=0, tiled=True),
            lax.all_gather(col_parts[4], "dp", axis=0, tiled=True),
            lax.all_gather(col_parts[5], "dp", axis=0, tiled=True),
            lax.all_gather(col_parts[6], "dp", axis=0, tiled=True),
        )
        resid_in = block_in.astype(jnp.float32).reshape(tok_count, model_width)
        rstd_one = lax.rsqrt(jnp.mean(resid_in * resid_in, axis=-1, keepdims=True) + eps_norm)
        normed_one = (resid_in * rstd_one * gain_attn).astype(jnp.bfloat16)
        query_lin = jnp.dot(normed_one, query_mat, preferred_element_type=jnp.float32)
        key_lin = jnp.dot(normed_one, key_mat, preferred_element_type=jnp.float32)
        value_lin = jnp.dot(normed_one, value_mat, preferred_element_type=jnp.float32)
        query_rot = rotate(
            query_lin.reshape(per_micro, row_count, head_count, HD), cos_own, sin_own
        ).astype(jnp.bfloat16)
        key_rot = (
            rotate(key_lin.reshape(per_micro, row_count, kv_heads, HD), cos_own, sin_own)
            .astype(jnp.bfloat16)
            .reshape(per_micro, row_count, kv_width)
        )
        value_low = value_lin.astype(jnp.bfloat16).reshape(per_micro, row_count, kv_width)
        key_all, value_all = (
            lax.all_gather(key_rot, "seq", axis=1, tiled=True),
            lax.all_gather(value_low, "seq", axis=1, tiled=True),
        )
        mixed_seq, log_total = lax.map(attend, (query_rot, key_all, value_all))
        mixed_low = mixed_seq.reshape(tok_count, model_width)
        hidden_mid = resid_in + jnp.dot(mixed_low, out_mat, preferred_element_type=jnp.float32)
        rstd_two = lax.rsqrt(jnp.mean(hidden_mid * hidden_mid, axis=-1, keepdims=True) + eps_norm)
        normed_two = (hidden_mid * rstd_two * gain_mlp).astype(jnp.bfloat16)
        gate_lin = jnp.dot(normed_two, gate_mat, preferred_element_type=jnp.float32)
        up_lin = jnp.dot(normed_two, up_mat, preferred_element_type=jnp.float32)
        gate_sig = jax.nn.sigmoid(gate_lin)
        inner_low = (gate_lin * gate_sig * up_lin).astype(jnp.bfloat16)
        mlp_out = jnp.dot(inner_low, down_mat, preferred_element_type=jnp.float32)
        outputs.append(
            (hidden_mid + mlp_out).astype(jnp.bfloat16).reshape(per_micro, row_count, model_width)
        )
        col_again = (
            lax.all_gather(q_weight, "seq", axis=1, tiled=True),
            lax.all_gather(k_weight, "seq", axis=1, tiled=True),
            lax.all_gather(v_weight, "seq", axis=1, tiled=True),
            lax.all_gather(o_weight, "seq", axis=1, tiled=True),
            lax.all_gather(gate_weight, "seq", axis=1, tiled=True),
            lax.all_gather(up_weight, "seq", axis=1, tiled=True),
            lax.all_gather(down_weight, "seq", axis=1, tiled=True),
        )
        query_mat, key_mat, value_mat, out_mat, gate_mat, up_mat, down_mat = (
            lax.all_gather(col_again[0], "dp", axis=0, tiled=True),
            lax.all_gather(col_again[1], "dp", axis=0, tiled=True),
            lax.all_gather(col_again[2], "dp", axis=0, tiled=True),
            lax.all_gather(col_again[3], "dp", axis=0, tiled=True),
            lax.all_gather(col_again[4], "dp", axis=0, tiled=True),
            lax.all_gather(col_again[5], "dp", axis=0, tiled=True),
            lax.all_gather(col_again[6], "dp", axis=0, tiled=True),
        )
        key_all, value_all = (
            lax.all_gather(key_rot, "seq", axis=1, tiled=True),
            lax.all_gather(value_low, "seq", axis=1, tiled=True),
        )
        grad_top = block_grad.astype(jnp.float32).reshape(tok_count, model_width)
        grad_top_low = grad_top.astype(jnp.bfloat16)
        down_term = jnp.einsum(
            "tf,td->fd", inner_low, grad_top_low, preferred_element_type=jnp.float32
        )
        grad_inner = jnp.einsum(
            "td,fd->tf", grad_top_low, down_mat, preferred_element_type=jnp.float32
        )
        grad_gate = (grad_inner * up_lin * gate_sig * (1.0 + gate_lin * (1.0 - gate_sig))).astype(
            jnp.bfloat16
        )
        grad_up = (grad_inner * gate_lin * gate_sig).astype(jnp.bfloat16)
        gate_term = jnp.einsum(
            "td,tf->df", normed_two, grad_gate, preferred_element_type=jnp.float32
        )
        up_term = jnp.einsum("td,tf->df", normed_two, grad_up, preferred_element_type=jnp.float32)
        grad_normed_two = jnp.einsum(
            "tf,df->td", grad_gate, gate_mat, preferred_element_type=jnp.float32
        ) + jnp.einsum("tf,df->td", grad_up, up_mat, preferred_element_type=jnp.float32)
        grad_mid_norm, gain_mlp_term = norm_back(hidden_mid, rstd_two, gain_mlp, grad_normed_two)
        grad_mid = grad_top + grad_mid_norm
        grad_mid_low = grad_mid.astype(jnp.bfloat16)
        out_term = jnp.einsum(
            "td,te->de", mixed_low, grad_mid_low, preferred_element_type=jnp.float32
        )
        grad_mixed = jnp.einsum(
            "te,de->td", grad_mid_low, out_mat, preferred_element_type=jnp.float32
        ).astype(jnp.bfloat16)
        grad_query_rot, key_terms, value_terms = lax.map(
            attend_back,
            (
                query_rot,
                key_all,
                value_all,
                grad_mixed.reshape(per_micro, row_count, model_width),
                log_total,
            ),
        )
        key_share, value_share = (
            lax.psum_scatter(key_terms, "seq", scatter_dimension=1, tiled=True),
            lax.psum_scatter(value_terms, "seq", scatter_dimension=1, tiled=True),
        )
        grad_query = (
            rotate_back(grad_query_rot, cos_own, sin_own)
            .astype(jnp.bfloat16)
            .reshape(tok_count, model_width)
        )
        grad_key = (
            rotate_back(key_share.reshape(per_micro, row_count, kv_heads, HD), cos_own, sin_own)
            .astype(jnp.bfloat16)
            .reshape(tok_count, kv_width)
        )
        grad_value = value_share.astype(jnp.bfloat16).reshape(tok_count, kv_width)
        query_term = jnp.einsum(
            "td,te->de", normed_one, grad_query, preferred_element_type=jnp.float32
        )
        key_term = jnp.einsum("td,te->de", normed_one, grad_key, preferred_element_type=jnp.float32)
        value_term = jnp.einsum(
            "td,te->de", normed_one, grad_value, preferred_element_type=jnp.float32
        )
        grad_normed_one = (
            jnp.einsum("te,de->td", grad_query, query_mat, preferred_element_type=jnp.float32)
            + jnp.einsum("te,de->td", grad_key, key_mat, preferred_element_type=jnp.float32)
            + jnp.einsum("te,de->td", grad_value, value_mat, preferred_element_type=jnp.float32)
        )
        grad_in_norm, gain_attn_term = norm_back(resid_in, rstd_one, gain_attn, grad_normed_one)
        in_grads.append((grad_mid + grad_in_norm).reshape(per_micro, row_count, model_width))
        totals = add_tuples(
            totals,
            (
                query_term,
                key_term,
                value_term,
                out_term,
                gate_term,
                up_term,
                down_term,
                gain_attn_term,
                gain_mlp_term,
            ),
        )
    col_sums = (
        lax.psum_scatter(
            totals[0].astype(jnp.bfloat16), "seq", scatter_dimension=1, tiled=True
        ).astype(jnp.float32),
        lax.psum_scatter(
            totals[1].astype(jnp.bfloat16), "seq", scatter_dimension=1, tiled=True
        ).astype(jnp.float32),
        lax.psum_scatter(
            totals[2].astype(jnp.bfloat16), "seq", scatter_dimension=1, tiled=True
        ).astype(jnp.float32),
        lax.psum_scatter(
            totals[3].astype(jnp.bfloat16), "seq", scatter_dimension=1, tiled=True
        ).astype(jnp.float32),
        lax.psum_scatter(
            totals[4].astype(jnp.bfloat16), "seq", scatter_dimension=1, tiled=True
        ).astype(jnp.float32),
        lax.psum_scatter(
            totals[5].astype(jnp.bfloat16), "seq", scatter_dimension=1, tiled=True
        ).astype(jnp.float32),
        lax.psum_scatter(
            totals[6].astype(jnp.bfloat16), "seq", scatter_dimension=1, tiled=True
        ).astype(jnp.float32),
    )
    owned = (
        lax.psum_scatter(
            col_sums[0].astype(jnp.bfloat16), "dp", scatter_dimension=0, tiled=True
        ).astype(jnp.float32),
        lax.psum_scatter(
            col_sums[1].astype(jnp.bfloat16), "dp", scatter_dimension=0, tiled=True
        ).astype(jnp.float32),
        lax.psum_scatter(
            col_sums[2].astype(jnp.bfloat16), "dp", scatter_dimension=0, tiled=True
        ).astype(jnp.float32),
        lax.psum_scatter(
            col_sums[3].astype(jnp.bfloat16), "dp", scatter_dimension=0, tiled=True
        ).astype(jnp.float32),
        lax.psum_scatter(
            col_sums[4].astype(jnp.bfloat16), "dp", scatter_dimension=0, tiled=True
        ).astype(jnp.float32),
        lax.psum_scatter(
            col_sums[5].astype(jnp.bfloat16), "dp", scatter_dimension=0, tiled=True
        ).astype(jnp.float32),
        lax.psum_scatter(
            col_sums[6].astype(jnp.bfloat16), "dp", scatter_dimension=0, tiled=True
        ).astype(jnp.float32),
    )
    gain_sums = lax.psum((totals[7], totals[8]), ("dp", "seq"))
    return (
        jnp.concatenate(outputs, axis=0),
        jnp.concatenate(in_grads, axis=0),
        gain_sums[0],
        owned[0],
        owned[1],
        owned[2],
        owned[3],
        gain_sums[1],
        owned[4],
        owned[5],
        owned[6],
    )


F32 = jnp.float32
BF16 = jnp.bfloat16
VMEM_BYTES = 56 * 2**20


def dot(left, right, left_dim, right_dim):
    dims = (((left_dim,), (right_dim,)), ((), ()))
    return lax.dot_general(left, right, dims, preferred_element_type=F32)


def span_slice(inv_ref, place, span):
    return pl.ds(pl.multiple_of(inv_ref[place] * span, span), span)


def lane_pair(ref, rows, inv_ref, block, span):
    first = ref[rows, span_slice(inv_ref, 2 * block, span)]
    second = ref[rows, span_slice(inv_ref, 2 * block + 1, span)]
    return jnp.concatenate([first, second], axis=1)


def row_pair(ref, head, inv_ref, block, span):
    first = ref[head, span_slice(inv_ref, 2 * block, span), :]
    second = ref[head, span_slice(inv_ref, 2 * block + 1, span), :]
    return jnp.concatenate([first, second], axis=0)


def attend_kernel(inv_ref, q_ref, k_ref, v_ref, o_ref, l_ref, acc_ref, *, blocks, span, group):
    wide = 2 * span
    row = lax.broadcasted_iota(jnp.int32, (wide, wide), 0)
    col = lax.broadcasted_iota(jnp.int32, (wide, wide), 1)
    keep = row <= col

    def one_block(block, odd):
        queries = [
            lane_pair(q_ref, slice(HD * h, HD * h + HD), inv_ref, block, span) for h in range(group)
        ]
        acc_ref[...] = jnp.zeros_like(acc_ref)

        def step(first, count, state, diagonal):
            state = list(state)
            keys = [row_pair(k_ref, 0, inv_ref, first + u, span) for u in range(count)]
            values = [lane_pair(v_ref, slice(0, HD), inv_ref, first + u, span) for u in range(count)]
            items = [(u, h) for u in range(count) for h in range(group)]
            scores = [dot(keys[u], queries[h], 1, 0) for u, h in items]
            probs = []
            for (u, h), score in zip(items, scores):
                peak, total = state[h]
                if diagonal and u == count - 1:
                    score = jnp.where(keep, score, neg_big)
                new_peak = jnp.maximum(peak, jnp.max(score, axis=0, keepdims=True))
                prob = jnp.exp(score - new_peak)
                shrink = jnp.exp(peak - new_peak)
                state[h] = (new_peak, total * shrink + jnp.sum(prob, axis=0, keepdims=True))
                probs.append((prob.astype(BF16), shrink))
            for (u, h), (prob, shrink) in zip(items, probs):
                cols = slice(h * wide, (h + 1) * wide)
                acc_ref[:, cols] = acc_ref[:, cols] * shrink + dot(values[u], prob, 1, 0)
            return tuple(state)

        state = tuple(
            (jnp.full((1, wide), neg_big, F32), jnp.zeros((1, wide), F32)) for _ in range(group)
        )
        state = lax.fori_loop(0, block // 4, lambda j, s: step(4 * j, 4, s, False), state)
        state = lax.fori_loop(
            2 * (block // 4), block // 2, lambda j, s: step(2 * j, 2, s, False), state
        )
        state = step(block - 1, 2, state, True) if odd else step(block, 1, state, True)
        mixed = jnp.concatenate(
            [acc_ref[:, wide * h : wide * (h + 1)] * (1.0 / state[h][1]) for h in range(group)], axis=0
        ).astype(BF16)
        logs = jnp.concatenate(
            [p + jnp.log(t) for p, t in state] + [jnp.zeros((8 - group, wide), F32)], axis=0
        )
        for part in range(2):
            where = span_slice(inv_ref, 2 * block + part, span)
            cols = slice(part * span, part * span + span)
            o_ref[:, where] = mixed[:, cols]
            l_ref[0, :, where] = logs[:, cols]

    def two_blocks(pair, _):
        for odd in (0, 1):
            one_block(2 * pair + odd, odd)
        return 0

    lax.fori_loop(0, blocks // 2, two_blocks, 0)


def attention_forward(inv, q_t, k_nat, v_t, span):
    tokens = q_t.shape[1]
    kv_heads = k_nat.shape[0]
    group = q_t.shape[0] // (kv_heads * HD)
    pairs = kv_heads * group * tokens * tokens
    wide_spec = pl.BlockSpec((group * HD, tokens), lambda g, i: (g, 0))
    nat_spec = pl.BlockSpec((1, tokens, HD), lambda g, i: (g, 0, 0))
    return pl.pallas_call(
        functools.partial(attend_kernel, blocks=tokens // (2 * span), span=span, group=group),
        grid_spec=pltpu.PrefetchScalarGridSpec(
            num_scalar_prefetch=1,
            grid=(kv_heads,),
            in_specs=[wide_spec, nat_spec, pl.BlockSpec((HD, tokens), lambda g, i: (g, 0))],
            out_specs=[
                wide_spec,
                pl.BlockSpec((1, 8, tokens), lambda g, i: (g, 0, 0)),
            ],
            scratch_shapes=[pltpu.VMEM((HD, group * 2 * span), F32)],
        ),
        out_shape=[
            jax.ShapeDtypeStruct(q_t.shape, BF16),
            jax.ShapeDtypeStruct((kv_heads, 8, tokens), F32),
        ],
        compiler_params=pltpu.CompilerParams(vmem_limit_bytes=VMEM_BYTES),
        cost_estimate=pl.CostEstimate(
            flops=16 * pairs * HD, bytes_accessed=tokens * 6000, transcendentals=pairs // 2
        ),
        name="attention_forward",
    )(inv, q_t, k_nat, v_t)


def attend_back_kernel(
    inv_ref, q_ref, kt_ref, k_ref, v_ref, o_ref, do_ref, l_ref, cos_ref, sin_ref,
    dq_ref, dk_ref, dv_ref, dk_sum, dv_sum, dq_sum, *, blocks, span, group,
):
    wide = 2 * span
    row = lax.broadcasted_iota(jnp.int32, (wide, wide), 0)
    col = lax.broadcasted_iota(jnp.int32, (wide, wide), 1)
    keep = row <= col
    half = HD // 2
    dk_sum[...] = jnp.zeros_like(dk_sum)
    dv_sum[...] = jnp.zeros_like(dv_sum)

    def rope_back(grad, cos, sin):
        top, low = grad[:half], grad[half:]
        return jnp.concatenate([top * cos + low * sin, low * cos - top * sin], axis=0)

    def one_block(block, odd):
        rows = [slice(HD * h, HD * h + HD) for h in range(group)]
        queries = [lane_pair(q_ref, r, inv_ref, block, span) for r in rows]
        grads = [lane_pair(do_ref, r, inv_ref, block, span) for r in rows]
        logs = lane_pair(l_ref.at[0], slice(None), inv_ref, block, span)
        deltas = [
            jnp.sum(
                lane_pair(o_ref, r, inv_ref, block, span).astype(F32) * grad.astype(F32),
                axis=0,
                keepdims=True,
            )
            for r, grad in zip(rows, grads)
        ]
        dq_sum[...] = jnp.zeros_like(dq_sum)

        def step(first, count, diagonal):
            keys = [row_pair(k_ref, 0, inv_ref, first + u, span) for u in range(count)]
            values = [row_pair(v_ref, 0, inv_ref, first + u, span) for u in range(count)]
            keys_t = [lane_pair(kt_ref, slice(0, HD), inv_ref, first + u, span) for u in range(count)]
            items = [(u, h) for u in range(count) for h in range(group)]
            ahead, ready, dqs, sums = {}, {}, {}, {}

            def products(i):
                u, h = items[i]
                ahead[i] = dot(keys[u], queries[h], 1, 0), dot(values[u], grads[h], 1, 0)

            def softmax_part(i):
                u, h = items[i]
                score, dprob = ahead.pop(i)
                prob = jnp.exp(score - logs[h : h + 1])
                if diagonal and u == count - 1:
                    prob = jnp.where(keep, prob, 0.0)
                ready[i] = prob.astype(BF16), (prob * (dprob - deltas[h])).astype(BF16)

            def gradients(i):
                u, h = items[i]
                prob, dscore = ready.pop(i)
                dq = dot(keys_t[u], dscore, 1, 0)
                dqs[h] = dqs[h] + dq if h in dqs else dq
                if u == count - 1:
                    dq_sum[:, wide * h : wide * (h + 1)] += dqs[h]
                dk, dv = dot(queries[h], dscore, 1, 1), dot(grads[h], prob, 1, 1)
                if u in sums:
                    dk, dv = dk + sums[u][0], dv + sums[u][1]
                sums[u] = dk, dv
                if h == group - 1:
                    place = pl.ds(pl.multiple_of((first + u) * wide, wide), wide)
                    dk_sum[:, place] += dk
                    dv_sum[:, place] += dv

            lead = 2
            for i in range(min(lead, len(items))):
                products(i)
            for i in range(len(items) + 1):
                if i + lead < len(items):
                    products(i + lead)
                if i > 0:
                    gradients(i - 1)
                if i < len(items):
                    softmax_part(i)

        def pair_step(j, _):
            step(2 * j, 2, False)
            return 0

        lax.fori_loop(0, block // 2, pair_step, 0)
        if odd:
            step(block - 1, 2, True)
        else:
            step(block, 1, True)
        cos = lane_pair(cos_ref, slice(None), inv_ref, block, span)
        sin = lane_pair(sin_ref, slice(None), inv_ref, block, span)
        dq = jnp.concatenate(
            [rope_back(dq_sum[:, wide * h : wide * (h + 1)] * HD**-0.5, cos, sin) for h in range(group)],
            axis=0,
        ).astype(BF16)
        place = pl.ds(pl.multiple_of(block * wide, wide), wide)
        dk = rope_back(dk_sum[:, place], cos, sin).astype(BF16)
        dv = dv_sum[:, place].astype(BF16)
        for part in range(2):
            where = span_slice(inv_ref, 2 * block + part, span)
            cols = slice(part * span, part * span + span)
            dq_ref[:, where] = dq[:, cols]
            dk_ref[:, where] = dk[:, cols]
            dv_ref[:, where] = dv[:, cols]

    def two_blocks(step, _):
        for odd in (1, 0):
            one_block(blocks - 2 - 2 * step + odd, odd)
        return 0

    lax.fori_loop(0, blocks // 2, two_blocks, 0)


def attention_backward(inv, q_t, k_t, k_nat, v_nat, o_t, do_t, logs, cos_t, sin_t, span):
    tokens = q_t.shape[1]
    kv_heads = k_nat.shape[0]
    group = q_t.shape[0] // (kv_heads * HD)
    pairs = kv_heads * group * tokens * tokens
    wide_spec = pl.BlockSpec((group * HD, tokens), lambda g, i: (g, 0))
    kv_spec = pl.BlockSpec((HD, tokens), lambda g, i: (g, 0))
    nat_spec = pl.BlockSpec((1, tokens, HD), lambda g, i: (g, 0, 0))
    tab_spec = pl.BlockSpec((HD // 2, tokens), lambda g, i: (0, 0))
    return pl.pallas_call(
        functools.partial(attend_back_kernel, blocks=tokens // (2 * span), span=span, group=group),
        grid_spec=pltpu.PrefetchScalarGridSpec(
            num_scalar_prefetch=1,
            grid=(kv_heads,),
            in_specs=[
                wide_spec, kv_spec, nat_spec, nat_spec, wide_spec, wide_spec,
                pl.BlockSpec((1, 8, tokens), lambda g, i: (g, 0, 0)), tab_spec, tab_spec,
            ],
            out_specs=[wide_spec, kv_spec, kv_spec],
            scratch_shapes=[
                pltpu.VMEM((HD, tokens), F32),
                pltpu.VMEM((HD, tokens), F32),
                pltpu.VMEM((HD, group * 2 * span), F32),
            ],
        ),
        out_shape=[
            jax.ShapeDtypeStruct(q_t.shape, BF16),
            jax.ShapeDtypeStruct(k_t.shape, BF16),
            jax.ShapeDtypeStruct(k_t.shape, BF16),
        ],
        compiler_params=pltpu.CompilerParams(vmem_limit_bytes=VMEM_BYTES),
        cost_estimate=pl.CostEstimate(
            flops=32 * pairs * HD, bytes_accessed=tokens * 9000, transcendentals=pairs // 2
        ),
        name="attention_backward",
    )(inv, q_t, k_t, k_nat, v_nat, o_t, do_t, logs, cos_t, sin_t)


def flip(index, bits):
    for bit in bits:
        index = index + bit * (1 - 2 * ((index // bit) % 2))
    return index


def bits_of(size):
    return [1 << i for i in range(size.bit_length() - 1)]


def seq_stages(seq):
    return [("seq", b) for b in reversed(bits_of(seq)[1:])] + [("seq", b) for b in bits_of(seq)[:1]]


def all_stages(dp, seq):
    return seq_stages(seq) + [("dp", b) for b in reversed(bits_of(dp))]


def arrival_order(stages, dp, seq, my_dp, my_seq):
    ids = jnp.arange(dp * seq, dtype=jnp.int32)
    away = {"dp": (ids // seq) ^ my_dp, "seq": (ids % seq) ^ my_seq}
    place = jnp.zeros_like(ids)
    for at, (axis, bit) in enumerate(stages):
        place = place + (1 << at) * ((away[axis] // bit) % 2)
    return place


def greet(peers):
    barrier = pltpu.get_barrier_semaphore()
    for peer in peers:
        pl.semaphore_signal(barrier, inc=1, device_id=peer, device_id_type=pl.DeviceIdType.MESH)
    pl.semaphore_wait(barrier, len(peers))


def seq_peer(my_dp, my_seq, away, seq):
    return my_dp, flip(my_seq, [b for b in bits_of(seq) if away & b])


def stage_peer(my_dp, my_seq, stage):
    axis, bit = stage
    return (flip(my_dp, [bit]), my_seq) if axis == "dp" else (my_dp, flip(my_seq, [bit]))


def all_peers(my_dp, my_seq, dp, seq):
    peers = [seq_peer(my_dp, my_seq, away, seq) for away in range(1, seq)]
    return peers + [(flip(my_dp, [b]), my_seq) for b in bits_of(dp)]


def bring_kernel(x_ref, first_ref, second_ref, out_ref, all_one_ref, all_two_ref,
                 local_sem, x_send, x_recv, w_send, w_recv, *, dp, seq):
    my_dp, my_seq = lax.axis_index("dp"), lax.axis_index("seq")
    orders = all_stages(dp, seq), seq_stages(seq)
    greet(all_peers(my_dp, my_seq, dp, seq))
    shards_in = (first_ref, second_ref)
    gathered = (all_one_ref, all_two_ref)

    def weight_copy(chain, stage):
        held = 1 << stage
        source = shards_in[chain] if stage == 0 else gathered[chain].at[pl.ds(0, held)]
        return pltpu.make_async_remote_copy(
            src_ref=source,
            dst_ref=gathered[chain].at[pl.ds(held, held)],
            send_sem=w_send.at[chain, stage],
            recv_sem=w_recv.at[chain, stage],
            device_id=stage_peer(my_dp, my_seq, orders[chain][stage]),
            device_id_type=pl.DeviceIdType.MESH,
        )

    copies = [[weight_copy(c, s) for s in range(len(orders[c]))] for c in range(2)]
    for c in range(2):
        copies[c][0].start()
    own = [
        pltpu.make_async_copy(shards_in[c], gathered[c].at[pl.ds(0, 1)], local_sem.at[c]) for c in range(2)
    ]
    own.append(pltpu.make_async_copy(x_ref.at[my_seq], out_ref.at[my_seq], local_sem.at[2]))
    for copy in own:
        copy.start()
    moves = []
    for away in range(1, seq):
        peer = seq_peer(my_dp, my_seq, away, seq)
        moves.append(
            pltpu.make_async_remote_copy(
                src_ref=x_ref.at[peer[1]],
                dst_ref=out_ref.at[my_seq],
                send_sem=x_send.at[away - 1],
                recv_sem=x_recv.at[away - 1],
                device_id=peer,
                device_id_type=pl.DeviceIdType.MESH,
            )
        )
    for c in range(2):
        own[c].wait()
    for stage in range(1, len(orders[0])):
        for c in range(2):
            if stage < len(orders[c]):
                copies[c][stage - 1].wait_recv()
                copies[c][stage].start()
        if stage == 1:
            for move in moves:
                move.start()
    for c in range(2):
        copies[c][-1].wait_recv()
        for copy in copies[c]:
            copy.wait_send()
    for move in moves:
        move.wait()
    own[2].wait()


def bring(x, first, second):
    dp, seq = lax.axis_size("dp"), lax.axis_size("seq")
    stages = len(all_stages(dp, seq))
    hbm = pl.BlockSpec(memory_space=pl.ANY)
    return pl.pallas_call(
        functools.partial(bring_kernel, dp=dp, seq=seq),
        in_specs=[hbm] * 3,
        out_specs=[hbm] * 3,
        out_shape=[
            jax.ShapeDtypeStruct(x.shape, x.dtype),
            jax.ShapeDtypeStruct((dp * seq, *first.shape[1:]), first.dtype),
            jax.ShapeDtypeStruct((seq, *second.shape[1:]), second.dtype),
        ],
        scratch_shapes=[
            pltpu.SemaphoreType.DMA((3,)),
            pltpu.SemaphoreType.DMA((seq - 1,)),
            pltpu.SemaphoreType.DMA((seq - 1,)),
            pltpu.SemaphoreType.DMA((2, stages)),
            pltpu.SemaphoreType.DMA((2, stages)),
        ],
        compiler_params=pltpu.CompilerParams(
            collective_id=1, has_side_effects=True, vmem_limit_bytes=VMEM_BYTES
        ),
        name="bring",
    )(x, first, second)


def qkv_kernel(where_ref, x_ref, gain_ref, packed_ref, cos_ref, sin_ref,
               q_ref, kt_ref, vt_ref, k_ref, v_ref, w_ref, w_wide, *, heads, kv_heads, dp, seq):
    half = HD // 2
    width = w_ref.shape[1]
    q_cols, kv_cols = width // seq, kv_heads * HD // seq
    kv_width = kv_heads * HD

    @pl.when(pl.program_id(0) == 0)
    def _():
        for s in range(seq):
            block = jnp.concatenate([packed_ref[where_ref[d * seq + s]] for d in range(dp)], axis=0)
            turned = block.astype(F32).T
            w_wide[q_cols * s : q_cols * s + q_cols, :] = turned[:q_cols]
            first = width + kv_cols * s
            w_wide[first : first + kv_cols, :] = turned[q_cols : q_cols + kv_cols]
            first += kv_width
            w_wide[first : first + kv_cols, :] = turned[q_cols + kv_cols : q_cols + 2 * kv_cols]
        w_ref[...] = w_wide[...].astype(BF16)

    x = x_ref[0].astype(F32)
    rstd = lax.rsqrt(jnp.mean(x * x, axis=0, keepdims=True) + eps_norm)
    normed = (x * rstd * gain_ref[...]).astype(BF16)
    lin = dot(w_ref[...], normed, 1, 0)
    cos, sin = cos_ref[...], sin_ref[...]
    for head in range(heads + kv_heads):
        top = lin[HD * head : HD * head + half]
        low = lin[HD * head + half : HD * head + HD]
        rot = jnp.concatenate([top * cos - low * sin, low * cos + top * sin], axis=0)
        if head < heads:
            q_ref[HD * head : HD * head + HD, :] = rot.astype(BF16) * jnp.asarray(HD**-0.5, BF16)
        else:
            kv = head - heads
            kt_ref[HD * kv : HD * kv + HD, :] = rot.astype(BF16)
            k_ref[kv] = rot.T.astype(BF16)
    for kv in range(kv_heads):
        first = HD * (heads + kv_heads + kv)
        val = lin[first : first + HD]
        vt_ref[HD * kv : HD * kv + HD, :] = val.astype(BF16)
        v_ref[kv] = val.T.astype(BF16)


def project_qkv(where, x, gain, packed, cos_t, sin_t, heads, kv_heads, rows):
    blocks, width, block = x.shape
    tokens = blocks * block
    feats = (heads + 2 * kv_heads) * HD
    dp, seq = lax.axis_size("dp"), lax.axis_size("seq")
    col = lambda rows: pl.BlockSpec((rows, block), lambda i, w: (0, i))
    nat = pl.BlockSpec((kv_heads, block, HD), lambda i, w: (0, i, 0))
    return pl.pallas_call(
        functools.partial(qkv_kernel, heads=heads, kv_heads=kv_heads, dp=dp, seq=seq),
        grid_spec=pltpu.PrefetchScalarGridSpec(
            num_scalar_prefetch=1,
            grid=(blocks,),
            in_specs=[
                pl.BlockSpec((1, width, block), lambda i, w: (i, 0, 0)),
                pl.BlockSpec((width, 1), lambda i, w: (0, 0)),
                pl.BlockSpec((dp * seq, rows, packed.shape[2]), lambda i, w: (0, 0, 0)),
                col(HD // 2),
                col(HD // 2),
            ],
            out_specs=[
                col(heads * HD), col(kv_heads * HD), col(kv_heads * HD), nat, nat,
                pl.BlockSpec((feats, width), lambda i, w: (0, 0)),
            ],
            scratch_shapes=[pltpu.VMEM((feats, width), F32)],
        ),
        out_shape=[
            jax.ShapeDtypeStruct((heads * HD, tokens), BF16),
            jax.ShapeDtypeStruct((kv_heads * HD, tokens), BF16),
            jax.ShapeDtypeStruct((kv_heads * HD, tokens), BF16),
            jax.ShapeDtypeStruct((kv_heads, tokens, HD), BF16),
            jax.ShapeDtypeStruct((kv_heads, tokens, HD), BF16),
            jax.ShapeDtypeStruct((feats, width), BF16),
        ],
        compiler_params=pltpu.CompilerParams(vmem_limit_bytes=VMEM_BYTES),
        cost_estimate=pl.CostEstimate(
            flops=4 * tokens * width * feats, bytes_accessed=tokens * 5000, transcendentals=0
        ),
        name="project_qkv",
    )(where, x, gain, packed, cos_t, sin_t)


def side_by_side(ref):
    return jnp.concatenate([ref[i] for i in range(ref.shape[0])], axis=1)


def mlp_kernel(
    where_ref, x_ref, mixed_ref, dy_ref, gain_ref, *more, chunk, dp, seq,
):
    packs = more[:dp]
    out_ref, dmid_ref, dmixed_ref, grads_ref, gain_grad_ref = more[dp : dp + 5]
    (o_w, o_t, gate_w, gate_t, up_w, up_t, down_w, down_t, o_sum, gate_sum, up_sum, down_sum, gain_sum,
     pack, pack_sem) = more[dp + 5 :]
    step, steps = pl.program_id(0), pl.num_programs(0)
    width, ff = gate_w.shape
    lanes = pack.shape[3]
    rows = width // dp
    o_cols, ff_cols, ff_rows = width // seq, ff // seq, ff // dp
    spare = ff_cols - lanes
    padded = -(-o_cols // 16) * 16

    @pl.when(step == 0)
    def _():
        for total in (o_sum, gate_sum, up_sum, down_sum, gain_sum):
            total[...] = jnp.zeros_like(total)
        fetches = [
            pltpu.make_async_copy(
                packs[i], pack.at[flip(lax.axis_index("dp"), row_bits(i, dp))], pack_sem.at[i]
            )
            for i in range(dp)
        ]
        for fetch in fetches:
            fetch.start()
        for fetch in fetches:
            fetch.wait()
        for s in range(seq):
            at = where_ref[s]
            stack = lambda first: jnp.concatenate(
                [pack[d, at, first : first + rows, :] for d in range(dp)], axis=0
            ).astype(F32).T
            o_sum[o_cols * s : o_cols * s + o_cols, :] = stack(0)[:o_cols]
            gate_t[ff_cols * s : ff_cols * s + lanes, :] = stack(rows).astype(BF16)
            up_t[ff_cols * s : ff_cols * s + lanes, :] = stack(2 * rows).astype(BF16)
            both = stack(3 * rows).astype(BF16)
            gate_t[ff_cols * s + lanes : ff_cols * (s + 1), :] = both[:spare]
            up_t[ff_cols * s + lanes : ff_cols * (s + 1), :] = both[spare : 2 * spare]
            for d in range(dp):
                for t in range(ff_rows // lanes):
                    first = 4 * rows + padded * t
                    piece = pack[d, at, first : first + padded, :].astype(F32)[:o_cols]
                    cols = slice(ff_rows * d + lanes * t, ff_rows * d + lanes * (t + 1))
                    down_sum[o_cols * s : o_cols * s + o_cols, cols] = piece
        o_t[...] = o_sum[...].astype(BF16)
        o_w[...] = o_sum[...].T.astype(BF16)
        down_t[...] = down_sum[...].astype(BF16)
        for first in range(0, ff, lanes):
            part = slice(first, first + lanes)
            down_w[part, :] = down_sum[:, part].T.astype(BF16)
            gate_w[:, part] = gate_t[part, :].T
            up_w[:, part] = up_t[part, :].T
        o_sum[...] = jnp.zeros_like(o_sum)
        down_sum[...] = jnp.zeros_like(down_sum)

    gain = gain_ref[...]
    mixed = mixed_ref[...]
    mid = dot(o_t[...], mixed, 1, 0) + side_by_side(x_ref).astype(F32)
    rstd = lax.rsqrt(jnp.mean(mid * mid, axis=0, keepdims=True) + eps_norm)
    normed = (mid * rstd * gain).astype(BF16)
    dy = side_by_side(dy_ref)
    added = jnp.zeros_like(mid)
    dnormed = jnp.zeros_like(mid)
    for first in range(0, ff, chunk):
        part = slice(first, first + chunk)
        gate = dot(gate_t[part, :], normed, 1, 0)
        up = dot(up_t[part, :], normed, 1, 0)
        dinner = dot(down_w[part, :], dy, 1, 0)
        sig = 1.0 / (1.0 + jnp.exp(-gate))
        silu = gate * sig
        inner = (silu * up).astype(BF16)
        dup = (dinner * silu).astype(BF16)
        dgate = (dinner * up * sig * (1.0 + gate * (1.0 - sig))).astype(BF16)
        added += dot(down_t[:, part], inner, 1, 0)
        dnormed += dot(gate_w[:, part], dgate, 1, 0)
        dnormed += dot(up_w[:, part], dup, 1, 0)
        down_sum[:, part] += dot(dy, inner, 1, 1)
        gate_sum[part, :] += dot(dgate, normed, 1, 1)
        up_sum[part, :] += dot(dup, normed, 1, 1)
    out = (mid + added).astype(BF16)
    scaled_mid = mid * rstd
    product = dnormed * scaled_mid
    gain_sum[...] += sum(product[:, c : c + lanes] for c in range(0, product.shape[1], lanes))
    scaled = dnormed * gain
    pull = jnp.mean(scaled * mid, axis=0, keepdims=True)
    dmid = dy.astype(F32) + rstd * scaled - scaled_mid * (rstd * rstd * pull)
    dmid_low = dmid.astype(BF16)
    block = out_ref.shape[2]
    for i in range(out_ref.shape[0]):
        out_ref[i] = out[:, block * i : block * (i + 1)]
        dmid_ref[i] = dmid[:, block * i : block * (i + 1)]
    o_sum[...] += dot(dmid_low, mixed, 1, 1)
    dmixed_ref[...] = dot(o_w[...], dmid_low, 1, 0).astype(BF16)

    @pl.when(step == steps - 1)
    def _():
        gain_grad_ref[...] = jnp.sum(gain_sum[...].T, axis=0, keepdims=True)
        for s in range(seq):
            tall = lambda total, first, count: total[first : first + count, :]
            blank = jnp.zeros((lanes - o_cols, width), F32)
            o_piece = jnp.concatenate([tall(o_sum, o_cols * s, o_cols), blank], axis=0).T.astype(BF16)
            gate_piece = tall(gate_sum, ff_cols * s, lanes).T.astype(BF16)
            up_piece = tall(up_sum, ff_cols * s, lanes).T.astype(BF16)
            both = jnp.concatenate(
                [tall(gate_sum, ff_cols * s + lanes, spare), tall(up_sum, ff_cols * s + lanes, spare)], axis=0
            ).T.astype(BF16)
            for d in range(dp):
                at = d * seq + s
                band = slice(rows * d, rows * (d + 1))
                for i, piece in enumerate((o_piece, gate_piece, up_piece, both)):
                    grads_ref[at, rows * i : rows * (i + 1), :] = piece[band]
                for t in range(ff_rows // lanes):
                    first = 4 * rows + padded * t
                    cols = slice(ff_rows * d + lanes * t, ff_rows * d + lanes * (t + 1))
                    piece = down_sum[o_cols * s : o_cols * (s + 1), cols]
                    piece = jnp.concatenate([piece, jnp.zeros((padded - o_cols, lanes), F32)], axis=0)
                    grads_ref[at, first : first + padded, :] = piece.astype(BF16)


def row_bits(at, dp):
    return [b for i, b in enumerate(reversed(bits_of(dp))) if (at >> i) & 1]


def gather_rows(array, dp):
    held = [array]
    for at in range(1, dp):
        mask = sum(row_bits(at, dp))
        held.append(lax.ppermute(array, "dp", [(i, i ^ mask) for i in range(dp)]))
    return held


def mlp_both(where, x, mixed, dy, gain, packs, ff, batch=2, chunk=512):
    blocks, width, block = x.shape
    tokens = blocks * block
    dp, seq = lax.axis_size("dp"), lax.axis_size("seq")
    grad_rows, lanes = packs[0].shape[1:]
    tok = pl.BlockSpec((batch, width, block), lambda i, w: (i, 0, 0))
    col = pl.BlockSpec((width, batch * block), lambda i, w: (0, i))
    once = lambda shape: pl.BlockSpec(
        shape, lambda i, w: (0,) * len(shape), pipeline_mode=pl.Buffered(1)
    )
    hbm = pl.BlockSpec(memory_space=pl.ANY)
    return pl.pallas_call(
        functools.partial(mlp_kernel, chunk=chunk, dp=dp, seq=seq),
        grid_spec=pltpu.PrefetchScalarGridSpec(
            num_scalar_prefetch=1,
            grid=(blocks // batch,),
            in_specs=[tok, col, tok, once((width, 1))] + [hbm] * dp,
            out_specs=[tok, tok, col, once((dp * seq, grad_rows, lanes)), once((1, width))],
            scratch_shapes=[
                pltpu.VMEM((width, width), BF16),
                pltpu.VMEM((width, width), BF16),
                pltpu.VMEM((width, ff), BF16),
                pltpu.VMEM((ff, width), BF16),
                pltpu.VMEM((width, ff), BF16),
                pltpu.VMEM((ff, width), BF16),
                pltpu.VMEM((ff, width), BF16),
                pltpu.VMEM((width, ff), BF16),
                pltpu.VMEM((width, width), F32),
                pltpu.VMEM((ff, width), F32),
                pltpu.VMEM((ff, width), F32),
                pltpu.VMEM((width, ff), F32),
                pltpu.VMEM((width, lanes), F32),
                pltpu.VMEM((dp, *packs[0].shape), BF16),
                pltpu.SemaphoreType.DMA((dp,)),
            ],
        ),
        out_shape=[
            jax.ShapeDtypeStruct(x.shape, BF16),
            jax.ShapeDtypeStruct(x.shape, F32),
            jax.ShapeDtypeStruct((width, tokens), BF16),
            jax.ShapeDtypeStruct((dp * seq, grad_rows, lanes), BF16),
            jax.ShapeDtypeStruct((1, width), F32),
        ],
        compiler_params=pltpu.CompilerParams(vmem_limit_bytes=60 * 2**20),
        cost_estimate=pl.CostEstimate(
            flops=2 * tokens * width * (9 * ff + 3 * width),
            bytes_accessed=tokens * width * 14,
            transcendentals=tokens * ff,
        ),
        name="mlp_both",
    )(where, x, mixed, dy, gain, *packs)


def across(index, other, size):
    for bit in bits_of(size):
        index = index + bit * ((other // bit) % 2) * (1 - 2 * ((index // bit) % 2))
    return index


def finish_kernel(
    x_ref, dmid_ref, dq_ref, dk_ref, dv_ref, gain_ref, w_t_ref, other_gain_ref,
    out_ref, grads_ref, gains_ref,
    w_nat, w_sum, gain_sum, din, packed, landed, gain_held, gain_landed,
    own_sem, d_send, d_recv, r_send, r_recv, g_send, g_recv, *, dp, seq, kv_width,
):
    step, steps = pl.program_id(0), seq // 2
    my_dp, my_seq = lax.axis_index("dp"), lax.axis_index("seq")
    width = w_nat.shape[0]
    lanes = grads_ref.shape[1]
    rows = width // dp
    q_cols, kv_cols = width // seq, kv_width // seq
    stages = all_stages(dp, seq)

    @pl.when(step == 0)
    def _():
        greet(all_peers(my_dp, my_seq, dp, seq))
        w_sum[...] = jnp.zeros_like(w_sum)
        gain_sum[...] = jnp.zeros_like(gain_sum)
        w_nat[...] = w_t_ref[...].T

    gain = gain_ref[...]
    x = side_by_side(x_ref).astype(F32)
    rstd = lax.rsqrt(jnp.mean(x * x, axis=0, keepdims=True) + eps_norm)
    scaled_x = x * rstd
    normed = (scaled_x * gain).astype(BF16)
    dlin = jnp.concatenate([dq_ref[...], dk_ref[...], dv_ref[...]], axis=0)
    w_sum[...] += dot(dlin, normed, 1, 1)
    dnormed = dot(w_nat[...], dlin, 1, 0)
    product = dnormed * scaled_x
    gain_sum[...] += sum(product[:, c : c + lanes] for c in range(0, product.shape[1], lanes))
    scaled = dnormed * gain
    pull = jnp.mean(scaled * x, axis=0, keepdims=True)
    total = side_by_side(dmid_ref) + rstd * scaled - scaled_x * (rstd * rstd * pull)
    pair = across(my_seq // 2, steps - 1 - step, seq // 2)
    block = din.shape[2]
    for i in range(2):
        din[2 * pair + i] = total[:, block * i : block * (i + 1)].astype(BF16)

    def move(away):
        peer = seq_peer(my_dp, my_seq, away, seq)
        return pltpu.make_async_remote_copy(
            src_ref=din.at[peer[1]],
            dst_ref=out_ref.at[my_seq],
            send_sem=d_send.at[away - 1],
            recv_sem=d_recv.at[away - 1],
            device_id=peer,
            device_id_type=pl.DeviceIdType.MESH,
        )

    for back in range(1, steps):

        @pl.when(step == steps - 1 - back)
        def _():
            move(2 * back).start()
            move(2 * back + 1).start()

    @pl.when(step == steps - 1)
    def _():
        move(1).start()
        own = pltpu.make_async_copy(din.at[my_seq], out_ref.at[my_seq], own_sem)
        own.start()
        blank = jnp.zeros((lanes - q_cols - 2 * kv_cols, width), F32)
        for s in range(seq):
            first = width + kv_cols * s
            piece = jnp.concatenate(
                [
                    w_sum[q_cols * s : q_cols * (s + 1), :],
                    w_sum[first : first + kv_cols, :],
                    w_sum[first + kv_width : first + kv_width + kv_cols, :],
                    blank,
                ],
                axis=0,
            ).T.astype(BF16)
            for d in range(dp):
                place = 0
                for at, (axis, bit) in enumerate(stages):
                    mine = ((my_dp if axis == "dp" else my_seq) // bit) % 2
                    theirs = ((d if axis == "dp" else s) // bit) % 2
                    place = place + (1 << at) * (1 - mine if theirs else mine)
                packed[place] = piece[rows * d : rows * (d + 1)]
        gain_row = jnp.sum(gain_sum[...].T, axis=0, keepdims=True)
        gain_held[0] = jnp.concatenate(
            [gain_row, other_gain_ref[...], jnp.zeros((6, width), F32)], axis=0
        )
        sent = []
        for turn, at in enumerate(reversed(range(len(stages)))):
            half = 1 << at
            peer = stage_peer(my_dp, my_seq, stages[at])
            send = pltpu.make_async_remote_copy(
                src_ref=packed.at[pl.ds(half, half)],
                dst_ref=landed.at[pl.ds(half, half)],
                send_sem=r_send.at[at],
                recv_sem=r_recv.at[at],
                device_id=peer,
                device_id_type=pl.DeviceIdType.MESH,
            )
            gain_copy = pltpu.make_async_remote_copy(
                src_ref=gain_held.at[turn],
                dst_ref=gain_landed.at[turn],
                send_sem=g_send.at[turn],
                recv_sem=g_recv.at[turn],
                device_id=peer,
                device_id_type=pl.DeviceIdType.MESH,
            )
            send.start()
            gain_copy.start()
            sent += [send, gain_copy]
            gain_copy.wait_recv()
            gain_held[turn + 1] = gain_held[turn] + gain_landed[turn]
            send.wait_recv()
            both = packed[0:half].astype(F32) + landed[half : 2 * half].astype(F32)
            if at == 0:
                grads_ref[...] = both[0]
            else:
                packed[0:half] = both.astype(BF16)
        gains_ref[...] = gain_held[len(stages)]
        for copy in sent:
            copy.wait_send()
        for away in range(1, seq):
            move(away).wait()
        own.wait()


def finish(x, dmid, dq_t, dk_t, dv_t, gain, w_t, other_gain, lanes):
    blocks, width, block = x.shape
    tokens = blocks * block
    feats = w_t.shape[0]
    dp, seq = lax.axis_size("dp"), lax.axis_size("seq")
    rows = width // dp
    stages = len(all_stages(dp, seq))

    def pair(i):
        return across(lax.axis_index("seq") // 2, seq // 2 - 1 - i, seq // 2)

    tok = pl.BlockSpec((2, width, block), lambda i: (pair(i), 0, 0))
    col = lambda rows: pl.BlockSpec((rows, 2 * block), lambda i: (0, pair(i)))
    once = lambda shape: pl.BlockSpec(shape, lambda i: (0,) * len(shape), pipeline_mode=pl.Buffered(1))
    return pl.pallas_call(
        functools.partial(finish_kernel, dp=dp, seq=seq, kv_width=dk_t.shape[0]),
        grid=(blocks // 2,),
        in_specs=[
            tok, tok, col(dq_t.shape[0]), col(dk_t.shape[0]), col(dv_t.shape[0]),
            once((width, 1)), once((feats, width)), once((1, width)),
        ],
        out_specs=[pl.BlockSpec(memory_space=pl.ANY), once((rows, lanes)), once((8, width))],
        out_shape=[
            jax.ShapeDtypeStruct(x.shape, BF16),
            jax.ShapeDtypeStruct((rows, lanes), F32),
            jax.ShapeDtypeStruct((8, width), F32),
        ],
        scratch_shapes=[
            pltpu.VMEM((width, feats), BF16),
            pltpu.VMEM((feats, width), F32),
            pltpu.VMEM((width, lanes), F32),
            pltpu.VMEM(x.shape, BF16),
            pltpu.VMEM((dp * seq, rows, lanes), BF16),
            pltpu.VMEM((dp * seq, rows, lanes), BF16),
            pltpu.VMEM((stages + 1, 8, width), F32),
            pltpu.VMEM((stages, 8, width), F32),
            pltpu.SemaphoreType.DMA,
            pltpu.SemaphoreType.DMA((seq - 1,)),
            pltpu.SemaphoreType.DMA((seq - 1,)),
            pltpu.SemaphoreType.DMA((stages,)),
            pltpu.SemaphoreType.DMA((stages,)),
            pltpu.SemaphoreType.DMA((stages,)),
            pltpu.SemaphoreType.DMA((stages,)),
        ],
        compiler_params=pltpu.CompilerParams(
            collective_id=2, has_side_effects=True, vmem_limit_bytes=VMEM_BYTES
        ),
        cost_estimate=pl.CostEstimate(
            flops=4 * tokens * width * feats, bytes_accessed=tokens * width * 12, transcendentals=0
        ),
        name="finish",
    )(x, dmid, dq_t, dk_t, dv_t, gain, w_t, other_gain)


def exchange(blocks):
    return lax.all_to_all(blocks, "seq", 0, 0, tiled=True)


def pad_lanes(matrix, lanes):
    return jnp.pad(matrix, ((0, 0), (0, lanes - matrix.shape[1])))


def shards_sequences(
    hidden_in, span_order, attn_gain, q_weight, k_weight, v_weight, o_weight, mlp_gain,
    gate_weight, up_weight, down_weight, out_grad,
):
    lanes = 128
    seqs, slots, width = hidden_in.shape
    dp, seq = lax.axis_size("dp"), lax.axis_size("seq")
    tokens = slots * seq
    span = tokens // span_order.shape[0]
    heads = width // HD
    kv_heads = k_weight.shape[1] * seq // HD
    rows, q_cols = q_weight.shape
    kv_cols = k_weight.shape[1]
    ff = down_weight.shape[0] * dp
    ff_rows = down_weight.shape[0]
    padded = -(-q_cols // 16) * 16

    first = pad_lanes(jnp.concatenate([q_weight, k_weight, v_weight], axis=1), lanes)
    down_turned = jnp.pad(down_weight.T, ((0, padded - q_cols), (0, 0)))
    second = jnp.concatenate(
        [
            pad_lanes(o_weight, lanes),
            gate_weight[:, :lanes],
            up_weight[:, :lanes],
            jnp.concatenate([gate_weight[:, lanes:], up_weight[:, lanes:]], axis=1),
        ]
        + [down_turned[:, c : c + lanes] for c in range(0, ff_rows, lanes)],
        axis=0,
    )
    x, first_all, second_row = bring(hidden_in.transpose(0, 2, 1), first[None], second[None])
    out_grad, x = lax.optimization_barrier((out_grad, x))
    dy = exchange(out_grad.transpose(0, 2, 1))
    second_all = gather_rows(second_row, dp)

    my_dp, my_seq = lax.axis_index("dp"), lax.axis_index("seq")
    where_first = arrival_order(all_stages(dp, seq), dp, seq, my_dp, my_seq)
    where_second = arrival_order(seq_stages(seq), dp, seq, my_dp, my_seq)[:seq]
    inv = jnp.argsort(span_order).astype(jnp.int32)
    slot_pos = slot_positions(jnp.arange(tokens, dtype=jnp.int32), span_order, span)
    inv_freq = rope_base ** (-(jnp.arange(HD // 2, dtype=F32) * 2.0) / HD)
    angles = slot_pos.astype(F32)[None, :] * inv_freq[:, None]
    cos_t, sin_t = jnp.cos(angles), jnp.sin(angles)
    gain_one = attn_gain.astype(F32)[:, None]
    gain_two = mlp_gain.astype(F32)[:, None]

    q_t, k_t, v_t, k_nat, v_nat, w_t = project_qkv(
        where_first, x, gain_one, first_all, cos_t, sin_t, heads, kv_heads, rows
    )
    o_t, logs = attention_forward(inv, q_t, k_nat, v_t, span)
    out, dmid, do_t, rest_grads, gain_two_term = mlp_both(
        where_second, x, o_t, dy, gain_two, second_all, ff
    )
    hidden_out = exchange(out).transpose(0, 2, 1)
    rest_sum = lax.psum_scatter(rest_grads, ("dp", "seq"), scatter_dimension=0, tiled=True)[0].astype(F32)

    dq_t, dk_t, dv_t = attention_backward(
        inv, q_t, k_t, k_nat, v_nat, o_t, do_t, logs, cos_t, sin_t, span
    )
    din, qkv_sum, gains = finish(x, dmid, dq_t, dk_t, dv_t, gain_one, w_t, gain_two_term, lanes)
    grad_in = din.astype(F32).transpose(0, 2, 1)
    o_sum, gate_sum, up_sum, both_sum = [rest_sum[rows * i : rows * (i + 1)] for i in range(4)]
    spare = gate_weight.shape[1] - lanes
    down_sum = jnp.concatenate(
        [
            rest_sum[4 * rows + padded * t : 4 * rows + padded * t + q_cols]
            for t in range(ff_rows // lanes)
        ],
        axis=1,
    )
    return (
        hidden_out,
        grad_in,
        gains[0],
        qkv_sum[:, :q_cols],
        qkv_sum[:, q_cols : q_cols + kv_cols],
        qkv_sum[:, q_cols + kv_cols : q_cols + 2 * kv_cols],
        o_sum[:, :q_cols],
        gains[1],
        jnp.concatenate([gate_sum, both_sum[:, :spare]], axis=1),
        jnp.concatenate([up_sum, both_sum[:, spare:]], axis=1),
        down_sum.T,
    )


def shards(*args):
    seqs, spans = args[0].shape[0], args[1].shape[0]
    if seqs == lax.axis_size("seq") and spans % 4 == 0:
        return shards_sequences(*args)
    return shards_general(*args)


def solution(mesh):
    placed = (
        P("dp", "seq", None),
        P(),
        P(),
        P("dp", "seq"),
        P("dp", "seq"),
        P("dp", "seq"),
        P("dp", "seq"),
        P(),
        P("dp", "seq"),
        P("dp", "seq"),
        P("dp", "seq"),
        P("dp", "seq", None),
    )
    return jax.shard_map(
        shards,
        mesh=mesh,
        in_specs=placed,
        out_specs=(
            P("dp", "seq", None),
            P("dp", "seq", None),
            P(),
            P("dp", "seq"),
            P("dp", "seq"),
            P("dp", "seq"),
            P("dp", "seq"),
            P(),
            P("dp", "seq"),
            P("dp", "seq"),
            P("dp", "seq"),
        ),
        check_vma=False,
    )
```

```python
import functools

import jax
import jax.numpy as jnp
from jax import lax
from jax.experimental import pallas as pl
from jax.experimental.pallas import tpu as pltpu
from jax.sharding import PartitionSpec as P

HD = 64
MICRO = 2


eps_norm = 1e-05
rope_base = 100000.0
neg_big = -1e30


def slot_positions(slot_ids, span_order, span_len):
    span_ids = slot_ids // span_len
    span_hits = span_ids[:, None] == jnp.arange(span_order.shape[0], dtype=jnp.int32)[None, :]
    starts = jnp.sum(jnp.where(span_hits, span_order[None, :], 0), axis=1)
    return starts * span_len + slot_ids % span_len


def rope_tables(slot_pos):
    half_width = HD // 2
    inv_freq = rope_base ** (-(jnp.arange(half_width, dtype=jnp.float32) * 2.0) / HD)
    angles = slot_pos.astype(jnp.float32)[:, None] * inv_freq[None, :]
    cosine = jnp.concatenate([jnp.cos(angles), jnp.cos(angles)], axis=1)
    sine_tab = jnp.concatenate([jnp.sin(angles), jnp.sin(angles)], axis=1)
    return (cosine[:, None, :], sine_tab[:, None, :])


def rotate(vector, cosine, sine_tab):
    half_width = vector.shape[-1] // 2
    turned = jnp.concatenate([-vector[..., half_width:], vector[..., :half_width]], axis=-1)
    return vector * cosine + turned * sine_tab


def rotate_back(grad_out, cosine, sine_tab):
    half_width = grad_out.shape[-1] // 2
    scaled = grad_out * sine_tab
    turned = jnp.concatenate([scaled[..., half_width:], -scaled[..., :half_width]], axis=-1)
    return grad_out * cosine + turned


def norm_back(vector, rstd_vec, gain_vec, grad_n):
    scaled = grad_n * gain_vec
    gain_term = jnp.sum(grad_n * vector * rstd_vec, axis=0)
    grad_vec = rstd_vec * scaled - vector * rstd_vec**3 * jnp.mean(
        scaled * vector, axis=-1, keepdims=True
    )
    return (grad_vec, gain_term)


def add_tuples(old_sums, new_terms):
    if old_sums is None:
        return tuple(new_terms)
    return tuple((old_sum + new_term for old_sum, new_term in zip(old_sums, new_terms)))


def shards_general(
    hidden_in,
    span_order,
    attn_gain,
    q_weight,
    k_weight,
    v_weight,
    o_weight,
    mlp_gain,
    gate_weight,
    up_weight,
    down_weight,
    out_grad,
):
    local_seqs, row_count, model_width = hidden_in.shape
    seq_parts = lax.axis_size("seq")
    full_length = row_count * seq_parts
    span_len = full_length // (2 * seq_parts)
    per_micro = local_seqs // MICRO
    kv_width = k_weight.shape[1] * seq_parts
    kv_heads = kv_width // HD
    head_count = model_width // HD
    group_size = head_count // kv_heads
    tok_count = per_micro * row_count
    score_scale = HD ** (-0.5)
    own_slots = lax.axis_index("seq") * row_count + jnp.arange(row_count, dtype=jnp.int32)
    own_pos = slot_positions(own_slots, span_order, span_len)
    all_pos = slot_positions(jnp.arange(full_length, dtype=jnp.int32), span_order, span_len)
    allowed = own_pos[:, None] >= all_pos[None, :]
    cos_own, sin_own = rope_tables(own_pos)
    gain_attn = attn_gain.astype(jnp.float32)
    gain_mlp = mlp_gain.astype(jnp.float32)

    def attend(inputs):
        queries, key_rows, value_rows = inputs
        query_grp = queries.reshape(row_count, kv_heads, group_size, HD)
        key_grp = key_rows.reshape(full_length, kv_heads, HD)
        value_grp = value_rows.reshape(full_length, kv_heads, HD)
        scores = (
            jnp.einsum("rkgd,lkd->kgrl", query_grp, key_grp, preferred_element_type=jnp.float32)
            * score_scale
        )
        scores = jnp.where(allowed, scores, neg_big)
        row_peak = jnp.max(scores, axis=-1, keepdims=True)
        exp_scores = jnp.exp(scores - row_peak)
        row_total = jnp.sum(exp_scores, axis=-1, keepdims=True)
        attn_probs = exp_scores / row_total
        log_total = row_peak + jnp.log(row_total)
        mixed = jnp.einsum(
            "kgrl,lkd->rkgd",
            attn_probs.astype(jnp.bfloat16),
            value_grp,
            preferred_element_type=jnp.float32,
        )
        return (mixed.astype(jnp.bfloat16).reshape(row_count, model_width), log_total)

    def attend_back(inputs):
        queries, key_rows, value_rows, grad_mix, log_total = inputs
        query_grp = queries.reshape(row_count, kv_heads, group_size, HD)
        key_grp = key_rows.reshape(full_length, kv_heads, HD)
        value_grp = value_rows.reshape(full_length, kv_heads, HD)
        grad_grp = grad_mix.reshape(row_count, kv_heads, group_size, HD)
        scores = (
            jnp.einsum("rkgd,lkd->kgrl", query_grp, key_grp, preferred_element_type=jnp.float32)
            * score_scale
        )
        scores = jnp.where(allowed, scores, neg_big)
        attn_probs = jnp.exp(scores - log_total)
        probs_low = attn_probs.astype(jnp.bfloat16)
        grad_probs = jnp.einsum(
            "rkgd,lkd->kgrl", grad_grp, value_grp, preferred_element_type=jnp.float32
        )
        row_delta = jnp.sum(attn_probs * grad_probs, axis=-1, keepdims=True)
        grad_scores = (attn_probs * (grad_probs - row_delta)).astype(jnp.bfloat16)
        grad_query_rot = (
            jnp.einsum("kgrl,lkd->rkgd", grad_scores, key_grp, preferred_element_type=jnp.float32)
            * score_scale
        )
        key_term = (
            jnp.einsum("kgrl,rkgd->lkd", grad_scores, query_grp, preferred_element_type=jnp.float32)
            * score_scale
        )
        value_term = jnp.einsum(
            "kgrl,rkgd->lkd", probs_low, grad_grp, preferred_element_type=jnp.float32
        )
        return (
            grad_query_rot.reshape(row_count, head_count, HD),
            key_term.reshape(full_length, kv_width),
            value_term.reshape(full_length, kv_width),
        )

    outputs = []
    in_grads = []
    totals = None
    for micro_idx in range(MICRO):
        first_seq = micro_idx * per_micro
        block_in = hidden_in[first_seq : first_seq + per_micro]
        block_grad = out_grad[first_seq : first_seq + per_micro]
        col_parts = (
            lax.all_gather(q_weight, "seq", axis=1, tiled=True),
            lax.all_gather(k_weight, "seq", axis=1, tiled=True),
            lax.all_gather(v_weight, "seq", axis=1, tiled=True),
            lax.all_gather(o_weight, "seq", axis=1, tiled=True),
            lax.all_gather(gate_weight, "seq", axis=1, tiled=True),
            lax.all_gather(up_weight, "seq", axis=1, tiled=True),
            lax.all_gather(down_weight, "seq", axis=1, tiled=True),
        )
        query_mat, key_mat, value_mat, out_mat, gate_mat, up_mat, down_mat = (
            lax.all_gather(col_parts[0], "dp", axis=0, tiled=True),
            lax.all_gather(col_parts[1], "dp", axis=0, tiled=True),
            lax.all_gather(col_parts[2], "dp", axis=0, tiled=True),
            lax.all_gather(col_parts[3], "dp", axis=0, tiled=True),
            lax.all_gather(col_parts[4], "dp", axis=0, tiled=True),
            lax.all_gather(col_parts[5], "dp", axis=0, tiled=True),
            lax.all_gather(col_parts[6], "dp", axis=0, tiled=True),
        )
        resid_in = block_in.astype(jnp.float32).reshape(tok_count, model_width)
        rstd_one = lax.rsqrt(jnp.mean(resid_in * resid_in, axis=-1, keepdims=True) + eps_norm)
        normed_one = (resid_in * rstd_one * gain_attn).astype(jnp.bfloat16)
        query_lin = jnp.dot(normed_one, query_mat, preferred_element_type=jnp.float32)
        key_lin = jnp.dot(normed_one, key_mat, preferred_element_type=jnp.float32)
        value_lin = jnp.dot(normed_one, value_mat, preferred_element_type=jnp.float32)
        query_rot = rotate(
            query_lin.reshape(per_micro, row_count, head_count, HD), cos_own, sin_own
        ).astype(jnp.bfloat16)
        key_rot = (
            rotate(key_lin.reshape(per_micro, row_count, kv_heads, HD), cos_own, sin_own)
            .astype(jnp.bfloat16)
            .reshape(per_micro, row_count, kv_width)
        )
        value_low = value_lin.astype(jnp.bfloat16).reshape(per_micro, row_count, kv_width)
        key_all, value_all = (
            lax.all_gather(key_rot, "seq", axis=1, tiled=True),
            lax.all_gather(value_low, "seq", axis=1, tiled=True),
        )
        mixed_seq, log_total = lax.map(attend, (query_rot, key_all, value_all))
        mixed_low = mixed_seq.reshape(tok_count, model_width)
        hidden_mid = resid_in + jnp.dot(mixed_low, out_mat, preferred_element_type=jnp.float32)
        rstd_two = lax.rsqrt(jnp.mean(hidden_mid * hidden_mid, axis=-1, keepdims=True) + eps_norm)
        normed_two = (hidden_mid * rstd_two * gain_mlp).astype(jnp.bfloat16)
        gate_lin = jnp.dot(normed_two, gate_mat, preferred_element_type=jnp.float32)
        up_lin = jnp.dot(normed_two, up_mat, preferred_element_type=jnp.float32)
        gate_sig = jax.nn.sigmoid(gate_lin)
        inner_low = (gate_lin * gate_sig * up_lin).astype(jnp.bfloat16)
        mlp_out = jnp.dot(inner_low, down_mat, preferred_element_type=jnp.float32)
        outputs.append(
            (hidden_mid + mlp_out).astype(jnp.bfloat16).reshape(per_micro, row_count, model_width)
        )
        col_again = (
            lax.all_gather(q_weight, "seq", axis=1, tiled=True),
            lax.all_gather(k_weight, "seq", axis=1, tiled=True),
            lax.all_gather(v_weight, "seq", axis=1, tiled=True),
            lax.all_gather(o_weight, "seq", axis=1, tiled=True),
            lax.all_gather(gate_weight, "seq", axis=1, tiled=True),
            lax.all_gather(up_weight, "seq", axis=1, tiled=True),
            lax.all_gather(down_weight, "seq", axis=1, tiled=True),
        )
        query_mat, key_mat, value_mat, out_mat, gate_mat, up_mat, down_mat = (
            lax.all_gather(col_again[0], "dp", axis=0, tiled=True),
            lax.all_gather(col_again[1], "dp", axis=0, tiled=True),
            lax.all_gather(col_again[2], "dp", axis=0, tiled=True),
            lax.all_gather(col_again[3], "dp", axis=0, tiled=True),
            lax.all_gather(col_again[4], "dp", axis=0, tiled=True),
            lax.all_gather(col_again[5], "dp", axis=0, tiled=True),
            lax.all_gather(col_again[6], "dp", axis=0, tiled=True),
        )
        key_all, value_all = (
            lax.all_gather(key_rot, "seq", axis=1, tiled=True),
            lax.all_gather(value_low, "seq", axis=1, tiled=True),
        )
        grad_top = block_grad.astype(jnp.float32).reshape(tok_count, model_width)
        grad_top_low = grad_top.astype(jnp.bfloat16)
        down_term = jnp.einsum(
            "tf,td->fd", inner_low, grad_top_low, preferred_element_type=jnp.float32
        )
        grad_inner = jnp.einsum(
            "td,fd->tf", grad_top_low, down_mat, preferred_element_type=jnp.float32
        )
        grad_gate = (grad_inner * up_lin * gate_sig * (1.0 + gate_lin * (1.0 - gate_sig))).astype(
            jnp.bfloat16
        )
        grad_up = (grad_inner * gate_lin * gate_sig).astype(jnp.bfloat16)
        gate_term = jnp.einsum(
            "td,tf->df", normed_two, grad_gate, preferred_element_type=jnp.float32
        )
        up_term = jnp.einsum("td,tf->df", normed_two, grad_up, preferred_element_type=jnp.float32)
        grad_normed_two = jnp.einsum(
            "tf,df->td", grad_gate, gate_mat, preferred_element_type=jnp.float32
        ) + jnp.einsum("tf,df->td", grad_up, up_mat, preferred_element_type=jnp.float32)
        grad_mid_norm, gain_mlp_term = norm_back(hidden_mid, rstd_two, gain_mlp, grad_normed_two)
        grad_mid = grad_top + grad_mid_norm
        grad_mid_low = grad_mid.astype(jnp.bfloat16)
        out_term = jnp.einsum(
            "td,te->de", mixed_low, grad_mid_low, preferred_element_type=jnp.float32
        )
        grad_mixed = jnp.einsum(
            "te,de->td", grad_mid_low, out_mat, preferred_element_type=jnp.float32
        ).astype(jnp.bfloat16)
        grad_query_rot, key_terms, value_terms = lax.map(
            attend_back,
            (
                query_rot,
                key_all,
                value_all,
                grad_mixed.reshape(per_micro, row_count, model_width),
                log_total,
            ),
        )
        key_share, value_share = (
            lax.psum_scatter(key_terms, "seq", scatter_dimension=1, tiled=True),
            lax.psum_scatter(value_terms, "seq", scatter_dimension=1, tiled=True),
        )
        grad_query = (
            rotate_back(grad_query_rot, cos_own, sin_own)
            .astype(jnp.bfloat16)
            .reshape(tok_count, model_width)
        )
        grad_key = (
            rotate_back(key_share.reshape(per_micro, row_count, kv_heads, HD), cos_own, sin_own)
            .astype(jnp.bfloat16)
            .reshape(tok_count, kv_width)
        )
        grad_value = value_share.astype(jnp.bfloat16).reshape(tok_count, kv_width)
        query_term = jnp.einsum(
            "td,te->de", normed_one, grad_query, preferred_element_type=jnp.float32
        )
        key_term = jnp.einsum("td,te->de", normed_one, grad_key, preferred_element_type=jnp.float32)
        value_term = jnp.einsum(
            "td,te->de", normed_one, grad_value, preferred_element_type=jnp.float32
        )
        grad_normed_one = (
            jnp.einsum("te,de->td", grad_query, query_mat, preferred_element_type=jnp.float32)
            + jnp.einsum("te,de->td", grad_key, key_mat, preferred_element_type=jnp.float32)
            + jnp.einsum("te,de->td", grad_value, value_mat, preferred_element_type=jnp.float32)
        )
        grad_in_norm, gain_attn_term = norm_back(resid_in, rstd_one, gain_attn, grad_normed_one)
        in_grads.append((grad_mid + grad_in_norm).reshape(per_micro, row_count, model_width))
        totals = add_tuples(
            totals,
            (
                query_term,
                key_term,
                value_term,
                out_term,
                gate_term,
                up_term,
                down_term,
                gain_attn_term,
                gain_mlp_term,
            ),
        )
    col_sums = (
        lax.psum_scatter(
            totals[0].astype(jnp.bfloat16), "seq", scatter_dimension=1, tiled=True
        ).astype(jnp.float32),
        lax.psum_scatter(
            totals[1].astype(jnp.bfloat16), "seq", scatter_dimension=1, tiled=True
        ).astype(jnp.float32),
        lax.psum_scatter(
            totals[2].astype(jnp.bfloat16), "seq", scatter_dimension=1, tiled=True
        ).astype(jnp.float32),
        lax.psum_scatter(
            totals[3].astype(jnp.bfloat16), "seq", scatter_dimension=1, tiled=True
        ).astype(jnp.float32),
        lax.psum_scatter(
            totals[4].astype(jnp.bfloat16), "seq", scatter_dimension=1, tiled=True
        ).astype(jnp.float32),
        lax.psum_scatter(
            totals[5].astype(jnp.bfloat16), "seq", scatter_dimension=1, tiled=True
        ).astype(jnp.float32),
        lax.psum_scatter(
            totals[6].astype(jnp.bfloat16), "seq", scatter_dimension=1, tiled=True
        ).astype(jnp.float32),
    )
    owned = (
        lax.psum_scatter(
            col_sums[0].astype(jnp.bfloat16), "dp", scatter_dimension=0, tiled=True
        ).astype(jnp.float32),
        lax.psum_scatter(
            col_sums[1].astype(jnp.bfloat16), "dp", scatter_dimension=0, tiled=True
        ).astype(jnp.float32),
        lax.psum_scatter(
            col_sums[2].astype(jnp.bfloat16), "dp", scatter_dimension=0, tiled=True
        ).astype(jnp.float32),
        lax.psum_scatter(
            col_sums[3].astype(jnp.bfloat16), "dp", scatter_dimension=0, tiled=True
        ).astype(jnp.float32),
        lax.psum_scatter(
            col_sums[4].astype(jnp.bfloat16), "dp", scatter_dimension=0, tiled=True
        ).astype(jnp.float32),
        lax.psum_scatter(
            col_sums[5].astype(jnp.bfloat16), "dp", scatter_dimension=0, tiled=True
        ).astype(jnp.float32),
        lax.psum_scatter(
            col_sums[6].astype(jnp.bfloat16), "dp", scatter_dimension=0, tiled=True
        ).astype(jnp.float32),
    )
    gain_sums = lax.psum((totals[7], totals[8]), ("dp", "seq"))
    return (
        jnp.concatenate(outputs, axis=0),
        jnp.concatenate(in_grads, axis=0),
        gain_sums[0],
        owned[0],
        owned[1],
        owned[2],
        owned[3],
        gain_sums[1],
        owned[4],
        owned[5],
        owned[6],
    )


F32 = jnp.float32
BF16 = jnp.bfloat16
VMEM_BYTES = 56 * 2**20


def dot(left, right, left_dim, right_dim):
    dims = (((left_dim,), (right_dim,)), ((), ()))
    return lax.dot_general(left, right, dims, preferred_element_type=F32)


def span_slice(inv_ref, place, span):
    return pl.ds(pl.multiple_of(inv_ref[place] * span, span), span)


def lane_pair(ref, rows, inv_ref, block, span):
    first = ref[rows, span_slice(inv_ref, 2 * block, span)]
    second = ref[rows, span_slice(inv_ref, 2 * block + 1, span)]
    return jnp.concatenate([first, second], axis=1)


def row_pair(ref, head, inv_ref, block, span):
    first = ref[head, span_slice(inv_ref, 2 * block, span), :]
    second = ref[head, span_slice(inv_ref, 2 * block + 1, span), :]
    return jnp.concatenate([first, second], axis=0)


def attend_kernel(inv_ref, q_ref, k_ref, v_ref, o_ref, l_ref, acc_ref, *, blocks, span, group):
    wide = 2 * span
    row = lax.broadcasted_iota(jnp.int32, (wide, wide), 0)
    col = lax.broadcasted_iota(jnp.int32, (wide, wide), 1)
    keep = row <= col

    def one_block(block, odd):
        queries = [
            lane_pair(q_ref, slice(HD * h, HD * h + HD), inv_ref, block, span) for h in range(group)
        ]
        acc_ref[...] = jnp.zeros_like(acc_ref)

        def step(first, count, state, diagonal):
            state = list(state)
            keys = [row_pair(k_ref, 0, inv_ref, first + u, span) for u in range(count)]
            values = [lane_pair(v_ref, slice(0, HD), inv_ref, first + u, span) for u in range(count)]
            items = [(u, h) for u in range(count) for h in range(group)]
            scores = [dot(keys[u], queries[h], 1, 0) for u, h in items]
            probs = []
            for (u, h), score in zip(items, scores):
                peak, total = state[h]
                if diagonal and u == count - 1:
                    score = jnp.where(keep, score, neg_big)
                new_peak = jnp.maximum(peak, jnp.max(score, axis=0, keepdims=True))
                prob = jnp.exp(score - new_peak)
                shrink = jnp.exp(peak - new_peak)
                state[h] = (new_peak, total * shrink + jnp.sum(prob, axis=0, keepdims=True))
                probs.append((prob.astype(BF16), shrink))
            for (u, h), (prob, shrink) in zip(items, probs):
                cols = slice(h * wide, (h + 1) * wide)
                acc_ref[:, cols] = acc_ref[:, cols] * shrink + dot(values[u], prob, 1, 0)
            return tuple(state)

        state = tuple(
            (jnp.full((1, wide), neg_big, F32), jnp.zeros((1, wide), F32)) for _ in range(group)
        )
        state = lax.fori_loop(0, block // 4, lambda j, s: step(4 * j, 4, s, False), state)
        state = lax.fori_loop(
            2 * (block // 4), block // 2, lambda j, s: step(2 * j, 2, s, False), state
        )
        state = step(block - 1, 2, state, True) if odd else step(block, 1, state, True)
        mixed = jnp.concatenate(
            [acc_ref[:, wide * h : wide * (h + 1)] * (1.0 / state[h][1]) for h in range(group)], axis=0
        ).astype(BF16)
        logs = jnp.concatenate(
            [p + jnp.log(t) for p, t in state] + [jnp.zeros((8 - group, wide), F32)], axis=0
        )
        for part in range(2):
            where = span_slice(inv_ref, 2 * block + part, span)
            cols = slice(part * span, part * span + span)
            o_ref[:, where] = mixed[:, cols]
            l_ref[0, :, where] = logs[:, cols]

    def two_blocks(pair, _):
        for odd in (0, 1):
            one_block(2 * pair + odd, odd)
        return 0

    lax.fori_loop(0, blocks // 2, two_blocks, 0)


def attention_forward(inv, q_t, k_nat, v_t, span):
    tokens = q_t.shape[1]
    kv_heads = k_nat.shape[0]
    group = q_t.shape[0] // (kv_heads * HD)
    pairs = kv_heads * group * tokens * tokens
    wide_spec = pl.BlockSpec((group * HD, tokens), lambda g, i: (g, 0))
    nat_spec = pl.BlockSpec((1, tokens, HD), lambda g, i: (g, 0, 0))
    return pl.pallas_call(
        functools.partial(attend_kernel, blocks=tokens // (2 * span), span=span, group=group),
        grid_spec=pltpu.PrefetchScalarGridSpec(
            num_scalar_prefetch=1,
            grid=(kv_heads,),
            in_specs=[wide_spec, nat_spec, pl.BlockSpec((HD, tokens), lambda g, i: (g, 0))],
            out_specs=[
                wide_spec,
                pl.BlockSpec((1, 8, tokens), lambda g, i: (g, 0, 0)),
            ],
            scratch_shapes=[pltpu.VMEM((HD, group * 2 * span), F32)],
        ),
        out_shape=[
            jax.ShapeDtypeStruct(q_t.shape, BF16),
            jax.ShapeDtypeStruct((kv_heads, 8, tokens), F32),
        ],
        compiler_params=pltpu.CompilerParams(vmem_limit_bytes=VMEM_BYTES),
        cost_estimate=pl.CostEstimate(
            flops=16 * pairs * HD, bytes_accessed=tokens * 6000, transcendentals=pairs // 2
        ),
        name="attention_forward",
    )(inv, q_t, k_nat, v_t)


def attend_back_kernel(
    inv_ref, q_ref, kt_ref, k_ref, v_ref, o_ref, do_ref, l_ref, cos_ref, sin_ref,
    dq_ref, dk_ref, dv_ref, dk_sum, dv_sum, dq_sum, *, blocks, span, group,
):
    wide = 2 * span
    row = lax.broadcasted_iota(jnp.int32, (wide, wide), 0)
    col = lax.broadcasted_iota(jnp.int32, (wide, wide), 1)
    keep = row <= col
    half = HD // 2
    dk_sum[...] = jnp.zeros_like(dk_sum)
    dv_sum[...] = jnp.zeros_like(dv_sum)

    def rope_back(grad, cos, sin):
        top, low = grad[:half], grad[half:]
        return jnp.concatenate([top * cos + low * sin, low * cos - top * sin], axis=0)

    def one_block(block, odd):
        rows = [slice(HD * h, HD * h + HD) for h in range(group)]
        queries = [lane_pair(q_ref, r, inv_ref, block, span) for r in rows]
        grads = [lane_pair(do_ref, r, inv_ref, block, span) for r in rows]
        logs = lane_pair(l_ref.at[0], slice(None), inv_ref, block, span)
        deltas = [
            jnp.sum(
                lane_pair(o_ref, r, inv_ref, block, span).astype(F32) * grad.astype(F32),
                axis=0,
                keepdims=True,
            )
            for r, grad in zip(rows, grads)
        ]
        dq_sum[...] = jnp.zeros_like(dq_sum)

        def step(first, count, diagonal):
            keys = [row_pair(k_ref, 0, inv_ref, first + u, span) for u in range(count)]
            values = [row_pair(v_ref, 0, inv_ref, first + u, span) for u in range(count)]
            keys_t = [lane_pair(kt_ref, slice(0, HD), inv_ref, first + u, span) for u in range(count)]
            items = [(u, h) for u in range(count) for h in range(group)]
            ahead, ready, dqs, sums = {}, {}, {}, {}

            def products(i):
                u, h = items[i]
                ahead[i] = dot(keys[u], queries[h], 1, 0), dot(values[u], grads[h], 1, 0)

            def softmax_part(i):
                u, h = items[i]
                score, dprob = ahead.pop(i)
                prob = jnp.exp(score - logs[h : h + 1])
                if diagonal and u == count - 1:
                    prob = jnp.where(keep, prob, 0.0)
                ready[i] = prob.astype(BF16), (prob * (dprob - deltas[h])).astype(BF16)

            def gradients(i):
                u, h = items[i]
                prob, dscore = ready.pop(i)
                dq = dot(keys_t[u], dscore, 1, 0)
                dqs[h] = dqs[h] + dq if h in dqs else dq
                if u == count - 1:
                    dq_sum[:, wide * h : wide * (h + 1)] += dqs[h]
                dk, dv = dot(queries[h], dscore, 1, 1), dot(grads[h], prob, 1, 1)
                if u in sums:
                    dk, dv = dk + sums[u][0], dv + sums[u][1]
                sums[u] = dk, dv
                if h == group - 1:
                    place = pl.ds(pl.multiple_of((first + u) * wide, wide), wide)
                    dk_sum[:, place] += dk
                    dv_sum[:, place] += dv

            lead = 2
            for i in range(min(lead, len(items))):
                products(i)
            for i in range(len(items) + 1):
                if i + lead < len(items):
                    products(i + lead)
                if i > 0:
                    gradients(i - 1)
                if i < len(items):
                    softmax_part(i)

        def pair_step(j, _):
            step(2 * j, 2, False)
            return 0

        lax.fori_loop(0, block // 2, pair_step, 0)
        if odd:
            step(block - 1, 2, True)
        else:
            step(block, 1, True)
        cos = lane_pair(cos_ref, slice(None), inv_ref, block, span)
        sin = lane_pair(sin_ref, slice(None), inv_ref, block, span)
        dq = jnp.concatenate(
            [rope_back(dq_sum[:, wide * h : wide * (h + 1)] * HD**-0.5, cos, sin) for h in range(group)],
            axis=0,
        ).astype(BF16)
        place = pl.ds(pl.multiple_of(block * wide, wide), wide)
        dk = rope_back(dk_sum[:, place], cos, sin).astype(BF16)
        dv = dv_sum[:, place].astype(BF16)
        for part in range(2):
            where = span_slice(inv_ref, 2 * block + part, span)
            cols = slice(part * span, part * span + span)
            dq_ref[:, where] = dq[:, cols]
            dk_ref[:, where] = dk[:, cols]
            dv_ref[:, where] = dv[:, cols]

    def two_blocks(step, _):
        for odd in (1, 0):
            one_block(blocks - 2 - 2 * step + odd, odd)
        return 0

    lax.fori_loop(0, blocks // 2, two_blocks, 0)


def attention_backward(inv, q_t, k_t, k_nat, v_nat, o_t, do_t, logs, cos_t, sin_t, span):
    tokens = q_t.shape[1]
    kv_heads = k_nat.shape[0]
    group = q_t.shape[0] // (kv_heads * HD)
    pairs = kv_heads * group * tokens * tokens
    wide_spec = pl.BlockSpec((group * HD, tokens), lambda g, i: (g, 0))
    kv_spec = pl.BlockSpec((HD, tokens), lambda g, i: (g, 0))
    nat_spec = pl.BlockSpec((1, tokens, HD), lambda g, i: (g, 0, 0))
    tab_spec = pl.BlockSpec((HD // 2, tokens), lambda g, i: (0, 0))
    return pl.pallas_call(
        functools.partial(attend_back_kernel, blocks=tokens // (2 * span), span=span, group=group),
        grid_spec=pltpu.PrefetchScalarGridSpec(
            num_scalar_prefetch=1,
            grid=(kv_heads,),
            in_specs=[
                wide_spec, kv_spec, nat_spec, nat_spec, wide_spec, wide_spec,
                pl.BlockSpec((1, 8, tokens), lambda g, i: (g, 0, 0)), tab_spec, tab_spec,
            ],
            out_specs=[wide_spec, kv_spec, kv_spec],
            scratch_shapes=[
                pltpu.VMEM((HD, tokens), F32),
                pltpu.VMEM((HD, tokens), F32),
                pltpu.VMEM((HD, group * 2 * span), F32),
            ],
        ),
        out_shape=[
            jax.ShapeDtypeStruct(q_t.shape, BF16),
            jax.ShapeDtypeStruct(k_t.shape, BF16),
            jax.ShapeDtypeStruct(k_t.shape, BF16),
        ],
        compiler_params=pltpu.CompilerParams(vmem_limit_bytes=VMEM_BYTES),
        cost_estimate=pl.CostEstimate(
            flops=32 * pairs * HD, bytes_accessed=tokens * 9000, transcendentals=pairs // 2
        ),
        name="attention_backward",
    )(inv, q_t, k_t, k_nat, v_nat, o_t, do_t, logs, cos_t, sin_t)


def flip(index, bits):
    for bit in bits:
        index = index + bit * (1 - 2 * ((index // bit) % 2))
    return index


def bits_of(size):
    return [1 << i for i in range(size.bit_length() - 1)]


def seq_stages(seq):
    return [("seq", b) for b in reversed(bits_of(seq)[1:])] + [("seq", b) for b in bits_of(seq)[:1]]


def all_stages(dp, seq):
    return seq_stages(seq) + [("dp", b) for b in reversed(bits_of(dp))]


def rest_chains(dp, seq):
    near, far = [("seq", b) for b in bits_of(seq)[:1]], [("seq", b) for b in reversed(bits_of(seq)[1:])]
    chip = [("dp", b) for b in reversed(bits_of(dp)[1:])]
    return far + near + chip, far + chip + near


def away_place(stages, d, s, my_dp, my_seq):
    place = 0
    for at, (axis, bit) in enumerate(stages):
        mine = ((my_dp if axis == "dp" else my_seq) // bit) % 2
        theirs = ((d if axis == "dp" else s) // bit) % 2
        place = place + (1 << at) * (1 - mine if theirs else mine)
    return place


def arrival_order(stages, dp, seq, my_dp, my_seq):
    ids = jnp.arange(dp * seq, dtype=jnp.int32)
    away = {"dp": (ids // seq) ^ my_dp, "seq": (ids % seq) ^ my_seq}
    place = jnp.zeros_like(ids)
    for at, (axis, bit) in enumerate(stages):
        place = place + (1 << at) * ((away[axis] // bit) % 2)
    return place


def greet(peers):
    barrier = pltpu.get_barrier_semaphore()
    for peer in peers:
        pl.semaphore_signal(barrier, inc=1, device_id=peer, device_id_type=pl.DeviceIdType.MESH)
    pl.semaphore_wait(barrier, len(peers))


def seq_peer(my_dp, my_seq, away, seq):
    return my_dp, flip(my_seq, [b for b in bits_of(seq) if away & b])


def stage_peer(my_dp, my_seq, stage):
    axis, bit = stage
    return (flip(my_dp, [bit]), my_seq) if axis == "dp" else (my_dp, flip(my_seq, [bit]))


def all_peers(my_dp, my_seq, dp, seq):
    peers = [seq_peer(my_dp, my_seq, away, seq) for away in range(1, seq)]
    return peers + [(flip(my_dp, [b]), my_seq) for b in bits_of(dp)]


def bring_kernel(x_ref, first_ref, second_ref, out_ref, all_one_ref, all_two_ref,
                 local_sem, x_send, x_recv, w_send, w_recv, *, dp, seq):
    my_dp, my_seq = lax.axis_index("dp"), lax.axis_index("seq")
    orders = all_stages(dp, seq), seq_stages(seq)
    greet(all_peers(my_dp, my_seq, dp, seq))
    shards_in = (first_ref, second_ref)
    gathered = (all_one_ref, all_two_ref)

    def weight_copy(chain, stage):
        held = 1 << stage
        source = shards_in[chain] if stage == 0 else gathered[chain].at[pl.ds(0, held)]
        return pltpu.make_async_remote_copy(
            src_ref=source,
            dst_ref=gathered[chain].at[pl.ds(held, held)],
            send_sem=w_send.at[chain, stage],
            recv_sem=w_recv.at[chain, stage],
            device_id=stage_peer(my_dp, my_seq, orders[chain][stage]),
            device_id_type=pl.DeviceIdType.MESH,
        )

    copies = [[weight_copy(c, s) for s in range(len(orders[c]))] for c in range(2)]
    for c in range(2):
        copies[c][0].start()
    own = [
        pltpu.make_async_copy(shards_in[c], gathered[c].at[pl.ds(0, 1)], local_sem.at[c]) for c in range(2)
    ]
    own.append(pltpu.make_async_copy(x_ref.at[my_seq], out_ref.at[my_seq], local_sem.at[2]))
    for copy in own:
        copy.start()
    moves = []
    for away in range(1, seq):
        peer = seq_peer(my_dp, my_seq, away, seq)
        moves.append(
            pltpu.make_async_remote_copy(
                src_ref=x_ref.at[peer[1]],
                dst_ref=out_ref.at[my_seq],
                send_sem=x_send.at[away - 1],
                recv_sem=x_recv.at[away - 1],
                device_id=peer,
                device_id_type=pl.DeviceIdType.MESH,
            )
        )
    for c in range(2):
        own[c].wait()
    for stage in range(1, len(orders[0])):
        for c in range(2):
            if stage < len(orders[c]):
                copies[c][stage - 1].wait_recv()
                copies[c][stage].start()
        if stage == 1:
            for move in moves:
                move.start()
    for c in range(2):
        copies[c][-1].wait_recv()
        for copy in copies[c]:
            copy.wait_send()
    for move in moves:
        move.wait()
    own[2].wait()


def bring(x, first, second):
    dp, seq = lax.axis_size("dp"), lax.axis_size("seq")
    stages = len(all_stages(dp, seq))
    hbm = pl.BlockSpec(memory_space=pl.ANY)
    return pl.pallas_call(
        functools.partial(bring_kernel, dp=dp, seq=seq),
        in_specs=[hbm] * 3,
        out_specs=[hbm] * 3,
        out_shape=[
            jax.ShapeDtypeStruct(x.shape, x.dtype),
            jax.ShapeDtypeStruct((dp * seq, *first.shape[1:]), first.dtype),
            jax.ShapeDtypeStruct((seq, *second.shape[1:]), second.dtype),
        ],
        scratch_shapes=[
            pltpu.SemaphoreType.DMA((3,)),
            pltpu.SemaphoreType.DMA((seq - 1,)),
            pltpu.SemaphoreType.DMA((seq - 1,)),
            pltpu.SemaphoreType.DMA((2, stages)),
            pltpu.SemaphoreType.DMA((2, stages)),
        ],
        compiler_params=pltpu.CompilerParams(
            collective_id=1, has_side_effects=True, vmem_limit_bytes=VMEM_BYTES
        ),
        name="bring",
    )(x, first, second)


def qkv_kernel(where_ref, x_ref, gain_ref, packed_ref, cos_ref, sin_ref,
               q_ref, kt_ref, vt_ref, k_ref, v_ref, w_ref, w_wide, *, heads, kv_heads, dp, seq):
    half = HD // 2
    width = w_ref.shape[1]
    q_cols, kv_cols = width // seq, kv_heads * HD // seq
    kv_width = kv_heads * HD

    @pl.when(pl.program_id(0) == 0)
    def _():
        for s in range(seq):
            block = jnp.concatenate([packed_ref[where_ref[d * seq + s]] for d in range(dp)], axis=0)
            turned = block.astype(F32).T
            w_wide[q_cols * s : q_cols * s + q_cols, :] = turned[:q_cols]
            first = width + kv_cols * s
            w_wide[first : first + kv_cols, :] = turned[q_cols : q_cols + kv_cols]
            first += kv_width
            w_wide[first : first + kv_cols, :] = turned[q_cols + kv_cols : q_cols + 2 * kv_cols]
        w_ref[...] = w_wide[...].astype(BF16)

    x = x_ref[0].astype(F32)
    rstd = lax.rsqrt(jnp.mean(x * x, axis=0, keepdims=True) + eps_norm)
    normed = (x * rstd * gain_ref[...]).astype(BF16)
    lin = dot(w_ref[...], normed, 1, 0)
    cos, sin = cos_ref[...], sin_ref[...]
    for head in range(heads + kv_heads):
        top = lin[HD * head : HD * head + half]
        low = lin[HD * head + half : HD * head + HD]
        rot = jnp.concatenate([top * cos - low * sin, low * cos + top * sin], axis=0)
        if head < heads:
            q_ref[HD * head : HD * head + HD, :] = rot.astype(BF16) * jnp.asarray(HD**-0.5, BF16)
        else:
            kv = head - heads
            kt_ref[HD * kv : HD * kv + HD, :] = rot.astype(BF16)
            k_ref[kv] = rot.T.astype(BF16)
    for kv in range(kv_heads):
        first = HD * (heads + kv_heads + kv)
        val = lin[first : first + HD]
        vt_ref[HD * kv : HD * kv + HD, :] = val.astype(BF16)
        v_ref[kv] = val.T.astype(BF16)


def project_qkv(where, x, gain, packed, cos_t, sin_t, heads, kv_heads, rows):
    blocks, width, block = x.shape
    tokens = blocks * block
    feats = (heads + 2 * kv_heads) * HD
    dp, seq = lax.axis_size("dp"), lax.axis_size("seq")
    col = lambda rows: pl.BlockSpec((rows, block), lambda i, w: (0, i))
    nat = pl.BlockSpec((kv_heads, block, HD), lambda i, w: (0, i, 0))
    return pl.pallas_call(
        functools.partial(qkv_kernel, heads=heads, kv_heads=kv_heads, dp=dp, seq=seq),
        grid_spec=pltpu.PrefetchScalarGridSpec(
            num_scalar_prefetch=1,
            grid=(blocks,),
            in_specs=[
                pl.BlockSpec((1, width, block), lambda i, w: (i, 0, 0)),
                pl.BlockSpec((width, 1), lambda i, w: (0, 0)),
                pl.BlockSpec((dp * seq, rows, packed.shape[2]), lambda i, w: (0, 0, 0)),
                col(HD // 2),
                col(HD // 2),
            ],
            out_specs=[
                col(heads * HD), col(kv_heads * HD), col(kv_heads * HD), nat, nat,
                pl.BlockSpec((feats, width), lambda i, w: (0, 0)),
            ],
            scratch_shapes=[pltpu.VMEM((feats, width), F32)],
        ),
        out_shape=[
            jax.ShapeDtypeStruct((heads * HD, tokens), BF16),
            jax.ShapeDtypeStruct((kv_heads * HD, tokens), BF16),
            jax.ShapeDtypeStruct((kv_heads * HD, tokens), BF16),
            jax.ShapeDtypeStruct((kv_heads, tokens, HD), BF16),
            jax.ShapeDtypeStruct((kv_heads, tokens, HD), BF16),
            jax.ShapeDtypeStruct((feats, width), BF16),
        ],
        compiler_params=pltpu.CompilerParams(vmem_limit_bytes=VMEM_BYTES),
        cost_estimate=pl.CostEstimate(
            flops=4 * tokens * width * feats, bytes_accessed=tokens * 5000, transcendentals=0
        ),
        name="project_qkv",
    )(where, x, gain, packed, cos_t, sin_t)


def side_by_side(ref):
    return jnp.concatenate([ref[i] for i in range(ref.shape[0])], axis=1)


def mlp_kernel(
    where_ref, x_ref, mixed_ref, dy_ref, gain_ref, *more, chunk, dp, seq,
):
    packs = more[:dp]
    out_ref, dmid_ref, dmixed_ref = more[dp : dp + 3]
    one_refs, two_refs, gain_grad_ref = more[dp + 3 : dp + 5], more[dp + 5 : dp + 7], more[dp + 7]
    (o_w, o_t, gate_w, gate_t, up_w, up_t, down_w, down_t, o_sum, gate_sum, up_sum, down_sum, gain_sum,
     pack, pack_sem) = more[dp + 8 :]
    step, steps = pl.program_id(0), pl.num_programs(0)
    width, ff = gate_w.shape
    lanes = pack.shape[3]
    rows = width // dp
    o_cols, ff_cols, ff_rows = width // seq, ff // seq, ff // dp
    spare = ff_cols - lanes
    padded = -(-o_cols // 16) * 16

    @pl.when(step == 0)
    def _():
        for total in (o_sum, gate_sum, up_sum, down_sum, gain_sum):
            total[...] = jnp.zeros_like(total)
        fetches = [
            pltpu.make_async_copy(
                packs[i], pack.at[flip(lax.axis_index("dp"), row_bits(i, dp))], pack_sem.at[i]
            )
            for i in range(dp)
        ]
        for fetch in fetches:
            fetch.start()
        for fetch in fetches:
            fetch.wait()
        for s in range(seq):
            at = where_ref[s]
            stack = lambda first: jnp.concatenate(
                [pack[d, at, first : first + rows, :] for d in range(dp)], axis=0
            ).astype(F32).T
            o_sum[o_cols * s : o_cols * s + o_cols, :] = stack(0)[:o_cols]
            gate_t[ff_cols * s : ff_cols * s + lanes, :] = stack(rows).astype(BF16)
            up_t[ff_cols * s : ff_cols * s + lanes, :] = stack(2 * rows).astype(BF16)
            both = stack(3 * rows).astype(BF16)
            gate_t[ff_cols * s + lanes : ff_cols * (s + 1), :] = both[:spare]
            up_t[ff_cols * s + lanes : ff_cols * (s + 1), :] = both[spare : 2 * spare]
            for d in range(dp):
                for t in range(ff_rows // lanes):
                    first = 4 * rows + padded * t
                    piece = pack[d, at, first : first + padded, :].astype(F32)[:o_cols]
                    cols = slice(ff_rows * d + lanes * t, ff_rows * d + lanes * (t + 1))
                    down_sum[o_cols * s : o_cols * s + o_cols, cols] = piece
        o_t[...] = o_sum[...].astype(BF16)
        o_w[...] = o_sum[...].T.astype(BF16)
        down_t[...] = down_sum[...].astype(BF16)
        for first in range(0, ff, lanes):
            part = slice(first, first + lanes)
            down_w[part, :] = down_sum[:, part].T.astype(BF16)
            gate_w[:, part] = gate_t[part, :].T
            up_w[:, part] = up_t[part, :].T
        o_sum[...] = jnp.zeros_like(o_sum)
        down_sum[...] = jnp.zeros_like(down_sum)

    gain = gain_ref[...]
    mixed = mixed_ref[...]
    mid = dot(o_t[...], mixed, 1, 0) + side_by_side(x_ref).astype(F32)
    rstd = lax.rsqrt(jnp.mean(mid * mid, axis=0, keepdims=True) + eps_norm)
    normed = (mid * rstd * gain).astype(BF16)
    dy = side_by_side(dy_ref)
    added = jnp.zeros_like(mid)
    dnormed = jnp.zeros_like(mid)
    for first in range(0, ff, chunk):
        part = slice(first, first + chunk)
        gate = dot(gate_t[part, :], normed, 1, 0)
        up = dot(up_t[part, :], normed, 1, 0)
        dinner = dot(down_w[part, :], dy, 1, 0)
        sig = 1.0 / (1.0 + jnp.exp(-gate))
        silu = gate * sig
        inner = (silu * up).astype(BF16)
        dup = (dinner * silu).astype(BF16)
        dgate = (dinner * up * sig * (1.0 + gate * (1.0 - sig))).astype(BF16)
        added += dot(down_t[:, part], inner, 1, 0)
        dnormed += dot(gate_w[:, part], dgate, 1, 0)
        dnormed += dot(up_w[:, part], dup, 1, 0)
        down_sum[:, part] += dot(dy, inner, 1, 1)
        gate_sum[part, :] += dot(dgate, normed, 1, 1)
        up_sum[part, :] += dot(dup, normed, 1, 1)
    out = (mid + added).astype(BF16)
    scaled_mid = mid * rstd
    product = dnormed * scaled_mid
    gain_sum[...] += sum(product[:, c : c + lanes] for c in range(0, product.shape[1], lanes))
    scaled = dnormed * gain
    pull = jnp.mean(scaled * mid, axis=0, keepdims=True)
    dmid = dy.astype(F32) + rstd * scaled - scaled_mid * (rstd * rstd * pull)
    dmid_low = dmid.astype(BF16)
    block = out_ref.shape[2]
    for i in range(out_ref.shape[0]):
        out_ref[i] = out[:, block * i : block * (i + 1)]
        dmid_ref[i] = dmid[:, block * i : block * (i + 1)]
    o_sum[...] += dot(dmid_low, mixed, 1, 1)
    dmixed_ref[...] = dot(o_w[...], dmid_low, 1, 0).astype(BF16)

    @pl.when(step == steps - 1)
    def _():
        gain_grad_ref[...] = jnp.sum(gain_sum[...].T, axis=0, keepdims=True)
        my_dp, my_seq = lax.axis_index("dp"), lax.axis_index("seq")
        upper = my_dp % 2 == 1

        def put(refs, place, first, even, odd):
            keep_ref, give_ref = refs
            span = slice(first, first + even.shape[0])
            keep_ref[place, span, :] = jnp.where(upper, odd, even).astype(BF16)
            give_ref[place, span, :] = jnp.where(upper, even, odd).astype(BF16)

        blank = jnp.zeros((lanes - o_cols, width), F32)
        edge = jnp.zeros((padded - o_cols, lanes), F32)
        for s in range(seq):
            tall = lambda total, first, count: total[first : first + count, :]
            o_piece = jnp.concatenate([tall(o_sum, o_cols * s, o_cols), blank], axis=0).T
            gate_piece = tall(gate_sum, ff_cols * s, lanes).T
            up_piece = tall(up_sum, ff_cols * s, lanes).T
            both = jnp.concatenate(
                [tall(gate_sum, ff_cols * s + lanes, spare), tall(up_sum, ff_cols * s + lanes, spare)], axis=0
            ).T
            for d in range(0, dp, 2):
                bands = slice(rows * d, rows * (d + 1)), slice(rows * (d + 1), rows * (d + 2))
                one, two = [away_place(c, d, s, my_dp, my_seq) for c in rest_chains(dp, seq)]
                for i, piece in enumerate((o_piece, gate_piece, up_piece)):
                    put(one_refs, one, rows * i, piece[bands[0]], piece[bands[1]])
                put(two_refs, two, 0, both[bands[0]], both[bands[1]])
                for t in range(ff_rows // lanes):
                    pair = []
                    for at in (d, d + 1):
                        cols = slice(ff_rows * at + lanes * t, ff_rows * at + lanes * (t + 1))
                        pair.append(
                            jnp.concatenate([down_sum[o_cols * s : o_cols * (s + 1), cols], edge], axis=0)
                        )
                    put(two_refs, two, rows + padded * t, *pair)


def row_bits(at, dp):
    return [b for i, b in enumerate(reversed(bits_of(dp))) if (at >> i) & 1]


def gather_rows(array, dp):
    held = [array]
    for at in range(1, dp):
        mask = sum(row_bits(at, dp))
        held.append(lax.ppermute(array, "dp", [(i, i ^ mask) for i in range(dp)]))
    return held


def mlp_both(where, x, mixed, dy, gain, packs, ff, batch=2, chunk=512):
    blocks, width, block = x.shape
    tokens = blocks * block
    dp, seq = lax.axis_size("dp"), lax.axis_size("seq")
    grad_rows, lanes = packs[0].shape[1:]
    first_rows = 3 * (width // dp)
    one = dp * seq // 2, first_rows, lanes
    two = dp * seq // 2, grad_rows - first_rows, lanes
    tok = pl.BlockSpec((batch, width, block), lambda i, w: (i, 0, 0))
    col = pl.BlockSpec((width, batch * block), lambda i, w: (0, i))
    once = lambda shape: pl.BlockSpec(
        shape, lambda i, w: (0,) * len(shape), pipeline_mode=pl.Buffered(1)
    )
    hbm = pl.BlockSpec(memory_space=pl.ANY)
    return pl.pallas_call(
        functools.partial(mlp_kernel, chunk=chunk, dp=dp, seq=seq),
        grid_spec=pltpu.PrefetchScalarGridSpec(
            num_scalar_prefetch=1,
            grid=(blocks // batch,),
            in_specs=[tok, col, tok, once((width, 1))] + [hbm] * dp,
            out_specs=[tok, tok, col, once(one), once(one), once(two), once(two), once((1, width))],
            scratch_shapes=[
                pltpu.VMEM((width, width), BF16),
                pltpu.VMEM((width, width), BF16),
                pltpu.VMEM((width, ff), BF16),
                pltpu.VMEM((ff, width), BF16),
                pltpu.VMEM((width, ff), BF16),
                pltpu.VMEM((ff, width), BF16),
                pltpu.VMEM((ff, width), BF16),
                pltpu.VMEM((width, ff), BF16),
                pltpu.VMEM((width, width), F32),
                pltpu.VMEM((ff, width), F32),
                pltpu.VMEM((ff, width), F32),
                pltpu.VMEM((width, ff), F32),
                pltpu.VMEM((width, lanes), F32),
                pltpu.VMEM((dp, *packs[0].shape), BF16),
                pltpu.SemaphoreType.DMA((dp,)),
            ],
        ),
        out_shape=[
            jax.ShapeDtypeStruct(x.shape, BF16),
            jax.ShapeDtypeStruct(x.shape, F32),
            jax.ShapeDtypeStruct((width, tokens), BF16),
            jax.ShapeDtypeStruct(one, BF16),
            jax.ShapeDtypeStruct(one, BF16),
            jax.ShapeDtypeStruct(two, BF16),
            jax.ShapeDtypeStruct(two, BF16),
            jax.ShapeDtypeStruct((1, width), F32),
        ],
        compiler_params=pltpu.CompilerParams(vmem_limit_bytes=60 * 2**20),
        cost_estimate=pl.CostEstimate(
            flops=2 * tokens * width * (9 * ff + 3 * width),
            bytes_accessed=tokens * width * 14,
            transcendentals=tokens * ff,
        ),
        name="mlp_both",
    )(where, x, mixed, dy, gain, *packs)


def across(index, other, size):
    for bit in bits_of(size):
        index = index + bit * ((other // bit) % 2) * (1 - 2 * ((index // bit) % 2))
    return index


def add_blocks(total_ref, term_ref, count, total_first=0, term_first=0):
    def one(i, _):
        total = total_ref[total_first + i].astype(F32) + term_ref[term_first + i].astype(F32)
        total_ref[total_first + i] = total.astype(BF16)
        return 0

    lax.fori_loop(0, count, one, 0)


def finish_kernel(
    x_ref, dmid_ref, dq_ref, dk_ref, dv_ref, gain_ref, w_t_ref, other_gain_ref,
    keep_one, keep_two, came_one, came_two,
    out_ref, gains_ref, q_ref, k_ref, v_ref, o_ref, gate_ref, up_ref, down_ref,
    w_nat, w_sum, gain_sum, din, packed, landed, one, one_came, one_landed, two, two_came, two_landed,
    gain_held, gain_landed,
    own_sem, d_send, d_recv, r_send, r_recv, g_send, g_recv, fetch_sem, *, dp, seq, kv_width,
):
    step, steps = pl.program_id(0), seq // 2
    my_dp, my_seq = lax.axis_index("dp"), lax.axis_index("seq")
    width = w_nat.shape[0]
    lanes = packed.shape[2]
    rows = width // dp
    q_cols, kv_cols = width // seq, kv_width // seq
    orders = [all_stages(dp, seq), *rest_chains(dp, seq)]
    held = [packed, one, two]
    arrived = [landed, one_landed, two_landed]
    fetches = [
        pltpu.make_async_copy(source, target, fetch_sem.at[i])
        for i, (source, target) in enumerate(
            ((keep_one, one), (keep_two, two), (came_one, one_came), (came_two, two_came))
        )
    ]

    def halve(chain, turn):
        at = len(orders[chain]) - 1 - turn
        half = 1 << at
        return pltpu.make_async_remote_copy(
            src_ref=held[chain].at[pl.ds(half, half)],
            dst_ref=arrived[chain].at[pl.ds(half, half)],
            send_sem=r_send.at[chain, turn],
            recv_sem=r_recv.at[chain, turn],
            device_id=stage_peer(my_dp, my_seq, orders[chain][at]),
            device_id_type=pl.DeviceIdType.MESH,
        )

    def take(chain, turn):
        halve(chain, turn).wait_recv()
        half = 1 << (len(orders[chain]) - 1 - turn)
        if half > 1:
            add_blocks(held[chain], arrived[chain], half, 0, half)
            halve(chain, turn + 1).start()

    def result(chain):
        return held[chain][0].astype(F32) + arrived[chain][1].astype(F32)

    @pl.when(step == 0)
    def _():
        for fetch in fetches:
            fetch.start()
        greet(all_peers(my_dp, my_seq, dp, seq))
        w_sum[...] = jnp.zeros_like(w_sum)
        gain_sum[...] = jnp.zeros_like(gain_sum)
        w_nat[...] = w_t_ref[...].T

    gain = gain_ref[...]
    x = side_by_side(x_ref).astype(F32)
    rstd = lax.rsqrt(jnp.mean(x * x, axis=0, keepdims=True) + eps_norm)
    scaled_x = x * rstd
    normed = (scaled_x * gain).astype(BF16)
    dlin = jnp.concatenate([dq_ref[...], dk_ref[...], dv_ref[...]], axis=0)
    w_sum[...] += dot(dlin, normed, 1, 1)
    dnormed = dot(w_nat[...], dlin, 1, 0)
    product = dnormed * scaled_x
    gain_sum[...] += sum(product[:, c : c + lanes] for c in range(0, product.shape[1], lanes))
    scaled = dnormed * gain
    pull = jnp.mean(scaled * x, axis=0, keepdims=True)
    total = side_by_side(dmid_ref) + rstd * scaled - scaled_x * (rstd * rstd * pull)
    pair = across(my_seq // 2, steps - 1 - step, seq // 2)
    block = din.shape[2]
    for i in range(2):
        din[2 * pair + i] = total[:, block * i : block * (i + 1)].astype(BF16)

    def move(away):
        peer = seq_peer(my_dp, my_seq, away, seq)
        return pltpu.make_async_remote_copy(
            src_ref=din.at[peer[1]],
            dst_ref=out_ref.at[my_seq],
            send_sem=d_send.at[away - 1],
            recv_sem=d_recv.at[away - 1],
            device_id=peer,
            device_id_type=pl.DeviceIdType.MESH,
        )

    for back in range(1, steps):

        @pl.when(step == steps - 1 - back)
        def _():
            move(2 * back).start()
            move(2 * back + 1).start()

    @pl.when(step == 0)
    def _():
        for fetch in fetches:
            fetch.wait()
        for chain, came in ((1, one_came), (2, two_came)):
            add_blocks(held[chain], came, came.shape[0])
            halve(chain, 0).start()

    @pl.when(step == steps - 1)
    def _():
        move(1).start()
        own = pltpu.make_async_copy(din.at[my_seq], out_ref.at[my_seq], own_sem)
        own.start()
        blank = jnp.zeros((lanes - q_cols - 2 * kv_cols, width), F32)
        for s in range(seq):
            first = width + kv_cols * s
            piece = jnp.concatenate(
                [
                    w_sum[q_cols * s : q_cols * (s + 1), :],
                    w_sum[first : first + kv_cols, :],
                    w_sum[first + kv_width : first + kv_width + kv_cols, :],
                    blank,
                ],
                axis=0,
            ).T.astype(BF16)
            for d in range(dp):
                packed[away_place(orders[0], d, s, my_dp, my_seq)] = piece[rows * d : rows * (d + 1)]
        gain_row = jnp.sum(gain_sum[...].T, axis=0, keepdims=True)
        gain_held[0] = jnp.concatenate(
            [gain_row, other_gain_ref[...], jnp.zeros((6, width), F32)], axis=0
        )
        turns = len(orders[0])
        gain_copies = [
            pltpu.make_async_remote_copy(
                src_ref=gain_held.at[turn],
                dst_ref=gain_landed.at[turn],
                send_sem=g_send.at[turn],
                recv_sem=g_recv.at[turn],
                device_id=stage_peer(my_dp, my_seq, orders[0][turns - 1 - turn]),
                device_id_type=pl.DeviceIdType.MESH,
            )
            for turn in range(turns)
        ]
        halve(0, 0).start()
        gain_copies[0].start()
        for turn in range(turns):
            gain_copies[turn].wait_recv()
            gain_held[turn + 1] = gain_held[turn] + gain_landed[turn]
            if turn + 1 < turns:
                gain_copies[turn + 1].start()
            take(0, turn)
            if turn > 0:
                for chain in (1, 2):
                    take(chain, turn - 1)
        gains_ref[...] = gain_held[turns]
        qkv = result(0)
        q_ref[...] = qkv[:, :q_cols]
        turned = qkv.T
        k_ref[...] = turned[q_cols : q_cols + kv_cols]
        v_ref[...] = turned[q_cols + kv_cols : q_cols + 2 * kv_cols]
        first, second = result(1), result(2)
        spare = gate_ref.shape[1] - lanes
        padded = -(-q_cols // 16) * 16
        o_ref[...] = first[:rows, :q_cols]
        gate_ref[...] = jnp.concatenate([first[rows : 2 * rows], second[:rows, :spare]], axis=1)
        up_ref[...] = jnp.concatenate([first[2 * rows :], second[:rows, spare : 2 * spare]], axis=1)
        for t in range(down_ref.shape[1] // lanes):
            at = rows + padded * t
            down_ref[:, lanes * t : lanes * (t + 1)] = second[at : at + q_cols]
        for copy in gain_copies:
            copy.wait_send()
        for chain in range(3):
            for turn in range(len(orders[chain])):
                halve(chain, turn).wait_send()
        for away in range(1, seq):
            move(away).wait()
        own.wait()


def finish(x, dmid, dq_t, dk_t, dv_t, gain, w_t, other_gain, keep_one, keep_two, came_one, came_two, ff):
    blocks, width, block = x.shape
    tokens = blocks * block
    feats = w_t.shape[0]
    kv_width = dk_t.shape[0]
    lanes = keep_one.shape[2]
    dp, seq = lax.axis_size("dp"), lax.axis_size("seq")
    rows = width // dp
    stages = len(all_stages(dp, seq))

    def pair(i):
        return across(lax.axis_index("seq") // 2, seq // 2 - 1 - i, seq // 2)

    tok = pl.BlockSpec((2, width, block), lambda i: (pair(i), 0, 0))
    col = lambda rows: pl.BlockSpec((rows, 2 * block), lambda i: (0, pair(i)))
    once = lambda shape: pl.BlockSpec(shape, lambda i: (0,) * len(shape), pipeline_mode=pl.Buffered(1))
    hbm = pl.BlockSpec(memory_space=pl.ANY)
    small = [
        (8, width),
        (rows, width // seq),
        (kv_width // seq, rows),
        (kv_width // seq, rows),
        (rows, width // seq),
        (rows, ff // seq),
        (rows, ff // seq),
        (width // seq, ff // dp),
    ]
    return pl.pallas_call(
        functools.partial(finish_kernel, dp=dp, seq=seq, kv_width=kv_width),
        grid=(blocks // 2,),
        in_specs=[
            tok, tok, col(dq_t.shape[0]), col(kv_width), col(kv_width),
            once((width, 1)), once((feats, width)), once((1, width)), hbm, hbm, hbm, hbm,
        ],
        out_specs=[hbm] + [once(shape) for shape in small],
        out_shape=[jax.ShapeDtypeStruct(x.shape, BF16)] + [jax.ShapeDtypeStruct(shape, F32) for shape in small],
        scratch_shapes=[
            pltpu.VMEM((width, feats), BF16),
            pltpu.VMEM((feats, width), F32),
            pltpu.VMEM((width, lanes), F32),
            pltpu.VMEM(x.shape, BF16),
            pltpu.VMEM((dp * seq, rows, lanes), BF16),
            pltpu.VMEM((dp * seq, rows, lanes), BF16),
            *[pltpu.VMEM(keep_one.shape, BF16)] * 3,
            *[pltpu.VMEM(keep_two.shape, BF16)] * 3,
            pltpu.VMEM((stages + 1, 8, width), F32),
            pltpu.VMEM((stages, 8, width), F32),
            pltpu.SemaphoreType.DMA,
            pltpu.SemaphoreType.DMA((seq - 1,)),
            pltpu.SemaphoreType.DMA((seq - 1,)),
            pltpu.SemaphoreType.DMA((3, stages)),
            pltpu.SemaphoreType.DMA((3, stages)),
            pltpu.SemaphoreType.DMA((stages,)),
            pltpu.SemaphoreType.DMA((stages,)),
            pltpu.SemaphoreType.DMA((4,)),
        ],
        compiler_params=pltpu.CompilerParams(
            collective_id=2, has_side_effects=True, vmem_limit_bytes=VMEM_BYTES
        ),
        cost_estimate=pl.CostEstimate(
            flops=4 * tokens * width * feats, bytes_accessed=tokens * width * 12, transcendentals=0
        ),
        name="finish",
    )(x, dmid, dq_t, dk_t, dv_t, gain, w_t, other_gain, keep_one, keep_two, came_one, came_two)


def exchange(blocks):
    return lax.all_to_all(blocks, "seq", 0, 0, tiled=True)


def pad_lanes(matrix, lanes):
    return jnp.pad(matrix, ((0, 0), (0, lanes - matrix.shape[1])))


def shards_sequences(
    hidden_in, span_order, attn_gain, q_weight, k_weight, v_weight, o_weight, mlp_gain,
    gate_weight, up_weight, down_weight, out_grad,
):
    lanes = 128
    seqs, slots, width = hidden_in.shape
    dp, seq = lax.axis_size("dp"), lax.axis_size("seq")
    tokens = slots * seq
    span = tokens // span_order.shape[0]
    heads = width // HD
    kv_heads = k_weight.shape[1] * seq // HD
    rows, q_cols = q_weight.shape
    kv_cols = k_weight.shape[1]
    ff = down_weight.shape[0] * dp
    ff_rows = down_weight.shape[0]
    padded = -(-q_cols // 16) * 16

    first = pad_lanes(jnp.concatenate([q_weight, k_weight, v_weight], axis=1), lanes)
    down_turned = jnp.pad(down_weight.T, ((0, padded - q_cols), (0, 0)))
    second = jnp.concatenate(
        [
            pad_lanes(o_weight, lanes),
            gate_weight[:, :lanes],
            up_weight[:, :lanes],
            jnp.concatenate([gate_weight[:, lanes:], up_weight[:, lanes:]], axis=1),
        ]
        + [down_turned[:, c : c + lanes] for c in range(0, ff_rows, lanes)],
        axis=0,
    )
    x, first_all, second_row = bring(hidden_in.transpose(0, 2, 1), first[None], second[None])
    out_grad, x = lax.optimization_barrier((out_grad, x))
    dy = exchange(out_grad.transpose(0, 2, 1))
    second_all = gather_rows(second_row, dp)

    my_dp, my_seq = lax.axis_index("dp"), lax.axis_index("seq")
    where_first = arrival_order(all_stages(dp, seq), dp, seq, my_dp, my_seq)
    where_second = arrival_order(seq_stages(seq), dp, seq, my_dp, my_seq)[:seq]
    inv = jnp.argsort(span_order).astype(jnp.int32)
    slot_pos = slot_positions(jnp.arange(tokens, dtype=jnp.int32), span_order, span)
    inv_freq = rope_base ** (-(jnp.arange(HD // 2, dtype=F32) * 2.0) / HD)
    angles = slot_pos.astype(F32)[None, :] * inv_freq[:, None]
    cos_t, sin_t = jnp.cos(angles), jnp.sin(angles)
    gain_one = attn_gain.astype(F32)[:, None]
    gain_two = mlp_gain.astype(F32)[:, None]

    q_t, k_t, v_t, k_nat, v_nat, w_t = project_qkv(
        where_first, x, gain_one, first_all, cos_t, sin_t, heads, kv_heads, rows
    )
    o_t, logs = attention_forward(inv, q_t, k_nat, v_t, span)
    out, dmid, do_t, keep_one, give_one, keep_two, give_two, gain_two_term = mlp_both(
        where_second, x, o_t, dy, gain_two, second_all, ff
    )
    sibling = [(i, i ^ 1) for i in range(dp)]
    came_one, came_two = lax.ppermute(give_one, "dp", sibling), lax.ppermute(give_two, "dp", sibling)
    hidden_out = exchange(out).transpose(0, 2, 1)

    dq_t, dk_t, dv_t = attention_backward(
        inv, q_t, k_t, k_nat, v_nat, o_t, do_t, logs, cos_t, sin_t, span
    )
    din, gains, q_grad, k_grad, v_grad, o_grad, gate_grad, up_grad, down_grad = finish(
        x, dmid, dq_t, dk_t, dv_t, gain_one, w_t, gain_two_term, keep_one, keep_two, came_one, came_two, ff
    )
    return (
        hidden_out,
        din.astype(F32).transpose(0, 2, 1),
        gains[0],
        q_grad,
        k_grad.T,
        v_grad.T,
        o_grad,
        gains[1],
        gate_grad,
        up_grad,
        down_grad.T,
    )


def shards(*args):
    seqs, spans = args[0].shape[0], args[1].shape[0]
    if seqs == lax.axis_size("seq") and spans % 4 == 0:
        return shards_sequences(*args)
    return shards_general(*args)


def solution(mesh):
    placed = (
        P("dp", "seq", None),
        P(),
        P(),
        P("dp", "seq"),
        P("dp", "seq"),
        P("dp", "seq"),
        P("dp", "seq"),
        P(),
        P("dp", "seq"),
        P("dp", "seq"),
        P("dp", "seq"),
        P("dp", "seq", None),
    )
    return jax.shard_map(
        shards,
        mesh=mesh,
        in_specs=placed,
        out_specs=(
            P("dp", "seq", None),
            P("dp", "seq", None),
            P(),
            P("dp", "seq"),
            P("dp", "seq"),
            P("dp", "seq"),
            P("dp", "seq"),
            P(),
            P("dp", "seq"),
            P("dp", "seq"),
            P("dp", "seq"),
        ),
        check_vma=False,
    )
```

```python
import functools

import jax
import jax.numpy as jnp
from jax import lax
from jax.experimental import pallas as pl
from jax.experimental.pallas import tpu as pltpu
from jax.sharding import PartitionSpec as P

HD = 64
MICRO = 2


eps_norm = 1e-05
rope_base = 100000.0
neg_big = -1e30


def slot_positions(slot_ids, span_order, span_len):
    span_ids = slot_ids // span_len
    span_hits = span_ids[:, None] == jnp.arange(span_order.shape[0], dtype=jnp.int32)[None, :]
    starts = jnp.sum(jnp.where(span_hits, span_order[None, :], 0), axis=1)
    return starts * span_len + slot_ids % span_len


def rope_tables(slot_pos):
    half_width = HD // 2
    inv_freq = rope_base ** (-(jnp.arange(half_width, dtype=jnp.float32) * 2.0) / HD)
    angles = slot_pos.astype(jnp.float32)[:, None] * inv_freq[None, :]
    cosine = jnp.concatenate([jnp.cos(angles), jnp.cos(angles)], axis=1)
    sine_tab = jnp.concatenate([jnp.sin(angles), jnp.sin(angles)], axis=1)
    return (cosine[:, None, :], sine_tab[:, None, :])


def rotate(vector, cosine, sine_tab):
    half_width = vector.shape[-1] // 2
    turned = jnp.concatenate([-vector[..., half_width:], vector[..., :half_width]], axis=-1)
    return vector * cosine + turned * sine_tab


def rotate_back(grad_out, cosine, sine_tab):
    half_width = grad_out.shape[-1] // 2
    scaled = grad_out * sine_tab
    turned = jnp.concatenate([scaled[..., half_width:], -scaled[..., :half_width]], axis=-1)
    return grad_out * cosine + turned


def norm_back(vector, rstd_vec, gain_vec, grad_n):
    scaled = grad_n * gain_vec
    gain_term = jnp.sum(grad_n * vector * rstd_vec, axis=0)
    grad_vec = rstd_vec * scaled - vector * rstd_vec**3 * jnp.mean(
        scaled * vector, axis=-1, keepdims=True
    )
    return (grad_vec, gain_term)


def add_tuples(old_sums, new_terms):
    if old_sums is None:
        return tuple(new_terms)
    return tuple((old_sum + new_term for old_sum, new_term in zip(old_sums, new_terms)))


def shards_general(
    hidden_in,
    span_order,
    attn_gain,
    q_weight,
    k_weight,
    v_weight,
    o_weight,
    mlp_gain,
    gate_weight,
    up_weight,
    down_weight,
    out_grad,
):
    local_seqs, row_count, model_width = hidden_in.shape
    seq_parts = lax.axis_size("seq")
    full_length = row_count * seq_parts
    span_len = full_length // (2 * seq_parts)
    per_micro = local_seqs // MICRO
    kv_width = k_weight.shape[1] * seq_parts
    kv_heads = kv_width // HD
    head_count = model_width // HD
    group_size = head_count // kv_heads
    tok_count = per_micro * row_count
    score_scale = HD ** (-0.5)
    own_slots = lax.axis_index("seq") * row_count + jnp.arange(row_count, dtype=jnp.int32)
    own_pos = slot_positions(own_slots, span_order, span_len)
    all_pos = slot_positions(jnp.arange(full_length, dtype=jnp.int32), span_order, span_len)
    allowed = own_pos[:, None] >= all_pos[None, :]
    cos_own, sin_own = rope_tables(own_pos)
    gain_attn = attn_gain.astype(jnp.float32)
    gain_mlp = mlp_gain.astype(jnp.float32)

    def attend(inputs):
        queries, key_rows, value_rows = inputs
        query_grp = queries.reshape(row_count, kv_heads, group_size, HD)
        key_grp = key_rows.reshape(full_length, kv_heads, HD)
        value_grp = value_rows.reshape(full_length, kv_heads, HD)
        scores = (
            jnp.einsum("rkgd,lkd->kgrl", query_grp, key_grp, preferred_element_type=jnp.float32)
            * score_scale
        )
        scores = jnp.where(allowed, scores, neg_big)
        row_peak = jnp.max(scores, axis=-1, keepdims=True)
        exp_scores = jnp.exp(scores - row_peak)
        row_total = jnp.sum(exp_scores, axis=-1, keepdims=True)
        attn_probs = exp_scores / row_total
        log_total = row_peak + jnp.log(row_total)
        mixed = jnp.einsum(
            "kgrl,lkd->rkgd",
            attn_probs.astype(jnp.bfloat16),
            value_grp,
            preferred_element_type=jnp.float32,
        )
        return (mixed.astype(jnp.bfloat16).reshape(row_count, model_width), log_total)

    def attend_back(inputs):
        queries, key_rows, value_rows, grad_mix, log_total = inputs
        query_grp = queries.reshape(row_count, kv_heads, group_size, HD)
        key_grp = key_rows.reshape(full_length, kv_heads, HD)
        value_grp = value_rows.reshape(full_length, kv_heads, HD)
        grad_grp = grad_mix.reshape(row_count, kv_heads, group_size, HD)
        scores = (
            jnp.einsum("rkgd,lkd->kgrl", query_grp, key_grp, preferred_element_type=jnp.float32)
            * score_scale
        )
        scores = jnp.where(allowed, scores, neg_big)
        attn_probs = jnp.exp(scores - log_total)
        probs_low = attn_probs.astype(jnp.bfloat16)
        grad_probs = jnp.einsum(
            "rkgd,lkd->kgrl", grad_grp, value_grp, preferred_element_type=jnp.float32
        )
        row_delta = jnp.sum(attn_probs * grad_probs, axis=-1, keepdims=True)
        grad_scores = (attn_probs * (grad_probs - row_delta)).astype(jnp.bfloat16)
        grad_query_rot = (
            jnp.einsum("kgrl,lkd->rkgd", grad_scores, key_grp, preferred_element_type=jnp.float32)
            * score_scale
        )
        key_term = (
            jnp.einsum("kgrl,rkgd->lkd", grad_scores, query_grp, preferred_element_type=jnp.float32)
            * score_scale
        )
        value_term = jnp.einsum(
            "kgrl,rkgd->lkd", probs_low, grad_grp, preferred_element_type=jnp.float32
        )
        return (
            grad_query_rot.reshape(row_count, head_count, HD),
            key_term.reshape(full_length, kv_width),
            value_term.reshape(full_length, kv_width),
        )

    outputs = []
    in_grads = []
    totals = None
    for micro_idx in range(MICRO):
        first_seq = micro_idx * per_micro
        block_in = hidden_in[first_seq : first_seq + per_micro]
        block_grad = out_grad[first_seq : first_seq + per_micro]
        col_parts = (
            lax.all_gather(q_weight, "seq", axis=1, tiled=True),
            lax.all_gather(k_weight, "seq", axis=1, tiled=True),
            lax.all_gather(v_weight, "seq", axis=1, tiled=True),
            lax.all_gather(o_weight, "seq", axis=1, tiled=True),
            lax.all_gather(gate_weight, "seq", axis=1, tiled=True),
            lax.all_gather(up_weight, "seq", axis=1, tiled=True),
            lax.all_gather(down_weight, "seq", axis=1, tiled=True),
        )
        query_mat, key_mat, value_mat, out_mat, gate_mat, up_mat, down_mat = (
            lax.all_gather(col_parts[0], "dp", axis=0, tiled=True),
            lax.all_gather(col_parts[1], "dp", axis=0, tiled=True),
            lax.all_gather(col_parts[2], "dp", axis=0, tiled=True),
            lax.all_gather(col_parts[3], "dp", axis=0, tiled=True),
            lax.all_gather(col_parts[4], "dp", axis=0, tiled=True),
            lax.all_gather(col_parts[5], "dp", axis=0, tiled=True),
            lax.all_gather(col_parts[6], "dp", axis=0, tiled=True),
        )
        resid_in = block_in.astype(jnp.float32).reshape(tok_count, model_width)
        rstd_one = lax.rsqrt(jnp.mean(resid_in * resid_in, axis=-1, keepdims=True) + eps_norm)
        normed_one = (resid_in * rstd_one * gain_attn).astype(jnp.bfloat16)
        query_lin = jnp.dot(normed_one, query_mat, preferred_element_type=jnp.float32)
        key_lin = jnp.dot(normed_one, key_mat, preferred_element_type=jnp.float32)
        value_lin = jnp.dot(normed_one, value_mat, preferred_element_type=jnp.float32)
        query_rot = rotate(
            query_lin.reshape(per_micro, row_count, head_count, HD), cos_own, sin_own
        ).astype(jnp.bfloat16)
        key_rot = (
            rotate(key_lin.reshape(per_micro, row_count, kv_heads, HD), cos_own, sin_own)
            .astype(jnp.bfloat16)
            .reshape(per_micro, row_count, kv_width)
        )
        value_low = value_lin.astype(jnp.bfloat16).reshape(per_micro, row_count, kv_width)
        key_all, value_all = (
            lax.all_gather(key_rot, "seq", axis=1, tiled=True),
            lax.all_gather(value_low, "seq", axis=1, tiled=True),
        )
        mixed_seq, log_total = lax.map(attend, (query_rot, key_all, value_all))
        mixed_low = mixed_seq.reshape(tok_count, model_width)
        hidden_mid = resid_in + jnp.dot(mixed_low, out_mat, preferred_element_type=jnp.float32)
        rstd_two = lax.rsqrt(jnp.mean(hidden_mid * hidden_mid, axis=-1, keepdims=True) + eps_norm)
        normed_two = (hidden_mid * rstd_two * gain_mlp).astype(jnp.bfloat16)
        gate_lin = jnp.dot(normed_two, gate_mat, preferred_element_type=jnp.float32)
        up_lin = jnp.dot(normed_two, up_mat, preferred_element_type=jnp.float32)
        gate_sig = jax.nn.sigmoid(gate_lin)
        inner_low = (gate_lin * gate_sig * up_lin).astype(jnp.bfloat16)
        mlp_out = jnp.dot(inner_low, down_mat, preferred_element_type=jnp.float32)
        outputs.append(
            (hidden_mid + mlp_out).astype(jnp.bfloat16).reshape(per_micro, row_count, model_width)
        )
        col_again = (
            lax.all_gather(q_weight, "seq", axis=1, tiled=True),
            lax.all_gather(k_weight, "seq", axis=1, tiled=True),
            lax.all_gather(v_weight, "seq", axis=1, tiled=True),
            lax.all_gather(o_weight, "seq", axis=1, tiled=True),
            lax.all_gather(gate_weight, "seq", axis=1, tiled=True),
            lax.all_gather(up_weight, "seq", axis=1, tiled=True),
            lax.all_gather(down_weight, "seq", axis=1, tiled=True),
        )
        query_mat, key_mat, value_mat, out_mat, gate_mat, up_mat, down_mat = (
            lax.all_gather(col_again[0], "dp", axis=0, tiled=True),
            lax.all_gather(col_again[1], "dp", axis=0, tiled=True),
            lax.all_gather(col_again[2], "dp", axis=0, tiled=True),
            lax.all_gather(col_again[3], "dp", axis=0, tiled=True),
            lax.all_gather(col_again[4], "dp", axis=0, tiled=True),
            lax.all_gather(col_again[5], "dp", axis=0, tiled=True),
            lax.all_gather(col_again[6], "dp", axis=0, tiled=True),
        )
        key_all, value_all = (
            lax.all_gather(key_rot, "seq", axis=1, tiled=True),
            lax.all_gather(value_low, "seq", axis=1, tiled=True),
        )
        grad_top = block_grad.astype(jnp.float32).reshape(tok_count, model_width)
        grad_top_low = grad_top.astype(jnp.bfloat16)
        down_term = jnp.einsum(
            "tf,td->fd", inner_low, grad_top_low, preferred_element_type=jnp.float32
        )
        grad_inner = jnp.einsum(
            "td,fd->tf", grad_top_low, down_mat, preferred_element_type=jnp.float32
        )
        grad_gate = (grad_inner * up_lin * gate_sig * (1.0 + gate_lin * (1.0 - gate_sig))).astype(
            jnp.bfloat16
        )
        grad_up = (grad_inner * gate_lin * gate_sig).astype(jnp.bfloat16)
        gate_term = jnp.einsum(
            "td,tf->df", normed_two, grad_gate, preferred_element_type=jnp.float32
        )
        up_term = jnp.einsum("td,tf->df", normed_two, grad_up, preferred_element_type=jnp.float32)
        grad_normed_two = jnp.einsum(
            "tf,df->td", grad_gate, gate_mat, preferred_element_type=jnp.float32
        ) + jnp.einsum("tf,df->td", grad_up, up_mat, preferred_element_type=jnp.float32)
        grad_mid_norm, gain_mlp_term = norm_back(hidden_mid, rstd_two, gain_mlp, grad_normed_two)
        grad_mid = grad_top + grad_mid_norm
        grad_mid_low = grad_mid.astype(jnp.bfloat16)
        out_term = jnp.einsum(
            "td,te->de", mixed_low, grad_mid_low, preferred_element_type=jnp.float32
        )
        grad_mixed = jnp.einsum(
            "te,de->td", grad_mid_low, out_mat, preferred_element_type=jnp.float32
        ).astype(jnp.bfloat16)
        grad_query_rot, key_terms, value_terms = lax.map(
            attend_back,
            (
                query_rot,
                key_all,
                value_all,
                grad_mixed.reshape(per_micro, row_count, model_width),
                log_total,
            ),
        )
        key_share, value_share = (
            lax.psum_scatter(key_terms, "seq", scatter_dimension=1, tiled=True),
            lax.psum_scatter(value_terms, "seq", scatter_dimension=1, tiled=True),
        )
        grad_query = (
            rotate_back(grad_query_rot, cos_own, sin_own)
            .astype(jnp.bfloat16)
            .reshape(tok_count, model_width)
        )
        grad_key = (
            rotate_back(key_share.reshape(per_micro, row_count, kv_heads, HD), cos_own, sin_own)
            .astype(jnp.bfloat16)
            .reshape(tok_count, kv_width)
        )
        grad_value = value_share.astype(jnp.bfloat16).reshape(tok_count, kv_width)
        query_term = jnp.einsum(
            "td,te->de", normed_one, grad_query, preferred_element_type=jnp.float32
        )
        key_term = jnp.einsum("td,te->de", normed_one, grad_key, preferred_element_type=jnp.float32)
        value_term = jnp.einsum(
            "td,te->de", normed_one, grad_value, preferred_element_type=jnp.float32
        )
        grad_normed_one = (
            jnp.einsum("te,de->td", grad_query, query_mat, preferred_element_type=jnp.float32)
            + jnp.einsum("te,de->td", grad_key, key_mat, preferred_element_type=jnp.float32)
            + jnp.einsum("te,de->td", grad_value, value_mat, preferred_element_type=jnp.float32)
        )
        grad_in_norm, gain_attn_term = norm_back(resid_in, rstd_one, gain_attn, grad_normed_one)
        in_grads.append((grad_mid + grad_in_norm).reshape(per_micro, row_count, model_width))
        totals = add_tuples(
            totals,
            (
                query_term,
                key_term,
                value_term,
                out_term,
                gate_term,
                up_term,
                down_term,
                gain_attn_term,
                gain_mlp_term,
            ),
        )
    col_sums = (
        lax.psum_scatter(
            totals[0].astype(jnp.bfloat16), "seq", scatter_dimension=1, tiled=True
        ).astype(jnp.float32),
        lax.psum_scatter(
            totals[1].astype(jnp.bfloat16), "seq", scatter_dimension=1, tiled=True
        ).astype(jnp.float32),
        lax.psum_scatter(
            totals[2].astype(jnp.bfloat16), "seq", scatter_dimension=1, tiled=True
        ).astype(jnp.float32),
        lax.psum_scatter(
            totals[3].astype(jnp.bfloat16), "seq", scatter_dimension=1, tiled=True
        ).astype(jnp.float32),
        lax.psum_scatter(
            totals[4].astype(jnp.bfloat16), "seq", scatter_dimension=1, tiled=True
        ).astype(jnp.float32),
        lax.psum_scatter(
            totals[5].astype(jnp.bfloat16), "seq", scatter_dimension=1, tiled=True
        ).astype(jnp.float32),
        lax.psum_scatter(
            totals[6].astype(jnp.bfloat16), "seq", scatter_dimension=1, tiled=True
        ).astype(jnp.float32),
    )
    owned = (
        lax.psum_scatter(
            col_sums[0].astype(jnp.bfloat16), "dp", scatter_dimension=0, tiled=True
        ).astype(jnp.float32),
        lax.psum_scatter(
            col_sums[1].astype(jnp.bfloat16), "dp", scatter_dimension=0, tiled=True
        ).astype(jnp.float32),
        lax.psum_scatter(
            col_sums[2].astype(jnp.bfloat16), "dp", scatter_dimension=0, tiled=True
        ).astype(jnp.float32),
        lax.psum_scatter(
            col_sums[3].astype(jnp.bfloat16), "dp", scatter_dimension=0, tiled=True
        ).astype(jnp.float32),
        lax.psum_scatter(
            col_sums[4].astype(jnp.bfloat16), "dp", scatter_dimension=0, tiled=True
        ).astype(jnp.float32),
        lax.psum_scatter(
            col_sums[5].astype(jnp.bfloat16), "dp", scatter_dimension=0, tiled=True
        ).astype(jnp.float32),
        lax.psum_scatter(
            col_sums[6].astype(jnp.bfloat16), "dp", scatter_dimension=0, tiled=True
        ).astype(jnp.float32),
    )
    gain_sums = lax.psum((totals[7], totals[8]), ("dp", "seq"))
    return (
        jnp.concatenate(outputs, axis=0),
        jnp.concatenate(in_grads, axis=0),
        gain_sums[0],
        owned[0],
        owned[1],
        owned[2],
        owned[3],
        gain_sums[1],
        owned[4],
        owned[5],
        owned[6],
    )


F32 = jnp.float32
BF16 = jnp.bfloat16
VMEM_BYTES = 56 * 2**20


def dot(left, right, left_dim, right_dim):
    dims = (((left_dim,), (right_dim,)), ((), ()))
    return lax.dot_general(left, right, dims, preferred_element_type=F32)


def span_slice(inv_ref, place, span):
    return pl.ds(pl.multiple_of(inv_ref[place] * span, span), span)


def lane_pair(ref, rows, inv_ref, block, span):
    first = ref[rows, span_slice(inv_ref, 2 * block, span)]
    second = ref[rows, span_slice(inv_ref, 2 * block + 1, span)]
    return jnp.concatenate([first, second], axis=1)


def row_pair(ref, head, inv_ref, block, span):
    first = ref[head, span_slice(inv_ref, 2 * block, span), :]
    second = ref[head, span_slice(inv_ref, 2 * block + 1, span), :]
    return jnp.concatenate([first, second], axis=0)


def attend_kernel(inv_ref, q_ref, k_ref, v_ref, o_ref, l_ref, acc_ref, *, blocks, span, group):
    wide = 2 * span
    row = lax.broadcasted_iota(jnp.int32, (wide, wide), 0)
    col = lax.broadcasted_iota(jnp.int32, (wide, wide), 1)
    keep = row <= col

    def one_block(block, odd):
        queries = [
            lane_pair(q_ref, slice(HD * h, HD * h + HD), inv_ref, block, span) for h in range(group)
        ]
        acc_ref[...] = jnp.zeros_like(acc_ref)

        def step(first, count, state, diagonal):
            state = list(state)
            keys = [row_pair(k_ref, 0, inv_ref, first + u, span) for u in range(count)]
            values = [lane_pair(v_ref, slice(0, HD), inv_ref, first + u, span) for u in range(count)]
            items = [(u, h) for u in range(count) for h in range(group)]
            scores = [dot(keys[u], queries[h], 1, 0) for u, h in items]
            probs = []
            for (u, h), score in zip(items, scores):
                peak, total = state[h]
                if diagonal and u == count - 1:
                    score = jnp.where(keep, score, neg_big)
                new_peak = jnp.maximum(peak, jnp.max(score, axis=0, keepdims=True))
                prob = jnp.exp(score - new_peak)
                shrink = jnp.exp(peak - new_peak)
                state[h] = (new_peak, total * shrink + jnp.sum(prob, axis=0, keepdims=True))
                probs.append((prob.astype(BF16), shrink))
            for (u, h), (prob, shrink) in zip(items, probs):
                cols = slice(h * wide, (h + 1) * wide)
                acc_ref[:, cols] = acc_ref[:, cols] * shrink + dot(values[u], prob, 1, 0)
            return tuple(state)

        state = tuple(
            (jnp.full((1, wide), neg_big, F32), jnp.zeros((1, wide), F32)) for _ in range(group)
        )
        state = lax.fori_loop(0, block // 4, lambda j, s: step(4 * j, 4, s, False), state)
        state = lax.fori_loop(
            2 * (block // 4), block // 2, lambda j, s: step(2 * j, 2, s, False), state
        )
        state = step(block - 1, 2, state, True) if odd else step(block, 1, state, True)
        mixed = jnp.concatenate(
            [acc_ref[:, wide * h : wide * (h + 1)] * (1.0 / state[h][1]) for h in range(group)], axis=0
        ).astype(BF16)
        logs = jnp.concatenate(
            [p + jnp.log(t) for p, t in state] + [jnp.zeros((8 - group, wide), F32)], axis=0
        )
        for part in range(2):
            where = span_slice(inv_ref, 2 * block + part, span)
            cols = slice(part * span, part * span + span)
            o_ref[:, where] = mixed[:, cols]
            l_ref[0, :, where] = logs[:, cols]

    def two_blocks(pair, _):
        for odd in (0, 1):
            one_block(2 * pair + odd, odd)
        return 0

    lax.fori_loop(0, blocks // 2, two_blocks, 0)


def attention_forward(inv, q_t, k_nat, v_t, span):
    tokens = q_t.shape[1]
    kv_heads = k_nat.shape[0]
    group = q_t.shape[0] // (kv_heads * HD)
    pairs = kv_heads * group * tokens * tokens
    wide_spec = pl.BlockSpec((group * HD, tokens), lambda g, i: (g, 0))
    nat_spec = pl.BlockSpec((1, tokens, HD), lambda g, i: (g, 0, 0))
    return pl.pallas_call(
        functools.partial(attend_kernel, blocks=tokens // (2 * span), span=span, group=group),
        grid_spec=pltpu.PrefetchScalarGridSpec(
            num_scalar_prefetch=1,
            grid=(kv_heads,),
            in_specs=[wide_spec, nat_spec, pl.BlockSpec((HD, tokens), lambda g, i: (g, 0))],
            out_specs=[
                wide_spec,
                pl.BlockSpec((1, 8, tokens), lambda g, i: (g, 0, 0)),
            ],
            scratch_shapes=[pltpu.VMEM((HD, group * 2 * span), F32)],
        ),
        out_shape=[
            jax.ShapeDtypeStruct(q_t.shape, BF16),
            jax.ShapeDtypeStruct((kv_heads, 8, tokens), F32),
        ],
        compiler_params=pltpu.CompilerParams(vmem_limit_bytes=VMEM_BYTES),
        cost_estimate=pl.CostEstimate(
            flops=16 * pairs * HD, bytes_accessed=tokens * 6000, transcendentals=pairs // 2
        ),
        name="attention_forward",
    )(inv, q_t, k_nat, v_t)


def attend_back_kernel(
    inv_ref, q_ref, kt_ref, k_ref, v_ref, o_ref, do_ref, l_ref, cos_ref, sin_ref,
    dq_ref, dk_ref, dv_ref, dk_sum, dv_sum, dq_sum, *, blocks, span, group,
):
    wide = 2 * span
    row = lax.broadcasted_iota(jnp.int32, (wide, wide), 0)
    col = lax.broadcasted_iota(jnp.int32, (wide, wide), 1)
    keep = row <= col
    half = HD // 2
    dk_sum[...] = jnp.zeros_like(dk_sum)
    dv_sum[...] = jnp.zeros_like(dv_sum)

    def rope_back(grad, cos, sin):
        top, low = grad[:half], grad[half:]
        return jnp.concatenate([top * cos + low * sin, low * cos - top * sin], axis=0)

    def one_block(block, odd):
        rows = [slice(HD * h, HD * h + HD) for h in range(group)]
        queries = [lane_pair(q_ref, r, inv_ref, block, span) for r in rows]
        grads = [lane_pair(do_ref, r, inv_ref, block, span) for r in rows]
        logs = lane_pair(l_ref.at[0], slice(None), inv_ref, block, span)
        deltas = [
            jnp.sum(
                lane_pair(o_ref, r, inv_ref, block, span).astype(F32) * grad.astype(F32),
                axis=0,
                keepdims=True,
            )
            for r, grad in zip(rows, grads)
        ]
        dq_sum[...] = jnp.zeros_like(dq_sum)

        def step(first, count, diagonal):
            keys = [row_pair(k_ref, 0, inv_ref, first + u, span) for u in range(count)]
            values = [row_pair(v_ref, 0, inv_ref, first + u, span) for u in range(count)]
            keys_t = [lane_pair(kt_ref, slice(0, HD), inv_ref, first + u, span) for u in range(count)]
            items = [(u, h) for u in range(count) for h in range(group)]
            ahead, ready, dqs, sums = {}, {}, {}, {}

            def products(i):
                u, h = items[i]
                ahead[i] = dot(keys[u], queries[h], 1, 0), dot(values[u], grads[h], 1, 0)

            def softmax_part(i):
                u, h = items[i]
                score, dprob = ahead.pop(i)
                prob = jnp.exp(score - logs[h : h + 1])
                if diagonal and u == count - 1:
                    prob = jnp.where(keep, prob, 0.0)
                ready[i] = prob.astype(BF16), (prob * (dprob - deltas[h])).astype(BF16)

            def gradients(i):
                u, h = items[i]
                prob, dscore = ready.pop(i)
                dq = dot(keys_t[u], dscore, 1, 0)
                dqs[h] = dqs[h] + dq if h in dqs else dq
                if u == count - 1:
                    dq_sum[:, wide * h : wide * (h + 1)] += dqs[h]
                dk, dv = dot(queries[h], dscore, 1, 1), dot(grads[h], prob, 1, 1)
                if u in sums:
                    dk, dv = dk + sums[u][0], dv + sums[u][1]
                sums[u] = dk, dv
                if h == group - 1:
                    place = pl.ds(pl.multiple_of((first + u) * wide, wide), wide)
                    dk_sum[:, place] += dk
                    dv_sum[:, place] += dv

            lead = 2
            for i in range(min(lead, len(items))):
                products(i)
            for i in range(len(items) + 1):
                if i + lead < len(items):
                    products(i + lead)
                if i > 0:
                    gradients(i - 1)
                if i < len(items):
                    softmax_part(i)

        def pair_step(j, _):
            step(2 * j, 2, False)
            return 0

        lax.fori_loop(0, block // 2, pair_step, 0)
        if odd:
            step(block - 1, 2, True)
        else:
            step(block, 1, True)
        cos = lane_pair(cos_ref, slice(None), inv_ref, block, span)
        sin = lane_pair(sin_ref, slice(None), inv_ref, block, span)
        dq = jnp.concatenate(
            [rope_back(dq_sum[:, wide * h : wide * (h + 1)] * HD**-0.5, cos, sin) for h in range(group)],
            axis=0,
        ).astype(BF16)
        place = pl.ds(pl.multiple_of(block * wide, wide), wide)
        dk = rope_back(dk_sum[:, place], cos, sin).astype(BF16)
        dv = dv_sum[:, place].astype(BF16)
        for part in range(2):
            where = span_slice(inv_ref, 2 * block + part, span)
            cols = slice(part * span, part * span + span)
            dq_ref[:, where] = dq[:, cols]
            dk_ref[:, where] = dk[:, cols]
            dv_ref[:, where] = dv[:, cols]

    def two_blocks(step, _):
        for odd in (1, 0):
            one_block(blocks - 2 - 2 * step + odd, odd)
        return 0

    lax.fori_loop(0, blocks // 2, two_blocks, 0)


def attention_backward(inv, q_t, k_t, k_nat, v_nat, o_t, do_t, logs, cos_t, sin_t, span, first, count):
    tokens = q_t.shape[1]
    kv_heads = k_nat.shape[0]
    group = q_t.shape[0] // (kv_heads * HD)
    pairs = count * group * tokens * tokens
    wide_spec = pl.BlockSpec((group * HD, tokens), lambda g, i: (g + first, 0))
    kv_spec = pl.BlockSpec((HD, tokens), lambda g, i: (g + first, 0))
    nat_spec = pl.BlockSpec((1, tokens, HD), lambda g, i: (g + first, 0, 0))
    tab_spec = pl.BlockSpec((HD // 2, tokens), lambda g, i: (0, 0))
    return pl.pallas_call(
        functools.partial(attend_back_kernel, blocks=tokens // (2 * span), span=span, group=group),
        grid_spec=pltpu.PrefetchScalarGridSpec(
            num_scalar_prefetch=1,
            grid=(count,),
            in_specs=[
                wide_spec, kv_spec, nat_spec, nat_spec, wide_spec, wide_spec,
                pl.BlockSpec((1, 8, tokens), lambda g, i: (g + first, 0, 0)), tab_spec, tab_spec,
            ],
            out_specs=[
                pl.BlockSpec((group * HD, tokens), lambda g, i: (g, 0)),
                pl.BlockSpec((HD, tokens), lambda g, i: (g, 0)),
                pl.BlockSpec((HD, tokens), lambda g, i: (g, 0)),
            ],
            scratch_shapes=[
                pltpu.VMEM((HD, tokens), F32),
                pltpu.VMEM((HD, tokens), F32),
                pltpu.VMEM((HD, group * 2 * span), F32),
            ],
        ),
        out_shape=[
            jax.ShapeDtypeStruct((count * group * HD, tokens), BF16),
            jax.ShapeDtypeStruct((count * HD, tokens), BF16),
            jax.ShapeDtypeStruct((count * HD, tokens), BF16),
        ],
        compiler_params=pltpu.CompilerParams(vmem_limit_bytes=VMEM_BYTES),
        cost_estimate=pl.CostEstimate(
            flops=32 * pairs * HD, bytes_accessed=tokens * 9000, transcendentals=pairs // 2
        ),
        name="attention_backward",
    )(inv, q_t, k_t, k_nat, v_nat, o_t, do_t, logs, cos_t, sin_t)


def flip(index, bits):
    for bit in bits:
        index = index + bit * (1 - 2 * ((index // bit) % 2))
    return index


def bits_of(size):
    return [1 << i for i in range(size.bit_length() - 1)]


def seq_stages(seq):
    return [("seq", b) for b in reversed(bits_of(seq)[1:])] + [("seq", b) for b in bits_of(seq)[:1]]


def all_stages(dp, seq):
    return seq_stages(seq) + [("dp", b) for b in reversed(bits_of(dp))]


def rest_chains(dp, seq):
    near, far = [("seq", b) for b in bits_of(seq)[:1]], [("seq", b) for b in reversed(bits_of(seq)[1:])]
    chip = [("dp", b) for b in reversed(bits_of(dp)[1:])]
    return far + near + chip, far + chip + near


def away_place(stages, d, s, my_dp, my_seq):
    place = 0
    for at, (axis, bit) in enumerate(stages):
        mine = ((my_dp if axis == "dp" else my_seq) // bit) % 2
        theirs = ((d if axis == "dp" else s) // bit) % 2
        place = place + (1 << at) * (1 - mine if theirs else mine)
    return place


def arrival_order(stages, dp, seq, my_dp, my_seq):
    ids = jnp.arange(dp * seq, dtype=jnp.int32)
    away = {"dp": (ids // seq) ^ my_dp, "seq": (ids % seq) ^ my_seq}
    place = jnp.zeros_like(ids)
    for at, (axis, bit) in enumerate(stages):
        place = place + (1 << at) * ((away[axis] // bit) % 2)
    return place


def greet(peers):
    barrier = pltpu.get_barrier_semaphore()
    for peer in peers:
        pl.semaphore_signal(barrier, inc=1, device_id=peer, device_id_type=pl.DeviceIdType.MESH)
    pl.semaphore_wait(barrier, len(peers))


def seq_peer(my_dp, my_seq, away, seq):
    return my_dp, flip(my_seq, [b for b in bits_of(seq) if away & b])


def stage_peer(my_dp, my_seq, stage):
    axis, bit = stage
    return (flip(my_dp, [bit]), my_seq) if axis == "dp" else (my_dp, flip(my_seq, [bit]))


def all_peers(my_dp, my_seq, dp, seq):
    peers = [seq_peer(my_dp, my_seq, away, seq) for away in range(1, seq)]
    return peers + [(flip(my_dp, [b]), my_seq) for b in bits_of(dp)]


def bring_kernel(x_ref, first_ref, second_ref, third_ref, out_ref, all_first, all_second, all_third,
                 local_sem, x_send, x_recv, w_send, w_recv, *, dp, seq):
    my_dp, my_seq = lax.axis_index("dp"), lax.axis_index("seq")
    orders = all_stages(dp, seq), seq_stages(seq), seq_stages(seq)
    chains = range(len(orders))
    greet(all_peers(my_dp, my_seq, dp, seq))
    shards_in = first_ref, second_ref, third_ref
    gathered = all_first, all_second, all_third

    def weight_copy(chain, stage):
        held = 1 << stage
        source = shards_in[chain] if stage == 0 else gathered[chain].at[pl.ds(0, held)]
        return pltpu.make_async_remote_copy(
            src_ref=source,
            dst_ref=gathered[chain].at[pl.ds(held, held)],
            send_sem=w_send.at[chain, stage],
            recv_sem=w_recv.at[chain, stage],
            device_id=stage_peer(my_dp, my_seq, orders[chain][stage]),
            device_id_type=pl.DeviceIdType.MESH,
        )

    copies = [[weight_copy(c, s) for s in range(len(orders[c]))] for c in chains]
    for c in chains:
        copies[c][0].start()
    own = [
        pltpu.make_async_copy(shards_in[c], gathered[c].at[pl.ds(0, 1)], local_sem.at[c]) for c in chains
    ]
    own.append(pltpu.make_async_copy(x_ref.at[my_seq], out_ref.at[my_seq], local_sem.at[len(orders)]))
    for copy in own:
        copy.start()
    moves = []
    for away in range(1, seq):
        peer = seq_peer(my_dp, my_seq, away, seq)
        moves.append(
            pltpu.make_async_remote_copy(
                src_ref=x_ref.at[peer[1]],
                dst_ref=out_ref.at[my_seq],
                send_sem=x_send.at[away - 1],
                recv_sem=x_recv.at[away - 1],
                device_id=peer,
                device_id_type=pl.DeviceIdType.MESH,
            )
        )
    for c in chains:
        own[c].wait()
    for stage in range(1, len(orders[0])):
        for c in chains:
            if stage < len(orders[c]):
                copies[c][stage - 1].wait_recv()
                copies[c][stage].start()
        if stage == 1:
            for move in moves:
                move.start()
    for c in chains:
        copies[c][-1].wait_recv()
        for copy in copies[c]:
            copy.wait_send()
    for move in moves:
        move.wait()
    own[-1].wait()


def bring(x, first, second, third):
    dp, seq = lax.axis_size("dp"), lax.axis_size("seq")
    stages = len(all_stages(dp, seq))
    hbm = pl.BlockSpec(memory_space=pl.ANY)
    return pl.pallas_call(
        functools.partial(bring_kernel, dp=dp, seq=seq),
        in_specs=[hbm] * 4,
        out_specs=[hbm] * 4,
        out_shape=[
            jax.ShapeDtypeStruct(x.shape, x.dtype),
            jax.ShapeDtypeStruct((dp * seq, *first.shape[1:]), first.dtype),
            jax.ShapeDtypeStruct((seq, *second.shape[1:]), second.dtype),
            jax.ShapeDtypeStruct((seq, *third.shape[1:]), third.dtype),
        ],
        scratch_shapes=[
            pltpu.SemaphoreType.DMA((4,)),
            pltpu.SemaphoreType.DMA((seq - 1,)),
            pltpu.SemaphoreType.DMA((seq - 1,)),
            pltpu.SemaphoreType.DMA((3, stages)),
            pltpu.SemaphoreType.DMA((3, stages)),
        ],
        compiler_params=pltpu.CompilerParams(
            collective_id=1, has_side_effects=True, vmem_limit_bytes=VMEM_BYTES
        ),
        name="bring",
    )(x, first, second, third)


def qkv_kernel(where_ref, x_ref, gain_ref, packed_ref, cos_ref, sin_ref,
               q_ref, kt_ref, vt_ref, k_ref, v_ref, w_ref, w_wide, *, heads, kv_heads, dp, seq):
    half = HD // 2
    width = w_ref.shape[1]
    q_cols, kv_cols = width // seq, kv_heads * HD // seq
    kv_width = kv_heads * HD

    @pl.when(pl.program_id(0) == 0)
    def _():
        for s in range(seq):
            block = jnp.concatenate([packed_ref[where_ref[d * seq + s]] for d in range(dp)], axis=0)
            turned = block.astype(F32).T
            w_wide[q_cols * s : q_cols * s + q_cols, :] = turned[:q_cols]
            first = width + kv_cols * s
            w_wide[first : first + kv_cols, :] = turned[q_cols : q_cols + kv_cols]
            first += kv_width
            w_wide[first : first + kv_cols, :] = turned[q_cols + kv_cols : q_cols + 2 * kv_cols]
        w_ref[...] = w_wide[...].astype(BF16)

    x = x_ref[0].astype(F32)
    rstd = lax.rsqrt(jnp.mean(x * x, axis=0, keepdims=True) + eps_norm)
    normed = (x * rstd * gain_ref[...]).astype(BF16)
    lin = dot(w_ref[...], normed, 1, 0)
    cos, sin = cos_ref[...], sin_ref[...]
    for head in range(heads + kv_heads):
        top = lin[HD * head : HD * head + half]
        low = lin[HD * head + half : HD * head + HD]
        rot = jnp.concatenate([top * cos - low * sin, low * cos + top * sin], axis=0)
        if head < heads:
            q_ref[HD * head : HD * head + HD, :] = rot.astype(BF16) * jnp.asarray(HD**-0.5, BF16)
        else:
            kv = head - heads
            kt_ref[HD * kv : HD * kv + HD, :] = rot.astype(BF16)
            k_ref[kv] = rot.T.astype(BF16)
    for kv in range(kv_heads):
        first = HD * (heads + kv_heads + kv)
        val = lin[first : first + HD]
        vt_ref[HD * kv : HD * kv + HD, :] = val.astype(BF16)
        v_ref[kv] = val.T.astype(BF16)


def project_qkv(where, x, gain, packed, cos_t, sin_t, heads, kv_heads, rows):
    blocks, width, block = x.shape
    tokens = blocks * block
    feats = (heads + 2 * kv_heads) * HD
    dp, seq = lax.axis_size("dp"), lax.axis_size("seq")
    col = lambda rows: pl.BlockSpec((rows, block), lambda i, w: (0, i))
    nat = pl.BlockSpec((kv_heads, block, HD), lambda i, w: (0, i, 0))
    return pl.pallas_call(
        functools.partial(qkv_kernel, heads=heads, kv_heads=kv_heads, dp=dp, seq=seq),
        grid_spec=pltpu.PrefetchScalarGridSpec(
            num_scalar_prefetch=1,
            grid=(blocks,),
            in_specs=[
                pl.BlockSpec((1, width, block), lambda i, w: (i, 0, 0)),
                pl.BlockSpec((width, 1), lambda i, w: (0, 0)),
                pl.BlockSpec((dp * seq, rows, packed.shape[2]), lambda i, w: (0, 0, 0)),
                col(HD // 2),
                col(HD // 2),
            ],
            out_specs=[
                col(heads * HD), col(kv_heads * HD), col(kv_heads * HD), nat, nat,
                pl.BlockSpec((feats, width), lambda i, w: (0, 0)),
            ],
            scratch_shapes=[pltpu.VMEM((feats, width), F32)],
        ),
        out_shape=[
            jax.ShapeDtypeStruct((heads * HD, tokens), BF16),
            jax.ShapeDtypeStruct((kv_heads * HD, tokens), BF16),
            jax.ShapeDtypeStruct((kv_heads * HD, tokens), BF16),
            jax.ShapeDtypeStruct((kv_heads, tokens, HD), BF16),
            jax.ShapeDtypeStruct((kv_heads, tokens, HD), BF16),
            jax.ShapeDtypeStruct((feats, width), BF16),
        ],
        compiler_params=pltpu.CompilerParams(vmem_limit_bytes=VMEM_BYTES),
        cost_estimate=pl.CostEstimate(
            flops=4 * tokens * width * feats, bytes_accessed=tokens * 5000, transcendentals=0
        ),
        name="project_qkv",
    )(where, x, gain, packed, cos_t, sin_t)


def side_by_side(ref):
    return jnp.concatenate([ref[i] for i in range(ref.shape[0])], axis=1)


def mlp_kernel(
    where_ref, x_ref, mixed_ref, dy_ref, gain_ref, *more, chunk, dp, seq,
):
    packs, more = more[: 2 * dp], more[2 * dp :]
    out_ref, dmid_ref, dmixed_ref = more[:3]
    one_refs, two_refs, gain_grad_ref = more[3:5], more[5:7], more[7]
    (o_w, o_t, gate_w, gate_t, up_w, up_t, down_w, down_t, o_sum, gate_sum, up_sum, down_sum, gain_sum,
     pack, pack_sem) = more[8:]
    step, steps = pl.program_id(0), pl.num_programs(0)
    width, ff = gate_w.shape
    lanes = pack.shape[3]
    rows = width // dp
    o_cols, ff_cols, ff_rows = width // seq, ff // seq, ff // dp
    spare = ff_cols - lanes
    padded = -(-o_cols // 16) * 16

    @pl.when(step == 0)
    def _():
        for total in (o_sum, gate_sum, up_sum, down_sum, gain_sum):
            total[...] = jnp.zeros_like(total)
        fetches = []
        for i in range(dp):
            owner = flip(lax.axis_index("dp"), row_bits(i, dp))
            first = 0
            for source, sem in ((packs[2 * i], pack_sem.at[2 * i]), (packs[2 * i + 1], pack_sem.at[2 * i + 1])):
                span = pl.ds(first, source.shape[1])
                fetches.append(pltpu.make_async_copy(source, pack.at[owner, :, span, :], sem))
                first += source.shape[1]
        for fetch in fetches:
            fetch.start()
        for fetch in fetches:
            fetch.wait()
        for s in range(seq):
            at = where_ref[s]
            stack = lambda first: jnp.concatenate(
                [pack[d, at, first : first + rows, :] for d in range(dp)], axis=0
            ).astype(F32).T
            o_sum[o_cols * s : o_cols * s + o_cols, :] = stack(0)[:o_cols]
            gate_t[ff_cols * s : ff_cols * s + lanes, :] = stack(rows).astype(BF16)
            up_t[ff_cols * s : ff_cols * s + lanes, :] = stack(2 * rows).astype(BF16)
            both = stack(3 * rows).astype(BF16)
            gate_t[ff_cols * s + lanes : ff_cols * (s + 1), :] = both[:spare]
            up_t[ff_cols * s + lanes : ff_cols * (s + 1), :] = both[spare : 2 * spare]
            for d in range(dp):
                for t in range(ff_rows // lanes):
                    first = 4 * rows + padded * t
                    piece = pack[d, at, first : first + padded, :].astype(F32)[:o_cols]
                    cols = slice(ff_rows * d + lanes * t, ff_rows * d + lanes * (t + 1))
                    down_sum[o_cols * s : o_cols * s + o_cols, cols] = piece
        o_t[...] = o_sum[...].astype(BF16)
        o_w[...] = o_sum[...].T.astype(BF16)
        down_t[...] = down_sum[...].astype(BF16)
        for first in range(0, ff, lanes):
            part = slice(first, first + lanes)
            down_w[part, :] = down_sum[:, part].T.astype(BF16)
            gate_w[:, part] = gate_t[part, :].T
            up_w[:, part] = up_t[part, :].T
        o_sum[...] = jnp.zeros_like(o_sum)
        down_sum[...] = jnp.zeros_like(down_sum)

    gain = gain_ref[...]
    mixed = mixed_ref[...]
    mid = dot(o_t[...], mixed, 1, 0) + side_by_side(x_ref).astype(F32)
    rstd = lax.rsqrt(jnp.mean(mid * mid, axis=0, keepdims=True) + eps_norm)
    normed = (mid * rstd * gain).astype(BF16)
    dy = side_by_side(dy_ref)
    added = jnp.zeros_like(mid)
    dnormed = jnp.zeros_like(mid)
    for first in range(0, ff, chunk):
        part = slice(first, first + chunk)
        gate = dot(gate_t[part, :], normed, 1, 0)
        up = dot(up_t[part, :], normed, 1, 0)
        dinner = dot(down_w[part, :], dy, 1, 0)
        sig = 1.0 / (1.0 + jnp.exp(-gate))
        silu = gate * sig
        inner = (silu * up).astype(BF16)
        dup = (dinner * silu).astype(BF16)
        dgate = (dinner * up * sig * (1.0 + gate * (1.0 - sig))).astype(BF16)
        added += dot(down_t[:, part], inner, 1, 0)
        dnormed += dot(gate_w[:, part], dgate, 1, 0)
        dnormed += dot(up_w[:, part], dup, 1, 0)
        down_sum[:, part] += dot(dy, inner, 1, 1)
        gate_sum[part, :] += dot(dgate, normed, 1, 1)
        up_sum[part, :] += dot(dup, normed, 1, 1)
    out = (mid + added).astype(BF16)
    scaled_mid = mid * rstd
    product = dnormed * scaled_mid
    gain_sum[...] += sum(product[:, c : c + lanes] for c in range(0, product.shape[1], lanes))
    scaled = dnormed * gain
    pull = jnp.mean(scaled * mid, axis=0, keepdims=True)
    dmid = dy.astype(F32) + rstd * scaled - scaled_mid * (rstd * rstd * pull)
    dmid_low = dmid.astype(BF16)
    block = out_ref.shape[2]
    for i in range(out_ref.shape[0]):
        out_ref[i] = out[:, block * i : block * (i + 1)]
        dmid_ref[i] = dmid[:, block * i : block * (i + 1)]
    o_sum[...] += dot(dmid_low, mixed, 1, 1)
    dmixed_ref[...] = dot(o_w[...], dmid_low, 1, 0).astype(BF16)

    @pl.when(step == steps - 1)
    def _():
        gain_grad_ref[...] = jnp.sum(gain_sum[...].T, axis=0, keepdims=True)
        my_dp, my_seq = lax.axis_index("dp"), lax.axis_index("seq")
        upper = my_dp % 2 == 1

        def put(refs, place, first, even, odd):
            keep_ref, give_ref = refs
            span = slice(first, first + even.shape[0])
            keep_ref[place, span, :] = jnp.where(upper, odd, even).astype(BF16)
            give_ref[place, span, :] = jnp.where(upper, even, odd).astype(BF16)

        blank = jnp.zeros((lanes - o_cols, width), F32)
        edge = jnp.zeros((padded - o_cols, lanes), F32)
        for s in range(seq):
            tall = lambda total, first, count: total[first : first + count, :]
            o_piece = jnp.concatenate([tall(o_sum, o_cols * s, o_cols), blank], axis=0).T
            gate_piece = tall(gate_sum, ff_cols * s, lanes).T
            up_piece = tall(up_sum, ff_cols * s, lanes).T
            both = jnp.concatenate(
                [tall(gate_sum, ff_cols * s + lanes, spare), tall(up_sum, ff_cols * s + lanes, spare)], axis=0
            ).T
            for d in range(0, dp, 2):
                bands = slice(rows * d, rows * (d + 1)), slice(rows * (d + 1), rows * (d + 2))
                one, two = [away_place(c, d, s, my_dp, my_seq) for c in rest_chains(dp, seq)]
                for i, piece in enumerate((o_piece, gate_piece, up_piece)):
                    put(one_refs, one, rows * i, piece[bands[0]], piece[bands[1]])
                put(two_refs, two, 0, both[bands[0]], both[bands[1]])
                for t in range(ff_rows // lanes):
                    pair = []
                    for at in (d, d + 1):
                        cols = slice(ff_rows * at + lanes * t, ff_rows * at + lanes * (t + 1))
                        pair.append(
                            jnp.concatenate([down_sum[o_cols * s : o_cols * (s + 1), cols], edge], axis=0)
                        )
                    put(two_refs, two, rows + padded * t, *pair)


def row_bits(at, dp):
    return [b for i, b in enumerate(reversed(bits_of(dp))) if (at >> i) & 1]


def over_rows(array, mask):
    return lax.ppermute(array, "dp", [(i, i ^ mask) for i in range(lax.axis_size("dp"))])


def mlp_both(where, x, mixed, dy, gain, packs, ff, batch=2, chunk=512):
    blocks, width, block = x.shape
    tokens = blocks * block
    dp, seq = lax.axis_size("dp"), lax.axis_size("seq")
    grad_rows, lanes = packs[0].shape[1] + packs[1].shape[1], packs[0].shape[2]
    first_rows = 3 * (width // dp)
    one = dp * seq // 2, first_rows, lanes
    two = dp * seq // 2, grad_rows - first_rows, lanes
    tok = pl.BlockSpec((batch, width, block), lambda i, w: (i, 0, 0))
    col = pl.BlockSpec((width, batch * block), lambda i, w: (0, i))
    once = lambda shape: pl.BlockSpec(
        shape, lambda i, w: (0,) * len(shape), pipeline_mode=pl.Buffered(1)
    )
    hbm = pl.BlockSpec(memory_space=pl.ANY)
    return pl.pallas_call(
        functools.partial(mlp_kernel, chunk=chunk, dp=dp, seq=seq),
        grid_spec=pltpu.PrefetchScalarGridSpec(
            num_scalar_prefetch=1,
            grid=(blocks // batch,),
            in_specs=[tok, col, tok, once((width, 1))] + [hbm] * (2 * dp),
            out_specs=[tok, tok, col, once(one), once(one), once(two), once(two), once((1, width))],
            scratch_shapes=[
                pltpu.VMEM((width, width), BF16),
                pltpu.VMEM((width, width), BF16),
                pltpu.VMEM((width, ff), BF16),
                pltpu.VMEM((ff, width), BF16),
                pltpu.VMEM((width, ff), BF16),
                pltpu.VMEM((ff, width), BF16),
                pltpu.VMEM((ff, width), BF16),
                pltpu.VMEM((width, ff), BF16),
                pltpu.VMEM((width, width), F32),
                pltpu.VMEM((ff, width), F32),
                pltpu.VMEM((ff, width), F32),
                pltpu.VMEM((width, ff), F32),
                pltpu.VMEM((width, lanes), F32),
                pltpu.VMEM((dp, packs[0].shape[0], grad_rows, lanes), BF16),
                pltpu.SemaphoreType.DMA((2 * dp,)),
            ],
        ),
        out_shape=[
            jax.ShapeDtypeStruct(x.shape, BF16),
            jax.ShapeDtypeStruct(x.shape, F32),
            jax.ShapeDtypeStruct((width, tokens), BF16),
            jax.ShapeDtypeStruct(one, BF16),
            jax.ShapeDtypeStruct(one, BF16),
            jax.ShapeDtypeStruct(two, BF16),
            jax.ShapeDtypeStruct(two, BF16),
            jax.ShapeDtypeStruct((1, width), F32),
        ],
        compiler_params=pltpu.CompilerParams(vmem_limit_bytes=60 * 2**20),
        cost_estimate=pl.CostEstimate(
            flops=2 * tokens * width * (9 * ff + 3 * width),
            bytes_accessed=tokens * width * 14,
            transcendentals=tokens * ff,
        ),
        name="mlp_both",
    )(where, x, mixed, dy, gain, *packs)


def across(index, other, size):
    for bit in bits_of(size):
        index = index + bit * ((other // bit) % 2) * (1 - 2 * ((index // bit) % 2))
    return index


def add_blocks(total_ref, term_ref, count, total_first=0, term_first=0):
    def one(i, _):
        total = total_ref[total_first + i].astype(F32) + term_ref[term_first + i].astype(F32)
        total_ref[total_first + i] = total.astype(BF16)
        return 0

    lax.fori_loop(0, count, one, 0)


def finish_kernel(
    x_ref, dmid_ref, dq_one, dq_two, dk_one, dk_two, dv_one, dv_two, gain_ref, w_t_ref, other_gain_ref,
    keep_one, keep_two, came_one, came_two, out_ref, gains_ref, qkv_ref, one_ref, two_ref,
    w_nat, w_sum, gain_sum, din, packed, landed, one, one_came, one_landed, two, two_came, two_landed,
    gain_held, gain_landed,
    own_sem, d_send, d_recv, r_send, r_recv, g_send, g_recv, fetch_sem, *, dp, seq, kv_width,
):
    step, steps = pl.program_id(0), seq // 2
    my_dp, my_seq = lax.axis_index("dp"), lax.axis_index("seq")
    width = w_nat.shape[0]
    lanes = packed.shape[2]
    rows = width // dp
    q_cols, kv_cols = width // seq, kv_width // seq
    orders = [all_stages(dp, seq), *[chain[:-1] for chain in rest_chains(dp, seq)]]
    held = [packed, one, two]
    arrived = [landed, one_landed, two_landed]
    fetches = [
        pltpu.make_async_copy(source, target, fetch_sem.at[i])
        for i, (source, target) in enumerate(
            ((keep_one, one), (keep_two, two), (came_one, one_came), (came_two, two_came))
        )
    ]

    def halve(chain, turn):
        at = len(orders[chain]) - 1 - turn
        half = 1 << at
        return pltpu.make_async_remote_copy(
            src_ref=held[chain].at[pl.ds(half, half)],
            dst_ref=arrived[chain].at[pl.ds(half, half)],
            send_sem=r_send.at[chain, turn],
            recv_sem=r_recv.at[chain, turn],
            device_id=stage_peer(my_dp, my_seq, orders[chain][at]),
            device_id_type=pl.DeviceIdType.MESH,
        )

    def take(chain, turn):
        halve(chain, turn).wait_recv()
        half = 1 << (len(orders[chain]) - 1 - turn)
        if half > 1:
            add_blocks(held[chain], arrived[chain], half, 0, half)
            halve(chain, turn + 1).start()

    def result(chain):
        return held[chain][0].astype(F32) + arrived[chain][1].astype(F32)

    @pl.when(step == 0)
    def _():
        for fetch in fetches:
            fetch.start()
        greet(all_peers(my_dp, my_seq, dp, seq))
        for fetch in fetches:
            fetch.wait()
        for chain, came in ((1, one_came), (2, two_came)):
            add_blocks(held[chain], came, came.shape[0])
            halve(chain, 0).start()
        w_sum[...] = jnp.zeros_like(w_sum)
        gain_sum[...] = jnp.zeros_like(gain_sum)
        w_nat[...] = w_t_ref[...].T

    gain = gain_ref[...]
    x = side_by_side(x_ref).astype(F32)
    rstd = lax.rsqrt(jnp.mean(x * x, axis=0, keepdims=True) + eps_norm)
    scaled_x = x * rstd
    normed = (scaled_x * gain).astype(BF16)
    dlins = dq_one, dq_two, dk_one, dk_two, dv_one, dv_two
    dlin = jnp.concatenate([ref[...] for ref in dlins], axis=0)
    w_sum[...] += dot(dlin, normed, 1, 1)
    dnormed = dot(w_nat[...], dlin, 1, 0)
    product = dnormed * scaled_x
    gain_sum[...] += sum(product[:, c : c + lanes] for c in range(0, product.shape[1], lanes))
    scaled = dnormed * gain
    pull = jnp.mean(scaled * x, axis=0, keepdims=True)
    total = side_by_side(dmid_ref) + rstd * scaled - scaled_x * (rstd * rstd * pull)
    pair = across(my_seq // 2, steps - 1 - step, seq // 2)
    block = din.shape[2]
    for i in range(2):
        din[2 * pair + i] = total[:, block * i : block * (i + 1)].astype(BF16)

    def move(away):
        peer = seq_peer(my_dp, my_seq, away, seq)
        return pltpu.make_async_remote_copy(
            src_ref=din.at[peer[1]],
            dst_ref=out_ref.at[my_seq],
            send_sem=d_send.at[away - 1],
            recv_sem=d_recv.at[away - 1],
            device_id=peer,
            device_id_type=pl.DeviceIdType.MESH,
        )

    @pl.when(step == 0)
    def _():
        for away in range(seq - 2, seq):
            move(away).start()

    @pl.when(step == max(steps - 2, 0))
    def _():
        for chain in (1, 2):
            take(chain, 0)

    @pl.when(step == steps - 1)
    def _():
        move(1).start()
        own = pltpu.make_async_copy(din.at[my_seq], out_ref.at[my_seq], own_sem)
        own.start()
        blank = jnp.zeros((lanes - q_cols - 2 * kv_cols, width), F32)
        for s in range(seq):
            first = width + kv_cols * s
            piece = jnp.concatenate(
                [
                    w_sum[q_cols * s : q_cols * (s + 1), :],
                    w_sum[first : first + kv_cols, :],
                    w_sum[first + kv_width : first + kv_width + kv_cols, :],
                    blank,
                ],
                axis=0,
            ).T.astype(BF16)
            for d in range(dp):
                packed[away_place(orders[0], d, s, my_dp, my_seq)] = piece[rows * d : rows * (d + 1)]
        gain_row = jnp.sum(gain_sum[...].T, axis=0, keepdims=True)
        gain_held[0] = jnp.concatenate(
            [gain_row, other_gain_ref[...], jnp.zeros((6, width), F32)], axis=0
        )
        turns = len(orders[0])
        gain_copies = [
            pltpu.make_async_remote_copy(
                src_ref=gain_held.at[turn],
                dst_ref=gain_landed.at[turn],
                send_sem=g_send.at[turn],
                recv_sem=g_recv.at[turn],
                device_id=stage_peer(my_dp, my_seq, orders[0][turns - 1 - turn]),
                device_id_type=pl.DeviceIdType.MESH,
            )
            for turn in range(turns)
        ]
        halve(0, 0).start()
        gain_copies[0].start()
        for turn in range(turns):
            gain_copies[turn].wait_recv()
            gain_held[turn + 1] = gain_held[turn] + gain_landed[turn]
            if turn + 1 < turns:
                gain_copies[turn + 1].start()
            take(0, turn)
            if turn == turns - 3:
                for chain in (1, 2):
                    take(chain, 1)
                for away in range(seq // 2, seq - 2):
                    move(away).start()
            if turn == turns - 2:
                for chain in (1, 2):
                    take(chain, 2)
                for away in range(2, seq // 2):
                    move(away).start()
        gains_ref[...] = gain_held[turns]
        qkv_ref[...], one_ref[...], two_ref[...] = result(0), result(1), result(2)
        for copy in gain_copies:
            copy.wait_send()
        for chain in range(3):
            for turn in range(len(orders[chain])):
                halve(chain, turn).wait_send()
        for away in range(1, seq):
            move(away).wait()
        own.wait()


def finish(x, dmid, dlins, gain, w_t, other_gain, keep_one, keep_two, came_one, came_two):
    blocks, width, block = x.shape
    tokens = blocks * block
    feats = w_t.shape[0]
    kv_width = (feats - width) // 2
    lanes = keep_one.shape[2]
    dp, seq = lax.axis_size("dp"), lax.axis_size("seq")
    rows = width // dp
    stages = len(all_stages(dp, seq))

    def pair(i):
        return across(lax.axis_index("seq") // 2, seq // 2 - 1 - i, seq // 2)

    tok = pl.BlockSpec((2, width, block), lambda i: (pair(i), 0, 0))
    col = lambda rows: pl.BlockSpec((rows, 2 * block), lambda i: (0, pair(i)))
    once = lambda shape: pl.BlockSpec(shape, lambda i: (0,) * len(shape), pipeline_mode=pl.Buffered(1))
    hbm = pl.BlockSpec(memory_space=pl.ANY)
    small = [(8, width), (rows, lanes), keep_one.shape[1:], keep_two.shape[1:]]
    return pl.pallas_call(
        functools.partial(finish_kernel, dp=dp, seq=seq, kv_width=kv_width),
        grid=(blocks // 2,),
        in_specs=[
            tok, tok, *[col(d.shape[0]) for d in dlins],
            once((width, 1)), once((feats, width)), once((1, width)), hbm, hbm, hbm, hbm,
        ],
        out_specs=[hbm] + [once(shape) for shape in small],
        out_shape=[jax.ShapeDtypeStruct(x.shape, BF16)] + [jax.ShapeDtypeStruct(shape, F32) for shape in small],
        scratch_shapes=[
            pltpu.VMEM((width, feats), BF16),
            pltpu.VMEM((feats, width), F32),
            pltpu.VMEM((width, lanes), F32),
            pltpu.VMEM(x.shape, BF16),
            pltpu.VMEM((dp * seq, rows, lanes), BF16),
            pltpu.VMEM((dp * seq, rows, lanes), BF16),
            *[pltpu.VMEM(keep_one.shape, BF16)] * 3,
            *[pltpu.VMEM(keep_two.shape, BF16)] * 3,
            pltpu.VMEM((stages + 1, 8, width), F32),
            pltpu.VMEM((stages, 8, width), F32),
            pltpu.SemaphoreType.DMA,
            pltpu.SemaphoreType.DMA((seq - 1,)),
            pltpu.SemaphoreType.DMA((seq - 1,)),
            pltpu.SemaphoreType.DMA((3, stages)),
            pltpu.SemaphoreType.DMA((3, stages)),
            pltpu.SemaphoreType.DMA((stages,)),
            pltpu.SemaphoreType.DMA((stages,)),
            pltpu.SemaphoreType.DMA((4,)),
        ],
        compiler_params=pltpu.CompilerParams(
            collective_id=2, has_side_effects=True, vmem_limit_bytes=VMEM_BYTES
        ),
        cost_estimate=pl.CostEstimate(
            flops=4 * tokens * width * feats, bytes_accessed=tokens * width * 12, transcendentals=0
        ),
        name="finish",
    )(x, dmid, *dlins, gain, w_t, other_gain, keep_one, keep_two, came_one, came_two)


def deliver_kernel(
    din_ref, gains_ref, qkv_ref, one_ref, two_ref,
    out_ref, gain_one, gain_two, q_ref, k_ref, v_ref, o_ref, gate_ref, up_ref, down_ref,
):
    out_ref[...] = din_ref[...].astype(F32)

    @pl.when(pl.program_id(0) == 0)
    def _():
        rows, q_cols = q_ref.shape
        kv_cols, lanes = k_ref.shape[0], qkv_ref.shape[1]
        spare = gate_ref.shape[1] - lanes
        padded = -(-q_cols // 16) * 16
        gain_one[...] = gains_ref[0]
        gain_two[...] = gains_ref[1]
        qkv = qkv_ref[...]
        turned = qkv.T
        q_ref[...] = qkv[:, :q_cols]
        k_ref[...] = turned[q_cols : q_cols + kv_cols]
        v_ref[...] = turned[q_cols + kv_cols : q_cols + 2 * kv_cols]
        o_ref[...] = one_ref[:rows, :q_cols]
        both = two_ref[:rows]
        gate_ref[...] = jnp.concatenate([one_ref[rows : 2 * rows], both[:, :spare]], axis=1)
        up_ref[...] = jnp.concatenate([one_ref[2 * rows : 3 * rows], both[:, spare : 2 * spare]], axis=1)
        for t in range(down_ref.shape[1] // lanes):
            at = rows + padded * t
            down_ref[:, lanes * t : lanes * (t + 1)] = two_ref[at : at + q_cols]


def deliver(din, gains, qkv, one, two, kv_cols, ff):
    blocks, width, block = din.shape
    rows = qkv.shape[0]
    dp, seq = lax.axis_size("dp"), lax.axis_size("seq")
    tok = pl.BlockSpec((2, width, block), lambda i: (i, 0, 0))
    once = lambda shape: pl.BlockSpec(shape, lambda i: (0,) * len(shape), pipeline_mode=pl.Buffered(1))
    small = [
        (width,),
        (width,),
        (rows, width // seq),
        (kv_cols, rows),
        (kv_cols, rows),
        (rows, width // seq),
        (rows, ff // seq),
        (rows, ff // seq),
        (width // seq, ff // dp),
    ]
    return pl.pallas_call(
        deliver_kernel,
        grid=(blocks // 2,),
        in_specs=[tok] + [once(a.shape) for a in (gains, qkv, one, two)],
        out_specs=[tok] + [once(shape) for shape in small],
        out_shape=[jax.ShapeDtypeStruct(shape, F32) for shape in [din.shape] + small],
        compiler_params=pltpu.CompilerParams(vmem_limit_bytes=VMEM_BYTES),
        name="deliver",
    )(din, gains, qkv, one, two)


def exchange(blocks):
    return lax.all_to_all(blocks, "seq", 0, 0, tiled=True)


def pad_lanes(matrix, lanes):
    return jnp.pad(matrix, ((0, 0), (0, lanes - matrix.shape[1])))


def shards_sequences(
    hidden_in, span_order, attn_gain, q_weight, k_weight, v_weight, o_weight, mlp_gain,
    gate_weight, up_weight, down_weight, out_grad,
):
    lanes = 128
    seqs, slots, width = hidden_in.shape
    dp, seq = lax.axis_size("dp"), lax.axis_size("seq")
    tokens = slots * seq
    span = tokens // span_order.shape[0]
    heads = width // HD
    kv_heads = k_weight.shape[1] * seq // HD
    rows, q_cols = q_weight.shape
    kv_cols = k_weight.shape[1]
    ff = down_weight.shape[0] * dp
    ff_rows = down_weight.shape[0]
    padded = -(-q_cols // 16) * 16

    first = pad_lanes(jnp.concatenate([q_weight, k_weight, v_weight], axis=1), lanes)
    down_turned = jnp.pad(down_weight.T, ((0, padded - q_cols), (0, 0)))
    second = jnp.concatenate(
        [
            pad_lanes(o_weight, lanes),
            gate_weight[:, :lanes],
            up_weight[:, :lanes],
            jnp.concatenate([gate_weight[:, lanes:], up_weight[:, lanes:]], axis=1),
        ]
        + [down_turned[:, c : c + lanes] for c in range(0, ff_rows, lanes)],
        axis=0,
    )
    at = second.shape[0] * 5 // 8 // 16 * 16
    x, first_all, straight, hopping = bring(
        hidden_in.transpose(0, 2, 1), first[None], second[None, :at], second[None, at:]
    )
    out_grad, x = lax.optimization_barrier((out_grad, x))
    masks = [sum(row_bits(i, dp)) for i in range(dp)]
    straight_all = [straight] + [over_rows(straight, m) for m in masks[1:]]
    hopping_all = [hopping if m == 0 else over_rows(hopping, m) if m & (m - 1) == 0 else None for m in masks]
    dy = exchange(out_grad.transpose(0, 2, 1))

    my_dp, my_seq = lax.axis_index("dp"), lax.axis_index("seq")
    where_first = arrival_order(all_stages(dp, seq), dp, seq, my_dp, my_seq)
    where_second = arrival_order(seq_stages(seq), dp, seq, my_dp, my_seq)[:seq]
    inv = jnp.argsort(span_order).astype(jnp.int32)
    slot_pos = slot_positions(jnp.arange(tokens, dtype=jnp.int32), span_order, span)
    inv_freq = rope_base ** (-(jnp.arange(HD // 2, dtype=F32) * 2.0) / HD)
    angles = slot_pos.astype(F32)[None, :] * inv_freq[:, None]
    cos_t, sin_t = jnp.cos(angles), jnp.sin(angles)
    gain_one = attn_gain.astype(F32)[:, None]
    gain_two = mlp_gain.astype(F32)[:, None]

    q_t, k_t, v_t, k_nat, v_nat, w_t = project_qkv(
        where_first, x, gain_one, first_all, cos_t, sin_t, heads, kv_heads, rows
    )
    o_t, logs = attention_forward(inv, q_t, k_nat, v_t, span)
    hopping_all, o_t = lax.optimization_barrier((hopping_all, o_t))
    for i, mask in enumerate(masks):
        if hopping_all[i] is None:
            low = mask & -mask
            hopping_all[i] = over_rows(hopping_all[masks.index(mask - low)], low)
    packs = [part for pair in zip(straight_all, hopping_all) for part in pair]
    out, dmid, do_t, keep_one, give_one, keep_two, give_two, gain_two_term = mlp_both(
        where_second, x, o_t, dy, gain_two, packs, ff
    )
    came_one, came_two = over_rows(give_one, 1), over_rows(give_two, 1)
    hidden_out = exchange(out).transpose(0, 2, 1)

    def back(queries, *heads):
        return attention_backward(
            inv, queries, k_t, k_nat, v_nat, o_t, do_t, logs, cos_t, sin_t, span, *heads
        )

    parts = [back(q_t, 0, 1)]
    came_one, came_two, parts[0] = lax.optimization_barrier((came_one, came_two, parts[0]))
    half = dp * seq // 4
    add = lambda a, b: (a.astype(F32) + b.astype(F32)).astype(BF16)
    sums = [
        (add(keep[:half], came[:half]), add(keep[half:], came[half:]))
        for keep, came in ((keep_one, came_one), (keep_two, came_two))
    ]
    sums, q_t = lax.optimization_barrier((sums, q_t))
    crossed = [
        lax.ppermute(high, axis, [(i, i ^ bit) for i in range(lax.axis_size(axis))])
        for (_, high), (axis, bit) in zip(sums, [chain[-1] for chain in rest_chains(dp, seq)])
    ]
    parts.append(back(q_t, 1, kv_heads - 1))
    dlins = [part[i] for i in range(3) for part in parts]
    din, gains, qkv_sum, one_sum, two_sum = finish(
        x, dmid, dlins, gain_one, w_t, gain_two_term, sums[0][0], sums[1][0], *crossed
    )
    grad_in, gain_one_sum, gain_two_sum, q_sum, k_sum, v_sum, o_sum, gate_sum, up_sum, down_sum = deliver(
        din, gains, qkv_sum, one_sum, two_sum, kv_cols, ff
    )
    return (
        hidden_out,
        grad_in.transpose(0, 2, 1),
        gain_one_sum,
        q_sum,
        k_sum.T,
        v_sum.T,
        o_sum,
        gain_two_sum,
        gate_sum,
        up_sum,
        down_sum.T,
    )


def shards(*args):
    seqs, spans = args[0].shape[0], args[1].shape[0]
    if seqs == lax.axis_size("seq") and spans % 4 == 0:
        return shards_sequences(*args)
    return shards_general(*args)


def solution(mesh):
    placed = (
        P("dp", "seq", None),
        P(),
        P(),
        P("dp", "seq"),
        P("dp", "seq"),
        P("dp", "seq"),
        P("dp", "seq"),
        P(),
        P("dp", "seq"),
        P("dp", "seq"),
        P("dp", "seq"),
        P("dp", "seq", None),
    )
    return jax.shard_map(
        shards,
        mesh=mesh,
        in_specs=placed,
        out_specs=(
            P("dp", "seq", None),
            P("dp", "seq", None),
            P(),
            P("dp", "seq"),
            P("dp", "seq"),
            P("dp", "seq"),
            P("dp", "seq"),
            P(),
            P("dp", "seq"),
            P("dp", "seq"),
            P("dp", "seq"),
        ),
        check_vma=False,
    )
```

```python
import functools

import jax
import jax.numpy as jnp
import numpy as np
from jax import lax
from jax.experimental import pallas as pl
from jax.experimental.pallas import tpu as pltpu
from jax.sharding import PartitionSpec as P

HD = 64
MICRO = 2


eps_norm = 1e-05
rope_base = 100000.0
neg_big = -1e30


def slot_positions(slot_ids, span_order, span_len):
    span_ids = slot_ids // span_len
    span_hits = span_ids[:, None] == jnp.arange(span_order.shape[0], dtype=jnp.int32)[None, :]
    starts = jnp.sum(jnp.where(span_hits, span_order[None, :], 0), axis=1)
    return starts * span_len + slot_ids % span_len


def rope_tables(slot_pos):
    half_width = HD // 2
    inv_freq = rope_base ** (-(jnp.arange(half_width, dtype=jnp.float32) * 2.0) / HD)
    angles = slot_pos.astype(jnp.float32)[:, None] * inv_freq[None, :]
    cosine = jnp.concatenate([jnp.cos(angles), jnp.cos(angles)], axis=1)
    sine_tab = jnp.concatenate([jnp.sin(angles), jnp.sin(angles)], axis=1)
    return (cosine[:, None, :], sine_tab[:, None, :])


def rotate(vector, cosine, sine_tab):
    half_width = vector.shape[-1] // 2
    turned = jnp.concatenate([-vector[..., half_width:], vector[..., :half_width]], axis=-1)
    return vector * cosine + turned * sine_tab


def rotate_back(grad_out, cosine, sine_tab):
    half_width = grad_out.shape[-1] // 2
    scaled = grad_out * sine_tab
    turned = jnp.concatenate([scaled[..., half_width:], -scaled[..., :half_width]], axis=-1)
    return grad_out * cosine + turned


def norm_back(vector, rstd_vec, gain_vec, grad_n):
    scaled = grad_n * gain_vec
    gain_term = jnp.sum(grad_n * vector * rstd_vec, axis=0)
    grad_vec = rstd_vec * scaled - vector * rstd_vec**3 * jnp.mean(
        scaled * vector, axis=-1, keepdims=True
    )
    return (grad_vec, gain_term)


def add_tuples(old_sums, new_terms):
    if old_sums is None:
        return tuple(new_terms)
    return tuple((old_sum + new_term for old_sum, new_term in zip(old_sums, new_terms)))


def shards_general(
    hidden_in,
    span_order,
    attn_gain,
    q_weight,
    k_weight,
    v_weight,
    o_weight,
    mlp_gain,
    gate_weight,
    up_weight,
    down_weight,
    out_grad,
):
    local_seqs, row_count, model_width = hidden_in.shape
    seq_parts = lax.axis_size("seq")
    full_length = row_count * seq_parts
    span_len = full_length // (2 * seq_parts)
    per_micro = local_seqs // MICRO
    kv_width = k_weight.shape[1] * seq_parts
    kv_heads = kv_width // HD
    head_count = model_width // HD
    group_size = head_count // kv_heads
    tok_count = per_micro * row_count
    score_scale = HD ** (-0.5)
    own_slots = lax.axis_index("seq") * row_count + jnp.arange(row_count, dtype=jnp.int32)
    own_pos = slot_positions(own_slots, span_order, span_len)
    all_pos = slot_positions(jnp.arange(full_length, dtype=jnp.int32), span_order, span_len)
    allowed = own_pos[:, None] >= all_pos[None, :]
    cos_own, sin_own = rope_tables(own_pos)
    gain_attn = attn_gain.astype(jnp.float32)
    gain_mlp = mlp_gain.astype(jnp.float32)

    def attend(inputs):
        queries, key_rows, value_rows = inputs
        query_grp = queries.reshape(row_count, kv_heads, group_size, HD)
        key_grp = key_rows.reshape(full_length, kv_heads, HD)
        value_grp = value_rows.reshape(full_length, kv_heads, HD)
        scores = (
            jnp.einsum("rkgd,lkd->kgrl", query_grp, key_grp, preferred_element_type=jnp.float32)
            * score_scale
        )
        scores = jnp.where(allowed, scores, neg_big)
        row_peak = jnp.max(scores, axis=-1, keepdims=True)
        exp_scores = jnp.exp(scores - row_peak)
        row_total = jnp.sum(exp_scores, axis=-1, keepdims=True)
        attn_probs = exp_scores / row_total
        log_total = row_peak + jnp.log(row_total)
        mixed = jnp.einsum(
            "kgrl,lkd->rkgd",
            attn_probs.astype(jnp.bfloat16),
            value_grp,
            preferred_element_type=jnp.float32,
        )
        return (mixed.astype(jnp.bfloat16).reshape(row_count, model_width), log_total)

    def attend_back(inputs):
        queries, key_rows, value_rows, grad_mix, log_total = inputs
        query_grp = queries.reshape(row_count, kv_heads, group_size, HD)
        key_grp = key_rows.reshape(full_length, kv_heads, HD)
        value_grp = value_rows.reshape(full_length, kv_heads, HD)
        grad_grp = grad_mix.reshape(row_count, kv_heads, group_size, HD)
        scores = (
            jnp.einsum("rkgd,lkd->kgrl", query_grp, key_grp, preferred_element_type=jnp.float32)
            * score_scale
        )
        scores = jnp.where(allowed, scores, neg_big)
        attn_probs = jnp.exp(scores - log_total)
        probs_low = attn_probs.astype(jnp.bfloat16)
        grad_probs = jnp.einsum(
            "rkgd,lkd->kgrl", grad_grp, value_grp, preferred_element_type=jnp.float32
        )
        row_delta = jnp.sum(attn_probs * grad_probs, axis=-1, keepdims=True)
        grad_scores = (attn_probs * (grad_probs - row_delta)).astype(jnp.bfloat16)
        grad_query_rot = (
            jnp.einsum("kgrl,lkd->rkgd", grad_scores, key_grp, preferred_element_type=jnp.float32)
            * score_scale
        )
        key_term = (
            jnp.einsum("kgrl,rkgd->lkd", grad_scores, query_grp, preferred_element_type=jnp.float32)
            * score_scale
        )
        value_term = jnp.einsum(
            "kgrl,rkgd->lkd", probs_low, grad_grp, preferred_element_type=jnp.float32
        )
        return (
            grad_query_rot.reshape(row_count, head_count, HD),
            key_term.reshape(full_length, kv_width),
            value_term.reshape(full_length, kv_width),
        )

    outputs = []
    in_grads = []
    totals = None
    for micro_idx in range(MICRO):
        first_seq = micro_idx * per_micro
        block_in = hidden_in[first_seq : first_seq + per_micro]
        block_grad = out_grad[first_seq : first_seq + per_micro]
        col_parts = (
            lax.all_gather(q_weight, "seq", axis=1, tiled=True),
            lax.all_gather(k_weight, "seq", axis=1, tiled=True),
            lax.all_gather(v_weight, "seq", axis=1, tiled=True),
            lax.all_gather(o_weight, "seq", axis=1, tiled=True),
            lax.all_gather(gate_weight, "seq", axis=1, tiled=True),
            lax.all_gather(up_weight, "seq", axis=1, tiled=True),
            lax.all_gather(down_weight, "seq", axis=1, tiled=True),
        )
        query_mat, key_mat, value_mat, out_mat, gate_mat, up_mat, down_mat = (
            lax.all_gather(col_parts[0], "dp", axis=0, tiled=True),
            lax.all_gather(col_parts[1], "dp", axis=0, tiled=True),
            lax.all_gather(col_parts[2], "dp", axis=0, tiled=True),
            lax.all_gather(col_parts[3], "dp", axis=0, tiled=True),
            lax.all_gather(col_parts[4], "dp", axis=0, tiled=True),
            lax.all_gather(col_parts[5], "dp", axis=0, tiled=True),
            lax.all_gather(col_parts[6], "dp", axis=0, tiled=True),
        )
        resid_in = block_in.astype(jnp.float32).reshape(tok_count, model_width)
        rstd_one = lax.rsqrt(jnp.mean(resid_in * resid_in, axis=-1, keepdims=True) + eps_norm)
        normed_one = (resid_in * rstd_one * gain_attn).astype(jnp.bfloat16)
        query_lin = jnp.dot(normed_one, query_mat, preferred_element_type=jnp.float32)
        key_lin = jnp.dot(normed_one, key_mat, preferred_element_type=jnp.float32)
        value_lin = jnp.dot(normed_one, value_mat, preferred_element_type=jnp.float32)
        query_rot = rotate(
            query_lin.reshape(per_micro, row_count, head_count, HD), cos_own, sin_own
        ).astype(jnp.bfloat16)
        key_rot = (
            rotate(key_lin.reshape(per_micro, row_count, kv_heads, HD), cos_own, sin_own)
            .astype(jnp.bfloat16)
            .reshape(per_micro, row_count, kv_width)
        )
        value_low = value_lin.astype(jnp.bfloat16).reshape(per_micro, row_count, kv_width)
        key_all, value_all = (
            lax.all_gather(key_rot, "seq", axis=1, tiled=True),
            lax.all_gather(value_low, "seq", axis=1, tiled=True),
        )
        mixed_seq, log_total = lax.map(attend, (query_rot, key_all, value_all))
        mixed_low = mixed_seq.reshape(tok_count, model_width)
        hidden_mid = resid_in + jnp.dot(mixed_low, out_mat, preferred_element_type=jnp.float32)
        rstd_two = lax.rsqrt(jnp.mean(hidden_mid * hidden_mid, axis=-1, keepdims=True) + eps_norm)
        normed_two = (hidden_mid * rstd_two * gain_mlp).astype(jnp.bfloat16)
        gate_lin = jnp.dot(normed_two, gate_mat, preferred_element_type=jnp.float32)
        up_lin = jnp.dot(normed_two, up_mat, preferred_element_type=jnp.float32)
        gate_sig = jax.nn.sigmoid(gate_lin)
        inner_low = (gate_lin * gate_sig * up_lin).astype(jnp.bfloat16)
        mlp_out = jnp.dot(inner_low, down_mat, preferred_element_type=jnp.float32)
        outputs.append(
            (hidden_mid + mlp_out).astype(jnp.bfloat16).reshape(per_micro, row_count, model_width)
        )
        col_again = (
            lax.all_gather(q_weight, "seq", axis=1, tiled=True),
            lax.all_gather(k_weight, "seq", axis=1, tiled=True),
            lax.all_gather(v_weight, "seq", axis=1, tiled=True),
            lax.all_gather(o_weight, "seq", axis=1, tiled=True),
            lax.all_gather(gate_weight, "seq", axis=1, tiled=True),
            lax.all_gather(up_weight, "seq", axis=1, tiled=True),
            lax.all_gather(down_weight, "seq", axis=1, tiled=True),
        )
        query_mat, key_mat, value_mat, out_mat, gate_mat, up_mat, down_mat = (
            lax.all_gather(col_again[0], "dp", axis=0, tiled=True),
            lax.all_gather(col_again[1], "dp", axis=0, tiled=True),
            lax.all_gather(col_again[2], "dp", axis=0, tiled=True),
            lax.all_gather(col_again[3], "dp", axis=0, tiled=True),
            lax.all_gather(col_again[4], "dp", axis=0, tiled=True),
            lax.all_gather(col_again[5], "dp", axis=0, tiled=True),
            lax.all_gather(col_again[6], "dp", axis=0, tiled=True),
        )
        key_all, value_all = (
            lax.all_gather(key_rot, "seq", axis=1, tiled=True),
            lax.all_gather(value_low, "seq", axis=1, tiled=True),
        )
        grad_top = block_grad.astype(jnp.float32).reshape(tok_count, model_width)
        grad_top_low = grad_top.astype(jnp.bfloat16)
        down_term = jnp.einsum(
            "tf,td->fd", inner_low, grad_top_low, preferred_element_type=jnp.float32
        )
        grad_inner = jnp.einsum(
            "td,fd->tf", grad_top_low, down_mat, preferred_element_type=jnp.float32
        )
        grad_gate = (grad_inner * up_lin * gate_sig * (1.0 + gate_lin * (1.0 - gate_sig))).astype(
            jnp.bfloat16
        )
        grad_up = (grad_inner * gate_lin * gate_sig).astype(jnp.bfloat16)
        gate_term = jnp.einsum(
            "td,tf->df", normed_two, grad_gate, preferred_element_type=jnp.float32
        )
        up_term = jnp.einsum("td,tf->df", normed_two, grad_up, preferred_element_type=jnp.float32)
        grad_normed_two = jnp.einsum(
            "tf,df->td", grad_gate, gate_mat, preferred_element_type=jnp.float32
        ) + jnp.einsum("tf,df->td", grad_up, up_mat, preferred_element_type=jnp.float32)
        grad_mid_norm, gain_mlp_term = norm_back(hidden_mid, rstd_two, gain_mlp, grad_normed_two)
        grad_mid = grad_top + grad_mid_norm
        grad_mid_low = grad_mid.astype(jnp.bfloat16)
        out_term = jnp.einsum(
            "td,te->de", mixed_low, grad_mid_low, preferred_element_type=jnp.float32
        )
        grad_mixed = jnp.einsum(
            "te,de->td", grad_mid_low, out_mat, preferred_element_type=jnp.float32
        ).astype(jnp.bfloat16)
        grad_query_rot, key_terms, value_terms = lax.map(
            attend_back,
            (
                query_rot,
                key_all,
                value_all,
                grad_mixed.reshape(per_micro, row_count, model_width),
                log_total,
            ),
        )
        key_share, value_share = (
            lax.psum_scatter(key_terms, "seq", scatter_dimension=1, tiled=True),
            lax.psum_scatter(value_terms, "seq", scatter_dimension=1, tiled=True),
        )
        grad_query = (
            rotate_back(grad_query_rot, cos_own, sin_own)
            .astype(jnp.bfloat16)
            .reshape(tok_count, model_width)
        )
        grad_key = (
            rotate_back(key_share.reshape(per_micro, row_count, kv_heads, HD), cos_own, sin_own)
            .astype(jnp.bfloat16)
            .reshape(tok_count, kv_width)
        )
        grad_value = value_share.astype(jnp.bfloat16).reshape(tok_count, kv_width)
        query_term = jnp.einsum(
            "td,te->de", normed_one, grad_query, preferred_element_type=jnp.float32
        )
        key_term = jnp.einsum("td,te->de", normed_one, grad_key, preferred_element_type=jnp.float32)
        value_term = jnp.einsum(
            "td,te->de", normed_one, grad_value, preferred_element_type=jnp.float32
        )
        grad_normed_one = (
            jnp.einsum("te,de->td", grad_query, query_mat, preferred_element_type=jnp.float32)
            + jnp.einsum("te,de->td", grad_key, key_mat, preferred_element_type=jnp.float32)
            + jnp.einsum("te,de->td", grad_value, value_mat, preferred_element_type=jnp.float32)
        )
        grad_in_norm, gain_attn_term = norm_back(resid_in, rstd_one, gain_attn, grad_normed_one)
        in_grads.append((grad_mid + grad_in_norm).reshape(per_micro, row_count, model_width))
        totals = add_tuples(
            totals,
            (
                query_term,
                key_term,
                value_term,
                out_term,
                gate_term,
                up_term,
                down_term,
                gain_attn_term,
                gain_mlp_term,
            ),
        )
    col_sums = (
        lax.psum_scatter(
            totals[0].astype(jnp.bfloat16), "seq", scatter_dimension=1, tiled=True
        ).astype(jnp.float32),
        lax.psum_scatter(
            totals[1].astype(jnp.bfloat16), "seq", scatter_dimension=1, tiled=True
        ).astype(jnp.float32),
        lax.psum_scatter(
            totals[2].astype(jnp.bfloat16), "seq", scatter_dimension=1, tiled=True
        ).astype(jnp.float32),
        lax.psum_scatter(
            totals[3].astype(jnp.bfloat16), "seq", scatter_dimension=1, tiled=True
        ).astype(jnp.float32),
        lax.psum_scatter(
            totals[4].astype(jnp.bfloat16), "seq", scatter_dimension=1, tiled=True
        ).astype(jnp.float32),
        lax.psum_scatter(
            totals[5].astype(jnp.bfloat16), "seq", scatter_dimension=1, tiled=True
        ).astype(jnp.float32),
        lax.psum_scatter(
            totals[6].astype(jnp.bfloat16), "seq", scatter_dimension=1, tiled=True
        ).astype(jnp.float32),
    )
    owned = (
        lax.psum_scatter(
            col_sums[0].astype(jnp.bfloat16), "dp", scatter_dimension=0, tiled=True
        ).astype(jnp.float32),
        lax.psum_scatter(
            col_sums[1].astype(jnp.bfloat16), "dp", scatter_dimension=0, tiled=True
        ).astype(jnp.float32),
        lax.psum_scatter(
            col_sums[2].astype(jnp.bfloat16), "dp", scatter_dimension=0, tiled=True
        ).astype(jnp.float32),
        lax.psum_scatter(
            col_sums[3].astype(jnp.bfloat16), "dp", scatter_dimension=0, tiled=True
        ).astype(jnp.float32),
        lax.psum_scatter(
            col_sums[4].astype(jnp.bfloat16), "dp", scatter_dimension=0, tiled=True
        ).astype(jnp.float32),
        lax.psum_scatter(
            col_sums[5].astype(jnp.bfloat16), "dp", scatter_dimension=0, tiled=True
        ).astype(jnp.float32),
        lax.psum_scatter(
            col_sums[6].astype(jnp.bfloat16), "dp", scatter_dimension=0, tiled=True
        ).astype(jnp.float32),
    )
    gain_sums = lax.psum((totals[7], totals[8]), ("dp", "seq"))
    return (
        jnp.concatenate(outputs, axis=0),
        jnp.concatenate(in_grads, axis=0),
        gain_sums[0],
        owned[0],
        owned[1],
        owned[2],
        owned[3],
        gain_sums[1],
        owned[4],
        owned[5],
        owned[6],
    )


F32 = jnp.float32
BF16 = jnp.bfloat16
VMEM_BYTES = 56 * 2**20


def dot(left, right, left_dim, right_dim):
    dims = (((left_dim,), (right_dim,)), ((), ()))
    return lax.dot_general(left, right, dims, preferred_element_type=F32)


def span_slice(inv_ref, place, span):
    return pl.ds(pl.multiple_of(inv_ref[place] * span, span), span)


def lane_pair(ref, rows, inv_ref, block, span):
    first = ref[rows, span_slice(inv_ref, 2 * block, span)]
    second = ref[rows, span_slice(inv_ref, 2 * block + 1, span)]
    return jnp.concatenate([first, second], axis=1)


def row_pair(ref, head, inv_ref, block, span):
    first = ref[head, span_slice(inv_ref, 2 * block, span), :]
    second = ref[head, span_slice(inv_ref, 2 * block + 1, span), :]
    return jnp.concatenate([first, second], axis=0)


def attend_kernel(inv_ref, q_ref, k_ref, v_ref, o_ref, l_ref, acc_ref, *, blocks, span, group):
    wide = 2 * span
    row = lax.broadcasted_iota(jnp.int32, (wide, wide), 0)
    col = lax.broadcasted_iota(jnp.int32, (wide, wide), 1)
    keep = row <= col

    def one_block(block, odd):
        queries = [
            lane_pair(q_ref, slice(HD * h, HD * h + HD), inv_ref, block, span) for h in range(group)
        ]
        acc_ref[...] = jnp.zeros_like(acc_ref)

        def step(first, count, state, diagonal):
            state = list(state)
            keys = [row_pair(k_ref, 0, inv_ref, first + u, span) for u in range(count)]
            values = [lane_pair(v_ref, slice(0, HD), inv_ref, first + u, span) for u in range(count)]
            items = [(u, h) for u in range(count) for h in range(group)]
            scores = [dot(keys[u], queries[h], 1, 0) for u, h in items]
            probs = []
            for (u, h), score in zip(items, scores):
                peak, total = state[h]
                if diagonal and u == count - 1:
                    score = jnp.where(keep, score, neg_big)
                new_peak = jnp.maximum(peak, jnp.max(score, axis=0, keepdims=True))
                prob = jnp.exp(score - new_peak)
                shrink = jnp.exp(peak - new_peak)
                state[h] = (new_peak, total * shrink + jnp.sum(prob, axis=0, keepdims=True))
                probs.append((prob.astype(BF16), shrink))
            for (u, h), (prob, shrink) in zip(items, probs):
                cols = slice(h * wide, (h + 1) * wide)
                acc_ref[:, cols] = acc_ref[:, cols] * shrink + dot(values[u], prob, 1, 0)
            return tuple(state)

        state = tuple(
            (jnp.full((1, wide), neg_big, F32), jnp.zeros((1, wide), F32)) for _ in range(group)
        )
        state = lax.fori_loop(0, block // 4, lambda j, s: step(4 * j, 4, s, False), state)
        state = lax.fori_loop(
            2 * (block // 4), block // 2, lambda j, s: step(2 * j, 2, s, False), state
        )
        state = step(block - 1, 2, state, True) if odd else step(block, 1, state, True)
        mixed = jnp.concatenate(
            [acc_ref[:, wide * h : wide * (h + 1)] * (1.0 / state[h][1]) for h in range(group)], axis=0
        ).astype(BF16)
        logs = jnp.concatenate(
            [p + jnp.log(t) for p, t in state] + [jnp.zeros((8 - group, wide), F32)], axis=0
        )
        for part in range(2):
            where = span_slice(inv_ref, 2 * block + part, span)
            cols = slice(part * span, part * span + span)
            o_ref[:, where] = mixed[:, cols]
            l_ref[0, :, where] = logs[:, cols]

    def two_blocks(pair, _):
        for odd in (0, 1):
            one_block(2 * pair + odd, odd)
        return 0

    lax.fori_loop(0, blocks // 2, two_blocks, 0)


def attention_forward(inv, q_t, k_nat, v_t, span):
    tokens = q_t.shape[1]
    kv_heads = k_nat.shape[0]
    group = q_t.shape[0] // (kv_heads * HD)
    pairs = kv_heads * group * tokens * tokens
    wide_spec = pl.BlockSpec((group * HD, tokens), lambda g, i: (g, 0))
    nat_spec = pl.BlockSpec((1, tokens, HD), lambda g, i: (g, 0, 0))
    return pl.pallas_call(
        functools.partial(attend_kernel, blocks=tokens // (2 * span), span=span, group=group),
        grid_spec=pltpu.PrefetchScalarGridSpec(
            num_scalar_prefetch=1,
            grid=(kv_heads,),
            in_specs=[wide_spec, nat_spec, pl.BlockSpec((HD, tokens), lambda g, i: (g, 0))],
            out_specs=[
                wide_spec,
                pl.BlockSpec((1, 8, tokens), lambda g, i: (g, 0, 0)),
            ],
            scratch_shapes=[pltpu.VMEM((HD, group * 2 * span), F32)],
        ),
        out_shape=[
            jax.ShapeDtypeStruct(q_t.shape, BF16),
            jax.ShapeDtypeStruct((kv_heads, 8, tokens), F32),
        ],
        compiler_params=pltpu.CompilerParams(vmem_limit_bytes=VMEM_BYTES),
        cost_estimate=pl.CostEstimate(
            flops=16 * pairs * HD, bytes_accessed=tokens * 6000, transcendentals=pairs // 2
        ),
        name="attention_forward",
    )(inv, q_t, k_nat, v_t)


def attend_back_kernel(
    inv_ref, q_ref, kt_ref, k_ref, v_ref, o_ref, do_ref, l_ref, cos_ref, sin_ref,
    dq_ref, dk_ref, dv_ref, dk_sum, dv_sum, dq_sum, *, blocks, span, group,
):
    wide = 2 * span
    row = lax.broadcasted_iota(jnp.int32, (wide, wide), 0)
    col = lax.broadcasted_iota(jnp.int32, (wide, wide), 1)
    keep = row <= col
    half = HD // 2
    dk_sum[...] = jnp.zeros_like(dk_sum)
    dv_sum[...] = jnp.zeros_like(dv_sum)

    def rope_back(grad, cos, sin):
        top, low = grad[:half], grad[half:]
        return jnp.concatenate([top * cos + low * sin, low * cos - top * sin], axis=0)

    def one_block(block, odd):
        rows = [slice(HD * h, HD * h + HD) for h in range(group)]
        queries = [lane_pair(q_ref, r, inv_ref, block, span) for r in rows]
        grads = [lane_pair(do_ref, r, inv_ref, block, span) for r in rows]
        logs = lane_pair(l_ref.at[0], slice(None), inv_ref, block, span)
        deltas = [
            jnp.sum(
                lane_pair(o_ref, r, inv_ref, block, span).astype(F32) * grad.astype(F32),
                axis=0,
                keepdims=True,
            )
            for r, grad in zip(rows, grads)
        ]
        dq_sum[...] = jnp.zeros_like(dq_sum)

        def step(first, count, diagonal):
            keys = [row_pair(k_ref, 0, inv_ref, first + u, span) for u in range(count)]
            values = [row_pair(v_ref, 0, inv_ref, first + u, span) for u in range(count)]
            keys_t = [lane_pair(kt_ref, slice(0, HD), inv_ref, first + u, span) for u in range(count)]
            items = [(u, h) for u in range(count) for h in range(group)]
            ahead, ready, dqs, sums = {}, {}, {}, {}

            def products(i):
                u, h = items[i]
                ahead[i] = dot(keys[u], queries[h], 1, 0), dot(values[u], grads[h], 1, 0)

            def softmax_part(i):
                u, h = items[i]
                score, dprob = ahead.pop(i)
                prob = jnp.exp(score - logs[h : h + 1])
                if diagonal and u == count - 1:
                    prob = jnp.where(keep, prob, 0.0)
                ready[i] = prob.astype(BF16), (prob * (dprob - deltas[h])).astype(BF16)

            def gradients(i):
                u, h = items[i]
                prob, dscore = ready.pop(i)
                dq = dot(keys_t[u], dscore, 1, 0)
                dqs[h] = dqs[h] + dq if h in dqs else dq
                if u == count - 1:
                    dq_sum[:, wide * h : wide * (h + 1)] += dqs[h]
                dk, dv = dot(queries[h], dscore, 1, 1), dot(grads[h], prob, 1, 1)
                if u in sums:
                    dk, dv = dk + sums[u][0], dv + sums[u][1]
                sums[u] = dk, dv
                if h == group - 1:
                    place = pl.ds(pl.multiple_of((first + u) * wide, wide), wide)
                    dk_sum[:, place] += dk
                    dv_sum[:, place] += dv

            lead = 2
            for i in range(min(lead, len(items))):
                products(i)
            for i in range(len(items) + 1):
                if i + lead < len(items):
                    products(i + lead)
                if i > 0:
                    gradients(i - 1)
                if i < len(items):
                    softmax_part(i)

        def pair_step(j, _):
            step(2 * j, 2, False)
            return 0

        lax.fori_loop(0, block // 2, pair_step, 0)
        if odd:
            step(block - 1, 2, True)
        else:
            step(block, 1, True)
        cos = lane_pair(cos_ref, slice(None), inv_ref, block, span)
        sin = lane_pair(sin_ref, slice(None), inv_ref, block, span)
        dq = jnp.concatenate(
            [rope_back(dq_sum[:, wide * h : wide * (h + 1)] * HD**-0.5, cos, sin) for h in range(group)],
            axis=0,
        ).astype(BF16)
        place = pl.ds(pl.multiple_of(block * wide, wide), wide)
        dk = rope_back(dk_sum[:, place], cos, sin).astype(BF16)
        dv = dv_sum[:, place].astype(BF16)
        for part in range(2):
            where = span_slice(inv_ref, 2 * block + part, span)
            cols = slice(part * span, part * span + span)
            dq_ref[:, where] = dq[:, cols]
            dk_ref[:, where] = dk[:, cols]
            dv_ref[:, where] = dv[:, cols]

    def two_blocks(step, _):
        for odd in (1, 0):
            one_block(blocks - 2 - 2 * step + odd, odd)
        return 0

    lax.fori_loop(0, blocks // 2, two_blocks, 0)


def attention_backward(inv, q_t, k_t, k_nat, v_nat, o_t, do_t, logs, cos_t, sin_t, span, first, count):
    tokens = q_t.shape[1]
    kv_heads = k_nat.shape[0]
    group = q_t.shape[0] // (kv_heads * HD)
    pairs = count * group * tokens * tokens
    wide_spec = pl.BlockSpec((group * HD, tokens), lambda g, i: (g + first, 0))
    kv_spec = pl.BlockSpec((HD, tokens), lambda g, i: (g + first, 0))
    nat_spec = pl.BlockSpec((1, tokens, HD), lambda g, i: (g + first, 0, 0))
    tab_spec = pl.BlockSpec((HD // 2, tokens), lambda g, i: (0, 0))
    return pl.pallas_call(
        functools.partial(attend_back_kernel, blocks=tokens // (2 * span), span=span, group=group),
        grid_spec=pltpu.PrefetchScalarGridSpec(
            num_scalar_prefetch=1,
            grid=(count,),
            in_specs=[
                wide_spec, kv_spec, nat_spec, nat_spec, wide_spec, wide_spec,
                pl.BlockSpec((1, 8, tokens), lambda g, i: (g + first, 0, 0)), tab_spec, tab_spec,
            ],
            out_specs=[
                pl.BlockSpec((group * HD, tokens), lambda g, i: (g, 0)),
                pl.BlockSpec((HD, tokens), lambda g, i: (g, 0)),
                pl.BlockSpec((HD, tokens), lambda g, i: (g, 0)),
            ],
            scratch_shapes=[
                pltpu.VMEM((HD, tokens), F32),
                pltpu.VMEM((HD, tokens), F32),
                pltpu.VMEM((HD, group * 2 * span), F32),
            ],
        ),
        out_shape=[
            jax.ShapeDtypeStruct((count * group * HD, tokens), BF16),
            jax.ShapeDtypeStruct((count * HD, tokens), BF16),
            jax.ShapeDtypeStruct((count * HD, tokens), BF16),
        ],
        compiler_params=pltpu.CompilerParams(vmem_limit_bytes=VMEM_BYTES),
        cost_estimate=pl.CostEstimate(
            flops=32 * pairs * HD, bytes_accessed=tokens * 9000, transcendentals=pairs // 2
        ),
        name="attention_backward",
    )(inv, q_t, k_t, k_nat, v_nat, o_t, do_t, logs, cos_t, sin_t)


def flip(index, bits):
    for bit in bits:
        index = index + bit * (1 - 2 * ((index // bit) % 2))
    return index


def bits_of(size):
    return [1 << i for i in range(size.bit_length() - 1)]


def seq_stages(seq):
    return [("seq", b) for b in reversed(bits_of(seq)[1:])] + [("seq", b) for b in bits_of(seq)[:1]]


def all_stages(dp, seq):
    return seq_stages(seq) + [("dp", b) for b in reversed(bits_of(dp))]


def rest_chains(dp, seq):
    near, far = [("seq", b) for b in bits_of(seq)[:1]], [("seq", b) for b in reversed(bits_of(seq)[1:])]
    chip = [("dp", b) for b in reversed(bits_of(dp)[1:])]
    return far + near + chip, far + chip + near


def away_place(stages, d, s, my_dp, my_seq):
    place = 0
    for at, (axis, bit) in enumerate(stages):
        mine = ((my_dp if axis == "dp" else my_seq) // bit) % 2
        theirs = ((d if axis == "dp" else s) // bit) % 2
        place = place + (1 << at) * (1 - mine if theirs else mine)
    return place


def arrival_order(stages, dp, seq, my_dp, my_seq):
    ids = jnp.arange(dp * seq, dtype=jnp.int32)
    away = {"dp": (ids // seq) ^ my_dp, "seq": (ids % seq) ^ my_seq}
    place = jnp.zeros_like(ids)
    for at, (axis, bit) in enumerate(stages):
        place = place + (1 << at) * ((away[axis] // bit) % 2)
    return place


def greet(peers):
    barrier = pltpu.get_barrier_semaphore()
    for peer in peers:
        pl.semaphore_signal(barrier, inc=1, device_id=peer, device_id_type=pl.DeviceIdType.MESH)
    pl.semaphore_wait(barrier, len(peers))


def seq_peer(my_dp, my_seq, away, seq):
    return my_dp, flip(my_seq, [b for b in bits_of(seq) if away & b])


def stage_peer(my_dp, my_seq, stage):
    axis, bit = stage
    return (flip(my_dp, [bit]), my_seq) if axis == "dp" else (my_dp, flip(my_seq, [bit]))


def all_peers(my_dp, my_seq, dp, seq):
    peers = [seq_peer(my_dp, my_seq, away, seq) for away in range(1, seq)]
    return peers + [(flip(my_dp, [b]), my_seq) for b in bits_of(dp)]


def bring_kernel(order_ref, freq_ref, gain_one, gain_two, q_ref, k_ref, v_ref, o_ref, gate_ref, up_ref,
                 down_ref, x_ref, inv_ref, cos_ref, sin_ref, one_ref, two_ref, out_ref,
                 all_first, all_second, all_third, first_ref, rest_ref, local_sem, x_send, x_recv, w_send, w_recv, *, dp, seq):
    my_dp, my_seq = lax.axis_index("dp"), lax.axis_index("seq")
    orders = all_stages(dp, seq), seq_stages(seq), seq_stages(seq)
    chains = range(len(orders))
    rows, q_cols = q_ref.shape
    lanes = rest_ref.shape[2]
    kv_cols = k_ref.shape[0]
    blank = lambda cols: jnp.zeros((rows, cols), F32)
    wide = lambda ref: ref[...].astype(F32)
    first_ref[0] = jnp.concatenate(
        [wide(q_ref), wide(k_ref).T, wide(v_ref).T, blank(lanes - q_cols - 2 * kv_cols)], axis=1
    ).astype(BF16)
    rest_ref[0, :rows] = jnp.concatenate([wide(o_ref), blank(lanes - q_cols)], axis=1).astype(BF16)
    rest_ref[0, rows : 2 * rows] = gate_ref[:, :lanes]
    rest_ref[0, 2 * rows : 3 * rows] = up_ref[:, :lanes]
    rest_ref[0, 3 * rows : 4 * rows] = jnp.concatenate([gate_ref[:, lanes:], up_ref[:, lanes:]], axis=1)
    padded = -(-q_cols // 16) * 16
    for t in range(down_ref.shape[1] // lanes):
        piece = down_ref[:, t * lanes : (t + 1) * lanes].astype(F32)
        piece = jnp.concatenate([piece, jnp.zeros((padded - q_cols, lanes), F32)], axis=0).astype(BF16)
        rest_ref[0, 4 * rows + padded * t : 4 * rows + padded * (t + 1)] = piece

    greet(all_peers(my_dp, my_seq, dp, seq))
    at = all_second.shape[1]
    shards_in = first_ref, rest_ref.at[:, pl.ds(0, at)], rest_ref.at[:, pl.ds(at, all_third.shape[1])]
    gathered = all_first, all_second, all_third

    def weight_copy(chain, stage):
        held = 1 << stage
        source = shards_in[chain] if stage == 0 else gathered[chain].at[pl.ds(0, held)]
        return pltpu.make_async_remote_copy(
            src_ref=source,
            dst_ref=gathered[chain].at[pl.ds(held, held)],
            send_sem=w_send.at[chain, stage],
            recv_sem=w_recv.at[chain, stage],
            device_id=stage_peer(my_dp, my_seq, orders[chain][stage]),
            device_id_type=pl.DeviceIdType.MESH,
        )

    copies = [[weight_copy(c, s) for s in range(len(orders[c]))] for c in chains]
    for c in chains:
        copies[c][0].start()
    own = [
        pltpu.make_async_copy(shards_in[c], gathered[c].at[pl.ds(0, 1)], local_sem.at[c]) for c in chains
    ]
    own.append(pltpu.make_async_copy(x_ref.at[my_seq], out_ref.at[my_seq], local_sem.at[len(orders)]))
    for copy in own:
        copy.start()
    moves = []
    for away in range(1, seq):
        peer = seq_peer(my_dp, my_seq, away, seq)
        moves.append(
            pltpu.make_async_remote_copy(
                src_ref=x_ref.at[peer[1]],
                dst_ref=out_ref.at[my_seq],
                send_sem=x_send.at[away - 1],
                recv_sem=x_recv.at[away - 1],
                device_id=peer,
                device_id_type=pl.DeviceIdType.MESH,
            )
        )
    for c in chains:
        own[c].wait()
    for stage in range(1, len(orders[0])):
        for c in chains:
            if stage < len(orders[c]):
                copies[c][stage - 1].wait_recv()
                copies[c][stage].start()
        if stage == 1:
            for move in moves:
                move.start()
            spans = order_ref.shape[0]
            span = cos_ref.shape[1] // spans
            inside = lax.broadcasted_iota(jnp.int32, (1, span), 1)
            for slot in range(spans):
                angles = (inside + order_ref[slot] * span).astype(F32) * freq_ref[...]
                cos_ref[:, slot * span : (slot + 1) * span] = jnp.cos(angles)
                sin_ref[:, slot * span : (slot + 1) * span] = jnp.sin(angles)
                found = 0
                for other in range(spans):
                    found = found + jnp.where(order_ref[other] == slot, other, 0)
                inv_ref[slot] = found
            for source, target in ((gain_one, one_ref), (gain_two, two_ref)):
                row = source[...].astype(F32)[None]
                target[...] = jnp.broadcast_to(row, (8, row.shape[1])).T[:, :1]
    for c in chains:
        copies[c][-1].wait_recv()
        for copy in copies[c]:
            copy.wait_send()
    for move in moves:
        move.wait()
    own[-1].wait()


def bring(span_order, inv_freq, gains, weights, x):
    dp, seq = lax.axis_size("dp"), lax.axis_size("seq")
    stages = len(all_stages(dp, seq))
    lanes = 128
    width = x.shape[1]
    rows, q_cols = weights[0].shape
    rest_rows = 4 * rows + -(-q_cols // 16) * 16 * (weights[-1].shape[1] // lanes)
    cut = rest_rows * 5 // 8 // 16 * 16
    hbm = pl.BlockSpec(memory_space=pl.ANY)
    smem = pl.BlockSpec(memory_space=pltpu.SMEM)
    vmem = pl.BlockSpec(memory_space=pltpu.VMEM)
    table = jax.ShapeDtypeStruct((inv_freq.shape[0], x.shape[0] * x.shape[2]), F32)
    return pl.pallas_call(
        functools.partial(bring_kernel, dp=dp, seq=seq),
        in_specs=[smem] + [vmem] * (3 + len(weights)) + [hbm],
        out_specs=[smem] + [vmem] * 4 + [hbm] * 4,
        out_shape=[
            jax.ShapeDtypeStruct(span_order.shape, jnp.int32),
            table,
            table,
            jax.ShapeDtypeStruct((width, 1), F32),
            jax.ShapeDtypeStruct((width, 1), F32),
            jax.ShapeDtypeStruct(x.shape, x.dtype),
            jax.ShapeDtypeStruct((dp * seq, rows, lanes), x.dtype),
            jax.ShapeDtypeStruct((seq, cut, lanes), x.dtype),
            jax.ShapeDtypeStruct((seq, rest_rows - cut, lanes), x.dtype),
        ],
        scratch_shapes=[
            pltpu.VMEM((1, rows, lanes), BF16),
            pltpu.VMEM((1, rest_rows, lanes), BF16),
            pltpu.SemaphoreType.DMA((4,)),
            pltpu.SemaphoreType.DMA((seq - 1,)),
            pltpu.SemaphoreType.DMA((seq - 1,)),
            pltpu.SemaphoreType.DMA((3, stages)),
            pltpu.SemaphoreType.DMA((3, stages)),
        ],
        compiler_params=pltpu.CompilerParams(
            collective_id=1, has_side_effects=True, vmem_limit_bytes=VMEM_BYTES
        ),
        name="bring",
    )(span_order, inv_freq, *gains, *weights, x)


def qkv_kernel(where_ref, x_ref, gain_ref, packed_ref, cos_ref, sin_ref,
               q_ref, kt_ref, vt_ref, k_ref, v_ref, w_ref, w_wide, *, heads, kv_heads, dp, seq):
    half = HD // 2
    width = w_ref.shape[1]
    q_cols, kv_cols = width // seq, kv_heads * HD // seq
    kv_width = kv_heads * HD

    @pl.when(pl.program_id(0) == 0)
    def _():
        for s in range(seq):
            block = jnp.concatenate([packed_ref[where_ref[d * seq + s]] for d in range(dp)], axis=0)
            turned = block.astype(F32).T
            w_wide[q_cols * s : q_cols * s + q_cols, :] = turned[:q_cols]
            first = width + kv_cols * s
            w_wide[first : first + kv_cols, :] = turned[q_cols : q_cols + kv_cols]
            first += kv_width
            w_wide[first : first + kv_cols, :] = turned[q_cols + kv_cols : q_cols + 2 * kv_cols]
        w_ref[...] = w_wide[...].astype(BF16)

    x = x_ref[0].astype(F32)
    rstd = lax.rsqrt(jnp.mean(x * x, axis=0, keepdims=True) + eps_norm)
    normed = (x * rstd * gain_ref[...]).astype(BF16)
    lin = dot(w_ref[...], normed, 1, 0)
    cos, sin = cos_ref[...], sin_ref[...]
    for head in range(heads + kv_heads):
        top = lin[HD * head : HD * head + half]
        low = lin[HD * head + half : HD * head + HD]
        rot = jnp.concatenate([top * cos - low * sin, low * cos + top * sin], axis=0)
        if head < heads:
            q_ref[HD * head : HD * head + HD, :] = rot.astype(BF16) * jnp.asarray(HD**-0.5, BF16)
        else:
            kv = head - heads
            kt_ref[HD * kv : HD * kv + HD, :] = rot.astype(BF16)
            k_ref[kv] = rot.T.astype(BF16)
    for kv in range(kv_heads):
        first = HD * (heads + kv_heads + kv)
        val = lin[first : first + HD]
        vt_ref[HD * kv : HD * kv + HD, :] = val.astype(BF16)
        v_ref[kv] = val.T.astype(BF16)


def project_qkv(where, x, gain, packed, cos_t, sin_t, heads, kv_heads, rows):
    blocks, width, block = x.shape
    tokens = blocks * block
    feats = (heads + 2 * kv_heads) * HD
    dp, seq = lax.axis_size("dp"), lax.axis_size("seq")
    col = lambda rows: pl.BlockSpec((rows, block), lambda i, w: (0, i))
    nat = pl.BlockSpec((kv_heads, block, HD), lambda i, w: (0, i, 0))
    return pl.pallas_call(
        functools.partial(qkv_kernel, heads=heads, kv_heads=kv_heads, dp=dp, seq=seq),
        grid_spec=pltpu.PrefetchScalarGridSpec(
            num_scalar_prefetch=1,
            grid=(blocks,),
            in_specs=[
                pl.BlockSpec((1, width, block), lambda i, w: (i, 0, 0)),
                pl.BlockSpec((width, 1), lambda i, w: (0, 0)),
                pl.BlockSpec((dp * seq, rows, packed.shape[2]), lambda i, w: (0, 0, 0)),
                col(HD // 2),
                col(HD // 2),
            ],
            out_specs=[
                col(heads * HD), col(kv_heads * HD), col(kv_heads * HD), nat, nat,
                pl.BlockSpec((feats, width), lambda i, w: (0, 0)),
            ],
            scratch_shapes=[pltpu.VMEM((feats, width), F32)],
        ),
        out_shape=[
            jax.ShapeDtypeStruct((heads * HD, tokens), BF16),
            jax.ShapeDtypeStruct((kv_heads * HD, tokens), BF16),
            jax.ShapeDtypeStruct((kv_heads * HD, tokens), BF16),
            jax.ShapeDtypeStruct((kv_heads, tokens, HD), BF16),
            jax.ShapeDtypeStruct((kv_heads, tokens, HD), BF16),
            jax.ShapeDtypeStruct((feats, width), BF16),
        ],
        compiler_params=pltpu.CompilerParams(vmem_limit_bytes=VMEM_BYTES),
        cost_estimate=pl.CostEstimate(
            flops=4 * tokens * width * feats, bytes_accessed=tokens * 5000, transcendentals=0
        ),
        name="project_qkv",
    )(where, x, gain, packed, cos_t, sin_t)


def side_by_side(ref):
    return jnp.concatenate([ref[i] for i in range(ref.shape[0])], axis=1)


def mlp_kernel(
    where_ref, x_ref, mixed_ref, dy_ref, gain_ref, *more, chunk, dp, seq,
):
    packs, more = more[: 2 * dp], more[2 * dp :]
    out_ref, dmid_ref, dmixed_ref = more[:3]
    one_refs, two_refs, gain_grad_ref = more[3:5], more[5:7], more[7]
    (o_w, o_t, gate_w, gate_t, up_w, up_t, down_w, down_t, o_sum, gate_sum, up_sum, down_sum, gain_sum,
     pack, pack_sem) = more[8:]
    step, steps = pl.program_id(0), pl.num_programs(0)
    width, ff = gate_w.shape
    lanes = pack.shape[3]
    rows = width // dp
    o_cols, ff_cols, ff_rows = width // seq, ff // seq, ff // dp
    spare = ff_cols - lanes
    padded = -(-o_cols // 16) * 16

    @pl.when(step == 0)
    def _():
        for total in (o_sum, gate_sum, up_sum, down_sum, gain_sum):
            total[...] = jnp.zeros_like(total)
        fetches = []
        for i in range(dp):
            owner = flip(lax.axis_index("dp"), row_bits(i, dp))
            first = 0
            for source, sem in ((packs[2 * i], pack_sem.at[2 * i]), (packs[2 * i + 1], pack_sem.at[2 * i + 1])):
                span = pl.ds(first, source.shape[1])
                fetches.append(pltpu.make_async_copy(source, pack.at[owner, :, span, :], sem))
                first += source.shape[1]
        for fetch in fetches:
            fetch.start()
        for fetch in fetches:
            fetch.wait()
        for s in range(seq):
            at = where_ref[s]
            stack = lambda first: jnp.concatenate(
                [pack[d, at, first : first + rows, :] for d in range(dp)], axis=0
            )
            o_sum[o_cols * s : o_cols * s + o_cols, :] = stack(0).astype(F32).T[:o_cols]
            gate_t[ff_cols * s : ff_cols * s + lanes, :] = stack(rows).T
            up_t[ff_cols * s : ff_cols * s + lanes, :] = stack(2 * rows).T
            both = stack(3 * rows).T
            gate_t[ff_cols * s + lanes : ff_cols * (s + 1), :] = both[:spare]
            up_t[ff_cols * s + lanes : ff_cols * (s + 1), :] = both[spare : 2 * spare]
            for d in range(dp):
                for t in range(ff_rows // lanes):
                    first = 4 * rows + padded * t
                    piece = pack[d, at, first : first + padded, :].astype(F32)[:o_cols]
                    cols = slice(ff_rows * d + lanes * t, ff_rows * d + lanes * (t + 1))
                    down_sum[o_cols * s : o_cols * s + o_cols, cols] = piece
        for s in range(0, seq, 2):
            for d in range(dp):
                halves = [pack[d, where_ref[s + i], 3 * rows : 4 * rows, :] for i in range(2)]
                for matrix, first, cut in ((gate_w, rows, 0), (up_w, 2 * rows, spare)):
                    pieces = []
                    for i in range(2):
                        pieces.append(pack[d, where_ref[s + i], first : first + rows, :])
                        pieces.append(halves[i][:, cut : cut + spare])
                    cols = slice(ff_cols * s, ff_cols * (s + 2))
                    matrix[rows * d : rows * (d + 1), cols] = jnp.concatenate(pieces, axis=1)
        o_t[...] = o_sum[...].astype(BF16)
        o_w[...] = o_sum[...].T.astype(BF16)
        down_t[...] = down_sum[...].astype(BF16)
        for first in range(0, ff, lanes):
            part = slice(first, first + lanes)
            down_w[part, :] = down_t[:, part].T
        o_sum[...] = jnp.zeros_like(o_sum)
        down_sum[...] = jnp.zeros_like(down_sum)

    gain = gain_ref[...]
    mixed = mixed_ref[...]
    mid = dot(o_t[...], mixed, 1, 0) + side_by_side(x_ref).astype(F32)
    rstd = lax.rsqrt(jnp.mean(mid * mid, axis=0, keepdims=True) + eps_norm)
    normed = (mid * rstd * gain).astype(BF16)
    dy = side_by_side(dy_ref)
    added = jnp.zeros_like(mid)
    dnormed = jnp.zeros_like(mid)
    for first in range(0, ff, chunk):
        part = slice(first, first + chunk)
        gate = dot(gate_t[part, :], normed, 1, 0)
        up = dot(up_t[part, :], normed, 1, 0)
        dinner = dot(down_w[part, :], dy, 1, 0)
        sig = 1.0 / (1.0 + jnp.exp(-gate))
        silu = gate * sig
        inner = (silu * up).astype(BF16)
        dup = (dinner * silu).astype(BF16)
        dgate = (dinner * up * sig * (1.0 + gate * (1.0 - sig))).astype(BF16)
        added += dot(down_t[:, part], inner, 1, 0)
        dnormed += dot(gate_w[:, part], dgate, 1, 0)
        dnormed += dot(up_w[:, part], dup, 1, 0)
        down_sum[:, part] += dot(dy, inner, 1, 1)
        gate_sum[:, part] += dot(normed, dgate, 1, 1)
        up_sum[:, part] += dot(normed, dup, 1, 1)
    out = (mid + added).astype(BF16)
    scaled_mid = mid * rstd
    product = dnormed * scaled_mid
    gain_sum[...] += sum(product[:, c : c + lanes] for c in range(0, product.shape[1], lanes))
    scaled = dnormed * gain
    pull = jnp.mean(scaled * mid, axis=0, keepdims=True)
    dmid = dy.astype(F32) + rstd * scaled - scaled_mid * (rstd * rstd * pull)
    dmid_low = dmid.astype(BF16)
    block = out_ref.shape[2]
    for i in range(out_ref.shape[0]):
        out_ref[i] = out[:, block * i : block * (i + 1)]
        dmid_ref[i] = dmid[:, block * i : block * (i + 1)]
    o_sum[...] += dot(dmid_low, mixed, 1, 1)
    dmixed_ref[...] = dot(o_w[...], dmid_low, 1, 0).astype(BF16)

    @pl.when(step == steps - 1)
    def _():
        gain_grad_ref[...] = jnp.sum(gain_sum[...].T, axis=0, keepdims=True)
        my_dp, my_seq = lax.axis_index("dp"), lax.axis_index("seq")
        upper = my_dp % 2 == 1

        def put(refs, place, first, even, odd):
            keep_ref, give_ref = refs
            span = slice(first, first + even.shape[0])
            keep_ref[place, span, :] = jnp.where(upper, odd, even).astype(BF16)
            give_ref[place, span, :] = jnp.where(upper, even, odd).astype(BF16)

        blank = jnp.zeros((lanes - o_cols, width), F32)
        edge = jnp.zeros((padded - o_cols, lanes), F32)
        for s in range(seq):
            o_piece = jnp.concatenate([o_sum[o_cols * s : o_cols * (s + 1), :], blank], axis=0).T
            pair_cols = slice(ff_cols * (s - s % 2), ff_cols * (s - s % 2 + 2))
            shift = ff_cols * (s % 2)
            for d in range(0, dp, 2):
                bands = slice(rows * d, rows * (d + 1)), slice(rows * (d + 1), rows * (d + 2))
                one, two = [away_place(c, d, s, my_dp, my_seq) for c in rest_chains(dp, seq)]
                put(one_refs, one, 0, o_piece[bands[0]], o_piece[bands[1]])
                rests = []
                for i, total in enumerate((gate_sum, up_sum)):
                    wide = [total[band, pair_cols] for band in bands]
                    put(one_refs, one, rows * (i + 1), *[w[:, shift : shift + lanes] for w in wide])
                    rests.append([w[:, shift + lanes : shift + ff_cols] for w in wide])
                put(two_refs, two, 0, *[jnp.concatenate([g, u], axis=1) for g, u in zip(*rests)])
                for t in range(ff_rows // lanes):
                    pair = []
                    for at in (d, d + 1):
                        cols = slice(ff_rows * at + lanes * t, ff_rows * at + lanes * (t + 1))
                        pair.append(
                            jnp.concatenate([down_sum[o_cols * s : o_cols * (s + 1), cols], edge], axis=0)
                        )
                    put(two_refs, two, rows + padded * t, *pair)


def row_bits(at, dp):
    return [b for i, b in enumerate(reversed(bits_of(dp))) if (at >> i) & 1]


def over_rows(array, mask):
    return lax.ppermute(array, "dp", [(i, i ^ mask) for i in range(lax.axis_size("dp"))])


def mlp_both(where, x, mixed, dy, gain, packs, ff, batch=2, chunk=768):
    blocks, width, block = x.shape
    tokens = blocks * block
    dp, seq = lax.axis_size("dp"), lax.axis_size("seq")
    grad_rows, lanes = packs[0].shape[1] + packs[1].shape[1], packs[0].shape[2]
    first_rows = 3 * (width // dp)
    one = dp * seq // 2, first_rows, lanes
    two = dp * seq // 2, grad_rows - first_rows, lanes
    tok = pl.BlockSpec((batch, width, block), lambda i, w: (i, 0, 0))
    col = pl.BlockSpec((width, batch * block), lambda i, w: (0, i))
    once = lambda shape: pl.BlockSpec(
        shape, lambda i, w: (0,) * len(shape), pipeline_mode=pl.Buffered(1)
    )
    hbm = pl.BlockSpec(memory_space=pl.ANY)
    return pl.pallas_call(
        functools.partial(mlp_kernel, chunk=chunk, dp=dp, seq=seq),
        grid_spec=pltpu.PrefetchScalarGridSpec(
            num_scalar_prefetch=1,
            grid=(blocks // batch,),
            in_specs=[tok, col, tok, once((width, 1))] + [hbm] * (2 * dp),
            out_specs=[tok, tok, col, once(one), once(one), once(two), once(two), once((1, width))],
            scratch_shapes=[
                pltpu.VMEM((width, width), BF16),
                pltpu.VMEM((width, width), BF16),
                pltpu.VMEM((width, ff), BF16),
                pltpu.VMEM((ff, width), BF16),
                pltpu.VMEM((width, ff), BF16),
                pltpu.VMEM((ff, width), BF16),
                pltpu.VMEM((ff, width), BF16),
                pltpu.VMEM((width, ff), BF16),
                pltpu.VMEM((width, width), F32),
                pltpu.VMEM((width, ff), F32),
                pltpu.VMEM((width, ff), F32),
                pltpu.VMEM((width, ff), F32),
                pltpu.VMEM((width, lanes), F32),
                pltpu.VMEM((dp, packs[0].shape[0], grad_rows, lanes), BF16),
                pltpu.SemaphoreType.DMA((2 * dp,)),
            ],
        ),
        out_shape=[
            jax.ShapeDtypeStruct(x.shape, BF16),
            jax.ShapeDtypeStruct(x.shape, F32),
            jax.ShapeDtypeStruct((width, tokens), BF16),
            jax.ShapeDtypeStruct(one, BF16),
            jax.ShapeDtypeStruct(one, BF16),
            jax.ShapeDtypeStruct(two, BF16),
            jax.ShapeDtypeStruct(two, BF16),
            jax.ShapeDtypeStruct((1, width), F32),
        ],
        compiler_params=pltpu.CompilerParams(vmem_limit_bytes=60 * 2**20),
        cost_estimate=pl.CostEstimate(
            flops=2 * tokens * width * (9 * ff + 3 * width),
            bytes_accessed=tokens * width * 14,
            transcendentals=tokens * ff,
        ),
        name="mlp_both",
    )(where, x, mixed, dy, gain, *packs)


def across(index, other, size):
    for bit in bits_of(size):
        index = index + bit * ((other // bit) % 2) * (1 - 2 * ((index // bit) % 2))
    return index


def add_blocks(total_ref, term_ref, count, total_first=0, term_first=0):
    def one(i, _):
        total = total_ref[total_first + i].astype(F32) + term_ref[term_first + i].astype(F32)
        total_ref[total_first + i] = total.astype(BF16)
        return 0

    lax.fori_loop(0, count, one, 0)


def finish_kernel(
    x_ref, dmid_ref, dq_one, dq_two, dk_one, dk_two, dv_one, dv_two, gain_ref, w_t_ref, other_gain_ref,
    keep_one, keep_two, came_one, came_two, out_ref, gains_ref, qkv_ref, one_ref, two_ref,
    w_nat, w_sum, gain_sum, din, packed, landed, one, one_came, one_landed, two, two_came, two_landed,
    gain_held, gain_landed,
    own_sem, d_send, d_recv, r_send, r_recv, g_send, g_recv, fetch_sem, *, dp, seq, kv_width,
):
    step, steps = pl.program_id(0), seq // 2
    my_dp, my_seq = lax.axis_index("dp"), lax.axis_index("seq")
    width = w_nat.shape[0]
    lanes = packed.shape[2]
    rows = width // dp
    q_cols, kv_cols = width // seq, kv_width // seq
    orders = [all_stages(dp, seq), *[chain[:-1] for chain in rest_chains(dp, seq)]]
    held = [packed, one, two]
    arrived = [landed, one_landed, two_landed]
    fetches = [
        pltpu.make_async_copy(source, target, fetch_sem.at[i])
        for i, (source, target) in enumerate(
            ((keep_one, one), (keep_two, two), (came_one, one_came), (came_two, two_came))
        )
    ]

    def halve(chain, turn):
        at = len(orders[chain]) - 1 - turn
        half = 1 << at
        return pltpu.make_async_remote_copy(
            src_ref=held[chain].at[pl.ds(half, half)],
            dst_ref=arrived[chain].at[pl.ds(half, half)],
            send_sem=r_send.at[chain, turn],
            recv_sem=r_recv.at[chain, turn],
            device_id=stage_peer(my_dp, my_seq, orders[chain][at]),
            device_id_type=pl.DeviceIdType.MESH,
        )

    def take(chain, turn):
        halve(chain, turn).wait_recv()
        half = 1 << (len(orders[chain]) - 1 - turn)
        if half > 1:
            add_blocks(held[chain], arrived[chain], half, 0, half)
            halve(chain, turn + 1).start()

    def result(chain):
        return held[chain][0].astype(F32) + arrived[chain][1].astype(F32)

    @pl.when(step == 0)
    def _():
        for fetch in fetches:
            fetch.start()
        greet(all_peers(my_dp, my_seq, dp, seq))
        for fetch in fetches:
            fetch.wait()
        for chain, came in ((1, one_came), (2, two_came)):
            add_blocks(held[chain], came, came.shape[0])
            halve(chain, 0).start()
        w_sum[...] = jnp.zeros_like(w_sum)
        gain_sum[...] = jnp.zeros_like(gain_sum)
        w_nat[...] = w_t_ref[...].T

    gain = gain_ref[...]
    x = side_by_side(x_ref).astype(F32)
    rstd = lax.rsqrt(jnp.mean(x * x, axis=0, keepdims=True) + eps_norm)
    scaled_x = x * rstd
    normed = (scaled_x * gain).astype(BF16)
    dlins = dq_one, dq_two, dk_one, dk_two, dv_one, dv_two
    dlin = jnp.concatenate([ref[...] for ref in dlins], axis=0)
    w_sum[...] += dot(dlin, normed, 1, 1)
    dnormed = dot(w_nat[...], dlin, 1, 0)
    product = dnormed * scaled_x
    gain_sum[...] += sum(product[:, c : c + lanes] for c in range(0, product.shape[1], lanes))
    scaled = dnormed * gain
    pull = jnp.mean(scaled * x, axis=0, keepdims=True)
    total = side_by_side(dmid_ref) + rstd * scaled - scaled_x * (rstd * rstd * pull)
    pair = across(my_seq // 2, steps - 1 - step, seq // 2)
    block = din.shape[2]
    for i in range(2):
        din[2 * pair + i] = total[:, block * i : block * (i + 1)].astype(BF16)

    def move(away):
        peer = seq_peer(my_dp, my_seq, away, seq)
        return pltpu.make_async_remote_copy(
            src_ref=din.at[peer[1]],
            dst_ref=out_ref.at[my_seq],
            send_sem=d_send.at[away - 1],
            recv_sem=d_recv.at[away - 1],
            device_id=peer,
            device_id_type=pl.DeviceIdType.MESH,
        )

    @pl.when(step == 0)
    def _():
        for away in range(seq - 2, seq):
            move(away).start()

    @pl.when(step == max(steps - 2, 0))
    def _():
        for chain in (1, 2):
            take(chain, 0)

    @pl.when(step == steps - 1)
    def _():
        move(1).start()
        own = pltpu.make_async_copy(din.at[my_seq], out_ref.at[my_seq], own_sem)
        own.start()
        blank = jnp.zeros((lanes - q_cols - 2 * kv_cols, width), F32)
        for s in range(seq):
            first = width + kv_cols * s
            piece = jnp.concatenate(
                [
                    w_sum[q_cols * s : q_cols * (s + 1), :],
                    w_sum[first : first + kv_cols, :],
                    w_sum[first + kv_width : first + kv_width + kv_cols, :],
                    blank,
                ],
                axis=0,
            ).T.astype(BF16)
            for d in range(dp):
                packed[away_place(orders[0], d, s, my_dp, my_seq)] = piece[rows * d : rows * (d + 1)]
        gain_row = jnp.sum(gain_sum[...].T, axis=0, keepdims=True)
        gain_held[0] = jnp.concatenate(
            [gain_row, other_gain_ref[...], jnp.zeros((6, width), F32)], axis=0
        )
        turns = len(orders[0])
        gain_copies = [
            pltpu.make_async_remote_copy(
                src_ref=gain_held.at[turn],
                dst_ref=gain_landed.at[turn],
                send_sem=g_send.at[turn],
                recv_sem=g_recv.at[turn],
                device_id=stage_peer(my_dp, my_seq, orders[0][turns - 1 - turn]),
                device_id_type=pl.DeviceIdType.MESH,
            )
            for turn in range(turns)
        ]
        halve(0, 0).start()
        gain_copies[0].start()
        for turn in range(turns):
            gain_copies[turn].wait_recv()
            gain_held[turn + 1] = gain_held[turn] + gain_landed[turn]
            if turn + 1 < turns:
                gain_copies[turn + 1].start()
            take(0, turn)
            if turn == turns - 3:
                for chain in (1, 2):
                    take(chain, 1)
                for away in range(seq // 2, seq - 2):
                    move(away).start()
            if turn == turns - 2:
                for chain in (1, 2):
                    take(chain, 2)
                for away in range(2, seq // 2):
                    move(away).start()
        gains_ref[...] = gain_held[turns]
        qkv_ref[...], one_ref[...], two_ref[...] = result(0), result(1), result(2)
        for copy in gain_copies:
            copy.wait_send()
        for chain in range(3):
            for turn in range(len(orders[chain])):
                halve(chain, turn).wait_send()
        for away in range(1, seq):
            move(away).wait()
        own.wait()


def finish(x, dmid, dlins, gain, w_t, other_gain, keep_one, keep_two, came_one, came_two):
    blocks, width, block = x.shape
    tokens = blocks * block
    feats = w_t.shape[0]
    kv_width = (feats - width) // 2
    lanes = keep_one.shape[2]
    dp, seq = lax.axis_size("dp"), lax.axis_size("seq")
    rows = width // dp
    stages = len(all_stages(dp, seq))

    def pair(i):
        return across(lax.axis_index("seq") // 2, seq // 2 - 1 - i, seq // 2)

    tok = pl.BlockSpec((2, width, block), lambda i: (pair(i), 0, 0))
    col = lambda rows: pl.BlockSpec((rows, 2 * block), lambda i: (0, pair(i)))
    once = lambda shape: pl.BlockSpec(shape, lambda i: (0,) * len(shape), pipeline_mode=pl.Buffered(1))
    hbm = pl.BlockSpec(memory_space=pl.ANY)
    small = [(8, width), (rows, lanes), keep_one.shape[1:], keep_two.shape[1:]]
    return pl.pallas_call(
        functools.partial(finish_kernel, dp=dp, seq=seq, kv_width=kv_width),
        grid=(blocks // 2,),
        in_specs=[
            tok, tok, *[col(d.shape[0]) for d in dlins],
            once((width, 1)), once((feats, width)), once((1, width)), hbm, hbm, hbm, hbm,
        ],
        out_specs=[hbm] + [once(shape) for shape in small],
        out_shape=[jax.ShapeDtypeStruct(x.shape, BF16)] + [jax.ShapeDtypeStruct(shape, F32) for shape in small],
        scratch_shapes=[
            pltpu.VMEM((width, feats), BF16),
            pltpu.VMEM((feats, width), F32),
            pltpu.VMEM((width, lanes), F32),
            pltpu.VMEM(x.shape, BF16),
            pltpu.VMEM((dp * seq, rows, lanes), BF16),
            pltpu.VMEM((dp * seq, rows, lanes), BF16),
            *[pltpu.VMEM(keep_one.shape, BF16)] * 3,
            *[pltpu.VMEM(keep_two.shape, BF16)] * 3,
            pltpu.VMEM((stages + 1, 8, width), F32),
            pltpu.VMEM((stages, 8, width), F32),
            pltpu.SemaphoreType.DMA,
            pltpu.SemaphoreType.DMA((seq - 1,)),
            pltpu.SemaphoreType.DMA((seq - 1,)),
            pltpu.SemaphoreType.DMA((3, stages)),
            pltpu.SemaphoreType.DMA((3, stages)),
            pltpu.SemaphoreType.DMA((stages,)),
            pltpu.SemaphoreType.DMA((stages,)),
            pltpu.SemaphoreType.DMA((4,)),
        ],
        compiler_params=pltpu.CompilerParams(
            collective_id=2, has_side_effects=True, vmem_limit_bytes=VMEM_BYTES
        ),
        cost_estimate=pl.CostEstimate(
            flops=4 * tokens * width * feats, bytes_accessed=tokens * width * 12, transcendentals=0
        ),
        name="finish",
    )(x, dmid, *dlins, gain, w_t, other_gain, keep_one, keep_two, came_one, came_two)


def deliver_kernel(
    din_ref, gains_ref, qkv_ref, one_ref, two_ref,
    out_ref, gain_one, gain_two, q_ref, k_ref, v_ref, o_ref, gate_ref, up_ref, down_ref,
):
    out_ref[...] = din_ref[...].astype(F32)

    @pl.when(pl.program_id(0) == 0)
    def _():
        rows, q_cols = q_ref.shape
        kv_cols, lanes = k_ref.shape[0], qkv_ref.shape[1]
        spare = gate_ref.shape[1] - lanes
        padded = -(-q_cols // 16) * 16
        gain_one[...] = gains_ref[0]
        gain_two[...] = gains_ref[1]
        qkv = qkv_ref[...]
        turned = qkv.T
        q_ref[...] = qkv[:, :q_cols]
        k_ref[...] = turned[q_cols : q_cols + kv_cols]
        v_ref[...] = turned[q_cols + kv_cols : q_cols + 2 * kv_cols]
        o_ref[...] = one_ref[:rows, :q_cols]
        both = two_ref[:rows]
        gate_ref[...] = jnp.concatenate([one_ref[rows : 2 * rows], both[:, :spare]], axis=1)
        up_ref[...] = jnp.concatenate([one_ref[2 * rows : 3 * rows], both[:, spare : 2 * spare]], axis=1)
        for t in range(down_ref.shape[1] // lanes):
            at = rows + padded * t
            down_ref[:, lanes * t : lanes * (t + 1)] = two_ref[at : at + q_cols]


def deliver(din, gains, qkv, one, two, kv_cols, ff):
    blocks, width, block = din.shape
    rows = qkv.shape[0]
    dp, seq = lax.axis_size("dp"), lax.axis_size("seq")
    tok = pl.BlockSpec((2, width, block), lambda i: (i, 0, 0))
    once = lambda shape: pl.BlockSpec(shape, lambda i: (0,) * len(shape), pipeline_mode=pl.Buffered(1))
    small = [
        (width,),
        (width,),
        (rows, width // seq),
        (kv_cols, rows),
        (kv_cols, rows),
        (rows, width // seq),
        (rows, ff // seq),
        (rows, ff // seq),
        (width // seq, ff // dp),
    ]
    return pl.pallas_call(
        deliver_kernel,
        grid=(blocks // 2,),
        in_specs=[tok] + [once(a.shape) for a in (gains, qkv, one, two)],
        out_specs=[tok] + [once(shape) for shape in small],
        out_shape=[jax.ShapeDtypeStruct(shape, F32) for shape in [din.shape] + small],
        compiler_params=pltpu.CompilerParams(vmem_limit_bytes=VMEM_BYTES),
        name="deliver",
    )(din, gains, qkv, one, two)


def exchange(blocks):
    return lax.all_to_all(blocks, "seq", 0, 0, tiled=True)


def shards_sequences(
    hidden_in, span_order, attn_gain, q_weight, k_weight, v_weight, o_weight, mlp_gain,
    gate_weight, up_weight, down_weight, out_grad,
):
    lanes = 128
    seqs, slots, width = hidden_in.shape
    dp, seq = lax.axis_size("dp"), lax.axis_size("seq")
    tokens = slots * seq
    span = tokens // span_order.shape[0]
    heads = width // HD
    kv_heads = k_weight.shape[1] * seq // HD
    rows, q_cols = q_weight.shape
    kv_cols = k_weight.shape[1]
    ff = down_weight.shape[0] * dp
    ff_rows = down_weight.shape[0]
    padded = -(-q_cols // 16) * 16

    inv_freq = np.float32(rope_base ** (-2.0 * np.arange(HD // 2) / HD))
    inv, cos_t, sin_t, gain_one, gain_two, x, first_all, straight, hopping = bring(
        span_order,
        inv_freq[:, None],
        (attn_gain, mlp_gain),
        (q_weight, k_weight.T, v_weight.T, o_weight, gate_weight, up_weight, down_weight.T),
        hidden_in.transpose(0, 2, 1),
    )
    out_grad, x = lax.optimization_barrier((out_grad, x))
    masks = [sum(row_bits(i, dp)) for i in range(dp)]
    straight_all = [straight] + [over_rows(straight, m) for m in masks[1:]]
    hopping_all = [hopping if m == 0 else over_rows(hopping, m) if m & (m - 1) == 0 else None for m in masks]
    dy = exchange(out_grad.transpose(0, 2, 1))

    my_dp, my_seq = lax.axis_index("dp"), lax.axis_index("seq")
    where_first = arrival_order(all_stages(dp, seq), dp, seq, my_dp, my_seq)
    where_second = arrival_order(seq_stages(seq), dp, seq, my_dp, my_seq)[:seq]
    q_t, k_t, v_t, k_nat, v_nat, w_t = project_qkv(
        where_first, x, gain_one, first_all, cos_t, sin_t, heads, kv_heads, rows
    )
    o_t, logs = attention_forward(inv, q_t, k_nat, v_t, span)
    hopping_all, o_t = lax.optimization_barrier((hopping_all, o_t))
    for i, mask in enumerate(masks):
        if hopping_all[i] is None:
            low = mask & -mask
            hopping_all[i] = over_rows(hopping_all[masks.index(mask - low)], low)
    packs = [part for pair in zip(straight_all, hopping_all) for part in pair]
    out, dmid, do_t, keep_one, give_one, keep_two, give_two, gain_two_term = mlp_both(
        where_second, x, o_t, dy, gain_two, packs, ff
    )
    came_one, came_two = over_rows(give_one, 1), over_rows(give_two, 1)
    hidden_out = exchange(out).transpose(0, 2, 1)

    def back(queries, *heads):
        return attention_backward(
            inv, queries, k_t, k_nat, v_nat, o_t, do_t, logs, cos_t, sin_t, span, *heads
        )

    parts = [back(q_t, 0, 1)]
    came_one, came_two, parts[0] = lax.optimization_barrier((came_one, came_two, parts[0]))
    half = dp * seq // 4
    add = lambda a, b: (a.astype(F32) + b.astype(F32)).astype(BF16)
    sums = [
        (add(keep[:half], came[:half]), add(keep[half:], came[half:]))
        for keep, came in ((keep_one, came_one), (keep_two, came_two))
    ]
    sums, q_t = lax.optimization_barrier((sums, q_t))
    crossed = [
        lax.ppermute(high, axis, [(i, i ^ bit) for i in range(lax.axis_size(axis))])
        for (_, high), (axis, bit) in zip(sums, [chain[-1] for chain in rest_chains(dp, seq)])
    ]
    parts.append(back(q_t, 1, kv_heads - 1))
    dlins = [part[i] for i in range(3) for part in parts]
    din, gains, qkv_sum, one_sum, two_sum = finish(
        x, dmid, dlins, gain_one, w_t, gain_two_term, sums[0][0], sums[1][0], *crossed
    )
    grad_in, gain_one_sum, gain_two_sum, q_sum, k_sum, v_sum, o_sum, gate_sum, up_sum, down_sum = deliver(
        din, gains, qkv_sum, one_sum, two_sum, kv_cols, ff
    )
    return (
        hidden_out,
        grad_in.transpose(0, 2, 1),
        gain_one_sum,
        q_sum,
        k_sum.T,
        v_sum.T,
        o_sum,
        gain_two_sum,
        gate_sum,
        up_sum,
        down_sum.T,
    )


def shards(*args):
    seqs, spans = args[0].shape[0], args[1].shape[0]
    if seqs == lax.axis_size("seq") and spans % 4 == 0:
        return shards_sequences(*args)
    return shards_general(*args)


def solution(mesh):
    placed = (
        P("dp", "seq", None),
        P(),
        P(),
        P("dp", "seq"),
        P("dp", "seq"),
        P("dp", "seq"),
        P("dp", "seq"),
        P(),
        P("dp", "seq"),
        P("dp", "seq"),
        P("dp", "seq"),
        P("dp", "seq", None),
    )
    return jax.shard_map(
        shards,
        mesh=mesh,
        in_specs=placed,
        out_specs=(
            P("dp", "seq", None),
            P("dp", "seq", None),
            P(),
            P("dp", "seq"),
            P("dp", "seq"),
            P("dp", "seq"),
            P("dp", "seq"),
            P(),
            P("dp", "seq"),
            P("dp", "seq"),
            P("dp", "seq"),
        ),
        check_vma=False,
    )
```

```python
import functools

import jax
import jax.numpy as jnp
import numpy as np
from jax import lax
from jax.experimental import pallas as pl
from jax.experimental.pallas import tpu as pltpu
from jax.sharding import PartitionSpec as P

HD = 64
MICRO = 2


eps_norm = 1e-05
rope_base = 100000.0
neg_big = -1e30


def slot_positions(slot_ids, span_order, span_len):
    span_ids = slot_ids // span_len
    span_hits = span_ids[:, None] == jnp.arange(span_order.shape[0], dtype=jnp.int32)[None, :]
    starts = jnp.sum(jnp.where(span_hits, span_order[None, :], 0), axis=1)
    return starts * span_len + slot_ids % span_len


def rope_tables(slot_pos):
    half_width = HD // 2
    inv_freq = rope_base ** (-(jnp.arange(half_width, dtype=jnp.float32) * 2.0) / HD)
    angles = slot_pos.astype(jnp.float32)[:, None] * inv_freq[None, :]
    cosine = jnp.concatenate([jnp.cos(angles), jnp.cos(angles)], axis=1)
    sine_tab = jnp.concatenate([jnp.sin(angles), jnp.sin(angles)], axis=1)
    return (cosine[:, None, :], sine_tab[:, None, :])


def rotate(vector, cosine, sine_tab):
    half_width = vector.shape[-1] // 2
    turned = jnp.concatenate([-vector[..., half_width:], vector[..., :half_width]], axis=-1)
    return vector * cosine + turned * sine_tab


def rotate_back(grad_out, cosine, sine_tab):
    half_width = grad_out.shape[-1] // 2
    scaled = grad_out * sine_tab
    turned = jnp.concatenate([scaled[..., half_width:], -scaled[..., :half_width]], axis=-1)
    return grad_out * cosine + turned


def norm_back(vector, rstd_vec, gain_vec, grad_n):
    scaled = grad_n * gain_vec
    gain_term = jnp.sum(grad_n * vector * rstd_vec, axis=0)
    grad_vec = rstd_vec * scaled - vector * rstd_vec**3 * jnp.mean(
        scaled * vector, axis=-1, keepdims=True
    )
    return (grad_vec, gain_term)


def add_tuples(old_sums, new_terms):
    if old_sums is None:
        return tuple(new_terms)
    return tuple((old_sum + new_term for old_sum, new_term in zip(old_sums, new_terms)))


def shards_general(
    hidden_in,
    span_order,
    attn_gain,
    q_weight,
    k_weight,
    v_weight,
    o_weight,
    mlp_gain,
    gate_weight,
    up_weight,
    down_weight,
    out_grad,
):
    local_seqs, row_count, model_width = hidden_in.shape
    seq_parts = lax.axis_size("seq")
    full_length = row_count * seq_parts
    span_len = full_length // (2 * seq_parts)
    per_micro = local_seqs // MICRO
    kv_width = k_weight.shape[1] * seq_parts
    kv_heads = kv_width // HD
    head_count = model_width // HD
    group_size = head_count // kv_heads
    tok_count = per_micro * row_count
    score_scale = HD ** (-0.5)
    own_slots = lax.axis_index("seq") * row_count + jnp.arange(row_count, dtype=jnp.int32)
    own_pos = slot_positions(own_slots, span_order, span_len)
    all_pos = slot_positions(jnp.arange(full_length, dtype=jnp.int32), span_order, span_len)
    allowed = own_pos[:, None] >= all_pos[None, :]
    cos_own, sin_own = rope_tables(own_pos)
    gain_attn = attn_gain.astype(jnp.float32)
    gain_mlp = mlp_gain.astype(jnp.float32)

    def attend(inputs):
        queries, key_rows, value_rows = inputs
        query_grp = queries.reshape(row_count, kv_heads, group_size, HD)
        key_grp = key_rows.reshape(full_length, kv_heads, HD)
        value_grp = value_rows.reshape(full_length, kv_heads, HD)
        scores = (
            jnp.einsum("rkgd,lkd->kgrl", query_grp, key_grp, preferred_element_type=jnp.float32)
            * score_scale
        )
        scores = jnp.where(allowed, scores, neg_big)
        row_peak = jnp.max(scores, axis=-1, keepdims=True)
        exp_scores = jnp.exp(scores - row_peak)
        row_total = jnp.sum(exp_scores, axis=-1, keepdims=True)
        attn_probs = exp_scores / row_total
        log_total = row_peak + jnp.log(row_total)
        mixed = jnp.einsum(
            "kgrl,lkd->rkgd",
            attn_probs.astype(jnp.bfloat16),
            value_grp,
            preferred_element_type=jnp.float32,
        )
        return (mixed.astype(jnp.bfloat16).reshape(row_count, model_width), log_total)

    def attend_back(inputs):
        queries, key_rows, value_rows, grad_mix, log_total = inputs
        query_grp = queries.reshape(row_count, kv_heads, group_size, HD)
        key_grp = key_rows.reshape(full_length, kv_heads, HD)
        value_grp = value_rows.reshape(full_length, kv_heads, HD)
        grad_grp = grad_mix.reshape(row_count, kv_heads, group_size, HD)
        scores = (
            jnp.einsum("rkgd,lkd->kgrl", query_grp, key_grp, preferred_element_type=jnp.float32)
            * score_scale
        )
        scores = jnp.where(allowed, scores, neg_big)
        attn_probs = jnp.exp(scores - log_total)
        probs_low = attn_probs.astype(jnp.bfloat16)
        grad_probs = jnp.einsum(
            "rkgd,lkd->kgrl", grad_grp, value_grp, preferred_element_type=jnp.float32
        )
        row_delta = jnp.sum(attn_probs * grad_probs, axis=-1, keepdims=True)
        grad_scores = (attn_probs * (grad_probs - row_delta)).astype(jnp.bfloat16)
        grad_query_rot = (
            jnp.einsum("kgrl,lkd->rkgd", grad_scores, key_grp, preferred_element_type=jnp.float32)
            * score_scale
        )
        key_term = (
            jnp.einsum("kgrl,rkgd->lkd", grad_scores, query_grp, preferred_element_type=jnp.float32)
            * score_scale
        )
        value_term = jnp.einsum(
            "kgrl,rkgd->lkd", probs_low, grad_grp, preferred_element_type=jnp.float32
        )
        return (
            grad_query_rot.reshape(row_count, head_count, HD),
            key_term.reshape(full_length, kv_width),
            value_term.reshape(full_length, kv_width),
        )

    outputs = []
    in_grads = []
    totals = None
    for micro_idx in range(MICRO):
        first_seq = micro_idx * per_micro
        block_in = hidden_in[first_seq : first_seq + per_micro]
        block_grad = out_grad[first_seq : first_seq + per_micro]
        col_parts = (
            lax.all_gather(q_weight, "seq", axis=1, tiled=True),
            lax.all_gather(k_weight, "seq", axis=1, tiled=True),
            lax.all_gather(v_weight, "seq", axis=1, tiled=True),
            lax.all_gather(o_weight, "seq", axis=1, tiled=True),
            lax.all_gather(gate_weight, "seq", axis=1, tiled=True),
            lax.all_gather(up_weight, "seq", axis=1, tiled=True),
            lax.all_gather(down_weight, "seq", axis=1, tiled=True),
        )
        query_mat, key_mat, value_mat, out_mat, gate_mat, up_mat, down_mat = (
            lax.all_gather(col_parts[0], "dp", axis=0, tiled=True),
            lax.all_gather(col_parts[1], "dp", axis=0, tiled=True),
            lax.all_gather(col_parts[2], "dp", axis=0, tiled=True),
            lax.all_gather(col_parts[3], "dp", axis=0, tiled=True),
            lax.all_gather(col_parts[4], "dp", axis=0, tiled=True),
            lax.all_gather(col_parts[5], "dp", axis=0, tiled=True),
            lax.all_gather(col_parts[6], "dp", axis=0, tiled=True),
        )
        resid_in = block_in.astype(jnp.float32).reshape(tok_count, model_width)
        rstd_one = lax.rsqrt(jnp.mean(resid_in * resid_in, axis=-1, keepdims=True) + eps_norm)
        normed_one = (resid_in * rstd_one * gain_attn).astype(jnp.bfloat16)
        query_lin = jnp.dot(normed_one, query_mat, preferred_element_type=jnp.float32)
        key_lin = jnp.dot(normed_one, key_mat, preferred_element_type=jnp.float32)
        value_lin = jnp.dot(normed_one, value_mat, preferred_element_type=jnp.float32)
        query_rot = rotate(
            query_lin.reshape(per_micro, row_count, head_count, HD), cos_own, sin_own
        ).astype(jnp.bfloat16)
        key_rot = (
            rotate(key_lin.reshape(per_micro, row_count, kv_heads, HD), cos_own, sin_own)
            .astype(jnp.bfloat16)
            .reshape(per_micro, row_count, kv_width)
        )
        value_low = value_lin.astype(jnp.bfloat16).reshape(per_micro, row_count, kv_width)
        key_all, value_all = (
            lax.all_gather(key_rot, "seq", axis=1, tiled=True),
            lax.all_gather(value_low, "seq", axis=1, tiled=True),
        )
        mixed_seq, log_total = lax.map(attend, (query_rot, key_all, value_all))
        mixed_low = mixed_seq.reshape(tok_count, model_width)
        hidden_mid = resid_in + jnp.dot(mixed_low, out_mat, preferred_element_type=jnp.float32)
        rstd_two = lax.rsqrt(jnp.mean(hidden_mid * hidden_mid, axis=-1, keepdims=True) + eps_norm)
        normed_two = (hidden_mid * rstd_two * gain_mlp).astype(jnp.bfloat16)
        gate_lin = jnp.dot(normed_two, gate_mat, preferred_element_type=jnp.float32)
        up_lin = jnp.dot(normed_two, up_mat, preferred_element_type=jnp.float32)
        gate_sig = jax.nn.sigmoid(gate_lin)
        inner_low = (gate_lin * gate_sig * up_lin).astype(jnp.bfloat16)
        mlp_out = jnp.dot(inner_low, down_mat, preferred_element_type=jnp.float32)
        outputs.append(
            (hidden_mid + mlp_out).astype(jnp.bfloat16).reshape(per_micro, row_count, model_width)
        )
        col_again = (
            lax.all_gather(q_weight, "seq", axis=1, tiled=True),
            lax.all_gather(k_weight, "seq", axis=1, tiled=True),
            lax.all_gather(v_weight, "seq", axis=1, tiled=True),
            lax.all_gather(o_weight, "seq", axis=1, tiled=True),
            lax.all_gather(gate_weight, "seq", axis=1, tiled=True),
            lax.all_gather(up_weight, "seq", axis=1, tiled=True),
            lax.all_gather(down_weight, "seq", axis=1, tiled=True),
        )
        query_mat, key_mat, value_mat, out_mat, gate_mat, up_mat, down_mat = (
            lax.all_gather(col_again[0], "dp", axis=0, tiled=True),
            lax.all_gather(col_again[1], "dp", axis=0, tiled=True),
            lax.all_gather(col_again[2], "dp", axis=0, tiled=True),
            lax.all_gather(col_again[3], "dp", axis=0, tiled=True),
            lax.all_gather(col_again[4], "dp", axis=0, tiled=True),
            lax.all_gather(col_again[5], "dp", axis=0, tiled=True),
            lax.all_gather(col_again[6], "dp", axis=0, tiled=True),
        )
        key_all, value_all = (
            lax.all_gather(key_rot, "seq", axis=1, tiled=True),
            lax.all_gather(value_low, "seq", axis=1, tiled=True),
        )
        grad_top = block_grad.astype(jnp.float32).reshape(tok_count, model_width)
        grad_top_low = grad_top.astype(jnp.bfloat16)
        down_term = jnp.einsum(
            "tf,td->fd", inner_low, grad_top_low, preferred_element_type=jnp.float32
        )
        grad_inner = jnp.einsum(
            "td,fd->tf", grad_top_low, down_mat, preferred_element_type=jnp.float32
        )
        grad_gate = (grad_inner * up_lin * gate_sig * (1.0 + gate_lin * (1.0 - gate_sig))).astype(
            jnp.bfloat16
        )
        grad_up = (grad_inner * gate_lin * gate_sig).astype(jnp.bfloat16)
        gate_term = jnp.einsum(
            "td,tf->df", normed_two, grad_gate, preferred_element_type=jnp.float32
        )
        up_term = jnp.einsum("td,tf->df", normed_two, grad_up, preferred_element_type=jnp.float32)
        grad_normed_two = jnp.einsum(
            "tf,df->td", grad_gate, gate_mat, preferred_element_type=jnp.float32
        ) + jnp.einsum("tf,df->td", grad_up, up_mat, preferred_element_type=jnp.float32)
        grad_mid_norm, gain_mlp_term = norm_back(hidden_mid, rstd_two, gain_mlp, grad_normed_two)
        grad_mid = grad_top + grad_mid_norm
        grad_mid_low = grad_mid.astype(jnp.bfloat16)
        out_term = jnp.einsum(
            "td,te->de", mixed_low, grad_mid_low, preferred_element_type=jnp.float32
        )
        grad_mixed = jnp.einsum(
            "te,de->td", grad_mid_low, out_mat, preferred_element_type=jnp.float32
        ).astype(jnp.bfloat16)
        grad_query_rot, key_terms, value_terms = lax.map(
            attend_back,
            (
                query_rot,
                key_all,
                value_all,
                grad_mixed.reshape(per_micro, row_count, model_width),
                log_total,
            ),
        )
        key_share, value_share = (
            lax.psum_scatter(key_terms, "seq", scatter_dimension=1, tiled=True),
            lax.psum_scatter(value_terms, "seq", scatter_dimension=1, tiled=True),
        )
        grad_query = (
            rotate_back(grad_query_rot, cos_own, sin_own)
            .astype(jnp.bfloat16)
            .reshape(tok_count, model_width)
        )
        grad_key = (
            rotate_back(key_share.reshape(per_micro, row_count, kv_heads, HD), cos_own, sin_own)
            .astype(jnp.bfloat16)
            .reshape(tok_count, kv_width)
        )
        grad_value = value_share.astype(jnp.bfloat16).reshape(tok_count, kv_width)
        query_term = jnp.einsum(
            "td,te->de", normed_one, grad_query, preferred_element_type=jnp.float32
        )
        key_term = jnp.einsum("td,te->de", normed_one, grad_key, preferred_element_type=jnp.float32)
        value_term = jnp.einsum(
            "td,te->de", normed_one, grad_value, preferred_element_type=jnp.float32
        )
        grad_normed_one = (
            jnp.einsum("te,de->td", grad_query, query_mat, preferred_element_type=jnp.float32)
            + jnp.einsum("te,de->td", grad_key, key_mat, preferred_element_type=jnp.float32)
            + jnp.einsum("te,de->td", grad_value, value_mat, preferred_element_type=jnp.float32)
        )
        grad_in_norm, gain_attn_term = norm_back(resid_in, rstd_one, gain_attn, grad_normed_one)
        in_grads.append((grad_mid + grad_in_norm).reshape(per_micro, row_count, model_width))
        totals = add_tuples(
            totals,
            (
                query_term,
                key_term,
                value_term,
                out_term,
                gate_term,
                up_term,
                down_term,
                gain_attn_term,
                gain_mlp_term,
            ),
        )
    col_sums = (
        lax.psum_scatter(
            totals[0].astype(jnp.bfloat16), "seq", scatter_dimension=1, tiled=True
        ).astype(jnp.float32),
        lax.psum_scatter(
            totals[1].astype(jnp.bfloat16), "seq", scatter_dimension=1, tiled=True
        ).astype(jnp.float32),
        lax.psum_scatter(
            totals[2].astype(jnp.bfloat16), "seq", scatter_dimension=1, tiled=True
        ).astype(jnp.float32),
        lax.psum_scatter(
            totals[3].astype(jnp.bfloat16), "seq", scatter_dimension=1, tiled=True
        ).astype(jnp.float32),
        lax.psum_scatter(
            totals[4].astype(jnp.bfloat16), "seq", scatter_dimension=1, tiled=True
        ).astype(jnp.float32),
        lax.psum_scatter(
            totals[5].astype(jnp.bfloat16), "seq", scatter_dimension=1, tiled=True
        ).astype(jnp.float32),
        lax.psum_scatter(
            totals[6].astype(jnp.bfloat16), "seq", scatter_dimension=1, tiled=True
        ).astype(jnp.float32),
    )
    owned = (
        lax.psum_scatter(
            col_sums[0].astype(jnp.bfloat16), "dp", scatter_dimension=0, tiled=True
        ).astype(jnp.float32),
        lax.psum_scatter(
            col_sums[1].astype(jnp.bfloat16), "dp", scatter_dimension=0, tiled=True
        ).astype(jnp.float32),
        lax.psum_scatter(
            col_sums[2].astype(jnp.bfloat16), "dp", scatter_dimension=0, tiled=True
        ).astype(jnp.float32),
        lax.psum_scatter(
            col_sums[3].astype(jnp.bfloat16), "dp", scatter_dimension=0, tiled=True
        ).astype(jnp.float32),
        lax.psum_scatter(
            col_sums[4].astype(jnp.bfloat16), "dp", scatter_dimension=0, tiled=True
        ).astype(jnp.float32),
        lax.psum_scatter(
            col_sums[5].astype(jnp.bfloat16), "dp", scatter_dimension=0, tiled=True
        ).astype(jnp.float32),
        lax.psum_scatter(
            col_sums[6].astype(jnp.bfloat16), "dp", scatter_dimension=0, tiled=True
        ).astype(jnp.float32),
    )
    gain_sums = lax.psum((totals[7], totals[8]), ("dp", "seq"))
    return (
        jnp.concatenate(outputs, axis=0),
        jnp.concatenate(in_grads, axis=0),
        gain_sums[0],
        owned[0],
        owned[1],
        owned[2],
        owned[3],
        gain_sums[1],
        owned[4],
        owned[5],
        owned[6],
    )


F32 = jnp.float32
BF16 = jnp.bfloat16
VMEM_BYTES = 56 * 2**20


def dot(left, right, left_dim, right_dim):
    dims = (((left_dim,), (right_dim,)), ((), ()))
    return lax.dot_general(left, right, dims, preferred_element_type=F32)


def span_slice(inv_ref, place, span):
    return pl.ds(pl.multiple_of(inv_ref[place] * span, span), span)


def lane_pair(ref, rows, inv_ref, block, span):
    first = ref[rows, span_slice(inv_ref, 2 * block, span)]
    second = ref[rows, span_slice(inv_ref, 2 * block + 1, span)]
    return jnp.concatenate([first, second], axis=1)


def row_pair(ref, head, inv_ref, block, span):
    first = ref[head, span_slice(inv_ref, 2 * block, span), :]
    second = ref[head, span_slice(inv_ref, 2 * block + 1, span), :]
    return jnp.concatenate([first, second], axis=0)


def attend_kernel(inv_ref, q_ref, k_ref, v_ref, o_ref, l_ref, acc_ref, *, blocks, span, group):
    wide = 2 * span
    row = lax.broadcasted_iota(jnp.int32, (wide, wide), 0)
    col = lax.broadcasted_iota(jnp.int32, (wide, wide), 1)
    keep = row <= col

    def one_block(block, odd):
        queries = [
            lane_pair(q_ref, slice(HD * h, HD * h + HD), inv_ref, block, span) for h in range(group)
        ]
        acc_ref[...] = jnp.zeros_like(acc_ref)

        def step(first, count, state, diagonal):
            state = list(state)
            keys = [row_pair(k_ref, 0, inv_ref, first + u, span) for u in range(count)]
            values = [lane_pair(v_ref, slice(0, HD), inv_ref, first + u, span) for u in range(count)]
            items = [(u, h) for u in range(count) for h in range(group)]
            scores = [dot(keys[u], queries[h], 1, 0) for u, h in items]
            probs = []
            for (u, h), score in zip(items, scores):
                peak, total = state[h]
                if diagonal and u == count - 1:
                    score = jnp.where(keep, score, neg_big)
                new_peak = jnp.maximum(peak, jnp.max(score, axis=0, keepdims=True))
                prob = jnp.exp(score - new_peak)
                shrink = jnp.exp(peak - new_peak)
                state[h] = (new_peak, total * shrink + jnp.sum(prob, axis=0, keepdims=True))
                probs.append((prob.astype(BF16), shrink))
            for (u, h), (prob, shrink) in zip(items, probs):
                cols = slice(h * wide, (h + 1) * wide)
                acc_ref[:, cols] = acc_ref[:, cols] * shrink + dot(values[u], prob, 1, 0)
            return tuple(state)

        state = tuple(
            (jnp.full((1, wide), neg_big, F32), jnp.zeros((1, wide), F32)) for _ in range(group)
        )
        state = lax.fori_loop(0, block // 4, lambda j, s: step(4 * j, 4, s, False), state)
        state = lax.fori_loop(
            2 * (block // 4), block // 2, lambda j, s: step(2 * j, 2, s, False), state
        )
        state = step(block - 1, 2, state, True) if odd else step(block, 1, state, True)
        mixed = jnp.concatenate(
            [acc_ref[:, wide * h : wide * (h + 1)] * (1.0 / state[h][1]) for h in range(group)], axis=0
        ).astype(BF16)
        logs = jnp.concatenate(
            [p + jnp.log(t) for p, t in state] + [jnp.zeros((8 - group, wide), F32)], axis=0
        )
        for part in range(2):
            where = span_slice(inv_ref, 2 * block + part, span)
            cols = slice(part * span, part * span + span)
            o_ref[:, where] = mixed[:, cols]
            l_ref[0, :, where] = logs[:, cols]

    def two_blocks(pair, _):
        for odd in (0, 1):
            one_block(2 * pair + odd, odd)
        return 0

    lax.fori_loop(0, blocks // 2, two_blocks, 0)


def attention_forward(inv, q_t, k_nat, v_t, span):
    tokens = q_t.shape[1]
    kv_heads = k_nat.shape[0]
    group = q_t.shape[0] // (kv_heads * HD)
    pairs = kv_heads * group * tokens * tokens
    wide_spec = pl.BlockSpec((group * HD, tokens), lambda g, i: (g, 0))
    nat_spec = pl.BlockSpec((1, tokens, HD), lambda g, i: (g, 0, 0))
    return pl.pallas_call(
        functools.partial(attend_kernel, blocks=tokens // (2 * span), span=span, group=group),
        grid_spec=pltpu.PrefetchScalarGridSpec(
            num_scalar_prefetch=1,
            grid=(kv_heads,),
            in_specs=[wide_spec, nat_spec, pl.BlockSpec((HD, tokens), lambda g, i: (g, 0))],
            out_specs=[
                wide_spec,
                pl.BlockSpec((1, 8, tokens), lambda g, i: (g, 0, 0)),
            ],
            scratch_shapes=[pltpu.VMEM((HD, group * 2 * span), F32)],
        ),
        out_shape=[
            jax.ShapeDtypeStruct(q_t.shape, BF16),
            jax.ShapeDtypeStruct((kv_heads, 8, tokens), F32),
        ],
        compiler_params=pltpu.CompilerParams(vmem_limit_bytes=VMEM_BYTES),
        cost_estimate=pl.CostEstimate(
            flops=16 * pairs * HD, bytes_accessed=tokens * 6000, transcendentals=pairs // 2
        ),
        name="attention_forward",
    )(inv, q_t, k_nat, v_t)


def attend_back_kernel(
    inv_ref, q_ref, kt_ref, k_ref, v_ref, o_ref, do_ref, l_ref, cos_ref, sin_ref,
    dq_ref, dk_ref, dv_ref, dk_sum, dv_sum, dq_sum, *, blocks, span, group,
):
    wide = 2 * span
    row = lax.broadcasted_iota(jnp.int32, (wide, wide), 0)
    col = lax.broadcasted_iota(jnp.int32, (wide, wide), 1)
    keep = row <= col
    half = HD // 2
    dk_sum[...] = jnp.zeros_like(dk_sum)
    dv_sum[...] = jnp.zeros_like(dv_sum)

    def rope_back(grad, cos, sin):
        top, low = grad[:half], grad[half:]
        return jnp.concatenate([top * cos + low * sin, low * cos - top * sin], axis=0)

    def one_block(block, odd):
        rows = [slice(HD * h, HD * h + HD) for h in range(group)]
        queries = [lane_pair(q_ref, r, inv_ref, block, span) for r in rows]
        grads = [lane_pair(do_ref, r, inv_ref, block, span) for r in rows]
        logs = lane_pair(l_ref.at[0], slice(None), inv_ref, block, span)
        deltas = [
            jnp.sum(
                lane_pair(o_ref, r, inv_ref, block, span).astype(F32) * grad.astype(F32),
                axis=0,
                keepdims=True,
            )
            for r, grad in zip(rows, grads)
        ]
        dq_sum[...] = jnp.zeros_like(dq_sum)

        def step(first, count, diagonal):
            keys = [row_pair(k_ref, 0, inv_ref, first + u, span) for u in range(count)]
            values = [row_pair(v_ref, 0, inv_ref, first + u, span) for u in range(count)]
            keys_t = [lane_pair(kt_ref, slice(0, HD), inv_ref, first + u, span) for u in range(count)]
            items = [(u, h) for u in range(count) for h in range(group)]
            ahead, ready, dqs, sums = {}, {}, {}, {}

            def products(i):
                u, h = items[i]
                ahead[i] = dot(keys[u], queries[h], 1, 0), dot(values[u], grads[h], 1, 0)

            def softmax_part(i):
                u, h = items[i]
                score, dprob = ahead.pop(i)
                prob = jnp.exp(score - logs[h : h + 1])
                if diagonal and u == count - 1:
                    prob = jnp.where(keep, prob, 0.0)
                ready[i] = prob.astype(BF16), (prob * (dprob - deltas[h])).astype(BF16)

            def gradients(i):
                u, h = items[i]
                prob, dscore = ready.pop(i)
                dq = dot(keys_t[u], dscore, 1, 0)
                dqs[h] = dqs[h] + dq if h in dqs else dq
                if u == count - 1:
                    dq_sum[:, wide * h : wide * (h + 1)] += dqs[h]
                dk, dv = dot(queries[h], dscore, 1, 1), dot(grads[h], prob, 1, 1)
                if u in sums:
                    dk, dv = dk + sums[u][0], dv + sums[u][1]
                sums[u] = dk, dv
                if h == group - 1:
                    place = pl.ds(pl.multiple_of((first + u) * wide, wide), wide)
                    dk_sum[:, place] += dk
                    dv_sum[:, place] += dv

            lead = 2
            for i in range(min(lead, len(items))):
                products(i)
            for i in range(len(items) + 1):
                if i + lead < len(items):
                    products(i + lead)
                if i > 0:
                    gradients(i - 1)
                if i < len(items):
                    softmax_part(i)

        def pair_step(j, _):
            step(2 * j, 2, False)
            return 0

        lax.fori_loop(0, block // 2, pair_step, 0)
        if odd:
            step(block - 1, 2, True)
        else:
            step(block, 1, True)
        cos = lane_pair(cos_ref, slice(None), inv_ref, block, span)
        sin = lane_pair(sin_ref, slice(None), inv_ref, block, span)
        dq = jnp.concatenate(
            [rope_back(dq_sum[:, wide * h : wide * (h + 1)] * HD**-0.5, cos, sin) for h in range(group)],
            axis=0,
        ).astype(BF16)
        place = pl.ds(pl.multiple_of(block * wide, wide), wide)
        dk = rope_back(dk_sum[:, place], cos, sin).astype(BF16)
        dv = dv_sum[:, place].astype(BF16)
        for part in range(2):
            where = span_slice(inv_ref, 2 * block + part, span)
            cols = slice(part * span, part * span + span)
            dq_ref[:, where] = dq[:, cols]
            dk_ref[:, where] = dk[:, cols]
            dv_ref[:, where] = dv[:, cols]

    def two_blocks(step, _):
        for odd in (1, 0):
            one_block(blocks - 2 - 2 * step + odd, odd)
        return 0

    lax.fori_loop(0, blocks // 2, two_blocks, 0)


def attention_backward(inv, q_t, k_t, k_nat, v_nat, o_t, do_t, logs, cos_t, sin_t, span, first, count):
    tokens = q_t.shape[1]
    kv_heads = k_nat.shape[0]
    group = q_t.shape[0] // (kv_heads * HD)
    pairs = count * group * tokens * tokens
    wide_spec = pl.BlockSpec((group * HD, tokens), lambda g, i: (g + first, 0))
    kv_spec = pl.BlockSpec((HD, tokens), lambda g, i: (g + first, 0))
    nat_spec = pl.BlockSpec((1, tokens, HD), lambda g, i: (g + first, 0, 0))
    tab_spec = pl.BlockSpec((HD // 2, tokens), lambda g, i: (0, 0))
    return pl.pallas_call(
        functools.partial(attend_back_kernel, blocks=tokens // (2 * span), span=span, group=group),
        grid_spec=pltpu.PrefetchScalarGridSpec(
            num_scalar_prefetch=1,
            grid=(count,),
            in_specs=[
                wide_spec, kv_spec, nat_spec, nat_spec, wide_spec, wide_spec,
                pl.BlockSpec((1, 8, tokens), lambda g, i: (g + first, 0, 0)), tab_spec, tab_spec,
            ],
            out_specs=[
                pl.BlockSpec((group * HD, tokens), lambda g, i: (g, 0)),
                pl.BlockSpec((HD, tokens), lambda g, i: (g, 0)),
                pl.BlockSpec((HD, tokens), lambda g, i: (g, 0)),
            ],
            scratch_shapes=[
                pltpu.VMEM((HD, tokens), F32),
                pltpu.VMEM((HD, tokens), F32),
                pltpu.VMEM((HD, group * 2 * span), F32),
            ],
        ),
        out_shape=[
            jax.ShapeDtypeStruct((count * group * HD, tokens), BF16),
            jax.ShapeDtypeStruct((count * HD, tokens), BF16),
            jax.ShapeDtypeStruct((count * HD, tokens), BF16),
        ],
        compiler_params=pltpu.CompilerParams(vmem_limit_bytes=VMEM_BYTES),
        cost_estimate=pl.CostEstimate(
            flops=32 * pairs * HD, bytes_accessed=tokens * 9000, transcendentals=pairs // 2
        ),
        name="attention_backward",
    )(inv, q_t, k_t, k_nat, v_nat, o_t, do_t, logs, cos_t, sin_t)


def flip(index, bits):
    for bit in bits:
        index = index + bit * (1 - 2 * ((index // bit) % 2))
    return index


def bits_of(size):
    return [1 << i for i in range(size.bit_length() - 1)]


def seq_stages(seq):
    return [("seq", b) for b in reversed(bits_of(seq)[1:])] + [("seq", b) for b in bits_of(seq)[:1]]


def all_stages(dp, seq):
    return seq_stages(seq) + [("dp", b) for b in reversed(bits_of(dp))]


def rest_chains(dp, seq):
    near, far = [("seq", b) for b in bits_of(seq)[:1]], [("seq", b) for b in reversed(bits_of(seq)[1:])]
    chip = [("dp", b) for b in reversed(bits_of(dp)[1:])]
    return far + near + chip, far + chip + near


def away_place(stages, d, s, my_dp, my_seq):
    place = 0
    for at, (axis, bit) in enumerate(stages):
        mine = ((my_dp if axis == "dp" else my_seq) // bit) % 2
        theirs = ((d if axis == "dp" else s) // bit) % 2
        place = place + (1 << at) * (1 - mine if theirs else mine)
    return place


def arrival_order(stages, dp, seq, my_dp, my_seq):
    ids = jnp.arange(dp * seq, dtype=jnp.int32)
    away = {"dp": (ids // seq) ^ my_dp, "seq": (ids % seq) ^ my_seq}
    place = jnp.zeros_like(ids)
    for at, (axis, bit) in enumerate(stages):
        place = place + (1 << at) * ((away[axis] // bit) % 2)
    return place


def greet(peers):
    barrier = pltpu.get_barrier_semaphore()
    for peer in peers:
        pl.semaphore_signal(barrier, inc=1, device_id=peer, device_id_type=pl.DeviceIdType.MESH)
    pl.semaphore_wait(barrier, len(peers))


def seq_peer(my_dp, my_seq, away, seq):
    return my_dp, flip(my_seq, [b for b in bits_of(seq) if away & b])


def stage_peer(my_dp, my_seq, stage):
    axis, bit = stage
    return (flip(my_dp, [bit]), my_seq) if axis == "dp" else (my_dp, flip(my_seq, [bit]))


def all_peers(my_dp, my_seq, dp, seq):
    peers = [seq_peer(my_dp, my_seq, away, seq) for away in range(1, seq)]
    return peers + [(flip(my_dp, [b]), my_seq) for b in bits_of(dp)]


def bring_kernel(order_ref, freq_ref, gain_one, gain_two, q_ref, k_ref, v_ref, o_ref, gate_ref, up_ref,
                 down_ref, x_ref, inv_ref, cos_ref, sin_ref, one_ref, two_ref, out_ref,
                 all_first, all_second, all_third, first_ref, rest_ref, local_sem, x_send, x_recv, w_send, w_recv, *, dp, seq):
    my_dp, my_seq = lax.axis_index("dp"), lax.axis_index("seq")
    orders = all_stages(dp, seq), seq_stages(seq), seq_stages(seq)
    chains = range(len(orders))
    rows, q_cols = q_ref.shape
    lanes = rest_ref.shape[2]
    kv_cols = k_ref.shape[0]
    blank = lambda cols: jnp.zeros((rows, cols), F32)
    wide = lambda ref: ref[...].astype(F32)
    first_ref[0] = jnp.concatenate(
        [wide(q_ref), wide(k_ref).T, wide(v_ref).T, blank(lanes - q_cols - 2 * kv_cols)], axis=1
    ).astype(BF16)
    rest_ref[0, :rows] = jnp.concatenate([wide(o_ref), blank(lanes - q_cols)], axis=1).astype(BF16)
    rest_ref[0, rows : 2 * rows] = gate_ref[:, :lanes]
    rest_ref[0, 2 * rows : 3 * rows] = up_ref[:, :lanes]
    rest_ref[0, 3 * rows : 4 * rows] = jnp.concatenate([gate_ref[:, lanes:], up_ref[:, lanes:]], axis=1)
    padded = -(-q_cols // 16) * 16
    for t in range(down_ref.shape[1] // lanes):
        piece = down_ref[:, t * lanes : (t + 1) * lanes].astype(F32)
        piece = jnp.concatenate([piece, jnp.zeros((padded - q_cols, lanes), F32)], axis=0).astype(BF16)
        rest_ref[0, 4 * rows + padded * t : 4 * rows + padded * (t + 1)] = piece

    greet(all_peers(my_dp, my_seq, dp, seq))
    at = all_second.shape[1]
    shards_in = first_ref, rest_ref.at[:, pl.ds(0, at)], rest_ref.at[:, pl.ds(at, all_third.shape[1])]
    gathered = all_first, all_second, all_third

    def weight_copy(chain, stage):
        held = 1 << stage
        source = shards_in[chain] if stage == 0 else gathered[chain].at[pl.ds(0, held)]
        return pltpu.make_async_remote_copy(
            src_ref=source,
            dst_ref=gathered[chain].at[pl.ds(held, held)],
            send_sem=w_send.at[chain, stage],
            recv_sem=w_recv.at[chain, stage],
            device_id=stage_peer(my_dp, my_seq, orders[chain][stage]),
            device_id_type=pl.DeviceIdType.MESH,
        )

    copies = [[weight_copy(c, s) for s in range(len(orders[c]))] for c in chains]
    for c in chains:
        copies[c][0].start()
    own = [
        pltpu.make_async_copy(shards_in[c], gathered[c].at[pl.ds(0, 1)], local_sem.at[c]) for c in chains
    ]
    own.append(pltpu.make_async_copy(x_ref.at[my_seq], out_ref.at[my_seq], local_sem.at[len(orders)]))
    for copy in own:
        copy.start()
    moves = []
    for away in range(1, seq):
        peer = seq_peer(my_dp, my_seq, away, seq)
        moves.append(
            pltpu.make_async_remote_copy(
                src_ref=x_ref.at[peer[1]],
                dst_ref=out_ref.at[my_seq],
                send_sem=x_send.at[away - 1],
                recv_sem=x_recv.at[away - 1],
                device_id=peer,
                device_id_type=pl.DeviceIdType.MESH,
            )
        )
    for c in chains:
        own[c].wait()
    for stage in range(1, len(orders[0])):
        for c in chains:
            if stage < len(orders[c]):
                copies[c][stage - 1].wait_recv()
                copies[c][stage].start()
        if stage == 1:
            for move in moves:
                move.start()
            spans = order_ref.shape[0]
            span = cos_ref.shape[1] // spans
            inside = lax.broadcasted_iota(jnp.int32, (1, span), 1)
            for slot in range(spans):
                angles = (inside + order_ref[slot] * span).astype(F32) * freq_ref[...]
                cos_ref[:, slot * span : (slot + 1) * span] = jnp.cos(angles)
                sin_ref[:, slot * span : (slot + 1) * span] = jnp.sin(angles)
                found = 0
                for other in range(spans):
                    found = found + jnp.where(order_ref[other] == slot, other, 0)
                inv_ref[slot] = found
            for source, target in ((gain_one, one_ref), (gain_two, two_ref)):
                row = source[...].astype(F32)[None]
                target[...] = jnp.broadcast_to(row, (8, row.shape[1])).T[:, :1]
    for c in chains:
        copies[c][-1].wait_recv()
        for copy in copies[c]:
            copy.wait_send()
    for move in moves:
        move.wait()
    own[-1].wait()


def bring(span_order, inv_freq, gains, weights, x):
    dp, seq = lax.axis_size("dp"), lax.axis_size("seq")
    stages = len(all_stages(dp, seq))
    lanes = 128
    width = x.shape[1]
    rows, q_cols = weights[0].shape
    rest_rows = 4 * rows + -(-q_cols // 16) * 16 * (weights[-1].shape[1] // lanes)
    cut = rest_rows * 5 // 8 // 16 * 16
    hbm = pl.BlockSpec(memory_space=pl.ANY)
    smem = pl.BlockSpec(memory_space=pltpu.SMEM)
    vmem = pl.BlockSpec(memory_space=pltpu.VMEM)
    table = jax.ShapeDtypeStruct((inv_freq.shape[0], x.shape[0] * x.shape[2]), F32)
    return pl.pallas_call(
        functools.partial(bring_kernel, dp=dp, seq=seq),
        in_specs=[smem] + [vmem] * (3 + len(weights)) + [hbm],
        out_specs=[smem] + [vmem] * 4 + [hbm] * 4,
        out_shape=[
            jax.ShapeDtypeStruct(span_order.shape, jnp.int32),
            table,
            table,
            jax.ShapeDtypeStruct((width, 1), F32),
            jax.ShapeDtypeStruct((width, 1), F32),
            jax.ShapeDtypeStruct(x.shape, x.dtype),
            jax.ShapeDtypeStruct((dp * seq, rows, lanes), x.dtype),
            jax.ShapeDtypeStruct((seq, cut, lanes), x.dtype),
            jax.ShapeDtypeStruct((seq, rest_rows - cut, lanes), x.dtype),
        ],
        scratch_shapes=[
            pltpu.VMEM((1, rows, lanes), BF16),
            pltpu.VMEM((1, rest_rows, lanes), BF16),
            pltpu.SemaphoreType.DMA((4,)),
            pltpu.SemaphoreType.DMA((seq - 1,)),
            pltpu.SemaphoreType.DMA((seq - 1,)),
            pltpu.SemaphoreType.DMA((3, stages)),
            pltpu.SemaphoreType.DMA((3, stages)),
        ],
        compiler_params=pltpu.CompilerParams(
            collective_id=1, has_side_effects=True, vmem_limit_bytes=VMEM_BYTES
        ),
        name="bring",
    )(span_order, inv_freq, *gains, *weights, x)


def qkv_kernel(where_ref, x_ref, gain_ref, packed_ref, cos_ref, sin_ref,
               q_ref, kt_ref, vt_ref, k_ref, v_ref, w_ref, w_wide, *, heads, kv_heads, dp, seq):
    half = HD // 2
    width = w_ref.shape[1]
    q_cols, kv_cols = width // seq, kv_heads * HD // seq
    kv_width = kv_heads * HD

    @pl.when(pl.program_id(0) == 0)
    def _():
        for s in range(seq):
            block = jnp.concatenate([packed_ref[where_ref[d * seq + s]] for d in range(dp)], axis=0)
            turned = block.astype(F32).T
            w_wide[q_cols * s : q_cols * s + q_cols, :] = turned[:q_cols]
            first = width + kv_cols * s
            w_wide[first : first + kv_cols, :] = turned[q_cols : q_cols + kv_cols]
            first += kv_width
            w_wide[first : first + kv_cols, :] = turned[q_cols + kv_cols : q_cols + 2 * kv_cols]
        w_ref[...] = w_wide[...].astype(BF16)

    x = x_ref[0].astype(F32)
    rstd = lax.rsqrt(jnp.mean(x * x, axis=0, keepdims=True) + eps_norm)
    normed = (x * rstd * gain_ref[...]).astype(BF16)
    lin = dot(w_ref[...], normed, 1, 0)
    cos, sin = cos_ref[...], sin_ref[...]
    for head in range(heads + kv_heads):
        top = lin[HD * head : HD * head + half]
        low = lin[HD * head + half : HD * head + HD]
        rot = jnp.concatenate([top * cos - low * sin, low * cos + top * sin], axis=0)
        if head < heads:
            q_ref[HD * head : HD * head + HD, :] = rot.astype(BF16) * jnp.asarray(HD**-0.5, BF16)
        else:
            kv = head - heads
            kt_ref[HD * kv : HD * kv + HD, :] = rot.astype(BF16)
            k_ref[kv] = rot.T.astype(BF16)
    for kv in range(kv_heads):
        first = HD * (heads + kv_heads + kv)
        val = lin[first : first + HD]
        vt_ref[HD * kv : HD * kv + HD, :] = val.astype(BF16)
        v_ref[kv] = val.T.astype(BF16)


def project_qkv(where, x, gain, packed, cos_t, sin_t, heads, kv_heads, rows):
    blocks, width, block = x.shape
    tokens = blocks * block
    feats = (heads + 2 * kv_heads) * HD
    dp, seq = lax.axis_size("dp"), lax.axis_size("seq")
    col = lambda rows: pl.BlockSpec((rows, block), lambda i, w: (0, i))
    nat = pl.BlockSpec((kv_heads, block, HD), lambda i, w: (0, i, 0))
    return pl.pallas_call(
        functools.partial(qkv_kernel, heads=heads, kv_heads=kv_heads, dp=dp, seq=seq),
        grid_spec=pltpu.PrefetchScalarGridSpec(
            num_scalar_prefetch=1,
            grid=(blocks,),
            in_specs=[
                pl.BlockSpec((1, width, block), lambda i, w: (i, 0, 0)),
                pl.BlockSpec((width, 1), lambda i, w: (0, 0)),
                pl.BlockSpec((dp * seq, rows, packed.shape[2]), lambda i, w: (0, 0, 0)),
                col(HD // 2),
                col(HD // 2),
            ],
            out_specs=[
                col(heads * HD), col(kv_heads * HD), col(kv_heads * HD), nat, nat,
                pl.BlockSpec((feats, width), lambda i, w: (0, 0)),
            ],
            scratch_shapes=[pltpu.VMEM((feats, width), F32)],
        ),
        out_shape=[
            jax.ShapeDtypeStruct((heads * HD, tokens), BF16),
            jax.ShapeDtypeStruct((kv_heads * HD, tokens), BF16),
            jax.ShapeDtypeStruct((kv_heads * HD, tokens), BF16),
            jax.ShapeDtypeStruct((kv_heads, tokens, HD), BF16),
            jax.ShapeDtypeStruct((kv_heads, tokens, HD), BF16),
            jax.ShapeDtypeStruct((feats, width), BF16),
        ],
        compiler_params=pltpu.CompilerParams(vmem_limit_bytes=VMEM_BYTES),
        cost_estimate=pl.CostEstimate(
            flops=4 * tokens * width * feats, bytes_accessed=tokens * 5000, transcendentals=0
        ),
        name="project_qkv",
    )(where, x, gain, packed, cos_t, sin_t)


def side_by_side(ref):
    return jnp.concatenate([ref[i] for i in range(ref.shape[0])], axis=1)


def mlp_kernel(
    where_ref, x_ref, mixed_ref, dy_ref, gain_ref, *more, chunk, dp, seq,
):
    packs, more = more[: 2 * dp], more[2 * dp :]
    out_ref, dmid_ref, dmixed_ref = more[:3]
    one_refs, two_refs, gain_grad_ref = more[3:5], more[5:7], more[7]
    (o_w, o_t, gate_w, gate_t, up_w, up_t, down_w, down_t, o_sum, gate_sum, up_sum, down_sum, gain_sum,
     pack, pack_sem) = more[8:]
    step, steps = pl.program_id(0), pl.num_programs(0)
    width, ff = gate_w.shape
    lanes = pack.shape[3]
    rows = width // dp
    o_cols, ff_cols, ff_rows = width // seq, ff // seq, ff // dp
    spare = ff_cols - lanes
    padded = -(-o_cols // 16) * 16

    @pl.when(step == 0)
    def _():
        for total in (o_sum, gate_sum, up_sum, down_sum, gain_sum):
            total[...] = jnp.zeros_like(total)
        fetches = []
        for i in range(dp):
            owner = flip(lax.axis_index("dp"), row_bits(i, dp))
            first = 0
            for source, sem in ((packs[2 * i], pack_sem.at[2 * i]), (packs[2 * i + 1], pack_sem.at[2 * i + 1])):
                span = pl.ds(first, source.shape[1])
                fetches.append(pltpu.make_async_copy(source, pack.at[owner, :, span, :], sem))
                first += source.shape[1]
        for fetch in fetches:
            fetch.start()
        for fetch in fetches:
            fetch.wait()
        for s in range(seq):
            at = where_ref[s]
            stack = lambda first: jnp.concatenate(
                [pack[d, at, first : first + rows, :] for d in range(dp)], axis=0
            )
            o_sum[o_cols * s : o_cols * s + o_cols, :] = stack(0).astype(F32).T[:o_cols]
            gate_t[ff_cols * s : ff_cols * s + lanes, :] = stack(rows).T
            up_t[ff_cols * s : ff_cols * s + lanes, :] = stack(2 * rows).T
            both = stack(3 * rows).T
            gate_t[ff_cols * s + lanes : ff_cols * (s + 1), :] = both[:spare]
            up_t[ff_cols * s + lanes : ff_cols * (s + 1), :] = both[spare : 2 * spare]
            for d in range(dp):
                for t in range(ff_rows // lanes):
                    first = 4 * rows + padded * t
                    piece = pack[d, at, first : first + padded, :].astype(F32)[:o_cols]
                    cols = slice(ff_rows * d + lanes * t, ff_rows * d + lanes * (t + 1))
                    down_sum[o_cols * s : o_cols * s + o_cols, cols] = piece
        for s in range(0, seq, 2):
            for d in range(dp):
                halves = [pack[d, where_ref[s + i], 3 * rows : 4 * rows, :] for i in range(2)]
                for matrix, first, cut in ((gate_w, rows, 0), (up_w, 2 * rows, spare)):
                    pieces = []
                    for i in range(2):
                        pieces.append(pack[d, where_ref[s + i], first : first + rows, :])
                        pieces.append(halves[i][:, cut : cut + spare])
                    cols = slice(ff_cols * s, ff_cols * (s + 2))
                    matrix[rows * d : rows * (d + 1), cols] = jnp.concatenate(pieces, axis=1)
        o_t[...] = o_sum[...].astype(BF16)
        o_w[...] = o_sum[...].T.astype(BF16)
        down_t[...] = down_sum[...].astype(BF16)
        for first in range(0, ff, lanes):
            part = slice(first, first + lanes)
            down_w[part, :] = down_t[:, part].T
        o_sum[...] = jnp.zeros_like(o_sum)
        down_sum[...] = jnp.zeros_like(down_sum)

    gain = gain_ref[...]
    mixed = mixed_ref[...]
    mid = dot(o_t[...], mixed, 1, 0) + side_by_side(x_ref).astype(F32)
    rstd = lax.rsqrt(jnp.mean(mid * mid, axis=0, keepdims=True) + eps_norm)
    normed = (mid * rstd * gain).astype(BF16)
    dy = side_by_side(dy_ref)
    added = jnp.zeros_like(mid)
    dnormed = jnp.zeros_like(mid)
    for first in range(0, ff, chunk):
        part = slice(first, first + chunk)
        gate = dot(gate_t[part, :], normed, 1, 0)
        up = dot(up_t[part, :], normed, 1, 0)
        dinner = dot(down_w[part, :], dy, 1, 0)
        sig = 1.0 / (1.0 + jnp.exp(-gate))
        silu = gate * sig
        inner = (silu * up).astype(BF16)
        dup = (dinner * silu).astype(BF16)
        dgate = (dinner * up * sig * (1.0 + gate * (1.0 - sig))).astype(BF16)
        added += dot(down_t[:, part], inner, 1, 0)
        dnormed += dot(gate_w[:, part], dgate, 1, 0)
        dnormed += dot(up_w[:, part], dup, 1, 0)
        down_sum[:, part] += dot(dy, inner, 1, 1)
        gate_sum[:, part] += dot(normed, dgate, 1, 1)
        up_sum[:, part] += dot(normed, dup, 1, 1)
    out = (mid + added).astype(BF16)
    scaled_mid = mid * rstd
    product = dnormed * scaled_mid
    gain_sum[...] += sum(product[:, c : c + lanes] for c in range(0, product.shape[1], lanes))
    scaled = dnormed * gain
    pull = jnp.mean(scaled * mid, axis=0, keepdims=True)
    dmid = dy.astype(F32) + rstd * scaled - scaled_mid * (rstd * rstd * pull)
    dmid_low = dmid.astype(BF16)
    block = out_ref.shape[2]
    for i in range(out_ref.shape[0]):
        out_ref[i] = out[:, block * i : block * (i + 1)]
        dmid_ref[i] = dmid[:, block * i : block * (i + 1)]
    o_sum[...] += dot(dmid_low, mixed, 1, 1)
    dmixed_ref[...] = dot(o_w[...], dmid_low, 1, 0).astype(BF16)

    @pl.when(step == steps - 1)
    def _():
        gain_grad_ref[...] = jnp.sum(gain_sum[...].T, axis=0, keepdims=True)
        my_dp, my_seq = lax.axis_index("dp"), lax.axis_index("seq")
        upper = my_dp % 2 == 1

        def put(refs, place, first, even, odd):
            keep_ref, give_ref = refs
            span = slice(first, first + even.shape[0])
            keep_ref[place, span, :] = jnp.where(upper, odd, even).astype(BF16)
            give_ref[place, span, :] = jnp.where(upper, even, odd).astype(BF16)

        blank = jnp.zeros((lanes - o_cols, width), F32)
        edge = jnp.zeros((padded - o_cols, lanes), F32)
        for s in range(seq):
            o_piece = jnp.concatenate([o_sum[o_cols * s : o_cols * (s + 1), :], blank], axis=0).T
            pair_cols = slice(ff_cols * (s - s % 2), ff_cols * (s - s % 2 + 2))
            shift = ff_cols * (s % 2)
            for d in range(0, dp, 2):
                bands = slice(rows * d, rows * (d + 1)), slice(rows * (d + 1), rows * (d + 2))
                one, two = [away_place(c, d, s, my_dp, my_seq) for c in rest_chains(dp, seq)]
                put(one_refs, one, 0, o_piece[bands[0]], o_piece[bands[1]])
                rests = []
                for i, total in enumerate((gate_sum, up_sum)):
                    wide = [total[band, pair_cols] for band in bands]
                    put(one_refs, one, rows * (i + 1), *[w[:, shift : shift + lanes] for w in wide])
                    rests.append([w[:, shift + lanes : shift + ff_cols] for w in wide])
                put(two_refs, two, 0, *[jnp.concatenate([g, u], axis=1) for g, u in zip(*rests)])
                for t in range(ff_rows // lanes):
                    pair = []
                    for at in (d, d + 1):
                        cols = slice(ff_rows * at + lanes * t, ff_rows * at + lanes * (t + 1))
                        pair.append(
                            jnp.concatenate([down_sum[o_cols * s : o_cols * (s + 1), cols], edge], axis=0)
                        )
                    put(two_refs, two, rows + padded * t, *pair)


def row_bits(at, dp):
    return [b for i, b in enumerate(reversed(bits_of(dp))) if (at >> i) & 1]


def over_rows(array, mask):
    return lax.ppermute(array, "dp", [(i, i ^ mask) for i in range(lax.axis_size("dp"))])


def mlp_both(where, x, mixed, dy, gain, packs, ff, batch=2, chunk=768):
    blocks, width, block = x.shape
    tokens = blocks * block
    dp, seq = lax.axis_size("dp"), lax.axis_size("seq")
    grad_rows, lanes = packs[0].shape[1] + packs[1].shape[1], packs[0].shape[2]
    first_rows = 3 * (width // dp)
    one = dp * seq // 2, first_rows, lanes
    two = dp * seq // 2, grad_rows - first_rows, lanes
    tok = pl.BlockSpec((batch, width, block), lambda i, w: (i, 0, 0))
    col = pl.BlockSpec((width, batch * block), lambda i, w: (0, i))
    once = lambda shape: pl.BlockSpec(
        shape, lambda i, w: (0,) * len(shape), pipeline_mode=pl.Buffered(1)
    )
    hbm = pl.BlockSpec(memory_space=pl.ANY)
    return pl.pallas_call(
        functools.partial(mlp_kernel, chunk=chunk, dp=dp, seq=seq),
        grid_spec=pltpu.PrefetchScalarGridSpec(
            num_scalar_prefetch=1,
            grid=(blocks // batch,),
            in_specs=[tok, col, tok, once((width, 1))] + [hbm] * (2 * dp),
            out_specs=[tok, tok, col, once(one), once(one), once(two), once(two), once((1, width))],
            scratch_shapes=[
                pltpu.VMEM((width, width), BF16),
                pltpu.VMEM((width, width), BF16),
                pltpu.VMEM((width, ff), BF16),
                pltpu.VMEM((ff, width), BF16),
                pltpu.VMEM((width, ff), BF16),
                pltpu.VMEM((ff, width), BF16),
                pltpu.VMEM((ff, width), BF16),
                pltpu.VMEM((width, ff), BF16),
                pltpu.VMEM((width, width), F32),
                pltpu.VMEM((width, ff), F32),
                pltpu.VMEM((width, ff), F32),
                pltpu.VMEM((width, ff), F32),
                pltpu.VMEM((width, lanes), F32),
                pltpu.VMEM((dp, packs[0].shape[0], grad_rows, lanes), BF16),
                pltpu.SemaphoreType.DMA((2 * dp,)),
            ],
        ),
        out_shape=[
            jax.ShapeDtypeStruct(x.shape, BF16),
            jax.ShapeDtypeStruct(x.shape, F32),
            jax.ShapeDtypeStruct((width, tokens), BF16),
            jax.ShapeDtypeStruct(one, BF16),
            jax.ShapeDtypeStruct(one, BF16),
            jax.ShapeDtypeStruct(two, BF16),
            jax.ShapeDtypeStruct(two, BF16),
            jax.ShapeDtypeStruct((1, width), F32),
        ],
        compiler_params=pltpu.CompilerParams(vmem_limit_bytes=60 * 2**20),
        cost_estimate=pl.CostEstimate(
            flops=2 * tokens * width * (9 * ff + 3 * width),
            bytes_accessed=tokens * width * 14,
            transcendentals=tokens * ff,
        ),
        name="mlp_both",
    )(where, x, mixed, dy, gain, *packs)


def across(index, other, size):
    for bit in bits_of(size):
        index = index + bit * ((other // bit) % 2) * (1 - 2 * ((index // bit) % 2))
    return index


def add_blocks(total_ref, term_ref, count, total_first=0, term_first=0):
    def one(i, _):
        total = total_ref[total_first + i].astype(F32) + term_ref[term_first + i].astype(F32)
        total_ref[total_first + i] = total.astype(BF16)
        return 0

    lax.fori_loop(0, count, one, 0)


def finish_kernel(
    x_ref, dmid_ref, dq_one, dq_two, dk_one, dk_two, dv_one, dv_two, gain_ref, w_t_ref, other_gain_ref,
    keep_one, keep_two, came_one, came_two, out_ref, gains_ref, qkv_ref, one_ref, two_ref,
    w_nat, w_sum, gain_sum, din, packed, landed, one, one_came, one_landed, two, two_came, two_landed,
    gain_held, gain_landed,
    own_sem, d_send, d_recv, r_send, r_recv, g_send, g_recv, fetch_sem, *, dp, seq, kv_width,
):
    step, steps = pl.program_id(0), seq // 2
    my_dp, my_seq = lax.axis_index("dp"), lax.axis_index("seq")
    width = w_nat.shape[0]
    lanes = packed.shape[2]
    rows = width // dp
    q_cols, kv_cols = width // seq, kv_width // seq
    orders = [all_stages(dp, seq), *[chain[:-1] for chain in rest_chains(dp, seq)]]
    held = [packed, one, two]
    arrived = [landed, one_landed, two_landed]
    fetches = [
        pltpu.make_async_copy(source, target, fetch_sem.at[i])
        for i, (source, target) in enumerate(
            ((keep_one, one), (keep_two, two), (came_one, one_came), (came_two, two_came))
        )
    ]

    def halve(chain, turn):
        at = len(orders[chain]) - 1 - turn
        half = 1 << at
        return pltpu.make_async_remote_copy(
            src_ref=held[chain].at[pl.ds(half, half)],
            dst_ref=arrived[chain].at[pl.ds(half, half)],
            send_sem=r_send.at[chain, turn],
            recv_sem=r_recv.at[chain, turn],
            device_id=stage_peer(my_dp, my_seq, orders[chain][at]),
            device_id_type=pl.DeviceIdType.MESH,
        )

    def take(chain, turn):
        halve(chain, turn).wait_recv()
        half = 1 << (len(orders[chain]) - 1 - turn)
        if half > 1:
            add_blocks(held[chain], arrived[chain], half, 0, half)
            halve(chain, turn + 1).start()

    def result(chain):
        return held[chain][0].astype(F32) + arrived[chain][1].astype(F32)

    @pl.when(step == 0)
    def _():
        for fetch in fetches:
            fetch.start()
        greet(all_peers(my_dp, my_seq, dp, seq))
        for fetch in fetches:
            fetch.wait()
        for chain, came in ((1, one_came), (2, two_came)):
            add_blocks(held[chain], came, came.shape[0])
            halve(chain, 0).start()
        w_sum[...] = jnp.zeros_like(w_sum)
        gain_sum[...] = jnp.zeros_like(gain_sum)
        w_nat[...] = w_t_ref[...].T

    gain = gain_ref[...]
    x = side_by_side(x_ref).astype(F32)
    rstd = lax.rsqrt(jnp.mean(x * x, axis=0, keepdims=True) + eps_norm)
    scaled_x = x * rstd
    normed = (scaled_x * gain).astype(BF16)
    dlins = dq_one, dq_two, dk_one, dk_two, dv_one, dv_two
    dlin = jnp.concatenate([ref[...] for ref in dlins], axis=0)
    w_sum[...] += dot(dlin, normed, 1, 1)
    dnormed = dot(w_nat[...], dlin, 1, 0)
    product = dnormed * scaled_x
    gain_sum[...] += sum(product[:, c : c + lanes] for c in range(0, product.shape[1], lanes))
    scaled = dnormed * gain
    pull = jnp.mean(scaled * x, axis=0, keepdims=True)
    total = side_by_side(dmid_ref) + rstd * scaled - scaled_x * (rstd * rstd * pull)
    pair = across(my_seq // 2, steps - 1 - step, seq // 2)
    block = din.shape[2]
    for i in range(2):
        din[2 * pair + i] = total[:, block * i : block * (i + 1)].astype(BF16)

    def move(away):
        peer = seq_peer(my_dp, my_seq, away, seq)
        return pltpu.make_async_remote_copy(
            src_ref=din.at[peer[1]],
            dst_ref=out_ref.at[my_seq],
            send_sem=d_send.at[away - 1],
            recv_sem=d_recv.at[away - 1],
            device_id=peer,
            device_id_type=pl.DeviceIdType.MESH,
        )

    @pl.when(step == 0)
    def _():
        for away in range(seq - 2, seq):
            move(away).start()

    @pl.when(step == max(steps - 2, 0))
    def _():
        for chain in (1, 2):
            take(chain, 0)

    @pl.when(step == steps - 1)
    def _():
        for away in range(seq // 2, seq - 2):
            move(away).start()
        move(1).start()
        own = pltpu.make_async_copy(din.at[my_seq], out_ref.at[my_seq], own_sem)
        own.start()
        blank = jnp.zeros((lanes - q_cols - 2 * kv_cols, width), F32)
        for s in range(seq):
            first = width + kv_cols * s
            piece = jnp.concatenate(
                [
                    w_sum[q_cols * s : q_cols * (s + 1), :],
                    w_sum[first : first + kv_cols, :],
                    w_sum[first + kv_width : first + kv_width + kv_cols, :],
                    blank,
                ],
                axis=0,
            ).T.astype(BF16)
            for d in range(dp):
                packed[away_place(orders[0], d, s, my_dp, my_seq)] = piece[rows * d : rows * (d + 1)]
        gain_row = jnp.sum(gain_sum[...].T, axis=0, keepdims=True)
        gain_held[0] = jnp.concatenate(
            [gain_row, other_gain_ref[...], jnp.zeros((6, width), F32)], axis=0
        )
        turns = len(orders[0])
        gain_copies = [
            pltpu.make_async_remote_copy(
                src_ref=gain_held.at[turn],
                dst_ref=gain_landed.at[turn],
                send_sem=g_send.at[turn],
                recv_sem=g_recv.at[turn],
                device_id=stage_peer(my_dp, my_seq, orders[0][turns - 1 - turn]),
                device_id_type=pl.DeviceIdType.MESH,
            )
            for turn in range(turns)
        ]
        halve(0, 0).start()
        gain_copies[0].start()
        for turn in range(turns):
            gain_copies[turn].wait_recv()
            gain_held[turn + 1] = gain_held[turn] + gain_landed[turn]
            if turn + 1 < turns:
                gain_copies[turn + 1].start()
            take(0, turn)
            if turn == turns - 3:
                for chain in (1, 2):
                    take(chain, 1)
                for away in range(2, seq // 2):
                    move(away).start()
            if turn == turns - 2:
                for chain in (1, 2):
                    take(chain, 2)
        gains_ref[...] = gain_held[turns]
        qkv_ref[...], one_ref[...], two_ref[...] = result(0), result(1), result(2)
        for copy in gain_copies:
            copy.wait_send()
        for chain in range(3):
            for turn in range(len(orders[chain])):
                halve(chain, turn).wait_send()
        for away in range(1, seq):
            move(away).wait()
        own.wait()


def finish(x, dmid, dlins, gain, w_t, other_gain, keep_one, keep_two, came_one, came_two):
    blocks, width, block = x.shape
    tokens = blocks * block
    feats = w_t.shape[0]
    kv_width = (feats - width) // 2
    lanes = keep_one.shape[2]
    dp, seq = lax.axis_size("dp"), lax.axis_size("seq")
    rows = width // dp
    stages = len(all_stages(dp, seq))

    def pair(i):
        return across(lax.axis_index("seq") // 2, seq // 2 - 1 - i, seq // 2)

    tok = pl.BlockSpec((2, width, block), lambda i: (pair(i), 0, 0))
    col = lambda rows: pl.BlockSpec((rows, 2 * block), lambda i: (0, pair(i)))
    once = lambda shape: pl.BlockSpec(shape, lambda i: (0,) * len(shape), pipeline_mode=pl.Buffered(1))
    hbm = pl.BlockSpec(memory_space=pl.ANY)
    small = [(8, width), (rows, lanes), keep_one.shape[1:], keep_two.shape[1:]]
    return pl.pallas_call(
        functools.partial(finish_kernel, dp=dp, seq=seq, kv_width=kv_width),
        grid=(blocks // 2,),
        in_specs=[
            tok, tok, *[col(d.shape[0]) for d in dlins],
            once((width, 1)), once((feats, width)), once((1, width)), hbm, hbm, hbm, hbm,
        ],
        out_specs=[hbm] + [once(shape) for shape in small],
        out_shape=[jax.ShapeDtypeStruct(x.shape, BF16)] + [jax.ShapeDtypeStruct(shape, F32) for shape in small],
        scratch_shapes=[
            pltpu.VMEM((width, feats), BF16),
            pltpu.VMEM((feats, width), F32),
            pltpu.VMEM((width, lanes), F32),
            pltpu.VMEM(x.shape, BF16),
            pltpu.VMEM((dp * seq, rows, lanes), BF16),
            pltpu.VMEM((dp * seq, rows, lanes), BF16),
            *[pltpu.VMEM(keep_one.shape, BF16)] * 3,
            *[pltpu.VMEM(keep_two.shape, BF16)] * 3,
            pltpu.VMEM((stages + 1, 8, width), F32),
            pltpu.VMEM((stages, 8, width), F32),
            pltpu.SemaphoreType.DMA,
            pltpu.SemaphoreType.DMA((seq - 1,)),
            pltpu.SemaphoreType.DMA((seq - 1,)),
            pltpu.SemaphoreType.DMA((3, stages)),
            pltpu.SemaphoreType.DMA((3, stages)),
            pltpu.SemaphoreType.DMA((stages,)),
            pltpu.SemaphoreType.DMA((stages,)),
            pltpu.SemaphoreType.DMA((4,)),
        ],
        compiler_params=pltpu.CompilerParams(
            collective_id=2, has_side_effects=True, vmem_limit_bytes=VMEM_BYTES
        ),
        cost_estimate=pl.CostEstimate(
            flops=4 * tokens * width * feats, bytes_accessed=tokens * width * 12, transcendentals=0
        ),
        name="finish",
    )(x, dmid, *dlins, gain, w_t, other_gain, keep_one, keep_two, came_one, came_two)


def deliver_kernel(
    din_ref, gains_ref, qkv_ref, one_ref, two_ref,
    out_ref, gain_one, gain_two, q_ref, k_ref, v_ref, o_ref, gate_ref, up_ref, down_ref,
):
    out_ref[...] = din_ref[...].astype(F32)

    @pl.when(pl.program_id(0) == 0)
    def _():
        rows, q_cols = q_ref.shape
        kv_cols, lanes = k_ref.shape[0], qkv_ref.shape[1]
        spare = gate_ref.shape[1] - lanes
        padded = -(-q_cols // 16) * 16
        gain_one[...] = gains_ref[0]
        gain_two[...] = gains_ref[1]
        qkv = qkv_ref[...]
        turned = qkv.T
        q_ref[...] = qkv[:, :q_cols]
        k_ref[...] = turned[q_cols : q_cols + kv_cols]
        v_ref[...] = turned[q_cols + kv_cols : q_cols + 2 * kv_cols]
        o_ref[...] = one_ref[:rows, :q_cols]
        both = two_ref[:rows]
        gate_ref[...] = jnp.concatenate([one_ref[rows : 2 * rows], both[:, :spare]], axis=1)
        up_ref[...] = jnp.concatenate([one_ref[2 * rows : 3 * rows], both[:, spare : 2 * spare]], axis=1)
        for t in range(down_ref.shape[1] // lanes):
            at = rows + padded * t
            down_ref[:, lanes * t : lanes * (t + 1)] = two_ref[at : at + q_cols]


def deliver(din, gains, qkv, one, two, kv_cols, ff):
    blocks, width, block = din.shape
    rows = qkv.shape[0]
    dp, seq = lax.axis_size("dp"), lax.axis_size("seq")
    tok = pl.BlockSpec((2, width, block), lambda i: (i, 0, 0))
    once = lambda shape: pl.BlockSpec(shape, lambda i: (0,) * len(shape), pipeline_mode=pl.Buffered(1))
    small = [
        (width,),
        (width,),
        (rows, width // seq),
        (kv_cols, rows),
        (kv_cols, rows),
        (rows, width // seq),
        (rows, ff // seq),
        (rows, ff // seq),
        (width // seq, ff // dp),
    ]
    return pl.pallas_call(
        deliver_kernel,
        grid=(blocks // 2,),
        in_specs=[tok] + [once(a.shape) for a in (gains, qkv, one, two)],
        out_specs=[tok] + [once(shape) for shape in small],
        out_shape=[jax.ShapeDtypeStruct(shape, F32) for shape in [din.shape] + small],
        compiler_params=pltpu.CompilerParams(vmem_limit_bytes=VMEM_BYTES),
        name="deliver",
    )(din, gains, qkv, one, two)


def exchange(blocks):
    return lax.all_to_all(blocks, "seq", 0, 0, tiled=True)


def shards_sequences(
    hidden_in, span_order, attn_gain, q_weight, k_weight, v_weight, o_weight, mlp_gain,
    gate_weight, up_weight, down_weight, out_grad,
):
    lanes = 128
    seqs, slots, width = hidden_in.shape
    dp, seq = lax.axis_size("dp"), lax.axis_size("seq")
    tokens = slots * seq
    span = tokens // span_order.shape[0]
    heads = width // HD
    kv_heads = k_weight.shape[1] * seq // HD
    rows, q_cols = q_weight.shape
    kv_cols = k_weight.shape[1]
    ff = down_weight.shape[0] * dp
    ff_rows = down_weight.shape[0]
    padded = -(-q_cols // 16) * 16

    inv_freq = np.float32(rope_base ** (-2.0 * np.arange(HD // 2) / HD))
    inv, cos_t, sin_t, gain_one, gain_two, x, first_all, straight, hopping = bring(
        span_order,
        inv_freq[:, None],
        (attn_gain, mlp_gain),
        (q_weight, k_weight.T, v_weight.T, o_weight, gate_weight, up_weight, down_weight.T),
        hidden_in.transpose(0, 2, 1),
    )
    out_grad, x = lax.optimization_barrier((out_grad, x))
    masks = [sum(row_bits(i, dp)) for i in range(dp)]
    straight_all = [straight] + [over_rows(straight, m) for m in masks[1:]]
    hopping_all = [hopping if m == 0 else over_rows(hopping, m) if m & (m - 1) == 0 else None for m in masks]
    dy = exchange(out_grad.transpose(0, 2, 1))

    my_dp, my_seq = lax.axis_index("dp"), lax.axis_index("seq")
    where_first = arrival_order(all_stages(dp, seq), dp, seq, my_dp, my_seq)
    where_second = arrival_order(seq_stages(seq), dp, seq, my_dp, my_seq)[:seq]
    q_t, k_t, v_t, k_nat, v_nat, w_t = project_qkv(
        where_first, x, gain_one, first_all, cos_t, sin_t, heads, kv_heads, rows
    )
    o_t, logs = attention_forward(inv, q_t, k_nat, v_t, span)
    hopping_all, o_t = lax.optimization_barrier((hopping_all, o_t))
    for i, mask in enumerate(masks):
        if hopping_all[i] is None:
            low = mask & -mask
            hopping_all[i] = over_rows(hopping_all[masks.index(mask - low)], low)
    packs = [part for pair in zip(straight_all, hopping_all) for part in pair]
    out, dmid, do_t, keep_one, give_one, keep_two, give_two, gain_two_term = mlp_both(
        where_second, x, o_t, dy, gain_two, packs, ff
    )
    came_one, came_two = over_rows(give_one, 1), over_rows(give_two, 1)
    hidden_out = exchange(out).transpose(0, 2, 1)

    def back(queries, *heads):
        return attention_backward(
            inv, queries, k_t, k_nat, v_nat, o_t, do_t, logs, cos_t, sin_t, span, *heads
        )

    parts = [back(q_t, 0, 1)]
    came_one, came_two, parts[0] = lax.optimization_barrier((came_one, came_two, parts[0]))
    half = dp * seq // 4
    add = lambda a, b: (a.astype(F32) + b.astype(F32)).astype(BF16)
    sums = [
        (add(keep[:half], came[:half]), add(keep[half:], came[half:]))
        for keep, came in ((keep_one, came_one), (keep_two, came_two))
    ]
    sums, q_t = lax.optimization_barrier((sums, q_t))
    crossed = [
        lax.ppermute(high, axis, [(i, i ^ bit) for i in range(lax.axis_size(axis))])
        for (_, high), (axis, bit) in zip(sums, [chain[-1] for chain in rest_chains(dp, seq)])
    ]
    parts.append(back(q_t, 1, kv_heads - 1))
    dlins = [part[i] for i in range(3) for part in parts]
    din, gains, qkv_sum, one_sum, two_sum = finish(
        x, dmid, dlins, gain_one, w_t, gain_two_term, sums[0][0], sums[1][0], *crossed
    )
    grad_in, gain_one_sum, gain_two_sum, q_sum, k_sum, v_sum, o_sum, gate_sum, up_sum, down_sum = deliver(
        din, gains, qkv_sum, one_sum, two_sum, kv_cols, ff
    )
    return (
        hidden_out,
        grad_in.transpose(0, 2, 1),
        gain_one_sum,
        q_sum,
        k_sum.T,
        v_sum.T,
        o_sum,
        gain_two_sum,
        gate_sum,
        up_sum,
        down_sum.T,
    )


def shards(*args):
    seqs, spans = args[0].shape[0], args[1].shape[0]
    if seqs == lax.axis_size("seq") and spans % 4 == 0:
        return shards_sequences(*args)
    return shards_general(*args)


def solution(mesh):
    placed = (
        P("dp", "seq", None),
        P(),
        P(),
        P("dp", "seq"),
        P("dp", "seq"),
        P("dp", "seq"),
        P("dp", "seq"),
        P(),
        P("dp", "seq"),
        P("dp", "seq"),
        P("dp", "seq"),
        P("dp", "seq", None),
    )
    return jax.shard_map(
        shards,
        mesh=mesh,
        in_specs=placed,
        out_specs=(
            P("dp", "seq", None),
            P("dp", "seq", None),
            P(),
            P("dp", "seq"),
            P("dp", "seq"),
            P("dp", "seq"),
            P("dp", "seq"),
            P(),
            P("dp", "seq"),
            P("dp", "seq"),
            P("dp", "seq"),
        ),
        check_vma=False,
    )
```

```python
import functools

import jax
import jax.numpy as jnp
import numpy as np
from jax import lax
from jax.experimental import pallas as pl
from jax.experimental.pallas import tpu as pltpu
from jax.sharding import PartitionSpec as P

HD = 64
MICRO = 2


eps_norm = 1e-05
rope_base = 100000.0
neg_big = -1e30


def slot_positions(slot_ids, span_order, span_len):
    span_ids = slot_ids // span_len
    span_hits = span_ids[:, None] == jnp.arange(span_order.shape[0], dtype=jnp.int32)[None, :]
    starts = jnp.sum(jnp.where(span_hits, span_order[None, :], 0), axis=1)
    return starts * span_len + slot_ids % span_len


def rope_tables(slot_pos):
    half_width = HD // 2
    inv_freq = rope_base ** (-(jnp.arange(half_width, dtype=jnp.float32) * 2.0) / HD)
    angles = slot_pos.astype(jnp.float32)[:, None] * inv_freq[None, :]
    cosine = jnp.concatenate([jnp.cos(angles), jnp.cos(angles)], axis=1)
    sine_tab = jnp.concatenate([jnp.sin(angles), jnp.sin(angles)], axis=1)
    return (cosine[:, None, :], sine_tab[:, None, :])


def rotate(vector, cosine, sine_tab):
    half_width = vector.shape[-1] // 2
    turned = jnp.concatenate([-vector[..., half_width:], vector[..., :half_width]], axis=-1)
    return vector * cosine + turned * sine_tab


def rotate_back(grad_out, cosine, sine_tab):
    half_width = grad_out.shape[-1] // 2
    scaled = grad_out * sine_tab
    turned = jnp.concatenate([scaled[..., half_width:], -scaled[..., :half_width]], axis=-1)
    return grad_out * cosine + turned


def norm_back(vector, rstd_vec, gain_vec, grad_n):
    scaled = grad_n * gain_vec
    gain_term = jnp.sum(grad_n * vector * rstd_vec, axis=0)
    grad_vec = rstd_vec * scaled - vector * rstd_vec**3 * jnp.mean(
        scaled * vector, axis=-1, keepdims=True
    )
    return (grad_vec, gain_term)


def add_tuples(old_sums, new_terms):
    if old_sums is None:
        return tuple(new_terms)
    return tuple((old_sum + new_term for old_sum, new_term in zip(old_sums, new_terms)))


def shards_general(
    hidden_in,
    span_order,
    attn_gain,
    q_weight,
    k_weight,
    v_weight,
    o_weight,
    mlp_gain,
    gate_weight,
    up_weight,
    down_weight,
    out_grad,
):
    local_seqs, row_count, model_width = hidden_in.shape
    seq_parts = lax.axis_size("seq")
    full_length = row_count * seq_parts
    span_len = full_length // (2 * seq_parts)
    per_micro = local_seqs // MICRO
    kv_width = k_weight.shape[1] * seq_parts
    kv_heads = kv_width // HD
    head_count = model_width // HD
    group_size = head_count // kv_heads
    tok_count = per_micro * row_count
    score_scale = HD ** (-0.5)
    own_slots = lax.axis_index("seq") * row_count + jnp.arange(row_count, dtype=jnp.int32)
    own_pos = slot_positions(own_slots, span_order, span_len)
    all_pos = slot_positions(jnp.arange(full_length, dtype=jnp.int32), span_order, span_len)
    allowed = own_pos[:, None] >= all_pos[None, :]
    cos_own, sin_own = rope_tables(own_pos)
    gain_attn = attn_gain.astype(jnp.float32)
    gain_mlp = mlp_gain.astype(jnp.float32)

    def attend(inputs):
        queries, key_rows, value_rows = inputs
        query_grp = queries.reshape(row_count, kv_heads, group_size, HD)
        key_grp = key_rows.reshape(full_length, kv_heads, HD)
        value_grp = value_rows.reshape(full_length, kv_heads, HD)
        scores = (
            jnp.einsum("rkgd,lkd->kgrl", query_grp, key_grp, preferred_element_type=jnp.float32)
            * score_scale
        )
        scores = jnp.where(allowed, scores, neg_big)
        row_peak = jnp.max(scores, axis=-1, keepdims=True)
        exp_scores = jnp.exp(scores - row_peak)
        row_total = jnp.sum(exp_scores, axis=-1, keepdims=True)
        attn_probs = exp_scores / row_total
        log_total = row_peak + jnp.log(row_total)
        mixed = jnp.einsum(
            "kgrl,lkd->rkgd",
            attn_probs.astype(jnp.bfloat16),
            value_grp,
            preferred_element_type=jnp.float32,
        )
        return (mixed.astype(jnp.bfloat16).reshape(row_count, model_width), log_total)

    def attend_back(inputs):
        queries, key_rows, value_rows, grad_mix, log_total = inputs
        query_grp = queries.reshape(row_count, kv_heads, group_size, HD)
        key_grp = key_rows.reshape(full_length, kv_heads, HD)
        value_grp = value_rows.reshape(full_length, kv_heads, HD)
        grad_grp = grad_mix.reshape(row_count, kv_heads, group_size, HD)
        scores = (
            jnp.einsum("rkgd,lkd->kgrl", query_grp, key_grp, preferred_element_type=jnp.float32)
            * score_scale
        )
        scores = jnp.where(allowed, scores, neg_big)
        attn_probs = jnp.exp(scores - log_total)
        probs_low = attn_probs.astype(jnp.bfloat16)
        grad_probs = jnp.einsum(
            "rkgd,lkd->kgrl", grad_grp, value_grp, preferred_element_type=jnp.float32
        )
        row_delta = jnp.sum(attn_probs * grad_probs, axis=-1, keepdims=True)
        grad_scores = (attn_probs * (grad_probs - row_delta)).astype(jnp.bfloat16)
        grad_query_rot = (
            jnp.einsum("kgrl,lkd->rkgd", grad_scores, key_grp, preferred_element_type=jnp.float32)
            * score_scale
        )
        key_term = (
            jnp.einsum("kgrl,rkgd->lkd", grad_scores, query_grp, preferred_element_type=jnp.float32)
            * score_scale
        )
        value_term = jnp.einsum(
            "kgrl,rkgd->lkd", probs_low, grad_grp, preferred_element_type=jnp.float32
        )
        return (
            grad_query_rot.reshape(row_count, head_count, HD),
            key_term.reshape(full_length, kv_width),
            value_term.reshape(full_length, kv_width),
        )

    outputs = []
    in_grads = []
    totals = None
    for micro_idx in range(MICRO):
        first_seq = micro_idx * per_micro
        block_in = hidden_in[first_seq : first_seq + per_micro]
        block_grad = out_grad[first_seq : first_seq + per_micro]
        col_parts = (
            lax.all_gather(q_weight, "seq", axis=1, tiled=True),
            lax.all_gather(k_weight, "seq", axis=1, tiled=True),
            lax.all_gather(v_weight, "seq", axis=1, tiled=True),
            lax.all_gather(o_weight, "seq", axis=1, tiled=True),
            lax.all_gather(gate_weight, "seq", axis=1, tiled=True),
            lax.all_gather(up_weight, "seq", axis=1, tiled=True),
            lax.all_gather(down_weight, "seq", axis=1, tiled=True),
        )
        query_mat, key_mat, value_mat, out_mat, gate_mat, up_mat, down_mat = (
            lax.all_gather(col_parts[0], "dp", axis=0, tiled=True),
            lax.all_gather(col_parts[1], "dp", axis=0, tiled=True),
            lax.all_gather(col_parts[2], "dp", axis=0, tiled=True),
            lax.all_gather(col_parts[3], "dp", axis=0, tiled=True),
            lax.all_gather(col_parts[4], "dp", axis=0, tiled=True),
            lax.all_gather(col_parts[5], "dp", axis=0, tiled=True),
            lax.all_gather(col_parts[6], "dp", axis=0, tiled=True),
        )
        resid_in = block_in.astype(jnp.float32).reshape(tok_count, model_width)
        rstd_one = lax.rsqrt(jnp.mean(resid_in * resid_in, axis=-1, keepdims=True) + eps_norm)
        normed_one = (resid_in * rstd_one * gain_attn).astype(jnp.bfloat16)
        query_lin = jnp.dot(normed_one, query_mat, preferred_element_type=jnp.float32)
        key_lin = jnp.dot(normed_one, key_mat, preferred_element_type=jnp.float32)
        value_lin = jnp.dot(normed_one, value_mat, preferred_element_type=jnp.float32)
        query_rot = rotate(
            query_lin.reshape(per_micro, row_count, head_count, HD), cos_own, sin_own
        ).astype(jnp.bfloat16)
        key_rot = (
            rotate(key_lin.reshape(per_micro, row_count, kv_heads, HD), cos_own, sin_own)
            .astype(jnp.bfloat16)
            .reshape(per_micro, row_count, kv_width)
        )
        value_low = value_lin.astype(jnp.bfloat16).reshape(per_micro, row_count, kv_width)
        key_all, value_all = (
            lax.all_gather(key_rot, "seq", axis=1, tiled=True),
            lax.all_gather(value_low, "seq", axis=1, tiled=True),
        )
        mixed_seq, log_total = lax.map(attend, (query_rot, key_all, value_all))
        mixed_low = mixed_seq.reshape(tok_count, model_width)
        hidden_mid = resid_in + jnp.dot(mixed_low, out_mat, preferred_element_type=jnp.float32)
        rstd_two = lax.rsqrt(jnp.mean(hidden_mid * hidden_mid, axis=-1, keepdims=True) + eps_norm)
        normed_two = (hidden_mid * rstd_two * gain_mlp).astype(jnp.bfloat16)
        gate_lin = jnp.dot(normed_two, gate_mat, preferred_element_type=jnp.float32)
        up_lin = jnp.dot(normed_two, up_mat, preferred_element_type=jnp.float32)
        gate_sig = jax.nn.sigmoid(gate_lin)
        inner_low = (gate_lin * gate_sig * up_lin).astype(jnp.bfloat16)
        mlp_out = jnp.dot(inner_low, down_mat, preferred_element_type=jnp.float32)
        outputs.append(
            (hidden_mid + mlp_out).astype(jnp.bfloat16).reshape(per_micro, row_count, model_width)
        )
        col_again = (
            lax.all_gather(q_weight, "seq", axis=1, tiled=True),
            lax.all_gather(k_weight, "seq", axis=1, tiled=True),
            lax.all_gather(v_weight, "seq", axis=1, tiled=True),
            lax.all_gather(o_weight, "seq", axis=1, tiled=True),
            lax.all_gather(gate_weight, "seq", axis=1, tiled=True),
            lax.all_gather(up_weight, "seq", axis=1, tiled=True),
            lax.all_gather(down_weight, "seq", axis=1, tiled=True),
        )
        query_mat, key_mat, value_mat, out_mat, gate_mat, up_mat, down_mat = (
            lax.all_gather(col_again[0], "dp", axis=0, tiled=True),
            lax.all_gather(col_again[1], "dp", axis=0, tiled=True),
            lax.all_gather(col_again[2], "dp", axis=0, tiled=True),
            lax.all_gather(col_again[3], "dp", axis=0, tiled=True),
            lax.all_gather(col_again[4], "dp", axis=0, tiled=True),
            lax.all_gather(col_again[5], "dp", axis=0, tiled=True),
            lax.all_gather(col_again[6], "dp", axis=0, tiled=True),
        )
        key_all, value_all = (
            lax.all_gather(key_rot, "seq", axis=1, tiled=True),
            lax.all_gather(value_low, "seq", axis=1, tiled=True),
        )
        grad_top = block_grad.astype(jnp.float32).reshape(tok_count, model_width)
        grad_top_low = grad_top.astype(jnp.bfloat16)
        down_term = jnp.einsum(
            "tf,td->fd", inner_low, grad_top_low, preferred_element_type=jnp.float32
        )
        grad_inner = jnp.einsum(
            "td,fd->tf", grad_top_low, down_mat, preferred_element_type=jnp.float32
        )
        grad_gate = (grad_inner * up_lin * gate_sig * (1.0 + gate_lin * (1.0 - gate_sig))).astype(
            jnp.bfloat16
        )
        grad_up = (grad_inner * gate_lin * gate_sig).astype(jnp.bfloat16)
        gate_term = jnp.einsum(
            "td,tf->df", normed_two, grad_gate, preferred_element_type=jnp.float32
        )
        up_term = jnp.einsum("td,tf->df", normed_two, grad_up, preferred_element_type=jnp.float32)
        grad_normed_two = jnp.einsum(
            "tf,df->td", grad_gate, gate_mat, preferred_element_type=jnp.float32
        ) + jnp.einsum("tf,df->td", grad_up, up_mat, preferred_element_type=jnp.float32)
        grad_mid_norm, gain_mlp_term = norm_back(hidden_mid, rstd_two, gain_mlp, grad_normed_two)
        grad_mid = grad_top + grad_mid_norm
        grad_mid_low = grad_mid.astype(jnp.bfloat16)
        out_term = jnp.einsum(
            "td,te->de", mixed_low, grad_mid_low, preferred_element_type=jnp.float32
        )
        grad_mixed = jnp.einsum(
            "te,de->td", grad_mid_low, out_mat, preferred_element_type=jnp.float32
        ).astype(jnp.bfloat16)
        grad_query_rot, key_terms, value_terms = lax.map(
            attend_back,
            (
                query_rot,
                key_all,
                value_all,
                grad_mixed.reshape(per_micro, row_count, model_width),
                log_total,
            ),
        )
        key_share, value_share = (
            lax.psum_scatter(key_terms, "seq", scatter_dimension=1, tiled=True),
            lax.psum_scatter(value_terms, "seq", scatter_dimension=1, tiled=True),
        )
        grad_query = (
            rotate_back(grad_query_rot, cos_own, sin_own)
            .astype(jnp.bfloat16)
            .reshape(tok_count, model_width)
        )
        grad_key = (
            rotate_back(key_share.reshape(per_micro, row_count, kv_heads, HD), cos_own, sin_own)
            .astype(jnp.bfloat16)
            .reshape(tok_count, kv_width)
        )
        grad_value = value_share.astype(jnp.bfloat16).reshape(tok_count, kv_width)
        query_term = jnp.einsum(
            "td,te->de", normed_one, grad_query, preferred_element_type=jnp.float32
        )
        key_term = jnp.einsum("td,te->de", normed_one, grad_key, preferred_element_type=jnp.float32)
        value_term = jnp.einsum(
            "td,te->de", normed_one, grad_value, preferred_element_type=jnp.float32
        )
        grad_normed_one = (
            jnp.einsum("te,de->td", grad_query, query_mat, preferred_element_type=jnp.float32)
            + jnp.einsum("te,de->td", grad_key, key_mat, preferred_element_type=jnp.float32)
            + jnp.einsum("te,de->td", grad_value, value_mat, preferred_element_type=jnp.float32)
        )
        grad_in_norm, gain_attn_term = norm_back(resid_in, rstd_one, gain_attn, grad_normed_one)
        in_grads.append((grad_mid + grad_in_norm).reshape(per_micro, row_count, model_width))
        totals = add_tuples(
            totals,
            (
                query_term,
                key_term,
                value_term,
                out_term,
                gate_term,
                up_term,
                down_term,
                gain_attn_term,
                gain_mlp_term,
            ),
        )
    col_sums = (
        lax.psum_scatter(
            totals[0].astype(jnp.bfloat16), "seq", scatter_dimension=1, tiled=True
        ).astype(jnp.float32),
        lax.psum_scatter(
            totals[1].astype(jnp.bfloat16), "seq", scatter_dimension=1, tiled=True
        ).astype(jnp.float32),
        lax.psum_scatter(
            totals[2].astype(jnp.bfloat16), "seq", scatter_dimension=1, tiled=True
        ).astype(jnp.float32),
        lax.psum_scatter(
            totals[3].astype(jnp.bfloat16), "seq", scatter_dimension=1, tiled=True
        ).astype(jnp.float32),
        lax.psum_scatter(
            totals[4].astype(jnp.bfloat16), "seq", scatter_dimension=1, tiled=True
        ).astype(jnp.float32),
        lax.psum_scatter(
            totals[5].astype(jnp.bfloat16), "seq", scatter_dimension=1, tiled=True
        ).astype(jnp.float32),
        lax.psum_scatter(
            totals[6].astype(jnp.bfloat16), "seq", scatter_dimension=1, tiled=True
        ).astype(jnp.float32),
    )
    owned = (
        lax.psum_scatter(
            col_sums[0].astype(jnp.bfloat16), "dp", scatter_dimension=0, tiled=True
        ).astype(jnp.float32),
        lax.psum_scatter(
            col_sums[1].astype(jnp.bfloat16), "dp", scatter_dimension=0, tiled=True
        ).astype(jnp.float32),
        lax.psum_scatter(
            col_sums[2].astype(jnp.bfloat16), "dp", scatter_dimension=0, tiled=True
        ).astype(jnp.float32),
        lax.psum_scatter(
            col_sums[3].astype(jnp.bfloat16), "dp", scatter_dimension=0, tiled=True
        ).astype(jnp.float32),
        lax.psum_scatter(
            col_sums[4].astype(jnp.bfloat16), "dp", scatter_dimension=0, tiled=True
        ).astype(jnp.float32),
        lax.psum_scatter(
            col_sums[5].astype(jnp.bfloat16), "dp", scatter_dimension=0, tiled=True
        ).astype(jnp.float32),
        lax.psum_scatter(
            col_sums[6].astype(jnp.bfloat16), "dp", scatter_dimension=0, tiled=True
        ).astype(jnp.float32),
    )
    gain_sums = lax.psum((totals[7], totals[8]), ("dp", "seq"))
    return (
        jnp.concatenate(outputs, axis=0),
        jnp.concatenate(in_grads, axis=0),
        gain_sums[0],
        owned[0],
        owned[1],
        owned[2],
        owned[3],
        gain_sums[1],
        owned[4],
        owned[5],
        owned[6],
    )


F32 = jnp.float32
BF16 = jnp.bfloat16
VMEM_BYTES = 56 * 2**20


def dot(left, right, left_dim, right_dim):
    dims = (((left_dim,), (right_dim,)), ((), ()))
    return lax.dot_general(left, right, dims, preferred_element_type=F32)


def span_slice(inv_ref, place, span):
    return pl.ds(pl.multiple_of(inv_ref[place] * span, span), span)


def lane_pair(ref, rows, inv_ref, block, span):
    first = ref[rows, span_slice(inv_ref, 2 * block, span)]
    second = ref[rows, span_slice(inv_ref, 2 * block + 1, span)]
    return jnp.concatenate([first, second], axis=1)


def row_pair(ref, head, inv_ref, block, span):
    first = ref[head, span_slice(inv_ref, 2 * block, span), :]
    second = ref[head, span_slice(inv_ref, 2 * block + 1, span), :]
    return jnp.concatenate([first, second], axis=0)


def attend_kernel(inv_ref, q_ref, k_ref, v_ref, o_ref, l_ref, acc_ref, *, blocks, span, group):
    wide = 2 * span
    row = lax.broadcasted_iota(jnp.int32, (wide, wide), 0)
    col = lax.broadcasted_iota(jnp.int32, (wide, wide), 1)
    keep = row <= col

    def one_block(block, odd):
        queries = [
            lane_pair(q_ref, slice(HD * h, HD * h + HD), inv_ref, block, span) for h in range(group)
        ]
        acc_ref[...] = jnp.zeros_like(acc_ref)

        def step(first, count, state, diagonal):
            state = list(state)
            keys = [row_pair(k_ref, 0, inv_ref, first + u, span) for u in range(count)]
            values = [lane_pair(v_ref, slice(0, HD), inv_ref, first + u, span) for u in range(count)]
            items = [(u, h) for u in range(count) for h in range(group)]
            scores = [dot(keys[u], queries[h], 1, 0) for u, h in items]
            probs = []
            for (u, h), score in zip(items, scores):
                peak, total = state[h]
                if diagonal and u == count - 1:
                    score = jnp.where(keep, score, neg_big)
                new_peak = jnp.maximum(peak, jnp.max(score, axis=0, keepdims=True))
                prob = jnp.exp(score - new_peak)
                shrink = jnp.exp(peak - new_peak)
                state[h] = (new_peak, total * shrink + jnp.sum(prob, axis=0, keepdims=True))
                probs.append((prob.astype(BF16), shrink))
            for (u, h), (prob, shrink) in zip(items, probs):
                cols = slice(h * wide, (h + 1) * wide)
                acc_ref[:, cols] = acc_ref[:, cols] * shrink + dot(values[u], prob, 1, 0)
            return tuple(state)

        state = tuple(
            (jnp.full((1, wide), neg_big, F32), jnp.zeros((1, wide), F32)) for _ in range(group)
        )
        state = lax.fori_loop(0, block // 4, lambda j, s: step(4 * j, 4, s, False), state)
        state = lax.fori_loop(
            2 * (block // 4), block // 2, lambda j, s: step(2 * j, 2, s, False), state
        )
        state = step(block - 1, 2, state, True) if odd else step(block, 1, state, True)
        mixed = jnp.concatenate(
            [acc_ref[:, wide * h : wide * (h + 1)] * (1.0 / state[h][1]) for h in range(group)], axis=0
        ).astype(BF16)
        logs = jnp.concatenate(
            [p + jnp.log(t) for p, t in state] + [jnp.zeros((8 - group, wide), F32)], axis=0
        )
        for part in range(2):
            where = span_slice(inv_ref, 2 * block + part, span)
            cols = slice(part * span, part * span + span)
            o_ref[:, where] = mixed[:, cols]
            l_ref[0, :, where] = logs[:, cols]

    def two_blocks(pair, _):
        for odd in (0, 1):
            one_block(2 * pair + odd, odd)
        return 0

    lax.fori_loop(0, blocks // 2, two_blocks, 0)


def attention_forward(inv, q_t, k_nat, v_t, span):
    tokens = q_t.shape[1]
    kv_heads = k_nat.shape[0]
    group = q_t.shape[0] // (kv_heads * HD)
    pairs = kv_heads * group * tokens * tokens
    wide_spec = pl.BlockSpec((group * HD, tokens), lambda g, i: (g, 0))
    nat_spec = pl.BlockSpec((1, tokens, HD), lambda g, i: (g, 0, 0))
    return pl.pallas_call(
        functools.partial(attend_kernel, blocks=tokens // (2 * span), span=span, group=group),
        grid_spec=pltpu.PrefetchScalarGridSpec(
            num_scalar_prefetch=1,
            grid=(kv_heads,),
            in_specs=[wide_spec, nat_spec, pl.BlockSpec((HD, tokens), lambda g, i: (g, 0))],
            out_specs=[
                wide_spec,
                pl.BlockSpec((1, 8, tokens), lambda g, i: (g, 0, 0)),
            ],
            scratch_shapes=[pltpu.VMEM((HD, group * 2 * span), F32)],
        ),
        out_shape=[
            jax.ShapeDtypeStruct(q_t.shape, BF16),
            jax.ShapeDtypeStruct((kv_heads, 8, tokens), F32),
        ],
        compiler_params=pltpu.CompilerParams(vmem_limit_bytes=VMEM_BYTES),
        cost_estimate=pl.CostEstimate(
            flops=16 * pairs * HD, bytes_accessed=tokens * 6000, transcendentals=pairs // 2
        ),
        name="attention_forward",
    )(inv, q_t, k_nat, v_t)


def attend_back_kernel(
    inv_ref, q_ref, kt_ref, k_ref, v_ref, o_ref, do_ref, l_ref, cos_ref, sin_ref,
    dq_ref, dk_ref, dv_ref, dk_sum, dv_sum, dq_sum, *, blocks, span, group,
):
    wide = 2 * span
    row = lax.broadcasted_iota(jnp.int32, (wide, wide), 0)
    col = lax.broadcasted_iota(jnp.int32, (wide, wide), 1)
    keep = row <= col
    half = HD // 2
    dk_sum[...] = jnp.zeros_like(dk_sum)
    dv_sum[...] = jnp.zeros_like(dv_sum)

    def rope_back(grad, cos, sin):
        top, low = grad[:half], grad[half:]
        return jnp.concatenate([top * cos + low * sin, low * cos - top * sin], axis=0)

    def one_block(block, odd):
        rows = [slice(HD * h, HD * h + HD) for h in range(group)]
        queries = [lane_pair(q_ref, r, inv_ref, block, span) for r in rows]
        grads = [lane_pair(do_ref, r, inv_ref, block, span) for r in rows]
        logs = lane_pair(l_ref.at[0], slice(None), inv_ref, block, span)
        deltas = [
            jnp.sum(
                lane_pair(o_ref, r, inv_ref, block, span).astype(F32) * grad.astype(F32),
                axis=0,
                keepdims=True,
            )
            for r, grad in zip(rows, grads)
        ]
        dq_sum[...] = jnp.zeros_like(dq_sum)

        def step(first, count, diagonal):
            keys = [row_pair(k_ref, 0, inv_ref, first + u, span) for u in range(count)]
            values = [row_pair(v_ref, 0, inv_ref, first + u, span) for u in range(count)]
            keys_t = [lane_pair(kt_ref, slice(0, HD), inv_ref, first + u, span) for u in range(count)]
            items = [(u, h) for u in range(count) for h in range(group)]
            ahead, ready, dqs, sums = {}, {}, {}, {}

            def products(i):
                u, h = items[i]
                ahead[i] = dot(keys[u], queries[h], 1, 0), dot(values[u], grads[h], 1, 0)

            def softmax_part(i):
                u, h = items[i]
                score, dprob = ahead.pop(i)
                prob = jnp.exp(score - logs[h : h + 1])
                if diagonal and u == count - 1:
                    prob = jnp.where(keep, prob, 0.0)
                ready[i] = prob.astype(BF16), (prob * (dprob - deltas[h])).astype(BF16)

            def gradients(i):
                u, h = items[i]
                prob, dscore = ready.pop(i)
                dq = dot(keys_t[u], dscore, 1, 0)
                dqs[h] = dqs[h] + dq if h in dqs else dq
                if u == count - 1:
                    dq_sum[:, wide * h : wide * (h + 1)] += dqs[h]
                dk, dv = dot(queries[h], dscore, 1, 1), dot(grads[h], prob, 1, 1)
                if u in sums:
                    dk, dv = dk + sums[u][0], dv + sums[u][1]
                sums[u] = dk, dv
                if h == group - 1:
                    place = pl.ds(pl.multiple_of((first + u) * wide, wide), wide)
                    dk_sum[:, place] += dk
                    dv_sum[:, place] += dv

            lead = 2
            for i in range(min(lead, len(items))):
                products(i)
            for i in range(len(items) + 1):
                if i + lead < len(items):
                    products(i + lead)
                if i > 0:
                    gradients(i - 1)
                if i < len(items):
                    softmax_part(i)

        def pair_step(j, _):
            step(2 * j, 2, False)
            return 0

        lax.fori_loop(0, block // 2, pair_step, 0)
        if odd:
            step(block - 1, 2, True)
        else:
            step(block, 1, True)
        cos = lane_pair(cos_ref, slice(None), inv_ref, block, span)
        sin = lane_pair(sin_ref, slice(None), inv_ref, block, span)
        dq = jnp.concatenate(
            [rope_back(dq_sum[:, wide * h : wide * (h + 1)] * HD**-0.5, cos, sin) for h in range(group)],
            axis=0,
        ).astype(BF16)
        place = pl.ds(pl.multiple_of(block * wide, wide), wide)
        dk = rope_back(dk_sum[:, place], cos, sin).astype(BF16)
        dv = dv_sum[:, place].astype(BF16)
        for part in range(2):
            where = span_slice(inv_ref, 2 * block + part, span)
            cols = slice(part * span, part * span + span)
            dq_ref[:, where] = dq[:, cols]
            dk_ref[:, where] = dk[:, cols]
            dv_ref[:, where] = dv[:, cols]

    def two_blocks(step, _):
        for odd in (1, 0):
            one_block(blocks - 2 - 2 * step + odd, odd)
        return 0

    lax.fori_loop(0, blocks // 2, two_blocks, 0)


def attention_backward(inv, q_t, k_t, k_nat, v_nat, o_t, do_t, logs, cos_t, sin_t, span, first, count):
    tokens = q_t.shape[1]
    kv_heads = k_nat.shape[0]
    group = q_t.shape[0] // (kv_heads * HD)
    pairs = count * group * tokens * tokens
    wide_spec = pl.BlockSpec((group * HD, tokens), lambda g, i: (g + first, 0))
    kv_spec = pl.BlockSpec((HD, tokens), lambda g, i: (g + first, 0))
    nat_spec = pl.BlockSpec((1, tokens, HD), lambda g, i: (g + first, 0, 0))
    tab_spec = pl.BlockSpec((HD // 2, tokens), lambda g, i: (0, 0))
    return pl.pallas_call(
        functools.partial(attend_back_kernel, blocks=tokens // (2 * span), span=span, group=group),
        grid_spec=pltpu.PrefetchScalarGridSpec(
            num_scalar_prefetch=1,
            grid=(count,),
            in_specs=[
                wide_spec, kv_spec, nat_spec, nat_spec, wide_spec, wide_spec,
                pl.BlockSpec((1, 8, tokens), lambda g, i: (g + first, 0, 0)), tab_spec, tab_spec,
            ],
            out_specs=[
                pl.BlockSpec((group * HD, tokens), lambda g, i: (g, 0)),
                pl.BlockSpec((HD, tokens), lambda g, i: (g, 0)),
                pl.BlockSpec((HD, tokens), lambda g, i: (g, 0)),
            ],
            scratch_shapes=[
                pltpu.VMEM((HD, tokens), F32),
                pltpu.VMEM((HD, tokens), F32),
                pltpu.VMEM((HD, group * 2 * span), F32),
            ],
        ),
        out_shape=[
            jax.ShapeDtypeStruct((count * group * HD, tokens), BF16),
            jax.ShapeDtypeStruct((count * HD, tokens), BF16),
            jax.ShapeDtypeStruct((count * HD, tokens), BF16),
        ],
        compiler_params=pltpu.CompilerParams(vmem_limit_bytes=VMEM_BYTES),
        cost_estimate=pl.CostEstimate(
            flops=32 * pairs * HD, bytes_accessed=tokens * 9000, transcendentals=pairs // 2
        ),
        name="attention_backward",
    )(inv, q_t, k_t, k_nat, v_nat, o_t, do_t, logs, cos_t, sin_t)


def flip(index, bits):
    for bit in bits:
        index = index + bit * (1 - 2 * ((index // bit) % 2))
    return index


def bits_of(size):
    return [1 << i for i in range(size.bit_length() - 1)]


def seq_stages(seq):
    return [("seq", b) for b in reversed(bits_of(seq)[1:])] + [("seq", b) for b in bits_of(seq)[:1]]


def all_stages(dp, seq):
    return seq_stages(seq) + [("dp", b) for b in reversed(bits_of(dp))]


def rest_chains(dp, seq):
    near, far = [("seq", b) for b in bits_of(seq)[:1]], [("seq", b) for b in reversed(bits_of(seq)[1:])]
    chip = [("dp", b) for b in reversed(bits_of(dp)[1:])]
    return far + near + chip, far + chip + near


def away_place(stages, d, s, my_dp, my_seq):
    place = 0
    for at, (axis, bit) in enumerate(stages):
        mine = ((my_dp if axis == "dp" else my_seq) // bit) % 2
        theirs = ((d if axis == "dp" else s) // bit) % 2
        place = place + (1 << at) * (1 - mine if theirs else mine)
    return place


def arrival_order(stages, dp, seq, my_dp, my_seq):
    ids = jnp.arange(dp * seq, dtype=jnp.int32)
    away = {"dp": (ids // seq) ^ my_dp, "seq": (ids % seq) ^ my_seq}
    place = jnp.zeros_like(ids)
    for at, (axis, bit) in enumerate(stages):
        place = place + (1 << at) * ((away[axis] // bit) % 2)
    return place


def greet(peers):
    barrier = pltpu.get_barrier_semaphore()
    for peer in peers:
        pl.semaphore_signal(barrier, inc=1, device_id=peer, device_id_type=pl.DeviceIdType.MESH)
    pl.semaphore_wait(barrier, len(peers))


def seq_peer(my_dp, my_seq, away, seq):
    return my_dp, flip(my_seq, [b for b in bits_of(seq) if away & b])


def stage_peer(my_dp, my_seq, stage):
    axis, bit = stage
    return (flip(my_dp, [bit]), my_seq) if axis == "dp" else (my_dp, flip(my_seq, [bit]))


def all_peers(my_dp, my_seq, dp, seq):
    peers = [seq_peer(my_dp, my_seq, away, seq) for away in range(1, seq)]
    return peers + [(flip(my_dp, [b]), my_seq) for b in bits_of(dp)]


def bring_kernel(order_ref, freq_ref, gain_one, gain_two, q_ref, k_ref, v_ref, o_ref, gate_ref, up_ref,
                 down_ref, x_ref, inv_ref, cos_ref, sin_ref, one_ref, two_ref, out_ref,
                 all_first, all_second, all_third, first_ref, rest_ref, local_sem, x_send, x_recv, w_send, w_recv, *, dp, seq):
    my_dp, my_seq = lax.axis_index("dp"), lax.axis_index("seq")
    orders = all_stages(dp, seq), seq_stages(seq), seq_stages(seq)
    chains = range(len(orders))
    rows, q_cols = q_ref.shape
    lanes = rest_ref.shape[2]
    kv_cols = k_ref.shape[0]
    blank = lambda cols: jnp.zeros((rows, cols), F32)
    wide = lambda ref: ref[...].astype(F32)
    first_ref[0] = jnp.concatenate(
        [wide(q_ref), wide(k_ref).T, wide(v_ref).T, blank(lanes - q_cols - 2 * kv_cols)], axis=1
    ).astype(BF16)
    rest_ref[0, :rows] = jnp.concatenate([wide(o_ref), blank(lanes - q_cols)], axis=1).astype(BF16)
    rest_ref[0, rows : 2 * rows] = gate_ref[:, :lanes]
    rest_ref[0, 2 * rows : 3 * rows] = up_ref[:, :lanes]
    rest_ref[0, 3 * rows : 4 * rows] = jnp.concatenate([gate_ref[:, lanes:], up_ref[:, lanes:]], axis=1)
    padded = -(-q_cols // 16) * 16
    for t in range(down_ref.shape[1] // lanes):
        piece = down_ref[:, t * lanes : (t + 1) * lanes].astype(F32)
        piece = jnp.concatenate([piece, jnp.zeros((padded - q_cols, lanes), F32)], axis=0).astype(BF16)
        rest_ref[0, 4 * rows + padded * t : 4 * rows + padded * (t + 1)] = piece

    greet(all_peers(my_dp, my_seq, dp, seq))
    at = all_second.shape[1]
    shards_in = first_ref, rest_ref.at[:, pl.ds(0, at)], rest_ref.at[:, pl.ds(at, all_third.shape[1])]
    gathered = all_first, all_second, all_third

    def weight_copy(chain, stage):
        held = 1 << stage
        source = shards_in[chain] if stage == 0 else gathered[chain].at[pl.ds(0, held)]
        return pltpu.make_async_remote_copy(
            src_ref=source,
            dst_ref=gathered[chain].at[pl.ds(held, held)],
            send_sem=w_send.at[chain, stage],
            recv_sem=w_recv.at[chain, stage],
            device_id=stage_peer(my_dp, my_seq, orders[chain][stage]),
            device_id_type=pl.DeviceIdType.MESH,
        )

    copies = [[weight_copy(c, s) for s in range(len(orders[c]))] for c in chains]
    for c in chains:
        copies[c][0].start()
    own = [
        pltpu.make_async_copy(shards_in[c], gathered[c].at[pl.ds(0, 1)], local_sem.at[c]) for c in chains
    ]
    own.append(pltpu.make_async_copy(x_ref.at[my_seq], out_ref.at[my_seq], local_sem.at[len(orders)]))
    for copy in own:
        copy.start()
    moves = []
    for away in range(1, seq):
        peer = seq_peer(my_dp, my_seq, away, seq)
        moves.append(
            pltpu.make_async_remote_copy(
                src_ref=x_ref.at[peer[1]],
                dst_ref=out_ref.at[my_seq],
                send_sem=x_send.at[away - 1],
                recv_sem=x_recv.at[away - 1],
                device_id=peer,
                device_id_type=pl.DeviceIdType.MESH,
            )
        )
    for c in chains:
        own[c].wait()
    for stage in range(1, len(orders[0])):
        for c in chains:
            if stage < len(orders[c]):
                copies[c][stage - 1].wait_recv()
                copies[c][stage].start()
        if stage == 1:
            for move in moves:
                move.start()
            spans = order_ref.shape[0]
            span = cos_ref.shape[1] // spans
            inside = lax.broadcasted_iota(jnp.int32, (1, span), 1)
            for slot in range(spans):
                angles = (inside + order_ref[slot] * span).astype(F32) * freq_ref[...]
                cos_ref[:, slot * span : (slot + 1) * span] = jnp.cos(angles)
                sin_ref[:, slot * span : (slot + 1) * span] = jnp.sin(angles)
                found = 0
                for other in range(spans):
                    found = found + jnp.where(order_ref[other] == slot, other, 0)
                inv_ref[slot] = found
            for source, target in ((gain_one, one_ref), (gain_two, two_ref)):
                row = source[...].astype(F32)[None]
                target[...] = jnp.broadcast_to(row, (8, row.shape[1])).T[:, :1]
    for c in chains:
        copies[c][-1].wait_recv()
        for copy in copies[c]:
            copy.wait_send()
    for move in moves:
        move.wait()
    own[-1].wait()


def bring(span_order, inv_freq, gains, weights, x):
    dp, seq = lax.axis_size("dp"), lax.axis_size("seq")
    stages = len(all_stages(dp, seq))
    lanes = 128
    width = x.shape[1]
    rows, q_cols = weights[0].shape
    rest_rows = 4 * rows + -(-q_cols // 16) * 16 * (weights[-1].shape[1] // lanes)
    cut = rest_rows * 5 // 8 // 16 * 16
    hbm = pl.BlockSpec(memory_space=pl.ANY)
    smem = pl.BlockSpec(memory_space=pltpu.SMEM)
    vmem = pl.BlockSpec(memory_space=pltpu.VMEM)
    table = jax.ShapeDtypeStruct((inv_freq.shape[0], x.shape[0] * x.shape[2]), F32)
    return pl.pallas_call(
        functools.partial(bring_kernel, dp=dp, seq=seq),
        in_specs=[smem] + [vmem] * (3 + len(weights)) + [hbm],
        out_specs=[smem] + [vmem] * 4 + [hbm] * 4,
        out_shape=[
            jax.ShapeDtypeStruct(span_order.shape, jnp.int32),
            table,
            table,
            jax.ShapeDtypeStruct((width, 1), F32),
            jax.ShapeDtypeStruct((width, 1), F32),
            jax.ShapeDtypeStruct(x.shape, x.dtype),
            jax.ShapeDtypeStruct((dp * seq, rows, lanes), x.dtype),
            jax.ShapeDtypeStruct((seq, cut, lanes), x.dtype),
            jax.ShapeDtypeStruct((seq, rest_rows - cut, lanes), x.dtype),
        ],
        scratch_shapes=[
            pltpu.VMEM((1, rows, lanes), BF16),
            pltpu.VMEM((1, rest_rows, lanes), BF16),
            pltpu.SemaphoreType.DMA((4,)),
            pltpu.SemaphoreType.DMA((seq - 1,)),
            pltpu.SemaphoreType.DMA((seq - 1,)),
            pltpu.SemaphoreType.DMA((3, stages)),
            pltpu.SemaphoreType.DMA((3, stages)),
        ],
        compiler_params=pltpu.CompilerParams(
            collective_id=1, has_side_effects=True, vmem_limit_bytes=VMEM_BYTES
        ),
        name="bring",
    )(span_order, inv_freq, *gains, *weights, x)


def qkv_kernel(where_ref, x_ref, gain_ref, packed_ref, cos_ref, sin_ref,
               q_ref, kt_ref, vt_ref, k_ref, v_ref, w_ref, w_wide, *, heads, kv_heads, dp, seq):
    half = HD // 2
    width = w_ref.shape[1]
    q_cols, kv_cols = width // seq, kv_heads * HD // seq
    kv_width = kv_heads * HD

    @pl.when(pl.program_id(0) == 0)
    def _():
        for s in range(seq):
            block = jnp.concatenate([packed_ref[where_ref[d * seq + s]] for d in range(dp)], axis=0)
            turned = block.astype(F32).T
            w_wide[q_cols * s : q_cols * s + q_cols, :] = turned[:q_cols]
            first = width + kv_cols * s
            w_wide[first : first + kv_cols, :] = turned[q_cols : q_cols + kv_cols]
            first += kv_width
            w_wide[first : first + kv_cols, :] = turned[q_cols + kv_cols : q_cols + 2 * kv_cols]
        w_ref[...] = w_wide[...].astype(BF16)

    x = x_ref[0].astype(F32)
    rstd = lax.rsqrt(jnp.mean(x * x, axis=0, keepdims=True) + eps_norm)
    normed = (x * rstd * gain_ref[...]).astype(BF16)
    lin = dot(w_ref[...], normed, 1, 0)
    cos, sin = cos_ref[...], sin_ref[...]
    for head in range(heads + kv_heads):
        top = lin[HD * head : HD * head + half]
        low = lin[HD * head + half : HD * head + HD]
        rot = jnp.concatenate([top * cos - low * sin, low * cos + top * sin], axis=0)
        if head < heads:
            q_ref[HD * head : HD * head + HD, :] = rot.astype(BF16) * jnp.asarray(HD**-0.5, BF16)
        else:
            kv = head - heads
            kt_ref[HD * kv : HD * kv + HD, :] = rot.astype(BF16)
            k_ref[kv] = rot.T.astype(BF16)
    for kv in range(kv_heads):
        first = HD * (heads + kv_heads + kv)
        val = lin[first : first + HD]
        vt_ref[HD * kv : HD * kv + HD, :] = val.astype(BF16)
        v_ref[kv] = val.T.astype(BF16)


def project_qkv(where, x, gain, packed, cos_t, sin_t, heads, kv_heads, rows):
    blocks, width, block = x.shape
    tokens = blocks * block
    feats = (heads + 2 * kv_heads) * HD
    dp, seq = lax.axis_size("dp"), lax.axis_size("seq")
    col = lambda rows: pl.BlockSpec((rows, block), lambda i, w: (0, i))
    nat = pl.BlockSpec((kv_heads, block, HD), lambda i, w: (0, i, 0))
    return pl.pallas_call(
        functools.partial(qkv_kernel, heads=heads, kv_heads=kv_heads, dp=dp, seq=seq),
        grid_spec=pltpu.PrefetchScalarGridSpec(
            num_scalar_prefetch=1,
            grid=(blocks,),
            in_specs=[
                pl.BlockSpec((1, width, block), lambda i, w: (i, 0, 0)),
                pl.BlockSpec((width, 1), lambda i, w: (0, 0)),
                pl.BlockSpec((dp * seq, rows, packed.shape[2]), lambda i, w: (0, 0, 0)),
                col(HD // 2),
                col(HD // 2),
            ],
            out_specs=[
                col(heads * HD), col(kv_heads * HD), col(kv_heads * HD), nat, nat,
                pl.BlockSpec((feats, width), lambda i, w: (0, 0)),
            ],
            scratch_shapes=[pltpu.VMEM((feats, width), F32)],
        ),
        out_shape=[
            jax.ShapeDtypeStruct((heads * HD, tokens), BF16),
            jax.ShapeDtypeStruct((kv_heads * HD, tokens), BF16),
            jax.ShapeDtypeStruct((kv_heads * HD, tokens), BF16),
            jax.ShapeDtypeStruct((kv_heads, tokens, HD), BF16),
            jax.ShapeDtypeStruct((kv_heads, tokens, HD), BF16),
            jax.ShapeDtypeStruct((feats, width), BF16),
        ],
        compiler_params=pltpu.CompilerParams(vmem_limit_bytes=VMEM_BYTES),
        cost_estimate=pl.CostEstimate(
            flops=4 * tokens * width * feats, bytes_accessed=tokens * 5000, transcendentals=0
        ),
        name="project_qkv",
    )(where, x, gain, packed, cos_t, sin_t)


def side_by_side(ref):
    return jnp.concatenate([ref[i] for i in range(ref.shape[0])], axis=1)


def mlp_kernel(
    where_ref, x_ref, mixed_ref, dy_ref, gain_ref, *more, chunk, dp, seq,
):
    packs, more = more[: 2 * dp], more[2 * dp :]
    out_ref, dmid_ref, dmixed_ref = more[:3]
    one_refs, two_refs, gain_grad_ref = more[3:5], more[5:7], more[7]
    (o_w, o_t, gate_w, gate_t, up_w, up_t, down_w, down_t, o_sum, gate_sum, up_sum, down_sum, gain_sum,
     pack, pack_sem) = more[8:]
    step, steps = pl.program_id(0), pl.num_programs(0)
    width, ff = gate_w.shape
    lanes = pack.shape[3]
    rows = width // dp
    o_cols, ff_cols, ff_rows = width // seq, ff // seq, ff // dp
    spare = ff_cols - lanes
    padded = -(-o_cols // 16) * 16

    @pl.when(step == 0)
    def _():
        for total in (o_sum, gate_sum, up_sum, down_sum, gain_sum):
            total[...] = jnp.zeros_like(total)
        fetches = []
        for i in range(dp):
            owner = flip(lax.axis_index("dp"), row_bits(i, dp))
            first = 0
            for source, sem in ((packs[2 * i], pack_sem.at[2 * i]), (packs[2 * i + 1], pack_sem.at[2 * i + 1])):
                span = pl.ds(first, source.shape[1])
                fetches.append(pltpu.make_async_copy(source, pack.at[owner, :, span, :], sem))
                first += source.shape[1]
        for fetch in fetches:
            fetch.start()
        for fetch in fetches:
            fetch.wait()
        for s in range(seq):
            at = where_ref[s]
            stack = lambda first: jnp.concatenate(
                [pack[d, at, first : first + rows, :] for d in range(dp)], axis=0
            )
            o_sum[o_cols * s : o_cols * s + o_cols, :] = stack(0).astype(F32).T[:o_cols]
            gate_t[ff_cols * s : ff_cols * s + lanes, :] = stack(rows).T
            up_t[ff_cols * s : ff_cols * s + lanes, :] = stack(2 * rows).T
            both = stack(3 * rows).T
            gate_t[ff_cols * s + lanes : ff_cols * (s + 1), :] = both[:spare]
            up_t[ff_cols * s + lanes : ff_cols * (s + 1), :] = both[spare : 2 * spare]
            for d in range(dp):
                for t in range(ff_rows // lanes):
                    first = 4 * rows + padded * t
                    piece = pack[d, at, first : first + padded, :].astype(F32)[:o_cols]
                    cols = slice(ff_rows * d + lanes * t, ff_rows * d + lanes * (t + 1))
                    down_sum[o_cols * s : o_cols * s + o_cols, cols] = piece
        for s in range(0, seq, 2):
            for d in range(dp):
                halves = [pack[d, where_ref[s + i], 3 * rows : 4 * rows, :] for i in range(2)]
                for matrix, first, cut in ((gate_w, rows, 0), (up_w, 2 * rows, spare)):
                    pieces = []
                    for i in range(2):
                        pieces.append(pack[d, where_ref[s + i], first : first + rows, :])
                        pieces.append(halves[i][:, cut : cut + spare])
                    cols = slice(ff_cols * s, ff_cols * (s + 2))
                    matrix[rows * d : rows * (d + 1), cols] = jnp.concatenate(pieces, axis=1)
        o_t[...] = o_sum[...].astype(BF16)
        o_w[...] = o_sum[...].T.astype(BF16)
        down_t[...] = down_sum[...].astype(BF16)
        for first in range(0, ff, lanes):
            part = slice(first, first + lanes)
            down_w[part, :] = down_t[:, part].T
        o_sum[...] = jnp.zeros_like(o_sum)
        down_sum[...] = jnp.zeros_like(down_sum)

    gain = gain_ref[...]
    mixed = mixed_ref[...]
    mid = dot(o_t[...], mixed, 1, 0) + side_by_side(x_ref).astype(F32)
    rstd = lax.rsqrt(jnp.mean(mid * mid, axis=0, keepdims=True) + eps_norm)
    normed = (mid * rstd * gain).astype(BF16)
    dy = side_by_side(dy_ref)
    added = jnp.zeros_like(mid)
    dnormed = jnp.zeros_like(mid)
    for first in range(0, ff, chunk):
        part = slice(first, first + chunk)
        gate = dot(gate_t[part, :], normed, 1, 0)
        up = dot(up_t[part, :], normed, 1, 0)
        dinner = dot(down_w[part, :], dy, 1, 0)
        sig = 1.0 / (1.0 + jnp.exp(-gate))
        silu = gate * sig
        inner = (silu * up).astype(BF16)
        dup = (dinner * silu).astype(BF16)
        dgate = (dinner * up * sig * (1.0 + gate * (1.0 - sig))).astype(BF16)
        added += dot(down_t[:, part], inner, 1, 0)
        dnormed += dot(gate_w[:, part], dgate, 1, 0)
        dnormed += dot(up_w[:, part], dup, 1, 0)
        down_sum[:, part] += dot(dy, inner, 1, 1)
        gate_sum[:, part] += dot(normed, dgate, 1, 1)
        up_sum[:, part] += dot(normed, dup, 1, 1)
    out = (mid + added).astype(BF16)
    scaled_mid = mid * rstd
    product = dnormed * scaled_mid
    gain_sum[...] += sum(product[:, c : c + lanes] for c in range(0, product.shape[1], lanes))
    scaled = dnormed * gain
    pull = jnp.mean(scaled * mid, axis=0, keepdims=True)
    dmid = dy.astype(F32) + rstd * scaled - scaled_mid * (rstd * rstd * pull)
    dmid_low = dmid.astype(BF16)
    block = out_ref.shape[2]
    for i in range(out_ref.shape[0]):
        out_ref[i] = out[:, block * i : block * (i + 1)]
        dmid_ref[i] = dmid[:, block * i : block * (i + 1)]
    o_sum[...] += dot(dmid_low, mixed, 1, 1)
    dmixed_ref[...] = dot(o_w[...], dmid_low, 1, 0).astype(BF16)

    @pl.when(step == steps - 1)
    def _():
        gain_grad_ref[...] = jnp.sum(gain_sum[...].T, axis=0, keepdims=True)
        my_dp, my_seq = lax.axis_index("dp"), lax.axis_index("seq")
        upper = my_dp % 2 == 1

        def put(refs, place, first, even, odd):
            keep_ref, give_ref = refs
            span = slice(first, first + even.shape[0])
            keep_ref[place, span, :] = jnp.where(upper, odd, even).astype(BF16)
            give_ref[place, span, :] = jnp.where(upper, even, odd).astype(BF16)

        blank = jnp.zeros((lanes - o_cols, width), F32)
        edge = jnp.zeros((padded - o_cols, lanes), F32)
        for s in range(seq):
            o_piece = jnp.concatenate([o_sum[o_cols * s : o_cols * (s + 1), :], blank], axis=0).T
            pair_cols = slice(ff_cols * (s - s % 2), ff_cols * (s - s % 2 + 2))
            shift = ff_cols * (s % 2)
            for d in range(0, dp, 2):
                bands = slice(rows * d, rows * (d + 1)), slice(rows * (d + 1), rows * (d + 2))
                one, two = [away_place(c, d, s, my_dp, my_seq) for c in rest_chains(dp, seq)]
                put(one_refs, one, 0, o_piece[bands[0]], o_piece[bands[1]])
                rests = []
                for i, total in enumerate((gate_sum, up_sum)):
                    wide = [total[band, pair_cols] for band in bands]
                    put(one_refs, one, rows * (i + 1), *[w[:, shift : shift + lanes] for w in wide])
                    rests.append([w[:, shift + lanes : shift + ff_cols] for w in wide])
                put(two_refs, two, 0, *[jnp.concatenate([g, u], axis=1) for g, u in zip(*rests)])
                for t in range(ff_rows // lanes):
                    pair = []
                    for at in (d, d + 1):
                        cols = slice(ff_rows * at + lanes * t, ff_rows * at + lanes * (t + 1))
                        pair.append(
                            jnp.concatenate([down_sum[o_cols * s : o_cols * (s + 1), cols], edge], axis=0)
                        )
                    put(two_refs, two, rows + padded * t, *pair)


def row_bits(at, dp):
    return [b for i, b in enumerate(reversed(bits_of(dp))) if (at >> i) & 1]


def over_rows(array, mask):
    return lax.ppermute(array, "dp", [(i, i ^ mask) for i in range(lax.axis_size("dp"))])


def mlp_both(where, x, mixed, dy, gain, packs, ff, batch=2, chunk=768):
    blocks, width, block = x.shape
    tokens = blocks * block
    dp, seq = lax.axis_size("dp"), lax.axis_size("seq")
    grad_rows, lanes = packs[0].shape[1] + packs[1].shape[1], packs[0].shape[2]
    first_rows = 3 * (width // dp)
    one = dp * seq // 2, first_rows, lanes
    two = dp * seq // 2, grad_rows - first_rows, lanes
    tok = pl.BlockSpec((batch, width, block), lambda i, w: (i, 0, 0))
    col = pl.BlockSpec((width, batch * block), lambda i, w: (0, i))
    once = lambda shape: pl.BlockSpec(
        shape, lambda i, w: (0,) * len(shape), pipeline_mode=pl.Buffered(1)
    )
    hbm = pl.BlockSpec(memory_space=pl.ANY)
    return pl.pallas_call(
        functools.partial(mlp_kernel, chunk=chunk, dp=dp, seq=seq),
        grid_spec=pltpu.PrefetchScalarGridSpec(
            num_scalar_prefetch=1,
            grid=(blocks // batch,),
            in_specs=[tok, col, tok, once((width, 1))] + [hbm] * (2 * dp),
            out_specs=[tok, tok, col, once(one), once(one), once(two), once(two), once((1, width))],
            scratch_shapes=[
                pltpu.VMEM((width, width), BF16),
                pltpu.VMEM((width, width), BF16),
                pltpu.VMEM((width, ff), BF16),
                pltpu.VMEM((ff, width), BF16),
                pltpu.VMEM((width, ff), BF16),
                pltpu.VMEM((ff, width), BF16),
                pltpu.VMEM((ff, width), BF16),
                pltpu.VMEM((width, ff), BF16),
                pltpu.VMEM((width, width), F32),
                pltpu.VMEM((width, ff), F32),
                pltpu.VMEM((width, ff), F32),
                pltpu.VMEM((width, ff), F32),
                pltpu.VMEM((width, lanes), F32),
                pltpu.VMEM((dp, packs[0].shape[0], grad_rows, lanes), BF16),
                pltpu.SemaphoreType.DMA((2 * dp,)),
            ],
        ),
        out_shape=[
            jax.ShapeDtypeStruct(x.shape, BF16),
            jax.ShapeDtypeStruct(x.shape, F32),
            jax.ShapeDtypeStruct((width, tokens), BF16),
            jax.ShapeDtypeStruct(one, BF16),
            jax.ShapeDtypeStruct(one, BF16),
            jax.ShapeDtypeStruct(two, BF16),
            jax.ShapeDtypeStruct(two, BF16),
            jax.ShapeDtypeStruct((1, width), F32),
        ],
        compiler_params=pltpu.CompilerParams(vmem_limit_bytes=60 * 2**20),
        cost_estimate=pl.CostEstimate(
            flops=2 * tokens * width * (9 * ff + 3 * width),
            bytes_accessed=tokens * width * 14,
            transcendentals=tokens * ff,
        ),
        name="mlp_both",
    )(where, x, mixed, dy, gain, *packs)


def across(index, other, size):
    for bit in bits_of(size):
        index = index + bit * ((other // bit) % 2) * (1 - 2 * ((index // bit) % 2))
    return index


def add_blocks(total_ref, term_ref, count, total_first=0, term_first=0):
    def one(i, _):
        total = total_ref[total_first + i].astype(F32) + term_ref[term_first + i].astype(F32)
        total_ref[total_first + i] = total.astype(BF16)
        return 0

    lax.fori_loop(0, count, one, 0)


def finish_kernel(
    x_ref, dmid_ref, dq_one, dq_two, dk_one, dk_two, dv_one, dv_two, gain_ref, w_t_ref, other_gain_ref,
    keep_one, keep_two, came_one, came_two, out_ref, gains_ref, qkv_ref, one_ref, two_ref,
    w_nat, w_sum, gain_sum, din, packed, landed, one, one_came, one_landed, two, two_came, two_landed,
    gain_held, gain_landed,
    own_sem, d_send, d_recv, r_send, r_recv, g_send, g_recv, fetch_sem, *, dp, seq, kv_width,
):
    step, steps = pl.program_id(0), seq // 2
    my_dp, my_seq = lax.axis_index("dp"), lax.axis_index("seq")
    width = w_nat.shape[0]
    lanes = packed.shape[2]
    rows = width // dp
    q_cols, kv_cols = width // seq, kv_width // seq
    orders = [all_stages(dp, seq), *[chain[:-1] for chain in rest_chains(dp, seq)]]
    held = [packed, one, two]
    arrived = [landed, one_landed, two_landed]
    fetches = [
        pltpu.make_async_copy(source, target, fetch_sem.at[i])
        for i, (source, target) in enumerate(
            ((keep_one, one), (keep_two, two), (came_one, one_came), (came_two, two_came))
        )
    ]

    def halve(chain, turn):
        at = len(orders[chain]) - 1 - turn
        half = 1 << at
        return pltpu.make_async_remote_copy(
            src_ref=held[chain].at[pl.ds(half, half)],
            dst_ref=arrived[chain].at[pl.ds(half, half)],
            send_sem=r_send.at[chain, turn],
            recv_sem=r_recv.at[chain, turn],
            device_id=stage_peer(my_dp, my_seq, orders[chain][at]),
            device_id_type=pl.DeviceIdType.MESH,
        )

    def take(chain, turn):
        halve(chain, turn).wait_recv()
        half = 1 << (len(orders[chain]) - 1 - turn)
        if half > 1:
            add_blocks(held[chain], arrived[chain], half, 0, half)
            halve(chain, turn + 1).start()

    def result(chain):
        return held[chain][0].astype(F32) + arrived[chain][1].astype(F32)

    @pl.when(step == 0)
    def _():
        for fetch in fetches:
            fetch.start()
        greet(all_peers(my_dp, my_seq, dp, seq))
        for fetch in fetches:
            fetch.wait()
        for chain, came in ((1, one_came), (2, two_came)):
            add_blocks(held[chain], came, came.shape[0])
            halve(chain, 0).start()
        w_sum[...] = jnp.zeros_like(w_sum)
        gain_sum[...] = jnp.zeros_like(gain_sum)
        w_nat[...] = w_t_ref[...].T

    gain = gain_ref[...]
    x = side_by_side(x_ref).astype(F32)
    rstd = lax.rsqrt(jnp.mean(x * x, axis=0, keepdims=True) + eps_norm)
    scaled_x = x * rstd
    normed = (scaled_x * gain).astype(BF16)
    dlins = dq_one, dq_two, dk_one, dk_two, dv_one, dv_two
    dlin = jnp.concatenate([ref[...] for ref in dlins], axis=0)
    w_sum[...] += dot(dlin, normed, 1, 1)
    dnormed = dot(w_nat[...], dlin, 1, 0)
    product = dnormed * scaled_x
    gain_sum[...] += sum(product[:, c : c + lanes] for c in range(0, product.shape[1], lanes))
    scaled = dnormed * gain
    pull = jnp.mean(scaled * x, axis=0, keepdims=True)
    total = side_by_side(dmid_ref) + rstd * scaled - scaled_x * (rstd * rstd * pull)
    pair = across(my_seq // 2, steps - 1 - step, seq // 2)
    block = din.shape[2]
    for i in range(2):
        din[2 * pair + i] = total[:, block * i : block * (i + 1)].astype(BF16)

    def move(away):
        peer = seq_peer(my_dp, my_seq, away, seq)
        return pltpu.make_async_remote_copy(
            src_ref=din.at[peer[1]],
            dst_ref=out_ref.at[my_seq],
            send_sem=d_send.at[away - 1],
            recv_sem=d_recv.at[away - 1],
            device_id=peer,
            device_id_type=pl.DeviceIdType.MESH,
        )

    @pl.when(step == 0)
    def _():
        for away in range(seq - 2, seq):
            move(away).start()

    @pl.when(step == max(steps - 2, 0))
    def _():
        for chain in (1, 2):
            take(chain, 0)

    @pl.when(step == steps - 1)
    def _():
        for away in range(seq // 2, seq - 2):
            move(away).start()
        move(1).start()
        own = pltpu.make_async_copy(din.at[my_seq], out_ref.at[my_seq], own_sem)
        own.start()
        blank = jnp.zeros((lanes - q_cols - 2 * kv_cols, width), F32)
        for s in range(seq):
            first = width + kv_cols * s
            piece = jnp.concatenate(
                [
                    w_sum[q_cols * s : q_cols * (s + 1), :],
                    w_sum[first : first + kv_cols, :],
                    w_sum[first + kv_width : first + kv_width + kv_cols, :],
                    blank,
                ],
                axis=0,
            ).T.astype(BF16)
            for d in range(dp):
                packed[away_place(orders[0], d, s, my_dp, my_seq)] = piece[rows * d : rows * (d + 1)]
        gain_row = jnp.sum(gain_sum[...].T, axis=0, keepdims=True)
        gain_held[0] = jnp.concatenate(
            [gain_row, other_gain_ref[...], jnp.zeros((6, width), F32)], axis=0
        )
        turns = len(orders[0])
        gain_copies = [
            pltpu.make_async_remote_copy(
                src_ref=gain_held.at[turn],
                dst_ref=gain_landed.at[turn],
                send_sem=g_send.at[turn],
                recv_sem=g_recv.at[turn],
                device_id=stage_peer(my_dp, my_seq, orders[0][turns - 1 - turn]),
                device_id_type=pl.DeviceIdType.MESH,
            )
            for turn in range(turns)
        ]
        halve(0, 0).start()
        gain_copies[0].start()
        for turn in range(turns):
            gain_copies[turn].wait_recv()
            gain_held[turn + 1] = gain_held[turn] + gain_landed[turn]
            if turn + 1 < turns:
                gain_copies[turn + 1].start()
            take(0, turn)
            if turn == turns - 4:
                for chain in (1, 2):
                    take(chain, 1)
                for away in range(2, seq // 2):
                    move(away).start()
            if turn == turns - 3:
                for chain in (1, 2):
                    take(chain, 2)
        gains_ref[...] = gain_held[turns]
        qkv_ref[...], one_ref[...], two_ref[...] = result(0), result(1), result(2)
        for copy in gain_copies:
            copy.wait_send()
        for chain in range(3):
            for turn in range(len(orders[chain])):
                halve(chain, turn).wait_send()
        for away in range(1, seq):
            move(away).wait()
        own.wait()


def finish(x, dmid, dlins, gain, w_t, other_gain, keep_one, keep_two, came_one, came_two):
    blocks, width, block = x.shape
    tokens = blocks * block
    feats = w_t.shape[0]
    kv_width = (feats - width) // 2
    lanes = keep_one.shape[2]
    dp, seq = lax.axis_size("dp"), lax.axis_size("seq")
    rows = width // dp
    stages = len(all_stages(dp, seq))

    def pair(i):
        return across(lax.axis_index("seq") // 2, seq // 2 - 1 - i, seq // 2)

    tok = pl.BlockSpec((2, width, block), lambda i: (pair(i), 0, 0))
    col = lambda rows: pl.BlockSpec((rows, 2 * block), lambda i: (0, pair(i)))
    once = lambda shape: pl.BlockSpec(shape, lambda i: (0,) * len(shape), pipeline_mode=pl.Buffered(1))
    hbm = pl.BlockSpec(memory_space=pl.ANY)
    small = [(8, width), (rows, lanes), keep_one.shape[1:], keep_two.shape[1:]]
    return pl.pallas_call(
        functools.partial(finish_kernel, dp=dp, seq=seq, kv_width=kv_width),
        grid=(blocks // 2,),
        in_specs=[
            tok, tok, *[col(d.shape[0]) for d in dlins],
            once((width, 1)), once((feats, width)), once((1, width)), hbm, hbm, hbm, hbm,
        ],
        out_specs=[hbm] + [once(shape) for shape in small],
        out_shape=[jax.ShapeDtypeStruct(x.shape, BF16)] + [jax.ShapeDtypeStruct(shape, F32) for shape in small],
        scratch_shapes=[
            pltpu.VMEM((width, feats), BF16),
            pltpu.VMEM((feats, width), F32),
            pltpu.VMEM((width, lanes), F32),
            pltpu.VMEM(x.shape, BF16),
            pltpu.VMEM((dp * seq, rows, lanes), BF16),
            pltpu.VMEM((dp * seq, rows, lanes), BF16),
            *[pltpu.VMEM(keep_one.shape, BF16)] * 3,
            *[pltpu.VMEM(keep_two.shape, BF16)] * 3,
            pltpu.VMEM((stages + 1, 8, width), F32),
            pltpu.VMEM((stages, 8, width), F32),
            pltpu.SemaphoreType.DMA,
            pltpu.SemaphoreType.DMA((seq - 1,)),
            pltpu.SemaphoreType.DMA((seq - 1,)),
            pltpu.SemaphoreType.DMA((3, stages)),
            pltpu.SemaphoreType.DMA((3, stages)),
            pltpu.SemaphoreType.DMA((stages,)),
            pltpu.SemaphoreType.DMA((stages,)),
            pltpu.SemaphoreType.DMA((4,)),
        ],
        compiler_params=pltpu.CompilerParams(
            collective_id=2, has_side_effects=True, vmem_limit_bytes=VMEM_BYTES
        ),
        cost_estimate=pl.CostEstimate(
            flops=4 * tokens * width * feats, bytes_accessed=tokens * width * 12, transcendentals=0
        ),
        name="finish",
    )(x, dmid, *dlins, gain, w_t, other_gain, keep_one, keep_two, came_one, came_two)


def deliver_kernel(
    din_ref, gains_ref, qkv_ref, one_ref, two_ref,
    out_ref, gain_one, gain_two, q_ref, k_ref, v_ref, o_ref, gate_ref, up_ref, down_ref,
):
    out_ref[...] = din_ref[...].astype(F32)

    @pl.when(pl.program_id(0) == 0)
    def _():
        rows, q_cols = q_ref.shape
        kv_cols, lanes = k_ref.shape[0], qkv_ref.shape[1]
        spare = gate_ref.shape[1] - lanes
        padded = -(-q_cols // 16) * 16
        gain_one[...] = gains_ref[0]
        gain_two[...] = gains_ref[1]
        qkv = qkv_ref[...]
        turned = qkv.T
        q_ref[...] = qkv[:, :q_cols]
        k_ref[...] = turned[q_cols : q_cols + kv_cols]
        v_ref[...] = turned[q_cols + kv_cols : q_cols + 2 * kv_cols]
        o_ref[...] = one_ref[:rows, :q_cols]
        both = two_ref[:rows]
        gate_ref[...] = jnp.concatenate([one_ref[rows : 2 * rows], both[:, :spare]], axis=1)
        up_ref[...] = jnp.concatenate([one_ref[2 * rows : 3 * rows], both[:, spare : 2 * spare]], axis=1)
        for t in range(down_ref.shape[1] // lanes):
            at = rows + padded * t
            down_ref[:, lanes * t : lanes * (t + 1)] = two_ref[at : at + q_cols]


def deliver(din, gains, qkv, one, two, kv_cols, ff):
    blocks, width, block = din.shape
    rows = qkv.shape[0]
    dp, seq = lax.axis_size("dp"), lax.axis_size("seq")
    tok = pl.BlockSpec((2, width, block), lambda i: (i, 0, 0))
    once = lambda shape: pl.BlockSpec(shape, lambda i: (0,) * len(shape), pipeline_mode=pl.Buffered(1))
    small = [
        (width,),
        (width,),
        (rows, width // seq),
        (kv_cols, rows),
        (kv_cols, rows),
        (rows, width // seq),
        (rows, ff // seq),
        (rows, ff // seq),
        (width // seq, ff // dp),
    ]
    return pl.pallas_call(
        deliver_kernel,
        grid=(blocks // 2,),
        in_specs=[tok] + [once(a.shape) for a in (gains, qkv, one, two)],
        out_specs=[tok] + [once(shape) for shape in small],
        out_shape=[jax.ShapeDtypeStruct(shape, F32) for shape in [din.shape] + small],
        compiler_params=pltpu.CompilerParams(vmem_limit_bytes=VMEM_BYTES),
        name="deliver",
    )(din, gains, qkv, one, two)


def exchange(blocks):
    return lax.all_to_all(blocks, "seq", 0, 0, tiled=True)


def shards_sequences(
    hidden_in, span_order, attn_gain, q_weight, k_weight, v_weight, o_weight, mlp_gain,
    gate_weight, up_weight, down_weight, out_grad,
):
    lanes = 128
    seqs, slots, width = hidden_in.shape
    dp, seq = lax.axis_size("dp"), lax.axis_size("seq")
    tokens = slots * seq
    span = tokens // span_order.shape[0]
    heads = width // HD
    kv_heads = k_weight.shape[1] * seq // HD
    rows, q_cols = q_weight.shape
    kv_cols = k_weight.shape[1]
    ff = down_weight.shape[0] * dp
    ff_rows = down_weight.shape[0]
    padded = -(-q_cols // 16) * 16

    inv_freq = np.float32(rope_base ** (-2.0 * np.arange(HD // 2) / HD))
    inv, cos_t, sin_t, gain_one, gain_two, x, first_all, straight, hopping = bring(
        span_order,
        inv_freq[:, None],
        (attn_gain, mlp_gain),
        (q_weight, k_weight.T, v_weight.T, o_weight, gate_weight, up_weight, down_weight.T),
        hidden_in.transpose(0, 2, 1),
    )
    out_grad, x = lax.optimization_barrier((out_grad, x))
    masks = [sum(row_bits(i, dp)) for i in range(dp)]
    straight_all = [straight] + [over_rows(straight, m) for m in masks[1:]]
    hopping_all = [hopping if m == 0 else over_rows(hopping, m) if m & (m - 1) == 0 else None for m in masks]
    dy = exchange(out_grad.transpose(0, 2, 1))

    my_dp, my_seq = lax.axis_index("dp"), lax.axis_index("seq")
    where_first = arrival_order(all_stages(dp, seq), dp, seq, my_dp, my_seq)
    where_second = arrival_order(seq_stages(seq), dp, seq, my_dp, my_seq)[:seq]
    q_t, k_t, v_t, k_nat, v_nat, w_t = project_qkv(
        where_first, x, gain_one, first_all, cos_t, sin_t, heads, kv_heads, rows
    )
    o_t, logs = attention_forward(inv, q_t, k_nat, v_t, span)
    hopping_all, o_t = lax.optimization_barrier((hopping_all, o_t))
    for i, mask in enumerate(masks):
        if hopping_all[i] is None:
            low = mask & -mask
            hopping_all[i] = over_rows(hopping_all[masks.index(mask - low)], low)
    packs = [part for pair in zip(straight_all, hopping_all) for part in pair]
    out, dmid, do_t, keep_one, give_one, keep_two, give_two, gain_two_term = mlp_both(
        where_second, x, o_t, dy, gain_two, packs, ff
    )
    came_one, came_two = over_rows(give_one, 1), over_rows(give_two, 1)
    hidden_out = exchange(out).transpose(0, 2, 1)

    def back(queries, *heads):
        return attention_backward(
            inv, queries, k_t, k_nat, v_nat, o_t, do_t, logs, cos_t, sin_t, span, *heads
        )

    parts = [back(q_t, 0, 1)]
    came_one, came_two, parts[0] = lax.optimization_barrier((came_one, came_two, parts[0]))
    half = dp * seq // 4
    add = lambda a, b: (a.astype(F32) + b.astype(F32)).astype(BF16)
    sums = [
        (add(keep[:half], came[:half]), add(keep[half:], came[half:]))
        for keep, came in ((keep_one, came_one), (keep_two, came_two))
    ]
    sums, q_t = lax.optimization_barrier((sums, q_t))
    crossed = [
        lax.ppermute(high, axis, [(i, i ^ bit) for i in range(lax.axis_size(axis))])
        for (_, high), (axis, bit) in zip(sums, [chain[-1] for chain in rest_chains(dp, seq)])
    ]
    parts.append(back(q_t, 1, kv_heads - 1))
    dlins = [part[i] for i in range(3) for part in parts]
    din, gains, qkv_sum, one_sum, two_sum = finish(
        x, dmid, dlins, gain_one, w_t, gain_two_term, sums[0][0], sums[1][0], *crossed
    )
    grad_in, gain_one_sum, gain_two_sum, q_sum, k_sum, v_sum, o_sum, gate_sum, up_sum, down_sum = deliver(
        din, gains, qkv_sum, one_sum, two_sum, kv_cols, ff
    )
    return (
        hidden_out,
        grad_in.transpose(0, 2, 1),
        gain_one_sum,
        q_sum,
        k_sum.T,
        v_sum.T,
        o_sum,
        gain_two_sum,
        gate_sum,
        up_sum,
        down_sum.T,
    )


def shards(*args):
    seqs, spans = args[0].shape[0], args[1].shape[0]
    if seqs == lax.axis_size("seq") and spans % 4 == 0:
        return shards_sequences(*args)
    return shards_general(*args)


def solution(mesh):
    placed = (
        P("dp", "seq", None),
        P(),
        P(),
        P("dp", "seq"),
        P("dp", "seq"),
        P("dp", "seq"),
        P("dp", "seq"),
        P(),
        P("dp", "seq"),
        P("dp", "seq"),
        P("dp", "seq"),
        P("dp", "seq", None),
    )
    return jax.shard_map(
        shards,
        mesh=mesh,
        in_specs=placed,
        out_specs=(
            P("dp", "seq", None),
            P("dp", "seq", None),
            P(),
            P("dp", "seq"),
            P("dp", "seq"),
            P("dp", "seq"),
            P("dp", "seq"),
            P(),
            P("dp", "seq"),
            P("dp", "seq"),
            P("dp", "seq"),
        ),
        check_vma=False,
    )
```
